32 devices in a mesh: rows: 16 (over z, y, core), heads: 2 (over x).
Axes of the slice: x: 2, y: 2, z: 4, core: 2. Of those that a mesh axis runs over, the one named last changes fastest.
Arguments:
- tokens: bfloat16 [8192, 1152], P(('rows', 'heads')), may hold values from -6 to 6
- cond: bfloat16 [64, 1152], P('rows'), may hold values from -6 to 6
- image_of: int32 [16, 512], P('rows'), may hold values from 0 to 63, as said below
- grid_row: int32 [16, 512], P('rows'), may hold values from 0 to 63, as said below
- grid_col: int32 [16, 512], P('rows'), may hold values from 0 to 15, as said below
- ada_weight: bfloat16 [2, 1152, 6912], P(None, 'rows', 'heads'), may hold values from -0.1875 to 0.1875
- ada_bias: bfloat16 [2, 6912], P(None, 'heads'), may hold values from -3 to 3
- qkv_weight: bfloat16 [2, 1152, 3456], P(None, 'rows', 'heads'), may hold values from -0.1875 to 0.1875
- qkv_bias: bfloat16 [2, 3456], P(None, 'heads'), may hold values from -3 to 3
- proj_weight: bfloat16 [2, 1152, 1152], P(None, 'heads', 'rows'), may hold values from -2 to 2
- gu_weight: bfloat16 [2, 1152, 2, 3072], P(None, 'rows', None, 'heads'), may hold values from -0.1875 to 0.1875
- down_weight: bfloat16 [2, 3072, 1152], P(None, 'heads', 'rows'), may hold values from -0.109375 to 0.109375
- cotangent: bfloat16 [8192, 1152], P(('rows', 'heads')), may hold values from -6 to 6
Outputs:
- block_out: bfloat16 [8192, 1152], P(('rows', 'heads'))
- tokens_grad: float32 [8192, 1152], P(('rows', 'heads'))
- cond_grad: float32 [64, 1152], P('rows')
- ada_grad: float32 [2, 1152, 6912], P(None, 'rows', 'heads')
- ada_bias_grad: float32 [2, 6912], P(None, 'heads')
- qkv_grad: float32 [2, 1152, 3456], P(None, 'rows', 'heads')
- qkv_bias_grad: float32 [2, 3456], P(None, 'heads')
- proj_grad: float32 [2, 1152, 1152], P(None, 'heads', 'rows')
- gu_grad: float32 [2, 1152, 2, 3072], P(None, 'rows', None, 'heads')
- down_grad: float32 [2, 3072, 1152], P(None, 'heads', 'rows')
The draws below stay inside these ranges and needn't reach their ends.
Inputs may be any that keep to these rules, and one draw needn't show every extreme that they name: `image_of`: packed row r holds 4 images numbered 4 * r to 4 * r + 3 in increasing order, each a run of consecutive tokens; every row has one image of 256 tokens and one of 64 tokens, and its other images lie between these lengths. `grid_row`: the token's place within its image divided by the image's width, rounded down; each image has one width from 4 to 16, and in every row the image of 256 tokens is 4 wide. `grid_col`: the token's place within its image modulo the image's width; in every row the image of 64 tokens is 16 wide.
All inputs are finite; a program needn't handle non-finite values.
Results may differ from the reference program's by a relative error of at most 0.03.
Values may be sent and summed in bfloat16 or wider, within the bound.
A program may use at most 256 MiB of HBM per device.

```python
import jax
import jax.numpy as jnp
from jax import lax

D = 1152
HEADS = 16
HD = 72
FF = 3072
BLOCKS = 2
ROW_LEN = 512
IMG_ROW = 4
ROWS = 16
TOKENS = 8192
IMAGES = 64


def shuffle(sub_key):
    return jax.random.permutation(sub_key, IMG_ROW)


def packing(key):
    subkeys = jax.random.split(key, 3)
    remainder = ROW_LEN - ROW_LEN // 2 - ROW_LEN // 8
    even_share = remainder // 2
    wobble = jax.random.randint(subkeys[0], (ROWS, 1), 0, remainder // 8 + 1).astype(jnp.int32)
    middle = jnp.concatenate([even_share + wobble, even_share - wobble], axis=1)
    middle = middle.at[:, 0].add(remainder - 2 * even_share)
    lengths = jnp.concatenate([jnp.full((ROWS, 1), ROW_LEN // 2, jnp.int32), jnp.full((ROWS, 1), ROW_LEN // 8, jnp.int32), middle], axis=1)
    widest = min(16, ROW_LEN // 8)
    other_widths = jax.random.randint(subkeys[2], (ROWS, IMG_ROW - 2), 4, widest + 1).astype(jnp.int32)
    widths = jnp.concatenate([jnp.full((ROWS, 1), 4, jnp.int32), jnp.full((ROWS, 1), widest, jnp.int32), other_widths], axis=1)
    ordering = jax.vmap(shuffle)(jax.random.split(subkeys[1], ROWS))
    lengths = jnp.take_along_axis(lengths, ordering, axis=1)
    widths = jnp.take_along_axis(widths, ordering, axis=1)
    run_ends = jnp.cumsum(lengths, axis=1)
    starts = run_ends - lengths
    positions = jnp.arange(ROW_LEN, dtype=jnp.int32)
    segment = jnp.sum((positions[None, :, None] >= run_ends[:, None, :]).astype(jnp.int32), axis=2)
    offset = positions[None, :] - jnp.take_along_axis(starts, segment, axis=1)
    width_tok = jnp.take_along_axis(widths, segment, axis=1)
    image_ids = segment + IMG_ROW * jnp.arange(ROWS, dtype=jnp.int32)[:, None]
    return (image_ids, offset // width_tok, offset % width_tok)


def draw_image_of(key, part):
    return packing(key)[0]


def draw_grid_row(key, part):
    return packing(key)[1]


def draw_grid_col(key, part):
    return packing(key)[2]


def block_levels(own_key, dims, shards, low, largest):
    level = 1.0
    for dim, blocks in shards:
        steps = jax.random.uniform(jax.random.fold_in(jax.random.fold_in(own_key, 6), dim), (blocks,), jnp.float32, low / len(shards), largest / len(shards))
        level = level * jnp.repeat(jnp.exp(steps), dims[dim] // blocks).reshape((-1,) + (1,) * (len(dims) - 1 - dim))
    return level


def centred(key, dims, spread, most, shards=(), held_as=jnp.bfloat16):
    loudness = block_levels(key, dims, shards, -0.22, 0.18) if shards else 1.0
    values = jax.random.normal(key, dims, jnp.float32) * spread * loudness
    return jnp.minimum(jnp.maximum(values, -most), most).astype(held_as)


def setup_inputs(seed: int = 0) -> dict:
    key_list = jax.random.split(jax.random.key(seed), 14)
    tokens = centred(key_list[0], (TOKENS, D), 1.0, 6.0, ((0, 32),))
    cond = centred(key_list[1], (IMAGES, D), 1.0, 6.0, ((0, 16),))
    image_of = draw_image_of(jax.random.fold_in(key_list[13], 71), 0)
    grid_row = draw_grid_row(jax.random.fold_in(key_list[13], 71), 0)
    grid_col = draw_grid_col(jax.random.fold_in(key_list[13], 71), 0)
    ada_weight = centred(key_list[5], (BLOCKS, D, 6 * D), D ** -0.5, 0.1875, ((1, 16), (2, 2)))
    ada_bias = centred(key_list[6], (BLOCKS, 6 * D), 0.5, 3.0, ((1, 2),))
    qkv_weight = centred(key_list[7], (BLOCKS, D, 3 * D), D ** -0.5, 0.1875, ((1, 16), (2, 2)))
    qkv_bias = centred(key_list[8], (BLOCKS, 3 * D), 0.5, 3.0, ((1, 2),))
    proj_weight = centred(key_list[9], (BLOCKS, D, D), (max(D // 128, 1)) ** -0.5, 2.0, ((1, 2), (2, 16)))
    gu_weight = centred(key_list[10], (BLOCKS, D, 2, FF), D ** -0.5, 0.1875, ((1, 16), (3, 2)))
    down_weight = centred(key_list[11], (BLOCKS, FF, D), FF ** -0.5, 0.109375, ((1, 2), (2, 16)))
    cotangent = centred(key_list[12], (TOKENS, D), 1.0, 6.0, ((0, 32),))
    return {"tokens": tokens, "cond": cond, "image_of": image_of, "grid_row": grid_row, "grid_col": grid_col, "ada_weight": ada_weight, "ada_bias": ada_bias, "qkv_weight": qkv_weight, "qkv_bias": qkv_bias, "proj_weight": proj_weight, "gu_weight": gu_weight, "down_weight": down_weight, "cotangent": cotangent}


@jax.custom_vjp
def low(v):
    return lax.optimization_barrier(v.astype(jnp.bfloat16)).astype(jnp.float32)

@jax.custom_vjp
def low_back(v):
    return v

def low_keep(v):
    return (low(v), None)

def low_pass(kept, grad):
    return (grad,)

def back_keep(v):
    return (v, None)

def back_low(kept, grad):
    return (low(grad),)
low.defvjp(low_keep, low_pass)
low_back.defvjp(back_keep, back_low)
epsilon = 1e-06
theta_base = 10000.0
highest = lax.Precision.HIGHEST

def matmul_hi(left_side, other):
    return jnp.dot(left_side, other, precision=highest)

def normalize(values):
    center = values - lax.optimization_barrier(jnp.mean(values, axis=-1, keepdims=True))
    return center * lax.rsqrt(lax.optimization_barrier(jnp.mean(center * center, axis=-1, keepdims=True)) + epsilon)

def angles(coords, quarter):
    frequency = theta_base ** (-jnp.arange(quarter, dtype=jnp.float32) / quarter)
    return coords.astype(jnp.float32)[..., None] * frequency

def rotate_pair(section, angle):
    half_width = section.shape[-1] // 2
    lower_half = section[..., :half_width]
    upper_half = section[..., half_width:]
    cosine = jnp.cos(angle)
    sine_term = jnp.sin(angle)
    return jnp.concatenate([lower_half * cosine - upper_half * sine_term, upper_half * cosine + lower_half * sine_term], axis=-1)

def rotary(vectors, row_angle, col_angle):
    half_width = vectors.shape[-1] // 2
    return jnp.concatenate([rotate_pair(vectors[..., :half_width], row_angle[:, :, None, :]), rotate_pair(vectors[..., half_width:], col_angle[:, :, None, :])], axis=-1)

def attend_row(row_data):
    queries, key_rows, value_rows, image_ids = row_data
    scores = low_back(jnp.einsum('qhe,khe->hqk', queries, key_rows, precision=highest) * HD ** (-0.5))
    same_image = image_ids[:, None] == image_ids[None, :]
    scores = jnp.where(same_image[None], scores, -1e+30)
    weights = low(jax.nn.softmax(scores, axis=-1))
    return jnp.einsum('hqk,khe->qhe', weights, value_rows, precision=highest)

def block_forward(residual, token_mods, qkv_w, qkv_b, proj_w, gu_w, down_w, geometry):
    image_ids, row_angle, col_angle = geometry
    shift_attn, scale_attn, gate_attn, shift_mlp, scale_mlp, gate_mlp = jnp.split(token_mods, 6, axis=1)
    input_attn = low(normalize(residual) * (1.0 + scale_attn) + shift_attn)
    packed = low_back(matmul_hi(input_attn, qkv_w) + qkv_b)
    packed = packed.reshape(ROWS, ROW_LEN, HEADS, 3, HD)
    queries = low(rotary(packed[:, :, :, 0], row_angle, col_angle))
    key_rows = low(rotary(packed[:, :, :, 1], row_angle, col_angle))
    value_rows = low(packed[:, :, :, 2])
    attended = lax.map(jax.checkpoint(attend_row), (queries, key_rows, value_rows, image_ids))
    attended = low(low_back(attended)).reshape(TOKENS, D)
    branch = low_back(matmul_hi(attended, proj_w))
    middle = residual + gate_attn * branch
    input_mlp = low(normalize(middle) * (1.0 + scale_mlp) + shift_mlp)
    gate_up = low_back(matmul_hi(input_mlp, gu_w.reshape(D, 2 * FF)))
    hidden = low(jax.nn.silu(gate_up[:, :FF]) * gate_up[:, FF:])
    mlp_out = low_back(matmul_hi(hidden, down_w))
    return middle + gate_mlp * mlp_out

def reference(tokens, cond, image_of, grid_row, grid_col, ada_weight, ada_bias, qkv_weight, qkv_bias, proj_weight, gu_weight, down_weight, cotangent):
    floats = tuple((item.astype(jnp.float32) for item in (tokens, cond, ada_weight, ada_bias, qkv_weight, qkv_bias, proj_weight, gu_weight, down_weight)))
    quarter = HD // 4
    geometry = (image_of, angles(grid_row, quarter), angles(grid_col, quarter))
    flat_images = image_of.reshape(-1)

    def forward(residual, cond_f, ada_w, ada_b, qkv_w, qkv_b, proj_w, gu_w, down_w):
        cond_act = low(jax.nn.silu(cond_f))
        for block_index in range(BLOCKS):
            modulation = low_back(matmul_hi(cond_act, ada_w[block_index]) + ada_b[block_index])
            token_mods = jnp.take(modulation, flat_images, axis=0)
            residual = block_forward(residual, token_mods, qkv_w[block_index], qkv_b[block_index], proj_w[block_index], gu_w[block_index], down_w[block_index], geometry)
        return residual
    result, pullback = jax.vjp(forward, *floats)
    gradients = pullback(cotangent.astype(jnp.float32))
    return (result.astype(jnp.bfloat16), gradients[0], gradients[1], gradients[2], gradients[3], gradients[4], gradients[5], gradients[6], gradients[7], gradients[8])
```

```python
import jax
import jax.numpy as jnp
from jax import lax
from jax.sharding import PartitionSpec as P

HD = 72


epsilon = 1e-06
theta_base = 10000.0
highest = lax.Precision.HIGHEST


def normalize(values):
    center = values - jnp.mean(values, axis=-1, keepdims=True)
    inverse = lax.rsqrt(jnp.mean(center * center, axis=-1, keepdims=True) + epsilon)
    return (center * inverse, inverse)


def norm_back(incoming, normed, inverse):
    return inverse * (
        incoming
        - jnp.mean(incoming, axis=-1, keepdims=True)
        - normed * jnp.mean(incoming * normed, axis=-1, keepdims=True)
    )


def lead_dot(operand, other):
    return lax.dot_general(
        operand, other, (((0,), (0,)), ((), ())), preferred_element_type=jnp.float32
    )


def tail_dot(operand, other):
    return lax.dot_general(
        operand, other, (((1,), (1,)), ((), ())), preferred_element_type=jnp.float32
    )


def angles(coords, quarter):
    frequency = theta_base ** (-jnp.arange(quarter, dtype=jnp.float32) / quarter)
    return coords.astype(jnp.float32)[..., None] * frequency


def row_factors():
    size = lax.axis_size("rows")
    return (4, size // 8, 2)


def row_place():
    sizes = row_factors()
    index = lax.axis_index("rows")
    return (index // (sizes[1] * sizes[2]), (index // sizes[2]) % sizes[1], index % sizes[2])


def row_move(value, dim, step):
    sizes = row_factors()
    pairs = []
    for target in range(lax.axis_size("rows")):
        place = [target // (sizes[1] * sizes[2]), (target // sizes[2]) % sizes[1], target % sizes[2]]
        place[dim] = (place[dim] + step) % sizes[dim]
        pairs.append(((place[0] * sizes[1] + place[1]) * sizes[2] + place[2], target))
    return lax.ppermute(value, "rows", pairs)


def head_move(value, flip):
    size = lax.axis_size("heads")
    return lax.ppermute(value, "heads", [(index, index ^ flip) for index in range(size)])


def in_order(chunks, mine, axis):
    count = len(chunks)
    placed = []
    for slot in range(count):
        value = chunks[0]
        for step in range(1, count):
            value = jnp.where(mine == (slot - step) % count, chunks[step], value)
        placed.append(value)
    return jnp.stack(placed, axis=axis)


def gather_rows(shard):
    sizes = row_factors()
    place = row_place()
    value = shard
    for dim in range(3):
        chunks = [value] + [row_move(value, dim, step) for step in range(1, sizes[dim])]
        value = in_order(chunks, place[dim], dim)
    return value.reshape(-1, shard.shape[-1])


def scatter_rows(parts):
    sizes = row_factors()
    place = row_place()
    pieces = [part.reshape(sizes + (-1, part.shape[-1])) for part in parts]
    for dim in (2, 1, 0):
        count = sizes[dim]

        def pick(step):
            taken = [
                lax.dynamic_index_in_dim(piece, (place[dim] + step) % count, dim, keepdims=False)
                for piece in pieces
            ]
            return taken[0] if len(taken) == 1 else jnp.concatenate(taken, axis=-1)

        arrived = [row_move(pick(step), dim, count - step) for step in range(1, count)]
        total = pick(0).astype(jnp.float32)
        for item in arrived:
            total = total + item.astype(jnp.float32)
        pieces = [total.astype(jnp.bfloat16) if dim else total]
    return pieces[0]


def rope_parts(coords):
    angle = angles(coords, HD // 4)
    return jnp.cos(angle), jnp.sin(angle)


def turn(vectors, geometry, sign):
    row_cos, row_sin, col_cos, col_sin = [item[:, :, None, :] for item in geometry]
    quarter = HD // 4
    a, b, c, d = [vectors[..., quarter * i : quarter * (i + 1)] for i in range(4)]
    return jnp.concatenate(
        [
            a * row_cos - b * (sign * row_sin),
            b * row_cos + a * (sign * row_sin),
            c * col_cos - d * (sign * col_sin),
            d * col_cos + c * (sign * col_sin),
        ],
        axis=-1,
    )


def masked_scores(queries, key_rows, image_ids):
    scores = jnp.einsum(
        "rqhe,rkhe->rhqk", queries, key_rows, preferred_element_type=jnp.float32
    ) * HD ** (-0.5)
    same_image = image_ids[:, :, None] == image_ids[:, None, :]
    return jnp.where(same_image[:, None], scores, -1e30)


def attend(queries, key_rows, value_rows, image_ids):
    scores = masked_scores(queries, key_rows, image_ids)
    maximum = jnp.max(scores, axis=-1, keepdims=True)
    scaled_exp = jnp.exp(scores - maximum)
    denominator = jnp.sum(scaled_exp, axis=-1, keepdims=True)
    weights = (scaled_exp / denominator).astype(jnp.bfloat16)
    attended = jnp.einsum("rhqk,rkhe->rqhe", weights, value_rows, preferred_element_type=jnp.float32)
    return (attended.astype(jnp.bfloat16), (maximum + jnp.log(denominator))[..., 0])


def attend_back(queries, key_rows, value_rows, image_ids, logsum, grad_attended):
    score_scale = HD ** (-0.5)
    probs = jnp.exp(masked_scores(queries, key_rows, image_ids) - logsum[..., None])
    weights = probs.astype(jnp.bfloat16)
    grad_value = jnp.einsum(
        "rhqk,rqhe->rkhe", weights, grad_attended, preferred_element_type=jnp.float32
    )
    grad_probs = jnp.einsum(
        "rqhe,rkhe->rhqk", grad_attended, value_rows, preferred_element_type=jnp.float32
    )
    inner_sum = jnp.sum(probs * grad_probs, axis=-1, keepdims=True)
    grad_scores = (probs * (grad_probs - inner_sum)).astype(jnp.bfloat16)
    grad_query = (
        jnp.einsum("rhqk,rkhe->rqhe", grad_scores, key_rows, preferred_element_type=jnp.float32)
        * score_scale
    )
    grad_key = (
        jnp.einsum("rhqk,rqhe->rkhe", grad_scores, queries, preferred_element_type=jnp.float32)
        * score_scale
    )
    return (grad_query, grad_key, grad_value)


def spread(values):
    return jnp.concatenate(
        [values] + [head_move(values, flip) for flip in range(1, lax.axis_size("heads"))], axis=0
    )


def collect(operand, product, own_rows):
    total = None
    arrived = []
    for flip in range(1, lax.axis_size("heads")):
        partial = product(operand[flip * own_rows : (flip + 1) * own_rows])
        arrived.append(head_move(partial.astype(jnp.bfloat16), flip))
    total = product(operand[:own_rows])
    for item in arrived:
        total = total + item.astype(jnp.float32)
    return total


def plain_dot(operand, other):
    return jnp.dot(operand, other, preferred_element_type=jnp.float32)


def piece_of(mods, picks, index):
    width = mods.shape[1] // 6
    value = mods[:, index * width : (index + 1) * width]
    total = jnp.zeros((picks.shape[0], width), jnp.float32)
    for image in range(mods.shape[0]):
        total = jnp.where(picks[:, None] == image, value[image][None, :], total)
    return total


def block_forward(residual, pieces, qkv_full, qkv_b, proj_t, gu_full, down_t, image_ids, geometry):
    shift_attn, scale_attn, gate_attn, shift_mlp, scale_mlp, gate_mlp = pieces
    own_rows = residual.shape[0]
    count_rows, row_len = image_ids.shape
    normed_attn, inverse_attn = normalize(residual)
    input_attn = spread((normed_attn * (1.0 + scale_attn) + shift_attn).astype(jnp.bfloat16))
    packed = plain_dot(input_attn, qkv_full) + qkv_b
    heads_here = packed.shape[1] // (3 * HD)
    packed = packed.reshape(count_rows, row_len, heads_here, 3, HD)
    queries = turn(packed[:, :, :, 0], geometry, 1.0).astype(jnp.bfloat16)
    key_rows = turn(packed[:, :, :, 1], geometry, 1.0).astype(jnp.bfloat16)
    value_rows = packed[:, :, :, 2].astype(jnp.bfloat16)
    attended, logsum = attend(queries, key_rows, value_rows, image_ids)
    attended = attended.reshape(count_rows * row_len, heads_here * HD)
    branch = collect(attended, lambda rows: tail_dot(rows, proj_t), own_rows)
    middle = residual + gate_attn * branch
    normed_mlp, inverse_mlp = normalize(middle)
    input_mlp = spread((normed_mlp * (1.0 + scale_mlp) + shift_mlp).astype(jnp.bfloat16))
    gate_up = plain_dot(input_mlp, gu_full)
    hidden_width = gate_up.shape[1] // 2
    gate_part = gate_up[:, :hidden_width]
    up_part = gate_up[:, hidden_width:]
    hidden = (jax.nn.silu(gate_part) * up_part).astype(jnp.bfloat16)
    mlp_out = collect(hidden, lambda rows: tail_dot(rows, down_t), own_rows)
    result = middle + gate_mlp * mlp_out
    stored = (
        normed_attn,
        inverse_attn,
        input_attn,
        queries,
        key_rows,
        value_rows,
        logsum,
        attended,
        branch,
        normed_mlp,
        inverse_mlp,
        input_mlp,
        gate_part,
        up_part,
        hidden,
        mlp_out,
    )
    return (result, stored)


def block_backward(incoming, pieces, stored, qkv_full, proj_t, gu_full, down_t, image_ids, geometry):
    shift_attn, scale_attn, gate_attn, shift_mlp, scale_mlp, gate_mlp = pieces
    (
        normed_attn,
        inverse_attn,
        input_attn,
        queries,
        key_rows,
        value_rows,
        logsum,
        attended,
        branch,
        normed_mlp,
        inverse_mlp,
        input_mlp,
        gate_part,
        up_part,
        hidden,
        mlp_out,
    ) = stored
    own_rows = incoming.shape[0]
    count_rows, row_len = image_ids.shape
    grad_mlp = (gate_mlp * incoming).astype(jnp.bfloat16)
    grad_gate_mlp = incoming * mlp_out
    gathered_mlp = spread(grad_mlp)
    down_grad = lead_dot(gathered_mlp, hidden).astype(jnp.bfloat16)
    grad_hidden = plain_dot(gathered_mlp, down_t)
    logistic = jax.nn.sigmoid(gate_part)
    grad_gate_part = grad_hidden * up_part * logistic * (1.0 + gate_part * (1.0 - logistic))
    grad_up_part = grad_hidden * gate_part * logistic
    grad_gate_up = jnp.concatenate([grad_gate_part, grad_up_part], axis=1).astype(jnp.bfloat16)
    gu_grad = lead_dot(input_mlp, grad_gate_up).astype(jnp.bfloat16)
    gu_out = lax.psum_scatter(gu_grad, "rows", scatter_dimension=0, tiled=True).astype(jnp.float32)
    grad_input_mlp = collect(grad_gate_up, lambda rows: tail_dot(rows, gu_full), own_rows)
    grad_middle = incoming + norm_back(grad_input_mlp * (1.0 + scale_mlp), normed_mlp, inverse_mlp)
    grad_branch = (gate_attn * grad_middle).astype(jnp.bfloat16)
    grad_gate_attn = grad_middle * branch
    heads_here = queries.shape[2]
    gathered_branch = spread(grad_branch)
    proj_grad = lead_dot(gathered_branch, attended).astype(jnp.bfloat16)
    side = scatter_rows([down_grad, proj_grad])
    down_out, proj_out = side[:, : hidden.shape[1]], side[:, hidden.shape[1] :]
    grad_attended = plain_dot(gathered_branch, proj_t).astype(jnp.bfloat16)
    grad_attended = grad_attended.reshape(count_rows, row_len, heads_here, HD)
    grad_query, grad_key, grad_value = attend_back(
        queries, key_rows, value_rows, image_ids, logsum, grad_attended
    )
    grad_query = turn(grad_query, geometry, -1.0)
    grad_key = turn(grad_key, geometry, -1.0)
    grad_packed = (
        jnp.stack([grad_query, grad_key, grad_value], axis=3)
        .reshape(count_rows * row_len, heads_here * 3 * HD)
        .astype(jnp.bfloat16)
    )
    qkv_bias_grad = jnp.sum(grad_packed, axis=0, dtype=jnp.float32)
    qkv_grad = lead_dot(input_attn, grad_packed).astype(jnp.bfloat16)
    qkv_out = scatter_rows([qkv_grad])
    grad_input_attn = collect(grad_packed, lambda rows: tail_dot(rows, qkv_full), own_rows)
    grad_input = grad_middle + norm_back(
        grad_input_attn * (1.0 + scale_attn), normed_attn, inverse_attn
    )
    grad_mods = jnp.concatenate(
        [
            grad_input_attn,
            grad_input_attn * normed_attn,
            grad_gate_attn,
            grad_input_mlp,
            grad_input_mlp * normed_mlp,
            grad_gate_mlp,
        ],
        axis=1,
    )
    return (grad_input, grad_mods, (qkv_out, qkv_bias_grad, proj_out, gu_out, down_out))


def heads_in_order(value):
    index = lax.axis_index("heads")
    count = lax.axis_size("heads")
    chunks = [value] + [head_move(value, flip) for flip in range(1, count)]
    placed = []
    for slot in range(count):
        item = chunks[0]
        for flip in range(1, count):
            item = jnp.where(index == slot ^ flip, chunks[flip], item)
        placed.append(item)
    return jnp.stack(placed)


def heads_share(value):
    index = lax.axis_index("heads")
    count = lax.axis_size("heads")
    width = value.shape[-1] // count

    def part(flip):
        return lax.dynamic_slice_in_dim(value, (index ^ flip) * width, width, value.ndim - 1)

    arrived = [head_move(part(flip), flip) for flip in range(1, count)]
    total = part(0)
    for item in arrived:
        total = total + item
    return total


def shards(
    tokens,
    cond,
    image_of,
    grid_row,
    grid_col,
    ada_weight,
    ada_bias,
    qkv_weight,
    qkv_bias,
    proj_weight,
    gu_weight,
    down_weight,
    cotangent,
):
    own_rows = tokens.shape[0]
    image_count = cond.shape[0]
    block_count = qkv_weight.shape[0]
    row_size = lax.axis_size("rows")
    head_size = lax.axis_size("heads")
    head_index = lax.axis_index("heads")

    def device_order(values):
        parts = values.reshape(head_size, own_rows)
        picked = [
            lax.dynamic_index_in_dim(parts, head_index ^ flip, 0, keepdims=False)
            for flip in range(head_size)
        ]
        return jnp.concatenate(picked).reshape(values.shape)

    image_ids = device_order(image_of - lax.axis_index("rows") * image_count)
    own_images = image_ids.reshape(-1)[:own_rows]
    picker = (own_images[:, None] == jnp.arange(image_count, dtype=jnp.int32)[None, :]).astype(
        jnp.float32
    )
    geometry = lax.optimization_barrier(
        rope_parts(device_order(grid_row)) + rope_parts(device_order(grid_col))
    )
    qkv_full = [None] * block_count
    gu_full = [None] * block_count
    down_t = [None] * block_count
    proj_t = [None] * block_count
    shard_rows = qkv_weight.shape[1]
    for b in range(block_count):
        if b == 0:
            qkv_full[b] = lax.all_gather(qkv_weight[b], "rows", axis=0, tiled=True)
        else:
            qkv_full[b] = gather_rows(qkv_weight[b])
        gu_full[b] = lax.all_gather(
            gu_weight[b].reshape(shard_rows, -1), "rows", axis=0, tiled=True
        )
        side = gather_rows(jnp.concatenate([down_weight[b].T, proj_weight[b].T], axis=1))
        down_t[b] = side[:, : down_weight.shape[1]]
        proj_t[b] = side[:, down_weight.shape[1] :]
    cond_wide = cond.astype(jnp.float32)
    cond_act = jax.nn.silu(cond_wide).astype(jnp.bfloat16)
    cond_mine = lax.all_to_all(
        cond_act.reshape(image_count, row_size, -1).transpose(1, 0, 2), "rows", 0, 0
    ).reshape(row_size * image_count, -1)
    mod_partial = jnp.stack([plain_dot(cond_mine, ada_weight[b]) for b in range(block_count)], axis=1)
    mod_arrived = lax.all_to_all(
        mod_partial.reshape(row_size, image_count, block_count, -1), "rows", 0, 0
    )
    mod_local = jnp.sum(mod_arrived, axis=0) + ada_bias.astype(jnp.float32)[None]
    mod_all = heads_in_order(mod_local)
    modulation = [
        jnp.concatenate([mod_all[index, :, b] for index in range(head_size)], axis=1)
        for b in range(block_count)
    ]
    pieces = [
        [piece_of(modulation[b], own_images, index) for index in range(6)] for b in range(block_count)
    ]
    residual = tokens.astype(jnp.float32)
    stored_all = []
    for b in range(block_count):
        residual, stored = block_forward(
            residual,
            pieces[b],
            qkv_full[b],
            qkv_bias[b].astype(jnp.float32),
            proj_t[b],
            gu_full[b],
            down_t[b],
            image_ids,
            geometry,
        )
        stored_all.append(stored)
    block_out = residual.astype(jnp.bfloat16)
    incoming = cotangent.astype(jnp.float32)
    block_grads = [None] * block_count
    ada_grads = [None] * block_count
    ada_bias_grads = [None] * block_count
    cond_partial = 0.0
    for b in reversed(range(block_count)):
        incoming, grad_mods, gradients = block_backward(
            incoming,
            pieces[b],
            stored_all[b],
            qkv_full[b],
            proj_t[b],
            gu_full[b],
            down_t[b],
            image_ids,
            geometry,
        )
        image_sums = lax.dot_general(
            picker, grad_mods, (((0,), (0,)), ((), ())), precision=highest
        )
        image_grads = heads_share(image_sums).astype(jnp.bfloat16)
        all_grads = lax.all_gather(image_grads, "rows", axis=0, tiled=True)
        ada_grads[b] = lead_dot(cond_mine, all_grads)
        ada_bias_grads[b] = jnp.sum(all_grads, axis=0, dtype=jnp.float32)
        cond_partial = cond_partial + tail_dot(all_grads, ada_weight[b])
        block_grads[b] = gradients
    cond_parts = lax.all_to_all(
        cond_partial.astype(jnp.bfloat16).reshape(row_size, image_count, -1), "rows", 0, 0
    )
    cond_rows = cond_parts.transpose(1, 0, 2).reshape(image_count, -1).astype(jnp.float32)
    cond_total = cond_rows
    for flip in range(1, head_size):
        cond_total = cond_total + head_move(cond_rows.astype(jnp.bfloat16), flip).astype(jnp.float32)
    logistic = jax.nn.sigmoid(cond_wide)
    cond_grad = cond_total * logistic * (1.0 + cond_wide * (1.0 - logistic))
    qkv_bias_out = lax.psum(jnp.stack([item[1] for item in block_grads]), "rows")
    return (
        block_out,
        incoming,
        cond_grad,
        jnp.stack(ada_grads),
        jnp.stack(ada_bias_grads),
        jnp.stack([item[0] for item in block_grads]),
        qkv_bias_out,
        jnp.stack([item[2].T for item in block_grads]),
        jnp.stack([item[3].reshape(gu_weight.shape[1:]) for item in block_grads]),
        jnp.stack([item[4].T for item in block_grads]),
    )


def solution(mesh):
    in_specs = (
        P(("rows", "heads"), None),
        P("rows", None),
        P("rows", None),
        P("rows", None),
        P("rows", None),
        P(None, "rows", "heads"),
        P(None, "heads"),
        P(None, "rows", "heads"),
        P(None, "heads"),
        P(None, "heads", "rows"),
        P(None, "rows", None, "heads"),
        P(None, "heads", "rows"),
        P(("rows", "heads"), None),
    )
    out_specs = (
        P(("rows", "heads"), None),
        P(("rows", "heads"), None),
        P("rows", None),
        P(None, "rows", "heads"),
        P(None, "heads"),
        P(None, "rows", "heads"),
        P(None, "heads"),
        P(None, "heads", "rows"),
        P(None, "rows", None, "heads"),
        P(None, "heads", "rows"),
    )
    return jax.shard_map(shards, mesh=mesh, in_specs=in_specs, out_specs=out_specs, check_vma=False)
```

```python
import functools

import jax
import jax.numpy as jnp
from jax import lax
from jax.experimental import pallas as pl
from jax.experimental.pallas import tpu as pltpu
from jax.sharding import PartitionSpec as P

HD = 72


epsilon = 1e-06
theta_base = 10000.0
highest = lax.Precision.HIGHEST


def normalize(values):
    center = values - jnp.mean(values, axis=-1, keepdims=True)
    inverse = lax.rsqrt(jnp.mean(center * center, axis=-1, keepdims=True) + epsilon)
    return (center * inverse, inverse)


def norm_back(incoming, normed, inverse):
    return inverse * (
        incoming
        - jnp.mean(incoming, axis=-1, keepdims=True)
        - normed * jnp.mean(incoming * normed, axis=-1, keepdims=True)
    )


def lead_dot(operand, other):
    return lax.dot_general(
        operand, other, (((0,), (0,)), ((), ())), preferred_element_type=jnp.float32
    )


def tail_dot(operand, other):
    return lax.dot_general(
        operand, other, (((1,), (1,)), ((), ())), preferred_element_type=jnp.float32
    )


def angles(coords, quarter):
    frequency = theta_base ** (-jnp.arange(quarter, dtype=jnp.float32) / quarter)
    return coords.astype(jnp.float32)[..., None] * frequency


def head_move(value, flip):
    size = lax.axis_size("heads")
    return lax.ppermute(value, "heads", [(index, index ^ flip) for index in range(size)])


MESH = pl.DeviceIdType.MESH


class Place:
    def __init__(self, row_size, head_size):
        self.sizes = (4, row_size // 8, 2)
        index = lax.axis_index("rows")
        a, b, c = self.sizes
        self.mine = (index // (b * c), (index // c) % b, index % c)
        self.heads = head_size
        self.head = lax.axis_index("heads")

    def step(self, dim, by):
        return (self.mine[dim] + by + self.sizes[dim]) % self.sizes[dim]

    def row(self, a, b, c):
        return (a * self.sizes[1] + b) * self.sizes[2] + c

    def near(self, dim, by):
        at = list(self.mine)
        at[dim] = self.step(dim, by)
        return {"rows": self.row(*at)}

    def flip(self, by):
        return {"heads": self.head ^ by}

    def partners(self, with_heads):
        found = [self.near(dim, by) for dim in range(3) for by in range(1, self.sizes[dim])]
        if with_heads:
            found += [self.flip(by) for by in range(1, self.heads)]
        return found

    def greet(self, with_heads):
        barrier = pltpu.get_barrier_semaphore()
        found = self.partners(with_heads)
        for partner in found:
            pl.semaphore_signal(barrier, inc=1, device_id=partner, device_id_type=MESH)
        pl.semaphore_wait(barrier, len(found))


def gather_count(row_size):
    a, b, c = 4, row_size // 8, 2
    return 2 * (a - 1) + (2 * a - 1) * (2 * b - 1)


class Gather:
    def __init__(self, place, shard, out, send, recv, local):
        self.place, self.shard, self.out = place, shard, out
        self.send, self.recv = send, recv
        self.used = 0
        self.keep = pltpu.make_async_copy(shard, out.at[place.row(*place.mine)], local)
        a, b, _ = place.sizes
        self.hops, self.along_b, self.along_c = {}, {}, {}
        names = [(0, 0)] + [(way, k) for k in range(1, a) for way in (1, -1)]
        for way, k in names:
            if k:
                self.hops[way, k] = self.copy(way, k - 1, 0, place.near(0, way))
        for way, k in names:
            for j in range(1, b):
                self.along_b[way, k, j] = self.copy(way, k, 0, place.near(1, j))
        for way, k in names:
            for j in range(b):
                self.along_c[way, k, j] = self.copy(way, k, j, place.near(2, 1))

    def copy(self, way, k, j, device):
        place, slot = self.place, self.used
        self.used += 1
        index = place.row(place.step(0, -way * k), place.step(1, -j), place.mine[2])
        return pltpu.make_async_remote_copy(
            src_ref=self.shard if k == 0 and j == 0 else self.out.at[index],
            dst_ref=self.out.at[index],
            send_sem=self.send.at[slot],
            recv_sem=self.recv.at[slot],
            device_id=device,
            device_id_type=MESH,
        )

    def holds(self, way, k):
        at = self.place.mine[0]
        return at >= k if way > 0 else at < self.place.sizes[0] - k

    def hop(self, way, k):
        at = self.place.mine[0]
        last = self.place.sizes[0] - 1
        return (at < last) & (at >= k - 1) if way > 0 else (at > 0) & (at <= last - (k - 1))

    def begin(self):
        self.keep.start()
        for way in (1, -1):
            pl.when(self.hop(way, 1))(self.hops[way, 1].start)
        self.pass_on(0, 0)

    def pass_on(self, way, k):
        for j in range(1, self.place.sizes[1]):
            self.along_b[way, k, j].start()
        self.along_c[way, k, 0].start()

    def first(self, k):
        for way in (1, -1):

            @pl.when(self.holds(way, k))
            def _():
                self.hops[way, k].wait_recv()
                if k + 1 < self.place.sizes[0]:
                    pl.when(self.hop(way, k + 1))(self.hops[way, k + 1].start)
                self.pass_on(way, k)

    def each(self, way, k, action):
        if k:
            pl.when(self.holds(way, k))(action)
        else:
            action()

    def second(self):
        for way, k, j in self.along_b:

            def action():
                self.along_b[way, k, j].wait_recv()
                self.along_c[way, k, j].start()

            self.each(way, k, action)

    def finish(self):
        for way, k, j in self.along_c:

            def action():
                self.along_c[way, k, j].wait_recv()
                self.along_c[way, k, j].wait_send()

            self.each(way, k, action)
        for way, k, j in self.along_b:
            self.each(way, k, self.along_b[way, k, j].wait_send)
        for way, k in self.hops:
            pl.when(self.hop(way, k))(self.hops[way, k].wait_send)
        self.keep.wait()


def gather_all(items):
    count = len(items)
    items[0].begin()
    for step in range(count + 1):
        if step < count:
            items[step].first(1)
            if step + 1 < count:
                items[step + 1].begin()
            for k in range(2, items[step].place.sizes[0]):
                items[step].first(k)
        if step >= 1:
            items[step - 1].second()
    for item in items:
        item.finish()


def scatter_count(row_size):
    a, b, c = 4, row_size // 8, 2
    return a * b + a * (b - 1) + (a - 1)


class Scatter:
    def __init__(self, place, source, out, held, met, side, far, send, recv, load):
        self.place, self.source, self.out = place, source, out
        self.held, self.met, self.side, self.far = held, met, side, far
        self.send, self.recv, self.load = send, recv, load

    def remote(self, source, target, slot, device):
        return pltpu.make_async_remote_copy(
            src_ref=source,
            dst_ref=target,
            send_sem=self.send.at[slot],
            recv_sem=self.recv.at[slot],
            device_id=device,
            device_id_type=MESH,
        )

    def across(self, k, j):
        place = self.place
        a, b = place.step(0, k), place.step(1, j)
        other = place.step(2, 1)
        return self.remote(
            self.source.at[place.row(a, b, other)],
            self.met.at[a, b],
            k * place.sizes[1] + j,
            place.near(2, 1),
        )

    def fetch(self, k, j):
        place = self.place
        a, b = place.step(0, k), place.step(1, j)
        return pltpu.make_async_copy(
            self.source.at[place.row(a, b, place.mine[2])],
            self.held.at[a, b],
            self.load.at[k * place.sizes[1] + j],
        )

    def along_b(self, k, j):
        place = self.place
        a, b = place.step(0, k), place.step(1, j)
        base = place.sizes[0] * place.sizes[1]
        return self.remote(
            self.held.at[a, b],
            self.side.at[j - 1, a],
            base + (j - 1) * place.sizes[0] + k,
            place.near(1, j),
        )

    def along_a(self, k):
        place = self.place
        base = place.sizes[0] * (2 * place.sizes[1] - 1)
        return self.remote(
            self.held.at[place.step(0, k), place.mine[1]],
            self.far.at[k - 1],
            base + k - 1,
            place.near(0, k),
        )

    def order(self):
        a, b, _ = self.place.sizes
        return [(k, j) for j in list(range(1, b)) + [0] for k in list(range(1, a)) + [0]]

    def begin(self):
        for k, j in self.order():
            self.fetch(k, j).start()
            self.across(k, j).start()

    def first(self):
        place = self.place
        a, b, _ = place.sizes
        for j in range(1, b):
            for k in list(range(1, a)) + [0]:
                self.fetch(k, j).wait()
                self.across(k, j).wait_recv()
                at = (place.step(0, k), place.step(1, j))
                self.held[at] = (
                    self.held[at].astype(jnp.float32) + self.met[at].astype(jnp.float32)
                ).astype(self.held.dtype)
                self.along_b(k, j).start()

    def total(self, k):
        place = self.place
        a, b = place.step(0, k), place.mine[1]
        value = self.held[a, b].astype(jnp.float32) + self.met[a, b].astype(jnp.float32)
        for j in range(1, place.sizes[1]):
            value = value + self.side[j - 1, a].astype(jnp.float32)
        return value

    def second(self):
        place = self.place
        a, b, _ = place.sizes
        for k in list(range(1, a)) + [0]:
            self.fetch(k, 0).wait()
            self.across(k, 0).wait_recv()
            for j in range(1, b):
                self.along_b(k, j).wait_recv()
            if k:
                self.held[place.step(0, k), place.mine[1]] = self.total(k).astype(self.held.dtype)
                self.along_a(k).start()
            else:
                self.out[...] = self.total(0)

    def finish(self):
        place = self.place
        a, b, _ = place.sizes
        for k in range(1, a):
            self.along_a(k).wait_recv()
            self.out[...] = self.out[...] + self.far[k - 1].astype(jnp.float32)
        for k, j in self.order():
            self.across(k, j).wait_send()
            if j:
                self.along_b(k, j).wait_send()
        for k in range(1, a):
            self.along_a(k).wait_send()


def scatter_all(items):
    count = len(items)
    for item in items:
        item.begin()
    for step in range(count + 2):
        if step < count:
            items[step].first()
        if 1 <= step <= count:
            items[step - 1].second()
        if step >= 2:
            items[step - 2].finish()


def start_kernel(row_size, head_size, images, blocks, weights, *refs):
    cond, ada, bias = refs[:3]
    shards = refs[3 : 3 + weights]
    outs = refs[3 + weights : 3 + 2 * weights]
    mods = refs[3 + 2 * weights]
    (conds, part, held, met, side, far, total, every, sends, recvs, keeps, mod_send, mod_recv, mod_load, head_send, head_recv) = refs[4 + 2 * weights :]
    place = Place(row_size, head_size)
    place.greet(True)
    items = [
        Gather(place, shard, out, sends.at[i], recvs.at[i], keeps.at[i])
        for i, (shard, out) in enumerate(zip((cond,) + shards, (conds,) + outs))
    ]
    lead, bulk = items[0], items[1:]
    lead.begin()
    bulk[0].begin()
    hops = range(1, place.sizes[0])
    for k in hops:
        lead.first(k)
    lead.second()
    lead.finish()
    width = cond.shape[1]
    share = ada.shape[1]
    pad = cond.shape[0]
    lane = lax.broadcasted_iota(jnp.int32, (width, share), 0)
    slot = lax.broadcasted_iota(jnp.int32, (width, share), 1)
    pick = jnp.where(lane == lax.axis_index("rows") * share + slot, 1.0, 0.0).astype(jnp.bfloat16)
    mine = jnp.dot(
        conds[...].reshape(row_size * pad, width), pick, preferred_element_type=jnp.float32
    ).astype(jnp.bfloat16)
    for b in range(blocks):
        value = jnp.dot(mine, ada[b], preferred_element_type=jnp.float32)
        part[:, b * images : (b + 1) * images, :] = value.reshape(row_size, pad, -1)[:, :images]
    sums = Scatter(place, part, total, held, met, side, far, mod_send, mod_recv, mod_load)
    sums.begin()
    bulk[0].first(1)
    for item in bulk[1:]:
        item.begin()
    sums.first()
    for k in hops[1:]:
        bulk[0].first(k)
    sums.second()
    for item in bulk[1:]:
        for k in hops:
            item.first(k)
    sums.finish()
    every[place.head] = total[...] + bias[...]
    across = [
        pltpu.make_async_remote_copy(
            src_ref=every.at[place.head],
            dst_ref=every.at[place.head],
            send_sem=head_send.at[by - 1],
            recv_sem=head_recv.at[by - 1],
            device_id=place.flip(by),
            device_id_type=MESH,
        )
        for by in range(1, head_size)
    ]
    for copy in across:
        copy.start()
    for item in bulk:
        item.second()
    for copy in across:
        copy.wait()
    mods[...] = every[...]
    for item in bulk:
        item.finish()


def start_call(row_size, head_size, cond, ada, bias, shards):
    images = bias.shape[0] // ada.shape[0]
    blocks = ada.shape[0]
    count = len(shards)
    a, b = 4, row_size // 8
    chunk = bias.shape
    copies = gather_count(row_size)
    anywhere = pl.BlockSpec(memory_space=pl.ANY)
    vmem = pl.BlockSpec(memory_space=pltpu.VMEM)
    f32 = jnp.float32
    return pl.pallas_call(
        functools.partial(start_kernel, row_size, head_size, images, blocks, count),
        out_shape=[jax.ShapeDtypeStruct((row_size,) + item.shape, item.dtype) for item in shards]
        + [jax.ShapeDtypeStruct((head_size,) + chunk, f32)],
        in_specs=[vmem] * 3 + [anywhere] * count,
        out_specs=[anywhere] * count + [vmem],
        scratch_shapes=[
            pltpu.VMEM((row_size,) + cond.shape, cond.dtype),
            pltpu.VMEM((row_size,) + chunk, f32),
            pltpu.VMEM((a, b) + chunk, f32),
            pltpu.VMEM((a, b) + chunk, f32),
            pltpu.VMEM((b - 1, a) + chunk, f32),
            pltpu.VMEM((a - 1,) + chunk, f32),
            pltpu.VMEM(chunk, f32),
            pltpu.VMEM((head_size,) + chunk, f32),
            pltpu.SemaphoreType.DMA((count + 1, copies)),
            pltpu.SemaphoreType.DMA((count + 1, copies)),
            pltpu.SemaphoreType.DMA((count + 1,)),
            pltpu.SemaphoreType.DMA((scatter_count(row_size),)),
            pltpu.SemaphoreType.DMA((scatter_count(row_size),)),
            pltpu.SemaphoreType.DMA((a * b,)),
            pltpu.SemaphoreType.DMA((head_size - 1,)),
            pltpu.SemaphoreType.DMA((head_size - 1,)),
        ],
        compiler_params=pltpu.CompilerParams(
            collective_id=1, has_side_effects=True, vmem_limit_bytes=48 * 2**20
        ),
        name="start",
    )(cond, ada, bias, *shards)


def scatter_kernel(row_size, head_size, count, *refs):
    ins, outs = refs[:count], refs[count : 2 * count]
    scratch = refs[2 * count : 6 * count]
    send, recv, load = refs[6 * count :]
    place = Place(row_size, head_size)
    place.greet(False)
    scatter_all(
        [
            Scatter(
                place, ins[i], outs[i], *scratch[4 * i : 4 * i + 4], send.at[i], recv.at[i], load.at[i]
            )
            for i in range(count)
        ]
    )


def scatter_call(row_size, head_size, grads):
    count = len(grads)
    copies = scatter_count(row_size)
    a, b = 4, row_size // 8
    scratch = []
    for grad in grads:
        chunk = grad.shape[1:]
        for lead in ((a, b), (a, b), (b - 1, a), (a - 1,)):
            scratch.append(pltpu.VMEM(lead + chunk, grad.dtype))
    return pl.pallas_call(
        functools.partial(scatter_kernel, row_size, head_size, count),
        out_shape=[jax.ShapeDtypeStruct(grad.shape[1:], jnp.float32) for grad in grads],
        in_specs=[pl.BlockSpec(memory_space=pl.ANY)] * count,
        out_specs=[pl.BlockSpec(memory_space=pltpu.VMEM)] * count,
        scratch_shapes=scratch
        + [
            pltpu.SemaphoreType.DMA((count, copies)),
            pltpu.SemaphoreType.DMA((count, copies)),
            pltpu.SemaphoreType.DMA((count, a * b)),
        ],
        compiler_params=pltpu.CompilerParams(
            collective_id=2, has_side_effects=True, vmem_limit_bytes=56 * 2**20
        ),
        name="sum_rows",
    )(*grads)


def rope_parts(coords):
    angle = angles(coords, HD // 4)
    return jnp.cos(angle), jnp.sin(angle)


def turn(vectors, geometry, sign):
    row_cos, row_sin, col_cos, col_sin = [item[:, :, None, :] for item in geometry]
    quarter = HD // 4
    a, b, c, d = [vectors[..., quarter * i : quarter * (i + 1)] for i in range(4)]
    return jnp.concatenate(
        [
            a * row_cos - b * (sign * row_sin),
            b * row_cos + a * (sign * row_sin),
            c * col_cos - d * (sign * col_sin),
            d * col_cos + c * (sign * col_sin),
        ],
        axis=-1,
    )


def masked_scores(queries, key_rows, image_ids):
    scores = jnp.einsum(
        "rqhe,rkhe->rhqk", queries, key_rows, preferred_element_type=jnp.float32
    ) * HD ** (-0.5)
    same_image = image_ids[:, :, None] == image_ids[:, None, :]
    return jnp.where(same_image[:, None], scores, -1e30)


def attend(queries, key_rows, value_rows, image_ids):
    scores = masked_scores(queries, key_rows, image_ids)
    maximum = jnp.max(scores, axis=-1, keepdims=True)
    scaled_exp = jnp.exp(scores - maximum)
    denominator = jnp.sum(scaled_exp, axis=-1, keepdims=True)
    weights = (scaled_exp / denominator).astype(jnp.bfloat16)
    attended = jnp.einsum("rhqk,rkhe->rqhe", weights, value_rows, preferred_element_type=jnp.float32)
    return (attended.astype(jnp.bfloat16), (maximum + jnp.log(denominator))[..., 0])


def attend_back(queries, key_rows, value_rows, image_ids, logsum, grad_attended):
    score_scale = HD ** (-0.5)
    probs = jnp.exp(masked_scores(queries, key_rows, image_ids) - logsum[..., None])
    weights = probs.astype(jnp.bfloat16)
    grad_value = jnp.einsum(
        "rhqk,rqhe->rkhe", weights, grad_attended, preferred_element_type=jnp.float32
    )
    grad_probs = jnp.einsum(
        "rqhe,rkhe->rhqk", grad_attended, value_rows, preferred_element_type=jnp.float32
    )
    inner_sum = jnp.sum(probs * grad_probs, axis=-1, keepdims=True)
    grad_scores = (probs * (grad_probs - inner_sum)).astype(jnp.bfloat16)
    grad_query = (
        jnp.einsum("rhqk,rkhe->rqhe", grad_scores, key_rows, preferred_element_type=jnp.float32)
        * score_scale
    )
    grad_key = (
        jnp.einsum("rhqk,rqhe->rkhe", grad_scores, queries, preferred_element_type=jnp.float32)
        * score_scale
    )
    return (grad_query, grad_key, grad_value)


def spread(values, beside=()):
    arrived = [head_move(values, flip) for flip in range(1, lax.axis_size("heads"))]
    arrived, beside = lax.optimization_barrier((arrived, beside))
    return jnp.concatenate([values] + arrived, axis=0), beside


def collect(operand, product, own_rows, beside=()):
    total = None
    arrived = []
    for flip in range(1, lax.axis_size("heads")):
        partial = product(operand[flip * own_rows : (flip + 1) * own_rows])
        arrived.append(head_move(partial.astype(jnp.bfloat16), flip))
    total = product(operand[:own_rows])
    total, arrived, beside = lax.optimization_barrier((total, arrived, beside))
    for item in arrived:
        total = total + item.astype(jnp.float32)
    return total, beside


def plain_dot(operand, other):
    return jnp.dot(operand, other, preferred_element_type=jnp.float32)


def piece_of(mods, picks, index):
    width = mods.shape[1] // 6
    value = mods[:, index * width : (index + 1) * width]
    total = jnp.zeros((picks.shape[0], width), jnp.float32)
    for image in range(mods.shape[0]):
        total = jnp.where(picks[:, None] == image, value[image][None, :], total)
    return total


def block_forward(residual, pieces, qkv_full, qkv_b, proj_t, gu_full, down_t, image_ids, geometry):
    shift_attn, scale_attn, gate_attn, shift_mlp, scale_mlp, gate_mlp = pieces
    own_rows = residual.shape[0]
    count_rows, row_len = image_ids.shape
    normed_attn, inverse_attn = normalize(residual)
    input_attn, _ = spread((normed_attn * (1.0 + scale_attn) + shift_attn).astype(jnp.bfloat16))
    packed = plain_dot(input_attn, qkv_full) + qkv_b
    heads_here = packed.shape[1] // (3 * HD)
    packed = packed.reshape(count_rows, row_len, heads_here, 3, HD)
    queries = turn(packed[:, :, :, 0], geometry, 1.0).astype(jnp.bfloat16)
    key_rows = turn(packed[:, :, :, 1], geometry, 1.0).astype(jnp.bfloat16)
    value_rows = packed[:, :, :, 2].astype(jnp.bfloat16)
    attended, logsum = attend(queries, key_rows, value_rows, image_ids)
    attended = attended.reshape(count_rows * row_len, heads_here * HD)
    branch, _ = collect(attended, lambda rows: tail_dot(rows, proj_t), own_rows)
    middle = residual + gate_attn * branch
    normed_mlp, inverse_mlp = normalize(middle)
    input_mlp, _ = spread((normed_mlp * (1.0 + scale_mlp) + shift_mlp).astype(jnp.bfloat16))
    gate_up = plain_dot(input_mlp, gu_full)
    hidden_width = gate_up.shape[1] // 2
    gate_part = gate_up[:, :hidden_width]
    up_part = gate_up[:, hidden_width:]
    hidden = (jax.nn.silu(gate_part) * up_part).astype(jnp.bfloat16)
    mlp_out, _ = collect(hidden, lambda rows: tail_dot(rows, down_t), own_rows)
    result = middle + gate_mlp * mlp_out
    stored = (
        normed_attn,
        inverse_attn,
        input_attn,
        queries,
        key_rows,
        value_rows,
        logsum,
        attended,
        branch,
        normed_mlp,
        inverse_mlp,
        input_mlp,
        gate_part,
        up_part,
        hidden,
        mlp_out,
    )
    return (result, stored)


def block_backward(incoming, pieces, stored, qkv_full, proj_t, gu_full, down_t, image_ids, geometry):
    shift_attn, scale_attn, gate_attn, shift_mlp, scale_mlp, gate_mlp = pieces
    (
        normed_attn,
        inverse_attn,
        input_attn,
        queries,
        key_rows,
        value_rows,
        logsum,
        attended,
        branch,
        normed_mlp,
        inverse_mlp,
        input_mlp,
        gate_part,
        up_part,
        hidden,
        mlp_out,
    ) = stored
    own_rows = incoming.shape[0]
    count_rows, row_len = image_ids.shape
    grad_mlp = (gate_mlp * incoming).astype(jnp.bfloat16)
    grad_gate_mlp = incoming * mlp_out
    gathered_mlp, _ = spread(grad_mlp)
    down_grad = lead_dot(gathered_mlp, hidden).astype(jnp.bfloat16)
    grad_hidden = plain_dot(gathered_mlp, down_t)
    logistic = jax.nn.sigmoid(gate_part)
    grad_gate_part = grad_hidden * up_part * logistic * (1.0 + gate_part * (1.0 - logistic))
    grad_up_part = grad_hidden * gate_part * logistic
    grad_gate_up = jnp.concatenate([grad_gate_part, grad_up_part], axis=1).astype(jnp.bfloat16)
    gu_grad = lead_dot(input_mlp, grad_gate_up).astype(jnp.bfloat16)
    grad_input_mlp, gu_grad = collect(
        grad_gate_up, lambda rows: tail_dot(rows, gu_full), own_rows, gu_grad
    )
    gu_out = lax.psum_scatter(gu_grad, "rows", scatter_dimension=0, tiled=True).astype(jnp.float32)
    grad_middle = incoming + norm_back(grad_input_mlp * (1.0 + scale_mlp), normed_mlp, inverse_mlp)
    grad_branch = (gate_attn * grad_middle).astype(jnp.bfloat16)
    grad_gate_attn = grad_middle * branch
    heads_here = queries.shape[2]
    gathered_branch, down_grad = spread(grad_branch, down_grad)
    proj_grad = lead_dot(gathered_branch, attended).astype(jnp.bfloat16)
    grad_attended = plain_dot(gathered_branch, proj_t).astype(jnp.bfloat16)
    grad_attended = grad_attended.reshape(count_rows, row_len, heads_here, HD)
    grad_query, grad_key, grad_value = attend_back(
        queries, key_rows, value_rows, image_ids, logsum, grad_attended
    )
    grad_query = turn(grad_query, geometry, -1.0)
    grad_key = turn(grad_key, geometry, -1.0)
    grad_packed = (
        jnp.stack([grad_query, grad_key, grad_value], axis=3)
        .reshape(count_rows * row_len, heads_here * 3 * HD)
        .astype(jnp.bfloat16)
    )
    qkv_bias_grad = jnp.sum(grad_packed, axis=0, dtype=jnp.float32)
    qkv_grad = lead_dot(input_attn, grad_packed).astype(jnp.bfloat16)
    grad_input_attn, (qkv_grad, proj_grad) = collect(
        grad_packed, lambda rows: tail_dot(rows, qkv_full), own_rows, (qkv_grad, proj_grad)
    )
    grad_input = grad_middle + norm_back(
        grad_input_attn * (1.0 + scale_attn), normed_attn, inverse_attn
    )
    grad_mods = jnp.concatenate(
        [
            grad_input_attn,
            grad_input_attn * normed_attn,
            grad_gate_attn,
            grad_input_mlp,
            grad_input_mlp * normed_mlp,
            grad_gate_mlp,
        ],
        axis=1,
    )
    return (grad_input, grad_mods, (qkv_grad, qkv_bias_grad, proj_grad, gu_out, down_grad))


def heads_in_order(value):
    index = lax.axis_index("heads")
    count = lax.axis_size("heads")
    chunks = [value] + [head_move(value, flip) for flip in range(1, count)]
    placed = []
    for slot in range(count):
        item = chunks[0]
        for flip in range(1, count):
            item = jnp.where(index == slot ^ flip, chunks[flip], item)
        placed.append(item)
    return jnp.stack(placed)


def heads_share(value):
    index = lax.axis_index("heads")
    count = lax.axis_size("heads")
    width = value.shape[-1] // count

    def part(flip):
        return lax.dynamic_slice_in_dim(value, (index ^ flip) * width, width, value.ndim - 1)

    arrived = [head_move(part(flip), flip) for flip in range(1, count)]
    total = part(0)
    for item in arrived:
        total = total + item
    return total


def shards(
    tokens,
    cond,
    image_of,
    grid_row,
    grid_col,
    ada_weight,
    ada_bias,
    qkv_weight,
    qkv_bias,
    proj_weight,
    gu_weight,
    down_weight,
    cotangent,
):
    own_rows = tokens.shape[0]
    image_count = cond.shape[0]
    block_count = qkv_weight.shape[0]
    row_size = lax.axis_size("rows")
    head_size = lax.axis_size("heads")
    head_index = lax.axis_index("heads")

    def device_order(values):
        parts = values.reshape(head_size, own_rows)
        picked = [
            lax.dynamic_index_in_dim(parts, head_index ^ flip, 0, keepdims=False)
            for flip in range(head_size)
        ]
        return jnp.concatenate(picked).reshape(values.shape)

    image_ids = device_order(image_of - lax.axis_index("rows") * image_count)
    own_images = image_ids.reshape(-1)[:own_rows]
    picker = (own_images[:, None] == jnp.arange(image_count, dtype=jnp.int32)[None, :]).astype(
        jnp.float32
    )
    geometry = lax.optimization_barrier(
        rope_parts(device_order(grid_row)) + rope_parts(device_order(grid_col))
    )
    shard_rows = qkv_weight.shape[1]

    def gathered(shard):
        return lax.all_gather(shard, "rows", axis=0, tiled=True)

    cond_wide = cond.astype(jnp.float32)
    cond_act = jax.nn.silu(cond_wide).astype(jnp.bfloat16)
    pad = -image_count % 16
    bias_rows = jnp.repeat(ada_bias.astype(jnp.float32), image_count, axis=0)
    first_qkv, first_proj, mods = start_call(
        row_size,
        head_size,
        jnp.pad(cond_act, ((0, pad), (0, 0))),
        ada_weight,
        bias_rows,
        [qkv_weight[0], proj_weight[0].T],
    )
    qkv_full, gu_full, down_t, proj_t = [], [], [], []
    for b in range(block_count):
        if b == 0:
            qkv_full.append(first_qkv.reshape(-1, first_qkv.shape[-1]))
            proj_t.append(first_proj.reshape(-1, first_proj.shape[-1]))
        else:
            qkv_full.append(gathered(qkv_weight[b]))
            proj_t.append(gathered(proj_weight[b].T))
        gu_full.append(gathered(gu_weight[b].reshape(shard_rows, -1)))
        down_t.append(gathered(down_weight[b].T))
    mod_all = mods.reshape(head_size, block_count, image_count, -1)
    cond_mine = lax.all_to_all(
        cond_act.reshape(image_count, row_size, -1).transpose(1, 0, 2), "rows", 0, 0
    ).reshape(row_size * image_count, -1)
    modulation = [
        jnp.concatenate([mod_all[index, b] for index in range(head_size)], axis=1)
        for b in range(block_count)
    ]
    pieces = [
        [piece_of(modulation[b], own_images, index) for index in range(6)] for b in range(block_count)
    ]
    residual = tokens.astype(jnp.float32)
    stored_all = []
    for b in range(block_count):
        residual, stored = block_forward(
            residual,
            pieces[b],
            qkv_full[b],
            qkv_bias[b].astype(jnp.float32),
            proj_t[b],
            gu_full[b],
            down_t[b],
            image_ids,
            geometry,
        )
        stored_all.append(stored)
    block_out = residual.astype(jnp.bfloat16)
    incoming = cotangent.astype(jnp.float32)
    block_grads = [None] * block_count
    image_sums = [None] * block_count
    for b in reversed(range(block_count)):
        incoming, grad_mods, gradients = block_backward(
            incoming,
            pieces[b],
            stored_all[b],
            qkv_full[b],
            proj_t[b],
            gu_full[b],
            down_t[b],
            image_ids,
            geometry,
        )
        image_sums[b] = lax.dot_general(
            picker, grad_mods, (((0,), (0,)), ((), ())), precision=highest
        )
        block_grads[b] = gradients
    image_grads = heads_share(jnp.stack(image_sums)).astype(jnp.bfloat16)
    bias_sums = jnp.stack([item[1] for item in block_grads])
    bias_high = bias_sums.astype(jnp.bfloat16)
    bias_rest = bias_sums - bias_high.astype(jnp.float32)
    bias_middle = bias_rest.astype(jnp.bfloat16)
    bias_low = (bias_rest - bias_middle.astype(jnp.float32)).astype(jnp.bfloat16)
    small = jnp.concatenate(
        [
            image_grads.reshape(1, -1),
            bias_high.reshape(1, -1),
            bias_middle.reshape(1, -1),
            bias_low.reshape(1, -1),
        ],
        axis=1,
    )
    small = lax.all_gather(small, "rows", axis=0, tiled=True)
    split = image_grads.size
    all_grads = small[:, :split].reshape((row_size,) + image_grads.shape)
    bias_all = small[:, split:].reshape((row_size, 3) + bias_sums.shape).astype(jnp.float32)
    qkv_bias_out = jnp.sum(bias_all, axis=(0, 1))
    ada_grads = []
    cond_partial = 0.0
    for b in range(block_count):
        block_grads_all = all_grads[:, b].reshape(row_size * image_count, -1)
        ada_grads.append(lead_dot(cond_mine, block_grads_all))
        cond_partial = cond_partial + tail_dot(block_grads_all, ada_weight[b])
    ada_bias_grads = jnp.sum(all_grads, axis=(0, 2), dtype=jnp.float32)
    cond_parts = lax.all_to_all(
        cond_partial.astype(jnp.bfloat16).reshape(row_size, image_count, -1), "rows", 0, 0
    )
    cond_rows = cond_parts.transpose(1, 0, 2).reshape(image_count, -1).astype(jnp.float32)
    cond_total = cond_rows
    for flip in range(1, head_size):
        cond_total = cond_total + head_move(cond_rows.astype(jnp.bfloat16), flip).astype(jnp.float32)
    logistic = jax.nn.sigmoid(cond_wide)
    cond_grad = cond_total * logistic * (1.0 + cond_wide * (1.0 - logistic))
    parts = []
    for b in reversed(range(block_count)):
        parts += [block_grads[b][4], block_grads[b][2], block_grads[b][0]]
    sums = scatter_call(
        row_size, head_size, [part.reshape(row_size, shard_rows, -1) for part in parts]
    )
    sums = [sums[3 * b : 3 * b + 3] for b in reversed(range(block_count))]
    return (
        block_out,
        incoming,
        cond_grad,
        jnp.stack(ada_grads),
        ada_bias_grads,
        jnp.stack([item[2] for item in sums]),
        qkv_bias_out,
        jnp.stack([item[1].T for item in sums]),
        jnp.stack([item[3].reshape(gu_weight.shape[1:]) for item in block_grads]),
        jnp.stack([item[0].T for item in sums]),
    )


def solution(mesh):
    in_specs = (
        P(("rows", "heads"), None),
        P("rows", None),
        P("rows", None),
        P("rows", None),
        P("rows", None),
        P(None, "rows", "heads"),
        P(None, "heads"),
        P(None, "rows", "heads"),
        P(None, "heads"),
        P(None, "heads", "rows"),
        P(None, "rows", None, "heads"),
        P(None, "heads", "rows"),
        P(("rows", "heads"), None),
    )
    out_specs = (
        P(("rows", "heads"), None),
        P(("rows", "heads"), None),
        P("rows", None),
        P(None, "rows", "heads"),
        P(None, "heads"),
        P(None, "rows", "heads"),
        P(None, "heads"),
        P(None, "heads", "rows"),
        P(None, "rows", None, "heads"),
        P(None, "heads", "rows"),
    )
    return jax.shard_map(shards, mesh=mesh, in_specs=in_specs, out_specs=out_specs, check_vma=False)
```

```python
import functools

import jax
import jax.numpy as jnp
from jax import lax
from jax.experimental import pallas as pl
from jax.experimental.pallas import tpu as pltpu
from jax.sharding import PartitionSpec as P

HD = 72


epsilon = 1e-06
theta_base = 10000.0
highest = lax.Precision.HIGHEST


def normalize(values):
    center = values - jnp.mean(values, axis=-1, keepdims=True)
    inverse = lax.rsqrt(jnp.mean(center * center, axis=-1, keepdims=True) + epsilon)
    return (center * inverse, inverse)


def norm_back(incoming, normed, inverse):
    return inverse * (
        incoming
        - jnp.mean(incoming, axis=-1, keepdims=True)
        - normed * jnp.mean(incoming * normed, axis=-1, keepdims=True)
    )


def lead_dot(operand, other):
    return lax.dot_general(
        operand, other, (((0,), (0,)), ((), ())), preferred_element_type=jnp.float32
    )


def tail_dot(operand, other):
    return lax.dot_general(
        operand, other, (((1,), (1,)), ((), ())), preferred_element_type=jnp.float32
    )


def angles(coords, quarter):
    frequency = theta_base ** (-jnp.arange(quarter, dtype=jnp.float32) / quarter)
    return coords.astype(jnp.float32)[..., None] * frequency


def head_move(value, flip):
    size = lax.axis_size("heads")
    return lax.ppermute(value, "heads", [(index, index ^ flip) for index in range(size)])


MESH = pl.DeviceIdType.MESH


class Place:
    def __init__(self, row_size, head_size):
        self.sizes = (4, row_size // 8, 2)
        index = lax.axis_index("rows")
        a, b, c = self.sizes
        self.mine = (index // (b * c), (index // c) % b, index % c)
        self.heads = head_size
        self.head = lax.axis_index("heads")

    def step(self, dim, by):
        return (self.mine[dim] + by + self.sizes[dim]) % self.sizes[dim]

    def row(self, a, b, c):
        return (a * self.sizes[1] + b) * self.sizes[2] + c

    def near(self, dim, by):
        at = list(self.mine)
        at[dim] = self.step(dim, by)
        return {"rows": self.row(*at)}

    def flip(self, by):
        return {"heads": self.head ^ by}

    def partners(self, with_heads):
        found = [self.near(dim, by) for dim in range(3) for by in range(1, self.sizes[dim])]
        if with_heads:
            found += [self.flip(by) for by in range(1, self.heads)]
        return found

    def greet(self, with_heads):
        barrier = pltpu.get_barrier_semaphore()
        found = self.partners(with_heads)
        for partner in found:
            pl.semaphore_signal(barrier, inc=1, device_id=partner, device_id_type=MESH)
        pl.semaphore_wait(barrier, len(found))


def gather_count(row_size):
    a, b, c = 4, row_size // 8, 2
    return 2 * (a - 1) + (2 * a - 1) * (2 * b - 1)


class Gather:
    def __init__(self, place, shard, out, send, recv, local):
        self.place, self.shard, self.out = place, shard, out
        self.send, self.recv = send, recv
        self.used = 0
        self.keep = pltpu.make_async_copy(shard, out.at[place.row(*place.mine)], local)
        a, b, _ = place.sizes
        self.hops, self.along_b, self.along_c = {}, {}, {}
        names = [(0, 0)] + [(way, k) for k in range(1, a) for way in (1, -1)]
        for way, k in names:
            if k:
                self.hops[way, k] = self.copy(way, k - 1, 0, place.near(0, way))
        for way, k in names:
            for j in range(1, b):
                self.along_b[way, k, j] = self.copy(way, k, 0, place.near(1, j))
        for way, k in names:
            for j in range(b):
                self.along_c[way, k, j] = self.copy(way, k, j, place.near(2, 1))

    def copy(self, way, k, j, device):
        place, slot = self.place, self.used
        self.used += 1
        index = place.row(place.step(0, -way * k), place.step(1, -j), place.mine[2])
        return pltpu.make_async_remote_copy(
            src_ref=self.shard if k == 0 and j == 0 else self.out.at[index],
            dst_ref=self.out.at[index],
            send_sem=self.send.at[slot],
            recv_sem=self.recv.at[slot],
            device_id=device,
            device_id_type=MESH,
        )

    def holds(self, way, k):
        at = self.place.mine[0]
        return at >= k if way > 0 else at < self.place.sizes[0] - k

    def hop(self, way, k):
        at = self.place.mine[0]
        last = self.place.sizes[0] - 1
        return (at < last) & (at >= k - 1) if way > 0 else (at > 0) & (at <= last - (k - 1))

    def begin(self):
        self.keep.start()
        for way in (1, -1):
            pl.when(self.hop(way, 1))(self.hops[way, 1].start)
        self.pass_on(0, 0)

    def pass_on(self, way, k):
        for j in range(1, self.place.sizes[1]):
            self.along_b[way, k, j].start()
        self.along_c[way, k, 0].start()

    def first(self, k):
        for way in (1, -1):

            @pl.when(self.holds(way, k))
            def _():
                self.hops[way, k].wait_recv()
                if k + 1 < self.place.sizes[0]:
                    pl.when(self.hop(way, k + 1))(self.hops[way, k + 1].start)
                self.pass_on(way, k)

    def each(self, way, k, action):
        if k:
            pl.when(self.holds(way, k))(action)
        else:
            action()

    def second(self):
        for way, k, j in self.along_b:

            def action():
                self.along_b[way, k, j].wait_recv()
                self.along_c[way, k, j].start()

            self.each(way, k, action)

    def finish(self):
        for way, k, j in self.along_c:

            def action():
                self.along_c[way, k, j].wait_recv()
                self.along_c[way, k, j].wait_send()

            self.each(way, k, action)
        for way, k, j in self.along_b:
            self.each(way, k, self.along_b[way, k, j].wait_send)
        for way, k in self.hops:
            pl.when(self.hop(way, k))(self.hops[way, k].wait_send)
        self.keep.wait()


def gather_all(items):
    count = len(items)
    items[0].begin()
    for step in range(count + 1):
        if step < count:
            items[step].first(1)
            if step + 1 < count:
                items[step + 1].begin()
            for k in range(2, items[step].place.sizes[0]):
                items[step].first(k)
        if step >= 1:
            items[step - 1].second()
    for item in items:
        item.finish()


def scatter_count(row_size):
    a, b, c = 4, row_size // 8, 2
    return a * b + a * (b - 1) + (a - 1)


class Scatter:
    def __init__(self, place, source, out, held, met, side, far, send, recv, load):
        self.place, self.source, self.out = place, source, out
        self.held, self.met, self.side, self.far = held, met, side, far
        self.send, self.recv, self.load = send, recv, load

    def remote(self, source, target, slot, device):
        return pltpu.make_async_remote_copy(
            src_ref=source,
            dst_ref=target,
            send_sem=self.send.at[slot],
            recv_sem=self.recv.at[slot],
            device_id=device,
            device_id_type=MESH,
        )

    def across(self, k, j):
        place = self.place
        a, b = place.step(0, k), place.step(1, j)
        other = place.step(2, 1)
        return self.remote(
            self.source.at[place.row(a, b, other)],
            self.met.at[a, b],
            k * place.sizes[1] + j,
            place.near(2, 1),
        )

    def fetch(self, k, j):
        place = self.place
        a, b = place.step(0, k), place.step(1, j)
        return pltpu.make_async_copy(
            self.source.at[place.row(a, b, place.mine[2])],
            self.held.at[a, b],
            self.load.at[k * place.sizes[1] + j],
        )

    def along_b(self, k, j):
        place = self.place
        a, b = place.step(0, k), place.step(1, j)
        base = place.sizes[0] * place.sizes[1]
        return self.remote(
            self.held.at[a, b],
            self.side.at[j - 1, a],
            base + (j - 1) * place.sizes[0] + k,
            place.near(1, j),
        )

    def along_a(self, k):
        place = self.place
        base = place.sizes[0] * (2 * place.sizes[1] - 1)
        return self.remote(
            self.held.at[place.step(0, k), place.mine[1]],
            self.far.at[k - 1],
            base + k - 1,
            place.near(0, k),
        )

    def order(self):
        a, b, _ = self.place.sizes
        return [(k, j) for j in list(range(1, b)) + [0] for k in list(range(1, a)) + [0]]

    def begin(self):
        for k, j in self.order():
            self.fetch(k, j).start()
            self.across(k, j).start()

    def first(self):
        place = self.place
        a, b, _ = place.sizes
        for j in range(1, b):
            for k in list(range(1, a)) + [0]:
                self.fetch(k, j).wait()
                self.across(k, j).wait_recv()
                at = (place.step(0, k), place.step(1, j))
                self.held[at] = (
                    self.held[at].astype(jnp.float32) + self.met[at].astype(jnp.float32)
                ).astype(self.held.dtype)
                self.along_b(k, j).start()

    def total(self, k):
        place = self.place
        a, b = place.step(0, k), place.mine[1]
        value = self.held[a, b].astype(jnp.float32) + self.met[a, b].astype(jnp.float32)
        for j in range(1, place.sizes[1]):
            value = value + self.side[j - 1, a].astype(jnp.float32)
        return value

    def second(self):
        place = self.place
        a, b, _ = place.sizes
        for k in list(range(1, a)) + [0]:
            self.fetch(k, 0).wait()
            self.across(k, 0).wait_recv()
            for j in range(1, b):
                self.along_b(k, j).wait_recv()
            if k:
                self.held[place.step(0, k), place.mine[1]] = self.total(k).astype(self.held.dtype)
                self.along_a(k).start()
            else:
                self.out[...] = self.total(0)

    def finish(self):
        place = self.place
        a, b, _ = place.sizes
        for k in range(1, a):
            self.along_a(k).wait_recv()
            self.out[...] = self.out[...] + self.far[k - 1].astype(jnp.float32)
        for k, j in self.order():
            self.across(k, j).wait_send()
            if j:
                self.along_b(k, j).wait_send()
        for k in range(1, a):
            self.along_a(k).wait_send()


def scatter_all(items):
    count = len(items)
    for item in items:
        item.begin()
    for step in range(count + 2):
        if step < count:
            items[step].first()
        if 1 <= step <= count:
            items[step - 1].second()
        if step >= 2:
            items[step - 2].finish()


def start_kernel(row_size, head_size, images, blocks, weights, *refs):
    cond, ada, bias = refs[:3]
    shards = refs[3 : 3 + weights]
    outs = refs[3 + weights : 3 + 2 * weights]
    mods = refs[3 + 2 * weights]
    (conds, part, held, met, side, far, total, every, sends, recvs, keeps, mod_send, mod_recv, mod_load, head_send, head_recv) = refs[4 + 2 * weights :]
    place = Place(row_size, head_size)
    place.greet(True)
    items = [
        Gather(place, shard, out, sends.at[i], recvs.at[i], keeps.at[i])
        for i, (shard, out) in enumerate(zip((cond,) + shards, (conds,) + outs))
    ]
    lead, bulk = items[0], items[1:]
    lead.begin()
    bulk[0].begin()
    hops = range(1, place.sizes[0])
    for k in hops:
        lead.first(k)
    lead.second()
    lead.finish()
    width = cond.shape[1]
    share = ada.shape[1]
    pad = cond.shape[0]
    lane = lax.broadcasted_iota(jnp.int32, (width, share), 0)
    slot = lax.broadcasted_iota(jnp.int32, (width, share), 1)
    pick = jnp.where(lane == lax.axis_index("rows") * share + slot, 1.0, 0.0).astype(jnp.bfloat16)
    mine = jnp.dot(
        conds[...].reshape(row_size * pad, width), pick, preferred_element_type=jnp.float32
    ).astype(jnp.bfloat16)
    for b in range(blocks):
        value = jnp.dot(mine, ada[b], preferred_element_type=jnp.float32)
        part[:, b * images : (b + 1) * images, :] = value.reshape(row_size, pad, -1)[:, :images]
    sums = Scatter(place, part, total, held, met, side, far, mod_send, mod_recv, mod_load)
    sums.begin()
    bulk[0].first(1)
    for item in bulk[1:]:
        item.begin()
    sums.first()
    for k in hops[1:]:
        bulk[0].first(k)
    sums.second()
    for item in bulk[1:]:
        for k in hops:
            item.first(k)
    sums.finish()
    every[place.head] = total[...] + bias[...]
    across = [
        pltpu.make_async_remote_copy(
            src_ref=every.at[place.head],
            dst_ref=every.at[place.head],
            send_sem=head_send.at[by - 1],
            recv_sem=head_recv.at[by - 1],
            device_id=place.flip(by),
            device_id_type=MESH,
        )
        for by in range(1, head_size)
    ]
    for copy in across:
        copy.start()
    for item in bulk:
        item.second()
    for copy in across:
        copy.wait()
    mods[...] = every[...]
    for item in bulk:
        item.finish()


def start_call(row_size, head_size, cond, ada, bias, shards):
    images = bias.shape[0] // ada.shape[0]
    blocks = ada.shape[0]
    count = len(shards)
    a, b = 4, row_size // 8
    chunk = bias.shape
    copies = gather_count(row_size)
    anywhere = pl.BlockSpec(memory_space=pl.ANY)
    vmem = pl.BlockSpec(memory_space=pltpu.VMEM)
    f32 = jnp.float32
    return pl.pallas_call(
        functools.partial(start_kernel, row_size, head_size, images, blocks, count),
        out_shape=[jax.ShapeDtypeStruct((row_size,) + item.shape, item.dtype) for item in shards]
        + [jax.ShapeDtypeStruct((head_size,) + chunk, f32)],
        in_specs=[vmem] * 3 + [anywhere] * count,
        out_specs=[anywhere] * count + [vmem],
        scratch_shapes=[
            pltpu.VMEM((row_size,) + cond.shape, cond.dtype),
            pltpu.VMEM((row_size,) + chunk, f32),
            pltpu.VMEM((a, b) + chunk, f32),
            pltpu.VMEM((a, b) + chunk, f32),
            pltpu.VMEM((b - 1, a) + chunk, f32),
            pltpu.VMEM((a - 1,) + chunk, f32),
            pltpu.VMEM(chunk, f32),
            pltpu.VMEM((head_size,) + chunk, f32),
            pltpu.SemaphoreType.DMA((count + 1, copies)),
            pltpu.SemaphoreType.DMA((count + 1, copies)),
            pltpu.SemaphoreType.DMA((count + 1,)),
            pltpu.SemaphoreType.DMA((scatter_count(row_size),)),
            pltpu.SemaphoreType.DMA((scatter_count(row_size),)),
            pltpu.SemaphoreType.DMA((a * b,)),
            pltpu.SemaphoreType.DMA((head_size - 1,)),
            pltpu.SemaphoreType.DMA((head_size - 1,)),
        ],
        compiler_params=pltpu.CompilerParams(
            collective_id=1, has_side_effects=True, vmem_limit_bytes=48 * 2**20
        ),
        name="start",
    )(cond, ada, bias, *shards)


def scatter_kernel(row_size, head_size, count, *refs):
    ins, small = refs[:count], refs[count]
    outs, smalls = refs[count + 1 : 2 * count + 1], refs[2 * count + 1]
    refs = refs[2 * count + 2 :]
    scratch = refs[: 4 * count]
    send, recv, load, small_send, small_recv, small_keep = refs[4 * count :]
    place = Place(row_size, head_size)
    place.greet(False)
    lead = Gather(place, small, smalls, small_send, small_recv, small_keep.at[0])
    lead.begin()
    items = [
        Scatter(
            place, ins[i], outs[i], *scratch[4 * i : 4 * i + 4], send.at[i], recv.at[i], load.at[i]
        )
        for i in range(count)
    ]
    for item in items:
        item.begin()
    for k in range(1, place.sizes[0]):
        lead.first(k)
    for step in range(count + 2):
        if step < count:
            items[step].first()
        if step == 0:
            lead.second()
        if 1 <= step <= count:
            items[step - 1].second()
        if step >= 2:
            items[step - 2].finish()
    lead.finish()


def scatter_call(row_size, head_size, grads, small):
    count = len(grads)
    copies = scatter_count(row_size)
    small_copies = gather_count(row_size)
    a, b = 4, row_size // 8
    scratch = []
    for grad in grads:
        chunk = grad.shape[1:]
        for lead in ((a, b), (a, b), (b - 1, a), (a - 1,)):
            scratch.append(pltpu.VMEM(lead + chunk, grad.dtype))
    anywhere = pl.BlockSpec(memory_space=pl.ANY)
    vmem = pl.BlockSpec(memory_space=pltpu.VMEM)
    return pl.pallas_call(
        functools.partial(scatter_kernel, row_size, head_size, count),
        out_shape=[jax.ShapeDtypeStruct(grad.shape[1:], jnp.float32) for grad in grads]
        + [jax.ShapeDtypeStruct((row_size,) + small.shape, small.dtype)],
        in_specs=[anywhere] * (count + 1),
        out_specs=[vmem] * count + [anywhere],
        scratch_shapes=scratch
        + [
            pltpu.SemaphoreType.DMA((count, copies)),
            pltpu.SemaphoreType.DMA((count, copies)),
            pltpu.SemaphoreType.DMA((count, a * b)),
            pltpu.SemaphoreType.DMA((small_copies,)),
            pltpu.SemaphoreType.DMA((small_copies,)),
            pltpu.SemaphoreType.DMA((1,)),
        ],
        compiler_params=pltpu.CompilerParams(
            collective_id=2, has_side_effects=True, vmem_limit_bytes=56 * 2**20
        ),
        name="sum_rows",
    )(*grads, small)


def rope_parts(coords):
    angle = angles(coords, HD // 4)
    return jnp.cos(angle), jnp.sin(angle)


def turn(vectors, geometry, sign):
    row_cos, row_sin, col_cos, col_sin = [item[:, :, None, :] for item in geometry]
    quarter = HD // 4
    a, b, c, d = [vectors[..., quarter * i : quarter * (i + 1)] for i in range(4)]
    return jnp.concatenate(
        [
            a * row_cos - b * (sign * row_sin),
            b * row_cos + a * (sign * row_sin),
            c * col_cos - d * (sign * col_sin),
            d * col_cos + c * (sign * col_sin),
        ],
        axis=-1,
    )


def masked_scores(queries, key_rows, image_ids):
    scores = jnp.einsum(
        "rqhe,rkhe->rhqk", queries, key_rows, preferred_element_type=jnp.float32
    ) * HD ** (-0.5)
    same_image = image_ids[:, :, None] == image_ids[:, None, :]
    return jnp.where(same_image[:, None], scores, -1e30)


def attend(queries, key_rows, value_rows, image_ids):
    scores = masked_scores(queries, key_rows, image_ids)
    maximum = jnp.max(scores, axis=-1, keepdims=True)
    scaled_exp = jnp.exp(scores - maximum)
    denominator = jnp.sum(scaled_exp, axis=-1, keepdims=True)
    weights = (scaled_exp / denominator).astype(jnp.bfloat16)
    attended = jnp.einsum("rhqk,rkhe->rqhe", weights, value_rows, preferred_element_type=jnp.float32)
    return (attended.astype(jnp.bfloat16), (maximum + jnp.log(denominator))[..., 0])


def attend_back(queries, key_rows, value_rows, image_ids, logsum, grad_attended):
    score_scale = HD ** (-0.5)
    probs = jnp.exp(masked_scores(queries, key_rows, image_ids) - logsum[..., None])
    weights = probs.astype(jnp.bfloat16)
    grad_value = jnp.einsum(
        "rhqk,rqhe->rkhe", weights, grad_attended, preferred_element_type=jnp.float32
    )
    grad_probs = jnp.einsum(
        "rqhe,rkhe->rhqk", grad_attended, value_rows, preferred_element_type=jnp.float32
    )
    inner_sum = jnp.sum(probs * grad_probs, axis=-1, keepdims=True)
    grad_scores = (probs * (grad_probs - inner_sum)).astype(jnp.bfloat16)
    grad_query = (
        jnp.einsum("rhqk,rkhe->rqhe", grad_scores, key_rows, preferred_element_type=jnp.float32)
        * score_scale
    )
    grad_key = (
        jnp.einsum("rhqk,rqhe->rkhe", grad_scores, queries, preferred_element_type=jnp.float32)
        * score_scale
    )
    return (grad_query, grad_key, grad_value)


def spread(values, beside=()):
    arrived = [head_move(values, flip) for flip in range(1, lax.axis_size("heads"))]
    arrived, beside = lax.optimization_barrier((arrived, beside))
    return jnp.concatenate([values] + arrived, axis=0), beside


def collect(operand, product, own_rows, beside=()):
    total = None
    arrived = []
    for flip in range(1, lax.axis_size("heads")):
        partial = product(operand[flip * own_rows : (flip + 1) * own_rows])
        arrived.append(head_move(partial.astype(jnp.bfloat16), flip))
    total = product(operand[:own_rows])
    total, arrived, beside = lax.optimization_barrier((total, arrived, beside))
    for item in arrived:
        total = total + item.astype(jnp.float32)
    return total, beside


def plain_dot(operand, other):
    return jnp.dot(operand, other, preferred_element_type=jnp.float32)


def piece_of(mods, picks, index):
    width = mods.shape[1] // 6
    value = mods[:, index * width : (index + 1) * width]
    total = jnp.zeros((picks.shape[0], width), jnp.float32)
    for image in range(mods.shape[0]):
        total = jnp.where(picks[:, None] == image, value[image][None, :], total)
    return total


def block_forward(residual, pieces, qkv_full, qkv_b, proj_t, gu_full, down_t, image_ids, geometry):
    shift_attn, scale_attn, gate_attn, shift_mlp, scale_mlp, gate_mlp = pieces
    own_rows = residual.shape[0]
    count_rows, row_len = image_ids.shape
    normed_attn, inverse_attn = normalize(residual)
    input_attn, _ = spread((normed_attn * (1.0 + scale_attn) + shift_attn).astype(jnp.bfloat16))
    packed = plain_dot(input_attn, qkv_full) + qkv_b
    heads_here = packed.shape[1] // (3 * HD)
    packed = packed.reshape(count_rows, row_len, heads_here, 3, HD)
    queries = turn(packed[:, :, :, 0], geometry, 1.0).astype(jnp.bfloat16)
    key_rows = turn(packed[:, :, :, 1], geometry, 1.0).astype(jnp.bfloat16)
    value_rows = packed[:, :, :, 2].astype(jnp.bfloat16)
    attended, logsum = attend(queries, key_rows, value_rows, image_ids)
    attended = attended.reshape(count_rows * row_len, heads_here * HD)
    branch, _ = collect(attended, lambda rows: tail_dot(rows, proj_t), own_rows)
    middle = residual + gate_attn * branch
    normed_mlp, inverse_mlp = normalize(middle)
    input_mlp, _ = spread((normed_mlp * (1.0 + scale_mlp) + shift_mlp).astype(jnp.bfloat16))
    gate_up = plain_dot(input_mlp, gu_full)
    hidden_width = gate_up.shape[1] // 2
    gate_part = gate_up[:, :hidden_width]
    up_part = gate_up[:, hidden_width:]
    hidden = (jax.nn.silu(gate_part) * up_part).astype(jnp.bfloat16)
    mlp_out, _ = collect(hidden, lambda rows: tail_dot(rows, down_t), own_rows)
    result = middle + gate_mlp * mlp_out
    stored = (
        normed_attn,
        inverse_attn,
        input_attn,
        queries,
        key_rows,
        value_rows,
        logsum,
        attended,
        branch,
        normed_mlp,
        inverse_mlp,
        input_mlp,
        gate_part,
        up_part,
        hidden,
        mlp_out,
    )
    return (result, stored)


def block_backward(incoming, pieces, stored, qkv_full, proj_t, gu_full, down_t, image_ids, geometry):
    shift_attn, scale_attn, gate_attn, shift_mlp, scale_mlp, gate_mlp = pieces
    (
        normed_attn,
        inverse_attn,
        input_attn,
        queries,
        key_rows,
        value_rows,
        logsum,
        attended,
        branch,
        normed_mlp,
        inverse_mlp,
        input_mlp,
        gate_part,
        up_part,
        hidden,
        mlp_out,
    ) = stored
    own_rows = incoming.shape[0]
    count_rows, row_len = image_ids.shape
    grad_mlp = (gate_mlp * incoming).astype(jnp.bfloat16)
    grad_gate_mlp = incoming * mlp_out
    gathered_mlp, _ = spread(grad_mlp)
    down_grad = lead_dot(gathered_mlp, hidden).astype(jnp.bfloat16)
    grad_hidden = plain_dot(gathered_mlp, down_t)
    logistic = jax.nn.sigmoid(gate_part)
    grad_gate_part = grad_hidden * up_part * logistic * (1.0 + gate_part * (1.0 - logistic))
    grad_up_part = grad_hidden * gate_part * logistic
    grad_gate_up = jnp.concatenate([grad_gate_part, grad_up_part], axis=1).astype(jnp.bfloat16)
    gu_grad = lead_dot(input_mlp, grad_gate_up).astype(jnp.bfloat16)
    grad_input_mlp, gu_grad = collect(
        grad_gate_up, lambda rows: tail_dot(rows, gu_full), own_rows, gu_grad
    )
    gu_out = lax.psum_scatter(gu_grad, "rows", scatter_dimension=0, tiled=True).astype(jnp.float32)
    grad_middle = incoming + norm_back(grad_input_mlp * (1.0 + scale_mlp), normed_mlp, inverse_mlp)
    grad_branch = (gate_attn * grad_middle).astype(jnp.bfloat16)
    grad_gate_attn = grad_middle * branch
    heads_here = queries.shape[2]
    gathered_branch, down_grad = spread(grad_branch, down_grad)
    proj_grad = lead_dot(gathered_branch, attended).astype(jnp.bfloat16)
    grad_attended = plain_dot(gathered_branch, proj_t).astype(jnp.bfloat16)
    grad_attended = grad_attended.reshape(count_rows, row_len, heads_here, HD)
    grad_query, grad_key, grad_value = attend_back(
        queries, key_rows, value_rows, image_ids, logsum, grad_attended
    )
    grad_query = turn(grad_query, geometry, -1.0)
    grad_key = turn(grad_key, geometry, -1.0)
    grad_packed = (
        jnp.stack([grad_query, grad_key, grad_value], axis=3)
        .reshape(count_rows * row_len, heads_here * 3 * HD)
        .astype(jnp.bfloat16)
    )
    qkv_bias_grad = jnp.sum(grad_packed, axis=0, dtype=jnp.float32)
    qkv_grad = lead_dot(input_attn, grad_packed).astype(jnp.bfloat16)
    grad_input_attn, (qkv_grad, proj_grad) = collect(
        grad_packed, lambda rows: tail_dot(rows, qkv_full), own_rows, (qkv_grad, proj_grad)
    )
    grad_input = grad_middle + norm_back(
        grad_input_attn * (1.0 + scale_attn), normed_attn, inverse_attn
    )
    grad_mods = jnp.concatenate(
        [
            grad_input_attn,
            grad_input_attn * normed_attn,
            grad_gate_attn,
            grad_input_mlp,
            grad_input_mlp * normed_mlp,
            grad_gate_mlp,
        ],
        axis=1,
    )
    return (grad_input, grad_mods, (qkv_grad, qkv_bias_grad, proj_grad, gu_out, down_grad))


def heads_in_order(value):
    index = lax.axis_index("heads")
    count = lax.axis_size("heads")
    chunks = [value] + [head_move(value, flip) for flip in range(1, count)]
    placed = []
    for slot in range(count):
        item = chunks[0]
        for flip in range(1, count):
            item = jnp.where(index == slot ^ flip, chunks[flip], item)
        placed.append(item)
    return jnp.stack(placed)


def heads_share(value):
    index = lax.axis_index("heads")
    count = lax.axis_size("heads")
    width = value.shape[-1] // count

    def part(flip):
        return lax.dynamic_slice_in_dim(value, (index ^ flip) * width, width, value.ndim - 1)

    arrived = [head_move(part(flip), flip) for flip in range(1, count)]
    total = part(0)
    for item in arrived:
        total = total + item
    return total


def shards(
    tokens,
    cond,
    image_of,
    grid_row,
    grid_col,
    ada_weight,
    ada_bias,
    qkv_weight,
    qkv_bias,
    proj_weight,
    gu_weight,
    down_weight,
    cotangent,
):
    own_rows = tokens.shape[0]
    image_count = cond.shape[0]
    block_count = qkv_weight.shape[0]
    row_size = lax.axis_size("rows")
    head_size = lax.axis_size("heads")
    head_index = lax.axis_index("heads")

    def device_order(values):
        parts = values.reshape(head_size, own_rows)
        picked = [
            lax.dynamic_index_in_dim(parts, head_index ^ flip, 0, keepdims=False)
            for flip in range(head_size)
        ]
        return jnp.concatenate(picked).reshape(values.shape)

    image_ids = device_order(image_of - lax.axis_index("rows") * image_count)
    own_images = image_ids.reshape(-1)[:own_rows]
    picker = (own_images[:, None] == jnp.arange(image_count, dtype=jnp.int32)[None, :]).astype(
        jnp.float32
    )
    geometry = lax.optimization_barrier(
        rope_parts(device_order(grid_row)) + rope_parts(device_order(grid_col))
    )
    shard_rows = qkv_weight.shape[1]

    def gathered(shard):
        return lax.all_gather(shard, "rows", axis=0, tiled=True)

    cond_wide = cond.astype(jnp.float32)
    cond_act = jax.nn.silu(cond_wide).astype(jnp.bfloat16)
    pad = -image_count % 16
    bias_rows = jnp.repeat(ada_bias.astype(jnp.float32), image_count, axis=0)
    *first, mods = start_call(
        row_size,
        head_size,
        jnp.pad(cond_act, ((0, pad), (0, 0))),
        ada_weight,
        bias_rows,
        [qkv_weight[0], proj_weight[0].T, gu_weight[0].reshape(shard_rows, -1), down_weight[0].T],
    )
    qkv_full, gu_full, down_t, proj_t = [], [], [], []
    for b in range(block_count):
        if b == 0:
            block = [item.reshape(-1, item.shape[-1]) for item in first]
        else:
            block = [
                gathered(qkv_weight[b]),
                gathered(proj_weight[b].T),
                gathered(gu_weight[b].reshape(shard_rows, -1)),
                gathered(down_weight[b].T),
            ]
        for held, item in zip((qkv_full, proj_t, gu_full, down_t), block):
            held.append(item)
    mod_all = mods.reshape(head_size, block_count, image_count, -1)
    cond_mine = lax.all_to_all(
        cond_act.reshape(image_count, row_size, -1).transpose(1, 0, 2), "rows", 0, 0
    ).reshape(row_size * image_count, -1)
    modulation = [
        jnp.concatenate([mod_all[index, b] for index in range(head_size)], axis=1)
        for b in range(block_count)
    ]
    pieces = [
        [piece_of(modulation[b], own_images, index) for index in range(6)] for b in range(block_count)
    ]
    residual = tokens.astype(jnp.float32)
    stored_all = []
    for b in range(block_count):
        residual, stored = block_forward(
            residual,
            pieces[b],
            qkv_full[b],
            qkv_bias[b].astype(jnp.float32),
            proj_t[b],
            gu_full[b],
            down_t[b],
            image_ids,
            geometry,
        )
        stored_all.append(stored)
    block_out = residual.astype(jnp.bfloat16)
    incoming = cotangent.astype(jnp.float32)
    block_grads = [None] * block_count
    image_sums = [None] * block_count
    for b in reversed(range(block_count)):
        incoming, grad_mods, gradients = block_backward(
            incoming,
            pieces[b],
            stored_all[b],
            qkv_full[b],
            proj_t[b],
            gu_full[b],
            down_t[b],
            image_ids,
            geometry,
        )
        image_sums[b] = lax.dot_general(
            picker, grad_mods, (((0,), (0,)), ((), ())), precision=highest
        )
        block_grads[b] = gradients
    image_grads = heads_share(jnp.stack(image_sums)).astype(jnp.bfloat16)
    bias_sums = jnp.stack([item[1] for item in block_grads])
    bias_high = bias_sums.astype(jnp.bfloat16)
    bias_rest = bias_sums - bias_high.astype(jnp.float32)
    bias_middle = bias_rest.astype(jnp.bfloat16)
    bias_low = (bias_rest - bias_middle.astype(jnp.float32)).astype(jnp.bfloat16)
    small = jnp.concatenate(
        [
            image_grads.reshape(1, -1),
            bias_high.reshape(1, -1),
            bias_middle.reshape(1, -1),
            bias_low.reshape(1, -1),
        ],
        axis=1,
    )
    small_size = small.size
    small = jnp.pad(small, ((0, 0), (0, -small_size % 2048))).reshape(16, -1)
    parts = []
    for b in reversed(range(block_count)):
        parts += [block_grads[b][4], block_grads[b][2], block_grads[b][0]]
    *sums, small = scatter_call(
        row_size, head_size, [part.reshape(row_size, shard_rows, -1) for part in parts], small
    )
    sums = [sums[3 * b : 3 * b + 3] for b in reversed(range(block_count))]
    small = small.reshape(row_size, -1)[:, :small_size]
    split = image_grads.size
    all_grads = small[:, :split].reshape((row_size,) + image_grads.shape)
    bias_all = small[:, split:].reshape((row_size, 3) + bias_sums.shape).astype(jnp.float32)
    qkv_bias_out = jnp.sum(bias_all, axis=(0, 1))
    ada_grads = []
    cond_partial = 0.0
    for b in range(block_count):
        block_grads_all = all_grads[:, b].reshape(row_size * image_count, -1)
        ada_grads.append(lead_dot(cond_mine, block_grads_all))
        cond_partial = cond_partial + tail_dot(block_grads_all, ada_weight[b])
    ada_bias_grads = jnp.sum(all_grads, axis=(0, 2), dtype=jnp.float32)
    cond_parts = lax.all_to_all(
        cond_partial.astype(jnp.bfloat16).reshape(row_size, image_count, -1), "rows", 0, 0
    )
    cond_rows = cond_parts.transpose(1, 0, 2).reshape(image_count, -1).astype(jnp.float32)
    cond_total = cond_rows
    for flip in range(1, head_size):
        cond_total = cond_total + head_move(cond_rows.astype(jnp.bfloat16), flip).astype(jnp.float32)
    logistic = jax.nn.sigmoid(cond_wide)
    cond_grad = cond_total * logistic * (1.0 + cond_wide * (1.0 - logistic))
    return (
        block_out,
        incoming,
        cond_grad,
        jnp.stack(ada_grads),
        ada_bias_grads,
        jnp.stack([item[2] for item in sums]),
        qkv_bias_out,
        jnp.stack([item[1].T for item in sums]),
        jnp.stack([item[3].reshape(gu_weight.shape[1:]) for item in block_grads]),
        jnp.stack([item[0].T for item in sums]),
    )


def solution(mesh):
    in_specs = (
        P(("rows", "heads"), None),
        P("rows", None),
        P("rows", None),
        P("rows", None),
        P("rows", None),
        P(None, "rows", "heads"),
        P(None, "heads"),
        P(None, "rows", "heads"),
        P(None, "heads"),
        P(None, "heads", "rows"),
        P(None, "rows", None, "heads"),
        P(None, "heads", "rows"),
        P(("rows", "heads"), None),
    )
    out_specs = (
        P(("rows", "heads"), None),
        P(("rows", "heads"), None),
        P("rows", None),
        P(None, "rows", "heads"),
        P(None, "heads"),
        P(None, "rows", "heads"),
        P(None, "heads"),
        P(None, "heads", "rows"),
        P(None, "rows", None, "heads"),
        P(None, "heads", "rows"),
    )
    return jax.shard_map(shards, mesh=mesh, in_specs=in_specs, out_specs=out_specs, check_vma=False)
```

```python
import functools

import jax
import jax.numpy as jnp
from jax import lax
from jax.experimental import pallas as pl
from jax.experimental.pallas import tpu as pltpu
from jax.sharding import PartitionSpec as P

HD = 72


epsilon = 1e-06
theta_base = 10000.0
highest = lax.Precision.HIGHEST


def normalize(values):
    center = values - jnp.mean(values, axis=-1, keepdims=True)
    inverse = lax.rsqrt(jnp.mean(center * center, axis=-1, keepdims=True) + epsilon)
    return (center * inverse, inverse)


def norm_back(incoming, normed, inverse):
    return inverse * (
        incoming
        - jnp.mean(incoming, axis=-1, keepdims=True)
        - normed * jnp.mean(incoming * normed, axis=-1, keepdims=True)
    )


def lead_dot(operand, other):
    return lax.dot_general(
        operand, other, (((0,), (0,)), ((), ())), preferred_element_type=jnp.float32
    )


def tail_dot(operand, other):
    return lax.dot_general(
        operand, other, (((1,), (1,)), ((), ())), preferred_element_type=jnp.float32
    )


def angles(coords, quarter):
    frequency = theta_base ** (-jnp.arange(quarter, dtype=jnp.float32) / quarter)
    return coords.astype(jnp.float32)[..., None] * frequency


def head_move(value, flip):
    size = lax.axis_size("heads")
    return lax.ppermute(value, "heads", [(index, index ^ flip) for index in range(size)])


MESH = pl.DeviceIdType.MESH


class Place:
    def __init__(self, row_size, head_size):
        self.sizes = (4, row_size // 8, 2)
        index = lax.axis_index("rows")
        a, b, c = self.sizes
        self.mine = (index // (b * c), (index // c) % b, index % c)
        self.heads = head_size
        self.head = lax.axis_index("heads")

    def step(self, dim, by):
        return (self.mine[dim] + by + self.sizes[dim]) % self.sizes[dim]

    def row(self, a, b, c):
        return (a * self.sizes[1] + b) * self.sizes[2] + c

    def near(self, dim, by):
        at = list(self.mine)
        at[dim] = self.step(dim, by)
        return {"rows": self.row(*at)}

    def flip(self, by):
        return {"heads": self.head ^ by}

    def partners(self, with_heads):
        found = [self.near(dim, by) for dim in range(3) for by in range(1, self.sizes[dim])]
        if with_heads:
            found += [self.flip(by) for by in range(1, self.heads)]
        return found

    def greet(self, with_heads):
        barrier = pltpu.get_barrier_semaphore()
        found = self.partners(with_heads)
        for partner in found:
            pl.semaphore_signal(barrier, inc=1, device_id=partner, device_id_type=MESH)
        pl.semaphore_wait(barrier, len(found))


def gather_count(row_size):
    a, b, c = 4, row_size // 8, 2
    return 2 * (a - 1) + (2 * a - 1) * (2 * b - 1)


class Gather:
    def __init__(self, place, shard, out, send, recv, local):
        self.place, self.shard, self.out = place, shard, out
        self.send, self.recv = send, recv
        self.used = 0
        self.keep = pltpu.make_async_copy(shard, out.at[place.row(*place.mine)], local)
        a, b, _ = place.sizes
        self.hops, self.along_b, self.along_c = {}, {}, {}
        names = [(0, 0)] + [(way, k) for k in range(1, a) for way in (1, -1)]
        for way, k in names:
            if k:
                self.hops[way, k] = self.copy(way, k - 1, 0, place.near(0, way))
        for way, k in names:
            for j in range(1, b):
                self.along_b[way, k, j] = self.copy(way, k, 0, place.near(1, j))
        for way, k in names:
            for j in range(b):
                self.along_c[way, k, j] = self.copy(way, k, j, place.near(2, 1))

    def copy(self, way, k, j, device):
        place, slot = self.place, self.used
        self.used += 1
        index = place.row(place.step(0, -way * k), place.step(1, -j), place.mine[2])
        return pltpu.make_async_remote_copy(
            src_ref=self.shard if k == 0 and j == 0 else self.out.at[index],
            dst_ref=self.out.at[index],
            send_sem=self.send.at[slot],
            recv_sem=self.recv.at[slot],
            device_id=device,
            device_id_type=MESH,
        )

    def holds(self, way, k):
        at = self.place.mine[0]
        return at >= k if way > 0 else at < self.place.sizes[0] - k

    def hop(self, way, k):
        at = self.place.mine[0]
        last = self.place.sizes[0] - 1
        return (at < last) & (at >= k - 1) if way > 0 else (at > 0) & (at <= last - (k - 1))

    def begin(self):
        self.keep.start()
        for way in (1, -1):
            pl.when(self.hop(way, 1))(self.hops[way, 1].start)
        self.pass_on(0, 0)

    def pass_on(self, way, k):
        for j in range(1, self.place.sizes[1]):
            self.along_b[way, k, j].start()
        self.along_c[way, k, 0].start()

    def first(self, k):
        for way in (1, -1):

            @pl.when(self.holds(way, k))
            def _():
                self.hops[way, k].wait_recv()
                if k + 1 < self.place.sizes[0]:
                    pl.when(self.hop(way, k + 1))(self.hops[way, k + 1].start)
                self.pass_on(way, k)

    def each(self, way, k, action):
        if k:
            pl.when(self.holds(way, k))(action)
        else:
            action()

    def second(self):
        for way, k, j in self.along_b:

            def action():
                self.along_b[way, k, j].wait_recv()
                self.along_c[way, k, j].start()

            self.each(way, k, action)

    def finish(self):
        for way, k, j in self.along_c:

            def action():
                self.along_c[way, k, j].wait_recv()
                self.along_c[way, k, j].wait_send()

            self.each(way, k, action)
        for way, k, j in self.along_b:
            self.each(way, k, self.along_b[way, k, j].wait_send)
        for way, k in self.hops:
            pl.when(self.hop(way, k))(self.hops[way, k].wait_send)
        self.keep.wait()


def gather_all(items):
    count = len(items)
    items[0].begin()
    for step in range(count + 1):
        if step < count:
            items[step].first(1)
            if step + 1 < count:
                items[step + 1].begin()
            for k in range(2, items[step].place.sizes[0]):
                items[step].first(k)
        if step >= 1:
            items[step - 1].second()
    for item in items:
        item.finish()


def scatter_count(row_size):
    a, b, c = 4, row_size // 8, 2
    return a * b + a * (b - 1) + (a - 1)


class Scatter:
    def __init__(self, place, source, out, held, met, side, far, send, recv, load):
        self.place, self.source, self.out = place, source, out
        self.held, self.met, self.side, self.far = held, met, side, far
        self.send, self.recv, self.load = send, recv, load

    def remote(self, source, target, slot, device):
        return pltpu.make_async_remote_copy(
            src_ref=source,
            dst_ref=target,
            send_sem=self.send.at[slot],
            recv_sem=self.recv.at[slot],
            device_id=device,
            device_id_type=MESH,
        )

    def across(self, k, j):
        place = self.place
        a, b = place.step(0, k), place.step(1, j)
        other = place.step(2, 1)
        return self.remote(
            self.source.at[place.row(a, b, other)],
            self.met.at[a, b],
            k * place.sizes[1] + j,
            place.near(2, 1),
        )

    def fetch(self, k, j):
        place = self.place
        a, b = place.step(0, k), place.step(1, j)
        return pltpu.make_async_copy(
            self.source.at[place.row(a, b, place.mine[2])],
            self.held.at[a, b],
            self.load.at[k * place.sizes[1] + j],
        )

    def along_b(self, k, j):
        place = self.place
        a, b = place.step(0, k), place.step(1, j)
        base = place.sizes[0] * place.sizes[1]
        return self.remote(
            self.held.at[a, b],
            self.side.at[j - 1, a],
            base + (j - 1) * place.sizes[0] + k,
            place.near(1, j),
        )

    def along_a(self, k):
        place = self.place
        base = place.sizes[0] * (2 * place.sizes[1] - 1)
        return self.remote(
            self.held.at[place.step(0, k), place.mine[1]],
            self.far.at[k - 1],
            base + k - 1,
            place.near(0, k),
        )

    def order(self):
        a, b, _ = self.place.sizes
        return [(k, j) for j in list(range(1, b)) + [0] for k in list(range(1, a)) + [0]]

    def begin(self):
        for k, j in self.order():
            self.fetch(k, j).start()
            self.across(k, j).start()

    def first(self):
        place = self.place
        a, b, _ = place.sizes
        for j in range(1, b):
            for k in list(range(1, a)) + [0]:
                self.fetch(k, j).wait()
                self.across(k, j).wait_recv()
                at = (place.step(0, k), place.step(1, j))
                self.held[at] = (
                    self.held[at].astype(jnp.float32) + self.met[at].astype(jnp.float32)
                ).astype(self.held.dtype)
                self.along_b(k, j).start()

    def total(self, k):
        place = self.place
        a, b = place.step(0, k), place.mine[1]
        value = self.held[a, b].astype(jnp.float32) + self.met[a, b].astype(jnp.float32)
        for j in range(1, place.sizes[1]):
            value = value + self.side[j - 1, a].astype(jnp.float32)
        return value

    def second(self):
        place = self.place
        a, b, _ = place.sizes
        for k in list(range(1, a)) + [0]:
            self.fetch(k, 0).wait()
            self.across(k, 0).wait_recv()
            for j in range(1, b):
                self.along_b(k, j).wait_recv()
            if k:
                self.held[place.step(0, k), place.mine[1]] = self.total(k).astype(self.held.dtype)
                self.along_a(k).start()
            else:
                self.out[...] = self.total(0)

    def finish(self):
        place = self.place
        a, b, _ = place.sizes
        for k in range(1, a):
            self.along_a(k).wait_recv()
            self.out[...] = self.out[...] + self.far[k - 1].astype(jnp.float32)
        for k, j in self.order():
            self.across(k, j).wait_send()
            if j:
                self.along_b(k, j).wait_send()
        for k in range(1, a):
            self.along_a(k).wait_send()


def scatter_all(items):
    count = len(items)
    for item in items:
        item.begin()
    for step in range(count + 2):
        if step < count:
            items[step].first()
        if 1 <= step <= count:
            items[step - 1].second()
        if step >= 2:
            items[step - 2].finish()


def start_kernel(row_size, head_size, images, blocks, weights, *refs):
    cond, ada, bias = refs[:3]
    shards = refs[3 : 3 + weights]
    outs = refs[3 + weights : 3 + 2 * weights]
    mods, mine_out = refs[3 + 2 * weights : 5 + 2 * weights]
    (conds, part, held, met, side, far, total, every, sends, recvs, keeps, mod_send, mod_recv, mod_load, head_send, head_recv) = refs[5 + 2 * weights :]
    place = Place(row_size, head_size)
    place.greet(True)
    items = [
        Gather(place, shard, out, sends.at[i], recvs.at[i], keeps.at[i])
        for i, (shard, out) in enumerate(zip((cond,) + shards, (conds,) + outs))
    ]
    lead, bulk = items[0], items[1:]
    lead.begin()
    bulk[0].begin()
    hops = range(1, place.sizes[0])
    for k in hops:
        lead.first(k)
    lead.second()
    lead.finish()
    width = cond.shape[1]
    share = ada.shape[1]
    pad = cond.shape[0]
    lane = lax.broadcasted_iota(jnp.int32, (width, share), 0)
    slot = lax.broadcasted_iota(jnp.int32, (width, share), 1)
    pick = jnp.where(lane == lax.axis_index("rows") * share + slot, 1.0, 0.0).astype(jnp.bfloat16)
    mine = jnp.dot(
        conds[...].reshape(row_size * pad, width), pick, preferred_element_type=jnp.float32
    ).astype(jnp.bfloat16)
    mine_out[...] = mine
    for b in range(blocks):
        value = jnp.dot(mine, ada[b], preferred_element_type=jnp.float32)
        part[:, b * images : (b + 1) * images, :] = value.reshape(row_size, pad, -1)[:, :images]
    sums = Scatter(place, part, total, held, met, side, far, mod_send, mod_recv, mod_load)
    sums.begin()
    bulk[0].first(1)
    for item in bulk[1:]:
        item.begin()
    sums.first()
    for k in hops[1:]:
        bulk[0].first(k)
    sums.second()
    for item in bulk[1:]:
        for k in hops:
            item.first(k)
    sums.finish()
    every[place.head] = total[...] + bias[...]
    across = [
        pltpu.make_async_remote_copy(
            src_ref=every.at[place.head],
            dst_ref=every.at[place.head],
            send_sem=head_send.at[by - 1],
            recv_sem=head_recv.at[by - 1],
            device_id=place.flip(by),
            device_id_type=MESH,
        )
        for by in range(1, head_size)
    ]
    for copy in across:
        copy.start()
    for item in bulk:
        item.second()
    for copy in across:
        copy.wait()
    mods[...] = every[...]
    for item in bulk:
        item.finish()


def start_call(row_size, head_size, cond, ada, bias, shards):
    images = bias.shape[0] // ada.shape[0]
    blocks = ada.shape[0]
    count = len(shards)
    a, b = 4, row_size // 8
    chunk = bias.shape
    copies = gather_count(row_size)
    anywhere = pl.BlockSpec(memory_space=pl.ANY)
    vmem = pl.BlockSpec(memory_space=pltpu.VMEM)
    f32 = jnp.float32
    return pl.pallas_call(
        functools.partial(start_kernel, row_size, head_size, images, blocks, count),
        out_shape=[jax.ShapeDtypeStruct((row_size,) + item.shape, item.dtype) for item in shards]
        + [
            jax.ShapeDtypeStruct((head_size,) + chunk, f32),
            jax.ShapeDtypeStruct((row_size * cond.shape[0], ada.shape[1]), cond.dtype),
        ],
        in_specs=[vmem] * 3 + [anywhere] * count,
        out_specs=[anywhere] * count + [vmem] * 2,
        scratch_shapes=[
            pltpu.VMEM((row_size,) + cond.shape, cond.dtype),
            pltpu.VMEM((row_size,) + chunk, f32),
            pltpu.VMEM((a, b) + chunk, f32),
            pltpu.VMEM((a, b) + chunk, f32),
            pltpu.VMEM((b - 1, a) + chunk, f32),
            pltpu.VMEM((a - 1,) + chunk, f32),
            pltpu.VMEM(chunk, f32),
            pltpu.VMEM((head_size,) + chunk, f32),
            pltpu.SemaphoreType.DMA((count + 1, copies)),
            pltpu.SemaphoreType.DMA((count + 1, copies)),
            pltpu.SemaphoreType.DMA((count + 1,)),
            pltpu.SemaphoreType.DMA((scatter_count(row_size),)),
            pltpu.SemaphoreType.DMA((scatter_count(row_size),)),
            pltpu.SemaphoreType.DMA((a * b,)),
            pltpu.SemaphoreType.DMA((head_size - 1,)),
            pltpu.SemaphoreType.DMA((head_size - 1,)),
        ],
        compiler_params=pltpu.CompilerParams(
            collective_id=1, has_side_effects=True, vmem_limit_bytes=48 * 2**20
        ),
        name="start",
    )(cond, ada, bias, *shards)


def finish_kernel(row_size, head_size, images, blocks, count, *refs):
    small, mine, ada, factor = refs[:4]
    ins = refs[4 : 4 + count]
    ada_out, ada_bias_out, qkv_bias_out, cond_out = refs[4 + count : 8 + count]
    outs = refs[8 + count : 8 + 2 * count]
    refs = refs[8 + 2 * count :]
    scratch = refs[: 4 * count]
    refs = refs[4 * count :]
    every, part, held, met, side, far, total, landed = refs[:8]
    send, recv, load, small_send, small_recv, small_keep = refs[8:14]
    cond_send, cond_recv, cond_load, head_send, head_recv = refs[14:]
    place = Place(row_size, head_size)
    place.greet(True)
    lead = Gather(place, small, every, small_send, small_recv, small_keep.at[0])
    lead.begin()
    items = [
        Scatter(
            place, ins[i], outs[i], *scratch[4 * i : 4 * i + 4], send.at[i], recv.at[i], load.at[i]
        )
        for i in range(count)
    ]
    for item in items:
        item.begin()
    hops = range(1, place.sizes[0])
    for k in hops:
        lead.first(k)
    for item in items:
        item.first()
    lead.second()
    items[0].second()
    lead.finish()
    rows = small.shape[0]
    share, width = ada.shape[1], cond_out.shape[1]
    grads = every[...].reshape(row_size * rows, -1)
    columns = qkv_bias_out.shape[1]
    for b in range(blocks):
        value = dot_tn(mine[b], grads)
        ada_out[b] = value[:share]
        ada_bias_out[b : b + 1, :] = value[share : share + 1]
        qkv_bias_out[b : b + 1, :] = value[share + 1 : share + 2, :columns]
    lane = lax.broadcasted_iota(jnp.int32, (share, width), 1)
    slot = lax.broadcasted_iota(jnp.int32, (share, width), 0)
    pick = jnp.where(lane == lax.axis_index("rows") * share + slot, 1.0, 0.0).astype(jnp.bfloat16)
    back = 0.0
    for b in range(blocks):
        value = dot_nt(grads, ada[b]).reshape(row_size, rows, share)
        back = back + value[:, b * images : (b + 1) * images]
    pad = part.shape[1]
    back = back.reshape(row_size * images, share).astype(jnp.bfloat16)
    part[...] = jnp.zeros_like(part)
    part[:, :images, :] = dot_nn(back, pick).reshape(row_size, images, width)
    sums = Scatter(place, part, total, held, met, side, far, cond_send, cond_recv, cond_load)
    sums.begin()
    sums.first()
    for item in items[1:2]:
        item.second()
    sums.second()
    for item in items[2:]:
        item.second()
    sums.finish()
    across = Across(
        place, lambda by: total, lambda by: landed.at[by - 1], head_send, head_recv, 0
    )
    for by in range(1, head_size):
        across.start(by)
    for item in items:
        item.finish()
    value = total[...]
    for by in range(1, head_size):
        across.arrived(by)
        value = value + landed[by - 1]
    cond_out[...] = value * factor[...]
    across.left()


def finish_call(row_size, head_size, images, grads, small, mine, ada, factor, columns):
    count = len(grads)
    copies = scatter_count(row_size)
    small_copies = gather_count(row_size)
    blocks, share, wide = ada.shape
    a, b = 4, row_size // 8
    f32 = jnp.float32
    shape = jax.ShapeDtypeStruct
    scratch = []
    for grad in grads:
        chunk = grad.shape[1:]
        for lead in ((a, b), (a, b), (b - 1, a), (a - 1,)):
            scratch.append(pltpu.VMEM(lead + chunk, grad.dtype))
    chunk = factor.shape
    anywhere = pl.BlockSpec(memory_space=pl.ANY)
    vmem = pl.BlockSpec(memory_space=pltpu.VMEM)
    return pl.pallas_call(
        functools.partial(finish_kernel, row_size, head_size, images, blocks, count),
        out_shape=[
            shape(ada.shape, f32),
            shape((blocks, wide), f32),
            shape((blocks, columns), f32),
            shape(factor.shape, f32),
        ]
        + [shape(grad.shape[1:], f32) for grad in grads],
        in_specs=[anywhere] + [vmem] * 3 + [anywhere] * count,
        out_specs=[vmem] * (4 + count),
        scratch_shapes=scratch
        + [
            pltpu.VMEM((row_size,) + small.shape, small.dtype),
            pltpu.VMEM((row_size,) + chunk, f32),
            pltpu.VMEM((a, b) + chunk, f32),
            pltpu.VMEM((a, b) + chunk, f32),
            pltpu.VMEM((b - 1, a) + chunk, f32),
            pltpu.VMEM((a - 1,) + chunk, f32),
            pltpu.VMEM(chunk, f32),
            pltpu.VMEM((head_size - 1,) + chunk, f32),
            pltpu.SemaphoreType.DMA((count, copies)),
            pltpu.SemaphoreType.DMA((count, copies)),
            pltpu.SemaphoreType.DMA((count, a * b)),
            pltpu.SemaphoreType.DMA((small_copies,)),
            pltpu.SemaphoreType.DMA((small_copies,)),
            pltpu.SemaphoreType.DMA((1,)),
            pltpu.SemaphoreType.DMA((copies,)),
            pltpu.SemaphoreType.DMA((copies,)),
            pltpu.SemaphoreType.DMA((a * b,)),
            pltpu.SemaphoreType.DMA((head_size - 1,)),
            pltpu.SemaphoreType.DMA((head_size - 1,)),
        ],
        compiler_params=pltpu.CompilerParams(
            collective_id=2, has_side_effects=True, vmem_limit_bytes=56 * 2**20
        ),
        name="finish",
    )(small, mine, ada, factor, *grads)


def weight_grads_kernel(*refs):
    count = len(refs) // 3
    for i in range(count):
        left, right, out = refs[2 * i], refs[2 * i + 1], refs[2 * count + i]
        columns = out.shape[1]
        for at in range(0, columns, 256):
            size = min(256, columns - at)
            out[:, at : at + size] = dot_tn(left[...], right[:, at : at + size]).astype(out.dtype)


def weight_grads(*pairs):
    vmem = pl.BlockSpec(memory_space=pltpu.VMEM)
    flat = [item for pair in pairs for item in pair]
    flops = sum(2 * left.size * right.shape[1] for left, right in pairs)
    moved = sum(2 * (left.size + right.size + left.shape[1] * right.shape[1]) for left, right in pairs)
    return pl.pallas_call(
        weight_grads_kernel,
        out_shape=[
            jax.ShapeDtypeStruct((left.shape[1], right.shape[1]), jnp.bfloat16)
            for left, right in pairs
        ],
        in_specs=[vmem] * len(flat),
        out_specs=[vmem] * len(pairs),
        compiler_params=pltpu.CompilerParams(vmem_limit_bytes=48 * 2**20),
        cost_estimate=pl.CostEstimate(flops=flops, bytes_accessed=moved, transcendentals=0),
        name="weight_grads",
    )(*flat)


def tile_of(width):
    return next(size for size in (256, 128, width) if width % size == 0)


def dot_nn(left, right):
    return jnp.dot(left, right, preferred_element_type=jnp.float32)


def dot_nt(left, right):
    return lax.dot_general(left, right, (((1,), (1,)), ((), ())), preferred_element_type=jnp.float32)


def dot_tn(left, right):
    return lax.dot_general(left, right, (((0,), (0,)), ((), ())), preferred_element_type=jnp.float32)


def tiles(width, size, body):
    @pl.loop(0, width // size)
    def _(step):
        body(step, pl.multiple_of(step * size, size))


class Across:
    def __init__(self, place, sources, targets, send, recv, stage):
        count = place.heads - 1
        self.copies = [
            pltpu.make_async_remote_copy(
                src_ref=sources(by),
                dst_ref=targets(by),
                send_sem=send.at[stage * count + by - 1],
                recv_sem=recv.at[stage * count + by - 1],
                device_id=place.flip(by),
                device_id_type=MESH,
            )
            for by in range(1, place.heads)
        ]

    def start(self, by):
        self.copies[by - 1].start()

    def arrived(self, by):
        self.copies[by - 1].wait_recv()

    def left(self):
        for copy in self.copies:
            copy.wait_send()


class Streamed:
    def __init__(self, buffer, out, sems, size):
        self.buffer, self.out, self.sems, self.size = buffer, out, sems, size

    def copy(self, step):
        return pltpu.make_async_copy(
            self.buffer.at[step % 2],
            self.out.at[:, pl.ds(pl.multiple_of(step * self.size, self.size), self.size)],
            self.sems.at[step % 2],
        )

    def put(self, step, value):
        @pl.when(step >= 2)
        def _():
            self.copy(step - 2).wait()

        self.buffer[step % 2] = value.astype(self.buffer.dtype)
        self.copy(step).start()

    def drain(self, steps):
        for step in range(max(steps - 2, 0), steps):
            self.copy(step).wait()


def mlp_back_kernel(row_size, head_size, count, *refs):
    (incoming, gate_mlp, scale_mlp, gate_attn, normed, inverse) = refs[:6]
    streams = refs[6:12]
    grads = refs[12 : 12 + count]
    outs = refs[12 + count : 18 + 2 * count]
    grad_in, grad_mid, branch_out, grad_att, gu_out, down_out = outs[:6]
    sums = outs[6:]
    refs = refs[18 + 2 * count :]
    down, gate_up, gu, inputs, hidden, proj = refs[:6]
    mlp_all, branch_all, ggu, parcel, landed, own_part, buffer = refs[6:13]
    loads, sends, recvs, tile_sems, out_sem = refs[13:18]
    scratch = refs[18 : 18 + 4 * count]
    sum_send, sum_recv, sum_load = refs[18 + 4 * count :]
    place = Place(row_size, head_size)
    heads = head_size
    own, width = incoming.shape
    units = hidden.shape[1]
    step_units = tile_of(units)
    step_width = tile_of(width)
    copies = [
        pltpu.make_async_copy(source, target, loads.at[i])
        for i, (source, target) in enumerate(
            zip(streams, (down, gate_up, gu, inputs, hidden, proj))
        )
    ]
    place.greet(True)
    mlp_all[0] = (gate_mlp[...] * incoming[...]).astype(jnp.bfloat16)
    first = Across(place, lambda by: mlp_all.at[0], lambda by: mlp_all.at[by], sends, recvs, 0)
    for by in range(1, heads):
        first.start(by)
    for copy in copies:
        copy.start()
    items = [
        Scatter(
            place,
            grads[i],
            sums[i],
            *scratch[4 * i : 4 * i + 4],
            sum_send.at[i],
            sum_recv.at[i],
            sum_load.at[i],
        )
        for i in range(count)
    ]
    for item in items:
        item.begin()

    def hidden_back(slot):
        rows = pl.ds(slot * own, own)

        def body(step, at):
            gate = gate_up[rows, pl.ds(at, step_units)]
            up = gate_up[rows, pl.ds(pl.multiple_of(units + at, 128), step_units)]
            grad = dot_nn(mlp_all[slot], down[:, pl.ds(at, step_units)])
            logistic = jax.nn.sigmoid(gate)
            ggu[rows, pl.ds(at, step_units)] = (
                grad * up * logistic * (1.0 + gate * (1.0 - logistic))
            ).astype(jnp.bfloat16)
            ggu[rows, pl.ds(pl.multiple_of(units + at, 128), step_units)] = (
                grad * gate * logistic
            ).astype(jnp.bfloat16)

        tiles(units, step_units, body)

    copies[0].wait()
    copies[1].wait()
    hidden_back(0)
    for item in items:
        item.first()
    for by in range(1, heads):
        first.arrived(by)
        hidden_back(by)
    copies[2].wait()
    second = Across(
        place, lambda by: parcel.at[by - 1], lambda by: landed.at[by - 1], sends, recvs, 1
    )
    for by in range(1, heads):

        def body(step, at):
            parcel[by - 1, :, pl.ds(at, step_width)] = dot_nt(
                ggu[pl.ds(by * own, own), :], gu[pl.ds(at, step_width), :]
            ).astype(jnp.bfloat16)

        tiles(width, step_width, body)
        second.start(by)

    def body(step, at):
        own_part[:, pl.ds(at, step_width)] = dot_nt(ggu[pl.ds(0, own), :], gu[pl.ds(at, step_width), :])

    tiles(width, step_width, body)
    for item in items[:1]:
        item.second()
    copies[3].wait()
    out = Streamed(buffer, gu_out, tile_sems, step_units)

    def body(step, at):
        out.put(step, dot_tn(inputs[...], ggu[:, pl.ds(at, step_units)]))

    tiles(2 * units, step_units, body)
    total = own_part[...]
    for by in range(1, heads):
        second.arrived(by)
        total = total + landed[by - 1].astype(jnp.float32)
    grad_in[...] = total
    scaled = total * (1.0 + scale_mlp[...])
    middle = incoming[...] + inverse[...] * (
        scaled
        - jnp.mean(scaled, axis=-1, keepdims=True)
        - normed[...] * jnp.mean(scaled * normed[...], axis=-1, keepdims=True)
    )
    grad_mid[...] = middle
    branch_all[0] = (gate_attn[...] * middle).astype(jnp.bfloat16)
    third = Across(place, lambda by: branch_all.at[0], lambda by: branch_all.at[by], sends, recvs, 2)
    for by in range(1, heads):
        third.start(by)
    for item in items[1:2]:
        item.second()
    out.drain(2 * units // step_units)
    copies[4].wait()
    copies[5].wait()
    out = Streamed(buffer, down_out, tile_sems, step_units)

    def body(step, at):
        out.put(
            step,
            dot_tn(mlp_all[...].reshape(heads * own, width), hidden[:, pl.ds(at, step_units)]),
        )

    tiles(units, step_units, body)
    grad_att[pl.ds(0, own), :] = dot_nn(branch_all[0], proj[...]).astype(jnp.bfloat16)
    for item in items[2:]:
        item.second()
    for by in range(1, heads):
        third.arrived(by)
        grad_att[pl.ds(by * own, own), :] = dot_nn(branch_all[by], proj[...]).astype(jnp.bfloat16)
    keep = pltpu.make_async_copy(branch_all, branch_out, out_sem.at[0])
    keep.start()
    out.drain(units // step_units)
    for item in items:
        item.finish()
    for stage in (first, second, third):
        stage.left()
    keep.wait()


def mlp_back_call(row_size, head_size, near, streams, grads):
    count = len(grads)
    own, width = near[0].shape
    down, gate_up, gu, inputs, hidden, proj = streams
    units = hidden.shape[1]
    tokens = hidden.shape[0]
    a, b = 4, row_size // 8
    copies = scatter_count(row_size)
    scratch = []
    for grad in grads:
        chunk = grad.shape[1:]
        for lead in ((a, b), (a, b), (b - 1, a), (a - 1,)):
            scratch.append(pltpu.VMEM(lead + chunk, grad.dtype))
    anywhere = pl.BlockSpec(memory_space=pl.ANY)
    vmem = pl.BlockSpec(memory_space=pltpu.VMEM)
    shape = jax.ShapeDtypeStruct
    f32, bf16 = jnp.float32, jnp.bfloat16
    return pl.pallas_call(
        functools.partial(mlp_back_kernel, row_size, head_size, count),
        out_shape=[
            shape((own, width), f32),
            shape((own, width), f32),
            shape((head_size, own, width), bf16),
            shape((tokens, proj.shape[1]), bf16),
            shape((width, 2 * units), bf16),
            shape((width, units), bf16),
        ]
        + [shape(grad.shape[1:], f32) for grad in grads],
        in_specs=[vmem] * 6 + [anywhere] * (6 + count),
        out_specs=[vmem, vmem, anywhere, vmem, anywhere, anywhere] + [vmem] * count,
        scratch_shapes=[pltpu.VMEM(item.shape, item.dtype) for item in streams]
        + [
            pltpu.VMEM((head_size, own, width), bf16),
            pltpu.VMEM((head_size, own, width), bf16),
            pltpu.VMEM((tokens, 2 * units), bf16),
            pltpu.VMEM((head_size - 1, own, width), bf16),
            pltpu.VMEM((head_size - 1, own, width), bf16),
            pltpu.VMEM((own, width), f32),
            pltpu.VMEM((2, width, tile_of(units)), bf16),
            pltpu.SemaphoreType.DMA((6,)),
            pltpu.SemaphoreType.DMA((3 * (head_size - 1),)),
            pltpu.SemaphoreType.DMA((3 * (head_size - 1),)),
            pltpu.SemaphoreType.DMA((2,)),
            pltpu.SemaphoreType.DMA((1,)),
        ]
        + scratch
        + [
            pltpu.SemaphoreType.DMA((count, copies)),
            pltpu.SemaphoreType.DMA((count, copies)),
            pltpu.SemaphoreType.DMA((count, a * b)),
        ],
        compiler_params=pltpu.CompilerParams(
            collective_id=3, has_side_effects=True, vmem_limit_bytes=62 * 2**20
        ),
        name="mlp_back",
    )(*near, *streams, *grads)


def rope_parts(coords):
    angle = angles(coords, HD // 4)
    return jnp.cos(angle), jnp.sin(angle)


def turn(vectors, geometry, sign):
    row_cos, row_sin, col_cos, col_sin = [item[:, :, None, :] for item in geometry]
    quarter = HD // 4
    a, b, c, d = [vectors[..., quarter * i : quarter * (i + 1)] for i in range(4)]
    return jnp.concatenate(
        [
            a * row_cos - b * (sign * row_sin),
            b * row_cos + a * (sign * row_sin),
            c * col_cos - d * (sign * col_sin),
            d * col_cos + c * (sign * col_sin),
        ],
        axis=-1,
    )


def masked_scores(queries, key_rows, image_ids):
    scores = jnp.einsum(
        "rqhe,rkhe->rhqk", queries, key_rows, preferred_element_type=jnp.float32
    ) * HD ** (-0.5)
    same_image = image_ids[:, :, None] == image_ids[:, None, :]
    return jnp.where(same_image[:, None], scores, -1e30)


def attend(queries, key_rows, value_rows, image_ids):
    scores = masked_scores(queries, key_rows, image_ids)
    maximum = jnp.max(scores, axis=-1, keepdims=True)
    scaled_exp = jnp.exp(scores - maximum)
    denominator = jnp.sum(scaled_exp, axis=-1, keepdims=True)
    weights = (scaled_exp / denominator).astype(jnp.bfloat16)
    attended = jnp.einsum("rhqk,rkhe->rqhe", weights, value_rows, preferred_element_type=jnp.float32)
    return (attended.astype(jnp.bfloat16), (maximum + jnp.log(denominator))[..., 0])


def attend_back(queries, key_rows, value_rows, image_ids, logsum, grad_attended):
    score_scale = HD ** (-0.5)
    probs = jnp.exp(masked_scores(queries, key_rows, image_ids) - logsum[..., None])
    weights = probs.astype(jnp.bfloat16)
    grad_value = jnp.einsum(
        "rhqk,rqhe->rkhe", weights, grad_attended, preferred_element_type=jnp.float32
    )
    grad_probs = jnp.einsum(
        "rqhe,rkhe->rhqk", grad_attended, value_rows, preferred_element_type=jnp.float32
    )
    inner_sum = jnp.sum(probs * grad_probs, axis=-1, keepdims=True)
    grad_scores = (probs * (grad_probs - inner_sum)).astype(jnp.bfloat16)
    grad_query = (
        jnp.einsum("rhqk,rkhe->rqhe", grad_scores, key_rows, preferred_element_type=jnp.float32)
        * score_scale
    )
    grad_key = (
        jnp.einsum("rhqk,rqhe->rkhe", grad_scores, queries, preferred_element_type=jnp.float32)
        * score_scale
    )
    return (grad_query, grad_key, grad_value)


def spread(values, beside=()):
    arrived = [head_move(values, flip) for flip in range(1, lax.axis_size("heads"))]
    arrived, beside = lax.optimization_barrier((arrived, beside))
    return jnp.concatenate([values] + arrived, axis=0), beside


def collect(operand, product, own_rows, beside=()):
    total = None
    arrived = []
    for flip in range(1, lax.axis_size("heads")):
        partial = product(operand[flip * own_rows : (flip + 1) * own_rows])
        arrived.append(head_move(partial.astype(jnp.bfloat16), flip))
    total = product(operand[:own_rows])
    total, arrived, beside = lax.optimization_barrier((total, arrived, beside))
    for item in arrived:
        total = total + item.astype(jnp.float32)
    return total, beside


def plain_dot(operand, other):
    return jnp.dot(operand, other, preferred_element_type=jnp.float32)


def piece_of(mods, picks, index):
    width = mods.shape[1] // 6
    value = mods[:, index * width : (index + 1) * width]
    total = jnp.zeros((picks.shape[0], width), jnp.float32)
    for image in range(mods.shape[0]):
        total = jnp.where(picks[:, None] == image, value[image][None, :], total)
    return total


def block_forward(residual, ready, pieces, qkv_full, qkv_b, proj_t, gu_full, down_t, image_ids, geometry):
    shift_attn, scale_attn, gate_attn, shift_mlp, scale_mlp, gate_mlp = pieces
    own_rows = residual.shape[0]
    count_rows, row_len = image_ids.shape
    if ready is None:
        normed_attn, inverse_attn = normalize(residual)
        input_attn, _ = spread((normed_attn * (1.0 + scale_attn) + shift_attn).astype(jnp.bfloat16))
    else:
        normed_attn, inverse_attn, input_attn = ready
    packed = plain_dot(input_attn, qkv_full) + qkv_b
    heads_here = packed.shape[1] // (3 * HD)
    packed = packed.reshape(count_rows, row_len, heads_here, 3, HD)
    queries = turn(packed[:, :, :, 0], geometry, 1.0).astype(jnp.bfloat16)
    key_rows = turn(packed[:, :, :, 1], geometry, 1.0).astype(jnp.bfloat16)
    value_rows = packed[:, :, :, 2].astype(jnp.bfloat16)
    attended, logsum = attend(queries, key_rows, value_rows, image_ids)
    attended = attended.reshape(count_rows * row_len, heads_here * HD)
    branch, _ = collect(attended, lambda rows: tail_dot(rows, proj_t), own_rows)
    middle = residual + gate_attn * branch
    normed_mlp, inverse_mlp = normalize(middle)
    input_mlp, _ = spread((normed_mlp * (1.0 + scale_mlp) + shift_mlp).astype(jnp.bfloat16))
    gate_up = plain_dot(input_mlp, gu_full)
    hidden_width = gate_up.shape[1] // 2
    gate_part = gate_up[:, :hidden_width]
    up_part = gate_up[:, hidden_width:]
    hidden = (jax.nn.silu(gate_part) * up_part).astype(jnp.bfloat16)
    mlp_out, _ = collect(hidden, lambda rows: tail_dot(rows, down_t), own_rows)
    result = middle + gate_mlp * mlp_out
    stored = (
        normed_attn,
        inverse_attn,
        input_attn,
        queries,
        key_rows,
        value_rows,
        logsum,
        attended,
        branch,
        normed_mlp,
        inverse_mlp,
        input_mlp,
        gate_up,
        hidden,
        mlp_out,
    )
    return (result, stored)


def block_backward(
    incoming, ready, later, pieces, stored, qkv_full, proj_t, gu_full, down_t, image_ids, geometry
):
    shift_attn, scale_attn, gate_attn, shift_mlp, scale_mlp, gate_mlp = pieces
    (
        normed_attn,
        inverse_attn,
        input_attn,
        queries,
        key_rows,
        value_rows,
        logsum,
        attended,
        branch,
        normed_mlp,
        inverse_mlp,
        input_mlp,
        gate_up,
        hidden,
        mlp_out,
    ) = stored
    own_rows = incoming.shape[0]
    count_rows, row_len = image_ids.shape
    units = hidden.shape[1]
    grad_gate_mlp = incoming * mlp_out
    sums = ()
    if later:
        grad_input_mlp, grad_middle, gathered_branch, grad_attended, gu_grad, down_grad, *sums = (
            mlp_back_call(
                lax.axis_size("rows"),
                lax.axis_size("heads"),
                (incoming, gate_mlp, scale_mlp, gate_attn, normed_mlp, inverse_mlp),
                (down_t, gate_up, gu_full, input_mlp, hidden, proj_t),
                later,
            )
        )
        gathered_branch = gathered_branch.reshape(-1, gathered_branch.shape[-1])
    else:
        gathered_mlp = ready
        down_grad = lead_dot(gathered_mlp, hidden).astype(jnp.bfloat16)
        grad_hidden = plain_dot(gathered_mlp, down_t)
        gate_part = gate_up[:, :units]
        up_part = gate_up[:, units:]
        logistic = jax.nn.sigmoid(gate_part)
        grad_gate_part = grad_hidden * up_part * logistic * (1.0 + gate_part * (1.0 - logistic))
        grad_up_part = grad_hidden * gate_part * logistic
        grad_gate_up = jnp.concatenate([grad_gate_part, grad_up_part], axis=1).astype(jnp.bfloat16)
        gu_grad = lead_dot(input_mlp, grad_gate_up).astype(jnp.bfloat16)
        grad_input_mlp, gu_grad = collect(
            grad_gate_up, lambda rows: tail_dot(rows, gu_full), own_rows, gu_grad
        )
        grad_middle = incoming + norm_back(
            grad_input_mlp * (1.0 + scale_mlp), normed_mlp, inverse_mlp
        )
        grad_branch = (gate_attn * grad_middle).astype(jnp.bfloat16)
        gathered_branch, down_grad = spread(grad_branch, down_grad)
        grad_attended = plain_dot(gathered_branch, proj_t).astype(jnp.bfloat16)
    gu_out = lax.psum_scatter(gu_grad, "rows", scatter_dimension=0, tiled=True).astype(jnp.float32)
    grad_gate_attn = grad_middle * branch
    heads_here = queries.shape[2]
    grad_attended = grad_attended.reshape(count_rows, row_len, heads_here, HD)
    grad_query, grad_key, grad_value = attend_back(
        queries, key_rows, value_rows, image_ids, logsum, grad_attended
    )
    grad_query = turn(grad_query, geometry, -1.0)
    grad_key = turn(grad_key, geometry, -1.0)
    grad_packed = (
        jnp.stack([grad_query, grad_key, grad_value], axis=3)
        .reshape(count_rows * row_len, heads_here * 3 * HD)
        .astype(jnp.bfloat16)
    )
    qkv_bias_grad = jnp.sum(grad_packed, axis=0, dtype=jnp.float32)
    qkv_grad, proj_grad = weight_grads((input_attn, grad_packed), (gathered_branch, attended))
    grad_input_attn, (qkv_grad, proj_grad) = collect(
        grad_packed, lambda rows: tail_dot(rows, qkv_full), own_rows, (qkv_grad, proj_grad)
    )
    grad_input = grad_middle + norm_back(
        grad_input_attn * (1.0 + scale_attn), normed_attn, inverse_attn
    )
    grad_mods = jnp.concatenate(
        [
            grad_input_attn,
            grad_input_attn * normed_attn,
            grad_gate_attn,
            grad_input_mlp,
            grad_input_mlp * normed_mlp,
            grad_gate_mlp,
        ],
        axis=1,
    )
    return (grad_input, grad_mods, (qkv_grad, qkv_bias_grad, proj_grad, gu_out, down_grad), sums)


def heads_in_order(value):
    index = lax.axis_index("heads")
    count = lax.axis_size("heads")
    chunks = [value] + [head_move(value, flip) for flip in range(1, count)]
    placed = []
    for slot in range(count):
        item = chunks[0]
        for flip in range(1, count):
            item = jnp.where(index == slot ^ flip, chunks[flip], item)
        placed.append(item)
    return jnp.stack(placed)


def heads_share(value):
    index = lax.axis_index("heads")
    count = lax.axis_size("heads")
    width = value.shape[-1] // count

    def part(flip):
        return lax.dynamic_slice_in_dim(value, (index ^ flip) * width, width, value.ndim - 1)

    arrived = [head_move(part(flip), flip) for flip in range(1, count)]
    total = part(0)
    for item in arrived:
        total = total + item
    return total


def shards(
    tokens,
    cond,
    image_of,
    grid_row,
    grid_col,
    ada_weight,
    ada_bias,
    qkv_weight,
    qkv_bias,
    proj_weight,
    gu_weight,
    down_weight,
    cotangent,
):
    own_rows = tokens.shape[0]
    image_count = cond.shape[0]
    block_count = qkv_weight.shape[0]
    row_size = lax.axis_size("rows")
    head_size = lax.axis_size("heads")
    head_index = lax.axis_index("heads")

    def device_order(values):
        parts = values.reshape(head_size, own_rows)
        picked = [
            lax.dynamic_index_in_dim(parts, head_index ^ flip, 0, keepdims=False)
            for flip in range(head_size)
        ]
        return jnp.concatenate(picked).reshape(values.shape)

    image_ids = device_order(image_of - lax.axis_index("rows") * image_count)
    own_images = image_ids.reshape(-1)[:own_rows]
    picker = (own_images[:, None] == jnp.arange(image_count, dtype=jnp.int32)[None, :]).astype(
        jnp.float32
    )
    geometry = lax.optimization_barrier(
        rope_parts(device_order(grid_row)) + rope_parts(device_order(grid_col))
    )
    shard_rows = qkv_weight.shape[1]

    def gathered(shard):
        return lax.all_gather(shard, "rows", axis=0, tiled=True)

    cond_wide = cond.astype(jnp.float32)
    cond_act = jax.nn.silu(cond_wide).astype(jnp.bfloat16)
    pad = -image_count % 16
    bias_rows = jnp.repeat(ada_bias.astype(jnp.float32), image_count, axis=0)
    *early, mods, cond_mine = start_call(
        row_size,
        head_size,
        jnp.pad(cond_act, ((0, pad), (0, 0))),
        ada_weight,
        bias_rows,
        [item for b in range(block_count) for item in (qkv_weight[b], proj_weight[b].T)],
    )
    qkv_full, gu_full, down_t, proj_t = [], [], [], []
    for b in range(block_count):
        qkv_full.append(early[2 * b].reshape(-1, early[2 * b].shape[-1]))
        proj_t.append(early[2 * b + 1].reshape(-1, early[2 * b + 1].shape[-1]))
        gu_full.append(gathered(gu_weight[b].reshape(shard_rows, -1)))
        down_t.append(gathered(down_weight[b].T))
    mod_all = mods.reshape(head_size, block_count, image_count, -1)
    modulation = [
        jnp.concatenate([mod_all[index, b] for index in range(head_size)], axis=1)
        for b in range(block_count)
    ]
    pieces = [
        [piece_of(modulation[b], own_images, index) for index in range(6)] for b in range(block_count)
    ]
    residual = tokens.astype(jnp.float32)
    all_images = image_ids.reshape(-1)
    every_token, _ = spread(tokens)
    every_token = every_token.astype(jnp.float32)
    normed, inverse = normalize(every_token)
    shift, scale = [piece_of(modulation[0], all_images, index) for index in range(2)]
    forward_ready = [None] * block_count
    forward_ready[0] = (
        normed[:own_rows],
        inverse[:own_rows],
        (normed * (1.0 + scale) + shift).astype(jnp.bfloat16),
    )
    every_cotangent, _ = spread(cotangent)
    gate = piece_of(modulation[-1], all_images, 5)
    backward_ready = [None] * block_count
    backward_ready[-1] = (gate * every_cotangent.astype(jnp.float32)).astype(jnp.bfloat16)
    stored_all = []
    for b in range(block_count):
        residual, stored = block_forward(
            residual,
            forward_ready[b],
            pieces[b],
            qkv_full[b],
            qkv_bias[b].astype(jnp.float32),
            proj_t[b],
            gu_full[b],
            down_t[b],
            image_ids,
            geometry,
        )
        stored_all.append(stored)
    block_out = residual.astype(jnp.bfloat16)
    incoming = cotangent.astype(jnp.float32)
    block_grads = [None] * block_count
    image_sums = [None] * block_count
    block_sums = [None] * block_count
    later = []
    for b in reversed(range(block_count)):
        incoming, grad_mods, gradients, sums = block_backward(
            incoming,
            backward_ready[b],
            later,
            pieces[b],
            stored_all[b],
            qkv_full[b],
            proj_t[b],
            gu_full[b],
            down_t[b],
            image_ids,
            geometry,
        )
        image_sums[b] = lax.dot_general(
            picker, grad_mods, (((0,), (0,)), ((), ())), precision=highest
        )
        block_grads[b] = gradients
        later = [
            gradients[which].reshape(row_size, shard_rows, -1) for which in (4, 0, 2)
        ]
        if b + 1 < block_count:
            block_sums[b + 1] = sums
    image_grads = heads_share(jnp.stack(image_sums)).astype(jnp.bfloat16)
    bias_sums = jnp.stack([item[1] for item in block_grads])
    bias_high = bias_sums.astype(jnp.bfloat16)
    bias_rest = bias_sums - bias_high.astype(jnp.float32)
    bias_middle = bias_rest.astype(jnp.bfloat16)
    bias_low = (bias_rest - bias_middle.astype(jnp.float32)).astype(jnp.bfloat16)
    wide = image_grads.shape[-1]
    bias_parts = jnp.stack([bias_high, bias_middle, bias_low], axis=1)
    columns = bias_sums.shape[1]
    bias_parts = jnp.pad(bias_parts, ((0, 0), (0, 0), (0, wide - columns)))
    small = jnp.concatenate([image_grads.reshape(-1, wide), bias_parts.reshape(-1, wide)])
    used = small.shape[0]
    small = jnp.pad(small, ((0, -used % 16), (0, 0)))
    cond_rows = cond_mine.reshape(row_size, -1, shard_rows)[:, :image_count]
    row = jnp.arange(small.shape[0])
    mine = []
    for b in range(block_count):
        first = b * image_count
        lead = jnp.pad(cond_rows, ((0, 0), (first, small.shape[0] - first - image_count), (0, 0)))
        is_image = (row >= first) & (row < first + image_count)
        start = block_count * image_count + 3 * b
        is_bias = (row >= start) & (row < start + 3)
        ones = jnp.stack([is_image, is_bias], axis=1).astype(jnp.bfloat16)
        ones = jnp.broadcast_to(ones[None], (row_size,) + ones.shape)
        both = jnp.concatenate([lead, ones], axis=2)
        both = jnp.pad(both, ((0, 0), (0, 0), (0, -both.shape[2] % 128)))
        mine.append(both.reshape(-1, both.shape[2]))
    logistic = jax.nn.sigmoid(cond_wide)
    factor = logistic * (1.0 + cond_wide * (1.0 - logistic))
    factor = jnp.pad(factor, ((0, -image_count % 8), (0, 0)))
    ada_grads, ada_bias_grads, qkv_bias_out, cond_grad, *block_sums[0] = finish_call(
        row_size,
        head_size,
        image_count,
        later,
        small,
        jnp.stack(mine),
        ada_weight,
        factor,
        columns,
    )
    cond_grad = cond_grad[:image_count]
    return (
        block_out,
        incoming,
        cond_grad,
        ada_grads,
        ada_bias_grads,
        jnp.stack([item[1] for item in block_sums]),
        qkv_bias_out,
        jnp.stack([item[2].T for item in block_sums]),
        jnp.stack([item[3].reshape(gu_weight.shape[1:]) for item in block_grads]),
        jnp.stack([item[0].T for item in block_sums]),
    )


def solution(mesh):
    in_specs = (
        P(("rows", "heads"), None),
        P("rows", None),
        P("rows", None),
        P("rows", None),
        P("rows", None),
        P(None, "rows", "heads"),
        P(None, "heads"),
        P(None, "rows", "heads"),
        P(None, "heads"),
        P(None, "heads", "rows"),
        P(None, "rows", None, "heads"),
        P(None, "heads", "rows"),
        P(("rows", "heads"), None),
    )
    out_specs = (
        P(("rows", "heads"), None),
        P(("rows", "heads"), None),
        P("rows", None),
        P(None, "rows", "heads"),
        P(None, "heads"),
        P(None, "rows", "heads"),
        P(None, "heads"),
        P(None, "heads", "rows"),
        P(None, "rows", None, "heads"),
        P(None, "heads", "rows"),
    )
    return jax.shard_map(shards, mesh=mesh, in_specs=in_specs, out_specs=out_specs, check_vma=False)
```

```python
import functools

import jax
import jax.numpy as jnp
from jax import lax
from jax.experimental import pallas as pl
from jax.experimental.pallas import tpu as pltpu
from jax.sharding import PartitionSpec as P

HD = 72


epsilon = 1e-06
theta_base = 10000.0
highest = lax.Precision.HIGHEST


def normalize(values):
    center = values - jnp.mean(values, axis=-1, keepdims=True)
    inverse = lax.rsqrt(jnp.mean(center * center, axis=-1, keepdims=True) + epsilon)
    return (center * inverse, inverse)


def norm_back(incoming, normed, inverse):
    return inverse * (
        incoming
        - jnp.mean(incoming, axis=-1, keepdims=True)
        - normed * jnp.mean(incoming * normed, axis=-1, keepdims=True)
    )


def lead_dot(operand, other):
    return lax.dot_general(
        operand, other, (((0,), (0,)), ((), ())), preferred_element_type=jnp.float32
    )


def tail_dot(operand, other):
    return lax.dot_general(
        operand, other, (((1,), (1,)), ((), ())), preferred_element_type=jnp.float32
    )


def angles(coords, quarter):
    frequency = theta_base ** (-jnp.arange(quarter, dtype=jnp.float32) / quarter)
    return coords.astype(jnp.float32)[..., None] * frequency


def head_move(value, flip):
    size = lax.axis_size("heads")
    return lax.ppermute(value, "heads", [(index, index ^ flip) for index in range(size)])


MESH = pl.DeviceIdType.MESH


class Place:
    def __init__(self, row_size, head_size):
        self.sizes = (4, row_size // 8, 2)
        index = lax.axis_index("rows")
        a, b, c = self.sizes
        self.mine = (index // (b * c), (index // c) % b, index % c)
        self.heads = head_size
        self.head = lax.axis_index("heads")

    def step(self, dim, by):
        return (self.mine[dim] + by + self.sizes[dim]) % self.sizes[dim]

    def row(self, a, b, c):
        return (a * self.sizes[1] + b) * self.sizes[2] + c

    def near(self, dim, by):
        at = list(self.mine)
        at[dim] = self.step(dim, by)
        return {"rows": self.row(*at)}

    def flip(self, by):
        return {"heads": self.head ^ by}

    def partners(self, with_heads):
        found = [self.near(dim, by) for dim in range(3) for by in range(1, self.sizes[dim])]
        if with_heads:
            found += [self.flip(by) for by in range(1, self.heads)]
        return found

    def greet(self, with_heads):
        barrier = pltpu.get_barrier_semaphore()
        found = self.partners(with_heads)
        for partner in found:
            pl.semaphore_signal(barrier, inc=1, device_id=partner, device_id_type=MESH)
        pl.semaphore_wait(barrier, len(found))


def gather_count(row_size):
    a, b, c = 4, row_size // 8, 2
    return 2 * (a - 1) + (2 * a - 1) * (2 * b - 1)


class Gather:
    def __init__(self, place, shard, out, send, recv, local):
        self.place, self.shard, self.out = place, shard, out
        self.send, self.recv = send, recv
        self.used = 0
        self.keep = pltpu.make_async_copy(shard, out.at[place.row(*place.mine)], local)
        a, b, _ = place.sizes
        self.hops, self.along_b, self.along_c = {}, {}, {}
        names = [(0, 0)] + [(way, k) for k in range(1, a) for way in (1, -1)]
        for way, k in names:
            if k:
                self.hops[way, k] = self.copy(way, k - 1, 0, place.near(0, way))
        for way, k in names:
            for j in range(1, b):
                self.along_b[way, k, j] = self.copy(way, k, 0, place.near(1, j))
        for way, k in names:
            for j in range(b):
                self.along_c[way, k, j] = self.copy(way, k, j, place.near(2, 1))

    def copy(self, way, k, j, device):
        place, slot = self.place, self.used
        self.used += 1
        index = place.row(place.step(0, -way * k), place.step(1, -j), place.mine[2])
        return pltpu.make_async_remote_copy(
            src_ref=self.shard if k == 0 and j == 0 else self.out.at[index],
            dst_ref=self.out.at[index],
            send_sem=self.send.at[slot],
            recv_sem=self.recv.at[slot],
            device_id=device,
            device_id_type=MESH,
        )

    def holds(self, way, k):
        at = self.place.mine[0]
        return at >= k if way > 0 else at < self.place.sizes[0] - k

    def hop(self, way, k):
        at = self.place.mine[0]
        last = self.place.sizes[0] - 1
        return (at < last) & (at >= k - 1) if way > 0 else (at > 0) & (at <= last - (k - 1))

    def begin(self):
        self.keep.start()
        for way in (1, -1):
            pl.when(self.hop(way, 1))(self.hops[way, 1].start)
        self.pass_on(0, 0)

    def pass_on(self, way, k):
        for j in range(1, self.place.sizes[1]):
            self.along_b[way, k, j].start()
        self.along_c[way, k, 0].start()

    def first(self, k):
        for way in (1, -1):

            @pl.when(self.holds(way, k))
            def _():
                self.hops[way, k].wait_recv()
                if k + 1 < self.place.sizes[0]:
                    pl.when(self.hop(way, k + 1))(self.hops[way, k + 1].start)
                self.pass_on(way, k)

    def each(self, way, k, action):
        if k:
            pl.when(self.holds(way, k))(action)
        else:
            action()

    def second(self):
        for way, k, j in self.along_b:

            def action():
                self.along_b[way, k, j].wait_recv()
                self.along_c[way, k, j].start()

            self.each(way, k, action)

    def finish(self):
        for way, k, j in self.along_c:

            def action():
                self.along_c[way, k, j].wait_recv()
                self.along_c[way, k, j].wait_send()

            self.each(way, k, action)
        for way, k, j in self.along_b:
            self.each(way, k, self.along_b[way, k, j].wait_send)
        for way, k in self.hops:
            pl.when(self.hop(way, k))(self.hops[way, k].wait_send)
        self.keep.wait()


def gather_all(items):
    count = len(items)
    items[0].begin()
    for step in range(count + 1):
        if step < count:
            items[step].first(1)
            if step + 1 < count:
                items[step + 1].begin()
            for k in range(2, items[step].place.sizes[0]):
                items[step].first(k)
        if step >= 1:
            items[step - 1].second()
    for item in items:
        item.finish()


def scatter_count(row_size):
    a, b, c = 4, row_size // 8, 2
    return a * b + a * (b - 1) + (a - 1)


class Scatter:
    def __init__(self, place, source, out, held, met, side, far, send, recv, load):
        self.place, self.source, self.out = place, source, out
        self.held, self.met, self.side, self.far = held, met, side, far
        self.send, self.recv, self.load = send, recv, load

    def remote(self, source, target, slot, device):
        return pltpu.make_async_remote_copy(
            src_ref=source,
            dst_ref=target,
            send_sem=self.send.at[slot],
            recv_sem=self.recv.at[slot],
            device_id=device,
            device_id_type=MESH,
        )

    def across(self, k, j):
        place = self.place
        a, b = place.step(0, k), place.step(1, j)
        other = place.step(2, 1)
        return self.remote(
            self.source.at[place.row(a, b, other)],
            self.met.at[a, b],
            k * place.sizes[1] + j,
            place.near(2, 1),
        )

    def fetch(self, k, j):
        place = self.place
        a, b = place.step(0, k), place.step(1, j)
        return pltpu.make_async_copy(
            self.source.at[place.row(a, b, place.mine[2])],
            self.held.at[a, b],
            self.load.at[k * place.sizes[1] + j],
        )

    def along_b(self, k, j):
        place = self.place
        a, b = place.step(0, k), place.step(1, j)
        base = place.sizes[0] * place.sizes[1]
        return self.remote(
            self.held.at[a, b],
            self.side.at[j - 1, a],
            base + (j - 1) * place.sizes[0] + k,
            place.near(1, j),
        )

    def along_a(self, k):
        place = self.place
        base = place.sizes[0] * (2 * place.sizes[1] - 1)
        return self.remote(
            self.held.at[place.step(0, k), place.mine[1]],
            self.far.at[k - 1],
            base + k - 1,
            place.near(0, k),
        )

    def order(self):
        a, b, _ = self.place.sizes
        return [(k, j) for j in list(range(1, b)) + [0] for k in list(range(1, a)) + [0]]

    def begin(self):
        for k, j in self.order():
            self.fetch(k, j).start()
            self.across(k, j).start()

    def first(self):
        place = self.place
        a, b, _ = place.sizes
        for j in range(1, b):
            for k in list(range(1, a)) + [0]:
                self.fetch(k, j).wait()
                self.across(k, j).wait_recv()
                at = (place.step(0, k), place.step(1, j))
                self.held[at] = (
                    self.held[at].astype(jnp.float32) + self.met[at].astype(jnp.float32)
                ).astype(self.held.dtype)
                self.along_b(k, j).start()

    def total(self, k):
        place = self.place
        a, b = place.step(0, k), place.mine[1]
        value = self.held[a, b].astype(jnp.float32) + self.met[a, b].astype(jnp.float32)
        for j in range(1, place.sizes[1]):
            value = value + self.side[j - 1, a].astype(jnp.float32)
        return value

    def second(self):
        place = self.place
        a, b, _ = place.sizes
        for k in list(range(1, a)) + [0]:
            self.fetch(k, 0).wait()
            self.across(k, 0).wait_recv()
            for j in range(1, b):
                self.along_b(k, j).wait_recv()
            if k:
                self.held[place.step(0, k), place.mine[1]] = self.total(k).astype(self.held.dtype)
                self.along_a(k).start()
            else:
                self.out[...] = self.total(0)

    def finish(self):
        place = self.place
        a, b, _ = place.sizes
        for k in range(1, a):
            self.along_a(k).wait_recv()
            self.out[...] = self.out[...] + self.far[k - 1].astype(jnp.float32)
        for k, j in self.order():
            self.across(k, j).wait_send()
            if j:
                self.along_b(k, j).wait_send()
        for k in range(1, a):
            self.along_a(k).wait_send()


def scatter_all(items):
    count = len(items)
    for item in items:
        item.begin()
    for step in range(count + 2):
        if step < count:
            items[step].first()
        if 1 <= step <= count:
            items[step - 1].second()
        if step >= 2:
            items[step - 2].finish()


def start_kernel(row_size, head_size, images, blocks, weights, *refs):
    cond, ada, bias = refs[:3]
    shards = refs[3 : 3 + weights]
    outs = refs[3 + weights : 3 + 2 * weights]
    mods, mine_out = refs[3 + 2 * weights : 5 + 2 * weights]
    (conds, part, held, met, side, far, total, every, sends, recvs, keeps, mod_send, mod_recv, mod_load, head_send, head_recv) = refs[5 + 2 * weights :]
    place = Place(row_size, head_size)
    place.greet(True)
    items = [
        Gather(place, shard, out, sends.at[i], recvs.at[i], keeps.at[i])
        for i, (shard, out) in enumerate(zip((cond,) + shards, (conds,) + outs))
    ]
    lead, bulk = items[0], items[1:]
    lead.begin()
    bulk[0].begin()
    hops = range(1, place.sizes[0])
    for k in hops:
        lead.first(k)
    lead.second()
    lead.finish()
    width = cond.shape[1]
    share = ada.shape[1]
    pad = cond.shape[0]
    lane = lax.broadcasted_iota(jnp.int32, (width, share), 0)
    slot = lax.broadcasted_iota(jnp.int32, (width, share), 1)
    pick = jnp.where(lane == lax.axis_index("rows") * share + slot, 1.0, 0.0).astype(jnp.bfloat16)
    mine = jnp.dot(
        conds[...].reshape(row_size * pad, width), pick, preferred_element_type=jnp.float32
    ).astype(jnp.bfloat16)
    mine_out[...] = mine
    for b in range(blocks):
        value = jnp.dot(mine, ada[b], preferred_element_type=jnp.float32)
        part[:, b * images : (b + 1) * images, :] = value.reshape(row_size, pad, -1)[:, :images]
    sums = Scatter(place, part, total, held, met, side, far, mod_send, mod_recv, mod_load)
    sums.begin()
    bulk[0].first(1)
    for item in bulk[1:]:
        item.begin()
    sums.first()
    for k in hops[1:]:
        bulk[0].first(k)
    sums.second()
    for item in bulk[1:]:
        for k in hops:
            item.first(k)
    sums.finish()
    every[place.head] = total[...] + bias[...]
    across = [
        pltpu.make_async_remote_copy(
            src_ref=every.at[place.head],
            dst_ref=every.at[place.head],
            send_sem=head_send.at[by - 1],
            recv_sem=head_recv.at[by - 1],
            device_id=place.flip(by),
            device_id_type=MESH,
        )
        for by in range(1, head_size)
    ]
    for copy in across:
        copy.start()
    for item in bulk:
        item.second()
    for copy in across:
        copy.wait()
    mods[...] = every[...]
    for item in bulk:
        item.finish()


def start_call(row_size, head_size, cond, ada, bias, shards):
    images = bias.shape[0] // ada.shape[0]
    blocks = ada.shape[0]
    count = len(shards)
    a, b = 4, row_size // 8
    chunk = bias.shape
    copies = gather_count(row_size)
    anywhere = pl.BlockSpec(memory_space=pl.ANY)
    vmem = pl.BlockSpec(memory_space=pltpu.VMEM)
    f32 = jnp.float32
    return pl.pallas_call(
        functools.partial(start_kernel, row_size, head_size, images, blocks, count),
        out_shape=[jax.ShapeDtypeStruct((row_size,) + item.shape, item.dtype) for item in shards]
        + [
            jax.ShapeDtypeStruct((head_size,) + chunk, f32),
            jax.ShapeDtypeStruct((row_size * cond.shape[0], ada.shape[1]), cond.dtype),
        ],
        in_specs=[vmem] * 3 + [anywhere] * count,
        out_specs=[anywhere] * count + [vmem] * 2,
        scratch_shapes=[
            pltpu.VMEM((row_size,) + cond.shape, cond.dtype),
            pltpu.VMEM((row_size,) + chunk, f32),
            pltpu.VMEM((a, b) + chunk, f32),
            pltpu.VMEM((a, b) + chunk, f32),
            pltpu.VMEM((b - 1, a) + chunk, f32),
            pltpu.VMEM((a - 1,) + chunk, f32),
            pltpu.VMEM(chunk, f32),
            pltpu.VMEM((head_size,) + chunk, f32),
            pltpu.SemaphoreType.DMA((count + 1, copies)),
            pltpu.SemaphoreType.DMA((count + 1, copies)),
            pltpu.SemaphoreType.DMA((count + 1,)),
            pltpu.SemaphoreType.DMA((scatter_count(row_size),)),
            pltpu.SemaphoreType.DMA((scatter_count(row_size),)),
            pltpu.SemaphoreType.DMA((a * b,)),
            pltpu.SemaphoreType.DMA((head_size - 1,)),
            pltpu.SemaphoreType.DMA((head_size - 1,)),
        ],
        compiler_params=pltpu.CompilerParams(
            collective_id=1, has_side_effects=True, vmem_limit_bytes=48 * 2**20
        ),
        name="start",
    )(cond, ada, bias, *shards)


def weight_grads_kernel(*refs):
    count = len(refs) // 3
    for i in range(count):
        left, right, out = refs[2 * i], refs[2 * i + 1], refs[2 * count + i]
        columns = out.shape[1]
        for at in range(0, columns, 256):
            size = min(256, columns - at)
            out[:, at : at + size] = dot_tn(left[...], right[:, at : at + size]).astype(out.dtype)


def weight_grads(*pairs):
    vmem = pl.BlockSpec(memory_space=pltpu.VMEM)
    flat = [item for pair in pairs for item in pair]
    flops = sum(2 * left.size * right.shape[1] for left, right in pairs)
    moved = sum(2 * (left.size + right.size + left.shape[1] * right.shape[1]) for left, right in pairs)
    return pl.pallas_call(
        weight_grads_kernel,
        out_shape=[
            jax.ShapeDtypeStruct((left.shape[1], right.shape[1]), jnp.bfloat16)
            for left, right in pairs
        ],
        in_specs=[vmem] * len(flat),
        out_specs=[vmem] * len(pairs),
        compiler_params=pltpu.CompilerParams(vmem_limit_bytes=48 * 2**20),
        cost_estimate=pl.CostEstimate(flops=flops, bytes_accessed=moved, transcendentals=0),
        name="weight_grads",
    )(*flat)


def tile_of(width):
    return next(size for size in (256, 128, width) if width % size == 0)


def dot_nn(left, right):
    return jnp.dot(left, right, preferred_element_type=jnp.float32)


def dot_nt(left, right):
    return lax.dot_general(left, right, (((1,), (1,)), ((), ())), preferred_element_type=jnp.float32)


def dot_tn(left, right):
    return lax.dot_general(left, right, (((0,), (0,)), ((), ())), preferred_element_type=jnp.float32)


def tiles(width, size, body):
    @pl.loop(0, width // size)
    def _(step):
        body(step, pl.multiple_of(step * size, size))


class Across:
    def __init__(self, place, sources, targets, send, recv, stage):
        count = place.heads - 1
        self.copies = [
            pltpu.make_async_remote_copy(
                src_ref=sources(by),
                dst_ref=targets(by),
                send_sem=send.at[stage * count + by - 1],
                recv_sem=recv.at[stage * count + by - 1],
                device_id=place.flip(by),
                device_id_type=MESH,
            )
            for by in range(1, place.heads)
        ]

    def start(self, by):
        self.copies[by - 1].start()

    def arrived(self, by):
        self.copies[by - 1].wait_recv()

    def left(self):
        for copy in self.copies:
            copy.wait_send()


class Streamed:
    def __init__(self, buffer, out, sems, size, begin=0):
        self.buffer, self.out, self.sems, self.size, self.begin = buffer, out, sems, size, begin

    def copy(self, step):
        at = pl.multiple_of(self.begin + step * self.size, 128)
        return pltpu.make_async_copy(
            self.buffer.at[step % 2], self.out.at[:, pl.ds(at, self.size)], self.sems.at[step % 2]
        )

    def put(self, step, value):
        @pl.when(step >= 2)
        def _():
            self.copy(step - 2).wait()

        self.buffer[step % 2] = value.astype(self.buffer.dtype)
        self.copy(step).start()

    def drain(self, steps):
        for step in range(max(steps - 2, 0), steps):
            self.copy(step).wait()


def finish_kernel(row_size, head_size, images, blocks, *refs):
    (packed, qkv, inputs, attended, branch, middle, scale, normed, inverse, owner) = refs[:10]
    known, bias, mine, ada, factor, down = refs[10:16]
    grad_tokens, ada_out, ada_bias_out, qkv_bias_out, cond_out = refs[16:21]
    outs = refs[21:24]
    parcel, landed, sheet, share_in, small, qkv_grad, proj_grad = refs[24:31]
    head_send, head_recv = refs[31:33]
    refs = refs[33:]
    scratch = refs[:12]
    every, part, held, met, side, far, total, cond_in = refs[12:20]
    send, recv, load, small_send, small_recv, small_keep = refs[20:26]
    cond_send, cond_recv, cond_load = refs[26:]
    place = Place(row_size, head_size)
    own, width = middle.shape
    step_width = tile_of(width)
    place.greet(True)
    items = [
        Scatter(
            place, source, outs[i], *scratch[4 * i : 4 * i + 4], send.at[i], recv.at[i], load.at[i]
        )
        for i, source in enumerate((down, qkv_grad, proj_grad))
    ]
    items[0].begin()
    first = Across(
        place, lambda by: parcel.at[by - 1], lambda by: landed.at[by - 1], head_send, head_recv, 0
    )
    for by in range(1, head_size):

        def body(step, at):
            parcel[by - 1, :, pl.ds(at, step_width)] = dot_nt(
                packed[pl.ds(by * own, own), :], qkv[pl.ds(at, step_width), :]
            ).astype(jnp.bfloat16)

        tiles(width, step_width, body)
        first.start(by)
    for left, right, out, item in (
        (inputs, packed, qkv_grad, items[1]),
        (branch, attended, proj_grad, items[2]),
    ):
        share = out.shape[1]
        for at in range(0, out.shape[2], 256):
            size = min(256, out.shape[2] - at)
            value = dot_tn(left[...], right[:, at : at + size])
            for row in range(row_size):
                out[row, :, at : at + size] = value[row * share : (row + 1) * share].astype(out.dtype)
        item.begin()
    items[0].first()
    value = dot_nt(packed[pl.ds(0, own), :], qkv[...])
    for by in range(1, head_size):
        first.arrived(by)
        value = value + landed[by - 1].astype(jnp.float32)
    scaled = value * (1.0 + scale[...])
    grad_tokens[...] = middle[...] + inverse[...] * (
        scaled
        - jnp.mean(scaled, axis=-1, keepdims=True)
        - normed[...] * jnp.mean(scaled * normed[...], axis=-1, keepdims=True)
    )
    sheet[...] = known[...]
    wide = sheet.shape[2]
    for image in range(images):
        here = owner[...] == image
        for piece, item in enumerate((value, value * normed[...])):
            row = jnp.sum(jnp.where(here, item, 0.0), axis=0, keepdims=True)
            begin = piece * width
            while begin < (piece + 1) * width:
                end = min((begin // wide + 1) * wide, (piece + 1) * width)
                sheet[begin // wide, image : image + 1, begin % wide : begin % wide + end - begin] = (
                    row[:, begin - piece * width : end - piece * width]
                )
                begin = end
    shares = Across(
        place,
        lambda by: sheet.at[place.head ^ by],
        lambda by: share_in.at[by - 1],
        head_send,
        head_recv,
        1,
    )
    for by in range(1, head_size):
        shares.start(by)
    mod_grads = sheet[place.head]
    for by in range(1, head_size):
        shares.arrived(by)
        mod_grads = mod_grads + share_in[by - 1]
    known_rows = mod_grads.shape[0]
    small[...] = jnp.concatenate([mod_grads, bias[known_rows:, :]], axis=0).astype(small.dtype)
    lead = Gather(place, small, every, small_send, small_recv, small_keep.at[0])
    lead.begin()
    for k in range(1, place.sizes[0]):
        lead.first(k)
    items[1].first()
    items[0].second()
    lead.second()
    lead.finish()
    rows = small.shape[0]
    share = ada.shape[1]
    grads = every[...].reshape(row_size * rows, -1)
    columns = qkv_bias_out.shape[1]
    for b in range(blocks):
        value = dot_tn(mine[b], grads)
        ada_out[b] = value[:share]
        ada_bias_out[b : b + 1, :] = value[share : share + 1]
        qkv_bias_out[b : b + 1, :] = value[share + 1 : share + 2, :columns]
    lane = lax.broadcasted_iota(jnp.int32, (share, width), 1)
    slot = lax.broadcasted_iota(jnp.int32, (share, width), 0)
    pick = jnp.where(lane == lax.axis_index("rows") * share + slot, 1.0, 0.0).astype(jnp.bfloat16)
    back = 0.0
    for b in range(blocks):
        value = dot_nt(grads, ada[b]).reshape(row_size, rows, share)
        back = back + value[:, b * images : (b + 1) * images]
    back = back.reshape(row_size * images, share).astype(jnp.bfloat16)
    part[...] = jnp.zeros_like(part)
    part[:, :images, :] = dot_nn(back, pick).reshape(row_size, images, width)
    sums = Scatter(place, part, total, held, met, side, far, cond_send, cond_recv, cond_load)
    sums.begin()
    sums.first()
    items[2].first()
    items[1].second()
    sums.second()
    items[2].second()
    sums.finish()
    last = Across(
        place, lambda by: total, lambda by: cond_in.at[by - 1], head_send, head_recv, 2
    )
    for by in range(1, head_size):
        last.start(by)
    for item in items:
        item.finish()
    value = total[...]
    for by in range(1, head_size):
        last.arrived(by)
        value = value + cond_in[by - 1]
    cond_out[...] = value * factor[...]
    for stage in (first, shares, last):
        stage.left()


def finish_call(row_size, head_size, images, near, known, bias, mine, ada, factor, down):
    packed, qkv, inputs, attended, branch, middle = near[:6]
    copies = scatter_count(row_size)
    small_copies = gather_count(row_size)
    blocks, share, wide = ada.shape
    own, width = middle.shape
    a, b = 4, row_size // 8
    f32, bf16 = jnp.float32, jnp.bfloat16
    shape = jax.ShapeDtypeStruct
    chunks = [(share, columns) for columns in (down.shape[2], qkv.shape[1], attended.shape[1])]
    scratch = []
    for chunk in chunks:
        for lead in ((a, b), (a, b), (b - 1, a), (a - 1,)):
            scratch.append(pltpu.VMEM(lead + chunk, bf16))
    chunk = factor.shape
    anywhere = pl.BlockSpec(memory_space=pl.ANY)
    vmem = pl.BlockSpec(memory_space=pltpu.VMEM)
    others = head_size - 1
    return pl.pallas_call(
        functools.partial(finish_kernel, row_size, head_size, images, blocks),
        out_shape=[
            shape((own, width), f32),
            shape(ada.shape, f32),
            shape((blocks, wide), f32),
            shape((blocks, qkv.shape[1]), f32),
            shape(factor.shape, f32),
        ]
        + [shape(item, f32) for item in chunks],
        in_specs=[vmem] * 15 + [anywhere],
        out_specs=[vmem] * 8,
        scratch_shapes=[
            pltpu.VMEM((others, own, width), bf16),
            pltpu.VMEM((others, own, width), bf16),
            pltpu.VMEM(known.shape, f32),
            pltpu.VMEM((others,) + known.shape[1:], f32),
            pltpu.VMEM(bias.shape, bf16),
            pltpu.VMEM((row_size,) + chunks[1], bf16),
            pltpu.VMEM((row_size,) + chunks[2], bf16),
            pltpu.SemaphoreType.DMA((3 * others,)),
            pltpu.SemaphoreType.DMA((3 * others,)),
        ]
        + scratch
        + [
            pltpu.VMEM((row_size,) + bias.shape, bf16),
            pltpu.VMEM((row_size,) + chunk, f32),
            pltpu.VMEM((a, b) + chunk, f32),
            pltpu.VMEM((a, b) + chunk, f32),
            pltpu.VMEM((b - 1, a) + chunk, f32),
            pltpu.VMEM((a - 1,) + chunk, f32),
            pltpu.VMEM(chunk, f32),
            pltpu.VMEM((others,) + chunk, f32),
            pltpu.SemaphoreType.DMA((3, copies)),
            pltpu.SemaphoreType.DMA((3, copies)),
            pltpu.SemaphoreType.DMA((3, a * b)),
            pltpu.SemaphoreType.DMA((small_copies,)),
            pltpu.SemaphoreType.DMA((small_copies,)),
            pltpu.SemaphoreType.DMA((1,)),
            pltpu.SemaphoreType.DMA((copies,)),
            pltpu.SemaphoreType.DMA((copies,)),
            pltpu.SemaphoreType.DMA((a * b,)),
        ],
        compiler_params=pltpu.CompilerParams(
            collective_id=2, has_side_effects=True, vmem_limit_bytes=60 * 2**20
        ),
        name="finish",
    )(*near, known, bias, mine, ada, factor, down)


class Pieces:
    def __init__(self, place, pieces, source, target, send, recv, stage):
        self.copies = {}
        for by in range(1, place.heads):
            for piece in range(pieces):
                slot = (stage * (place.heads - 1) + by - 1) * pieces + piece
                self.copies[by, piece] = pltpu.make_async_remote_copy(
                    src_ref=source(by, piece),
                    dst_ref=target(by, piece),
                    send_sem=send.at[slot],
                    recv_sem=recv.at[slot],
                    device_id=place.flip(by),
                    device_id_type=MESH,
                )

    def start(self, by, piece):
        self.copies[by, piece].start()

    def arrived(self, by, piece):
        self.copies[by, piece].wait_recv()

    def left(self):
        for key in self.copies:
            self.copies[key].wait_send()


class Mlp:
    def __init__(self, place, pieces, own, width, units, sends, recvs):
        self.place, self.pieces, self.own, self.width, self.units = place, pieces, own, width, units
        self.sends, self.recvs = sends, recvs
        self.rows = own // pieces
        self.others = [(by, p) for p in range(pieces) for by in range(1, place.heads)]

    def at(self, piece):
        return pl.ds(piece * self.rows, self.rows)

    def flat(self, by, piece):
        return pl.ds(by * self.own + piece * self.rows, self.rows)

    def sum_stage(self, parcel, landed, stage):
        return Pieces(
            self.place,
            self.pieces,
            lambda by, p: parcel.at[by - 1, self.at(p)],
            lambda by, p: landed.at[by - 1, self.at(p)],
            self.sends,
            self.recvs,
            stage,
        )

    def spread_stage(self, every, stage):
        return Pieces(
            self.place,
            self.pieces,
            lambda by, p: every.at[0, self.at(p)],
            lambda by, p: every.at[by, self.at(p)],
            self.sends,
            self.recvs,
            stage,
        )

    def send_all(self, stage, piece):
        for by in range(1, self.place.heads):
            stage.start(by, piece)

    def arrive_all(self, stage, piece):
        for by in range(1, self.place.heads):
            stage.arrived(by, piece)

    def total(self, own_part, landed, piece):
        value = own_part[self.at(piece)]
        for by in range(1, self.place.heads):
            value = value + landed[by - 1, self.at(piece)].astype(jnp.float32)
        return value

    def modulation(self, table, owner, index, piece):
        here = owner[self.at(piece)]
        total = jnp.zeros((self.rows, self.width), jnp.float32)
        for image in range(table.shape[0]):
            row = table[image : image + 1, index * self.width : (index + 1) * self.width]
            total = jnp.where(here == image, row, total)
        return total

    def partial(self, out, left, rows, right):
        size = tile_of(self.width)

        def body(step, at):
            out[:, pl.ds(at, size)] = dot_nt(left[rows, :], right[pl.ds(at, size), :]).astype(out.dtype)

        tiles(self.width, size, body)

    def front(self, attended, proj, residual, table, owner, parcel, landed, own_part, branch, middle, normed, inverse, inputs, tick=None):
        first = self.sum_stage(parcel, landed, 0)
        for by, p in self.others:
            parcel[by - 1, self.at(p)] = dot_nt(attended[self.flat(by, p), :], proj[...]).astype(
                jnp.bfloat16
            )
            first.start(by, p)
        own_part[...] = dot_nt(attended[pl.ds(0, self.own), :], proj[...])
        if tick:
            tick()
        second = self.spread_stage(inputs, 1)
        for p in range(self.pieces):
            at = self.at(p)
            self.arrive_all(first, p)
            value = self.total(own_part, landed, p)
            branch[at] = value
            value = residual[at] + self.modulation(table, owner, 2, p) * value
            middle[at] = value
            unit, scale = normalize(value)
            normed[at] = unit
            inverse[at] = scale
            inputs[0, at] = (
                unit * (1.0 + self.modulation(table, owner, 4, p))
                + self.modulation(table, owner, 3, p)
            ).astype(jnp.bfloat16)
            self.send_all(second, p)
        return first, second

    def gate_up(self, inputs, gu, out, hidden, by, begin, rows):
        flat = pl.ds(by * self.own + begin, rows)
        size = tile_of(self.units)

        def body(step, at):
            far = pl.ds(pl.multiple_of(self.units + at, 128), size)
            value = inputs[by, pl.ds(begin, rows)]
            gate = dot_nn(value, gu[:, pl.ds(at, size)])
            up = dot_nn(value, gu[:, far])
            out[flat, pl.ds(at, size)] = gate
            out[flat, far] = up
            hidden[flat, pl.ds(at, size)] = (jax.nn.silu(gate) * up).astype(jnp.bfloat16)

        tiles(self.units, size, body)

    def hidden_back(self, grads, down, gate_up, ggu, by, begin, rows):
        flat = pl.ds(by * self.own + begin, rows)
        size = tile_of(self.units)

        def body(step, at):
            far = pl.ds(pl.multiple_of(self.units + at, 128), size)
            gate = gate_up[flat, pl.ds(at, size)]
            up = gate_up[flat, far]
            grad = dot_nn(grads[by, pl.ds(begin, rows)], down[:, pl.ds(at, size)])
            logistic = jax.nn.sigmoid(gate)
            ggu[flat, pl.ds(at, size)] = (
                grad * up * logistic * (1.0 + gate * (1.0 - logistic))
            ).astype(jnp.bfloat16)
            ggu[flat, far] = (grad * gate * logistic).astype(jnp.bfloat16)

        tiles(self.units, size, body)


def mlp_kernel(row_size, head_size, pieces, count, *refs):
    attended, residual, owner, table, following = refs[:5]
    streams, shards = refs[5:8], refs[8 : 8 + count]
    refs = refs[8 + count :]
    kept_out, refs = refs[:5], refs[5:]
    inverse, mlp_out, result, next_normed, next_inverse, next_out = refs[:6]
    gathered, refs = refs[6 : 6 + count], refs[6 + count :]
    weights, kept = refs[:3], refs[3:8]
    proj, gu, down = weights
    branch, normed, inputs, gate_up, hidden = kept
    parcel, landed, middle, own_part, next_all = refs[8:13]
    loads, stores, sends, recvs, gather_send, gather_recv, gather_keep = refs[13:]
    place = Place(row_size, head_size)
    own, width = residual.shape
    units = hidden.shape[1]
    work = Mlp(place, pieces, own, width, units, sends, recvs)
    copies = [
        pltpu.make_async_copy(source, target, loads.at[i])
        for i, (source, target) in enumerate(zip(streams, weights))
    ]
    out_copies = [
        pltpu.make_async_copy(source, target, stores.at[i])
        for i, (source, target) in enumerate(zip(kept, kept_out))
    ]
    items = [
        Gather(place, shards[i], gathered[i], gather_send.at[i], gather_recv.at[i], gather_keep.at[i])
        for i in range(count)
    ]
    for copy in copies:
        copy.start()
    place.greet(True)
    for item in items:
        item.begin()

    def hop(k):
        for item in items:
            item.first(k)

    copies[0].wait()
    first, second = work.front(
        attended,
        proj,
        residual,
        table,
        owner,
        parcel.at[0],
        landed.at[0],
        own_part,
        branch,
        middle,
        normed,
        inverse,
        inputs,
        lambda: hop(1),
    )
    hop(2)
    out_copies[0].start()
    out_copies[1].start()
    copies[1].wait()
    work.gate_up(inputs, gu, gate_up, hidden, 0, 0, own)
    for k in range(3, place.sizes[0]):
        hop(k)
    copies[2].wait()
    third = work.sum_stage(parcel.at[1], landed.at[1], 2)
    for by, p in work.others:
        second.arrived(by, p)
        work.gate_up(inputs, gu, gate_up, hidden, by, p * work.rows, work.rows)
        work.partial(parcel.at[1, by - 1, work.at(p)], hidden, work.flat(by, p), down)
        third.start(by, p)
    for copy in out_copies[2:]:
        copy.start()
    work.partial(own_part, hidden, pl.ds(0, own), down)
    for item in items:
        item.second()
    fourth = work.spread_stage(next_all, 3)
    for p in range(pieces):
        at = work.at(p)
        work.arrive_all(third, p)
        value = work.total(own_part, landed.at[1], p)
        mlp_out[at] = value
        value = middle[at] + work.modulation(table, owner, 5, p) * value
        result[at] = value
        unit, scale = normalize(value)
        next_normed[at] = unit
        next_inverse[at] = scale
        next_all[0, at] = (
            unit * (1.0 + work.modulation(following, owner, 1, p))
            + work.modulation(following, owner, 0, p)
        ).astype(jnp.bfloat16)
        work.send_all(fourth, p)
    next_out[0] = next_all[0]
    for by, p in work.others:
        fourth.arrived(by, p)
        next_out[by, work.at(p)] = next_all[by, work.at(p)]
    for item in items:
        item.finish()
    for stage in (first, second, third, fourth):
        stage.left()
    for copy in out_copies:
        copy.wait()


def pieces_of(own):
    return 2 if own % 32 == 0 else 1


def mlp_call(row_size, head_size, attended, residual, owner, table, following, weights, shards):
    own, width = residual.shape
    tokens = attended.shape[0]
    units = weights[2].shape[1]
    count = len(shards)
    pieces = pieces_of(own)
    others = head_size - 1
    copies = gather_count(row_size)
    anywhere = pl.BlockSpec(memory_space=pl.ANY)
    vmem = pl.BlockSpec(memory_space=pltpu.VMEM)
    shape = jax.ShapeDtypeStruct
    f32, bf16 = jnp.float32, jnp.bfloat16
    kept = [
        shape((own, width), f32),
        shape((own, width), f32),
        shape((head_size, own, width), bf16),
        shape((tokens, 2 * units), f32),
        shape((tokens, units), bf16),
    ]
    return pl.pallas_call(
        functools.partial(mlp_kernel, row_size, head_size, pieces, count),
        out_shape=kept
        + [
            shape((own, 1), f32),
            shape((own, width), f32),
            shape((own, width), f32),
            shape((own, width), f32),
            shape((own, 1), f32),
            shape((head_size, own, width), bf16),
        ]
        + [shape((row_size,) + item.shape, item.dtype) for item in shards],
        in_specs=[vmem] * 5 + [anywhere] * (3 + count),
        out_specs=[anywhere] * 5 + [vmem] * 6 + [anywhere] * count,
        scratch_shapes=[pltpu.VMEM(item.shape, item.dtype) for item in weights]
        + [pltpu.VMEM(item.shape, item.dtype) for item in kept]
        + [
            pltpu.VMEM((2, others, own, width), bf16),
            pltpu.VMEM((2, others, own, width), bf16),
            pltpu.VMEM((own, width), f32),
            pltpu.VMEM((own, width), f32),
            pltpu.VMEM((head_size, own, width), bf16),
            pltpu.SemaphoreType.DMA((3,)),
            pltpu.SemaphoreType.DMA((5,)),
            pltpu.SemaphoreType.DMA((4 * others * pieces,)),
            pltpu.SemaphoreType.DMA((4 * others * pieces,)),
            pltpu.SemaphoreType.DMA((count, copies)),
            pltpu.SemaphoreType.DMA((count, copies)),
            pltpu.SemaphoreType.DMA((count,)),
        ],
        compiler_params=pltpu.CompilerParams(
            collective_id=4, has_side_effects=True, vmem_limit_bytes=60 * 2**20
        ),
        name="mlp",
    )(attended, residual, owner, table, following, *weights, *shards)


def mlp_back_kernel(row_size, head_size, pieces, count, *refs):
    incoming, owner, table, normed, inverse = refs[:5]
    streams = refs[5:11]
    grads = refs[11 : 11 + count]
    outs = refs[11 + count : 17 + 2 * count]
    grad_in, grad_mid, branch_out, grad_att, gu_out, down_out = outs[:6]
    sums = outs[6:]
    refs = refs[17 + 2 * count :]
    down, gate_up, gu, inputs, hidden, proj = refs[:6]
    mlp_all, branch_all, ggu, parcel, landed, own_part, buffer = refs[6:13]
    loads, sends, recvs, tile_sems, out_sem = refs[13:18]
    scratch = refs[18 : 18 + 4 * count]
    sum_send, sum_recv, sum_load = refs[18 + 4 * count :]
    place = Place(row_size, head_size)
    own, width = incoming.shape
    units = hidden.shape[1]
    work = Mlp(place, pieces, own, width, units, sends, recvs)
    step_units = tile_of(units)
    copies = [
        pltpu.make_async_copy(source, target, loads.at[i])
        for i, (source, target) in enumerate(
            zip(streams, (down, gate_up, gu, inputs, hidden, proj))
        )
    ]
    for copy in copies:
        copy.start()
    place.greet(True)
    first = work.spread_stage(mlp_all, 0)
    for p in range(pieces):
        at = work.at(p)
        mlp_all[0, at] = (work.modulation(table, owner, 5, p) * incoming[at]).astype(jnp.bfloat16)
        work.send_all(first, p)
    items = [
        Scatter(
            place,
            grads[i],
            sums[i],
            *scratch[4 * i : 4 * i + 4],
            sum_send.at[i],
            sum_recv.at[i],
            sum_load.at[i],
        )
        for i in range(count)
    ]
    for item in items:
        item.begin()
    copies[0].wait()
    copies[1].wait()
    work.hidden_back(mlp_all, down, gate_up, ggu, 0, 0, own)
    for item in items:
        item.first()
    copies[2].wait()
    second = work.sum_stage(parcel, landed, 1)
    for by, p in work.others:
        first.arrived(by, p)
        work.hidden_back(mlp_all, down, gate_up, ggu, by, p * work.rows, work.rows)
        work.partial(parcel.at[by - 1, work.at(p)], ggu, work.flat(by, p), gu)
        second.start(by, p)
    work.partial(own_part, ggu, pl.ds(0, own), gu)
    copies[3].wait()
    out = Streamed(buffer, gu_out, tile_sems, step_units)

    def body(step, at):
        out.put(step, dot_tn(inputs[...], ggu[:, pl.ds(at, step_units)]))

    tiles(2 * units, step_units, body)
    for item in items[:1]:
        item.second()
    third = work.spread_stage(branch_all, 2)
    for p in range(pieces):
        at = work.at(p)
        work.arrive_all(second, p)
        value = work.total(own_part, landed, p)
        grad_in[at] = value
        unit = normed[at]
        value = value * (1.0 + work.modulation(table, owner, 4, p))
        value = incoming[at] + inverse[at] * (
            value
            - jnp.mean(value, axis=-1, keepdims=True)
            - unit * jnp.mean(value * unit, axis=-1, keepdims=True)
        )
        grad_mid[at] = value
        branch_all[0, at] = (work.modulation(table, owner, 2, p) * value).astype(jnp.bfloat16)
        work.send_all(third, p)
    out.drain(2 * units // step_units)
    copies[4].wait()
    copies[5].wait()
    out = Streamed(buffer, down_out, tile_sems, step_units)

    def body(step, at):
        out.put(
            step,
            dot_tn(mlp_all[...].reshape(head_size * own, width), hidden[:, pl.ds(at, step_units)]),
        )

    tiles(units, step_units, body)
    for item in items[1:]:
        item.second()
    grad_att[pl.ds(0, own), :] = dot_nn(branch_all[0], proj[...]).astype(jnp.bfloat16)
    for by, p in work.others:
        third.arrived(by, p)
        grad_att[work.flat(by, p), :] = dot_nn(branch_all[by, work.at(p)], proj[...]).astype(
            jnp.bfloat16
        )
    keep = pltpu.make_async_copy(branch_all, branch_out, out_sem.at[0])
    keep.start()
    out.drain(units // step_units)
    for item in items:
        item.finish()
    for stage in (first, second, third):
        stage.left()
    keep.wait()


def mlp_back_call(row_size, head_size, near, streams, grads):
    count = len(grads)
    own, width = near[0].shape
    pieces = pieces_of(own)
    others = head_size - 1
    down, gate_up, gu, inputs, hidden, proj = streams
    units = hidden.shape[1]
    tokens = hidden.shape[0]
    a, b = 4, row_size // 8
    copies = scatter_count(row_size)
    scratch = []
    for grad in grads:
        chunk = grad.shape[1:]
        for lead in ((a, b), (a, b), (b - 1, a), (a - 1,)):
            scratch.append(pltpu.VMEM(lead + chunk, grad.dtype))
    anywhere = pl.BlockSpec(memory_space=pl.ANY)
    vmem = pl.BlockSpec(memory_space=pltpu.VMEM)
    shape = jax.ShapeDtypeStruct
    f32, bf16 = jnp.float32, jnp.bfloat16
    return pl.pallas_call(
        functools.partial(mlp_back_kernel, row_size, head_size, pieces, count),
        out_shape=[
            shape((own, width), f32),
            shape((own, width), f32),
            shape((head_size, own, width), bf16),
            shape((tokens, proj.shape[1]), bf16),
            shape((width, 2 * units), bf16),
            shape((width, units), bf16),
        ]
        + [shape(grad.shape[1:], f32) for grad in grads],
        in_specs=[vmem] * 5 + [anywhere] * (6 + count),
        out_specs=[vmem, vmem, anywhere, vmem, anywhere, anywhere] + [vmem] * count,
        scratch_shapes=[pltpu.VMEM(item.shape, item.dtype) for item in streams]
        + [
            pltpu.VMEM((head_size, own, width), bf16),
            pltpu.VMEM((head_size, own, width), bf16),
            pltpu.VMEM((tokens, 2 * units), bf16),
            pltpu.VMEM((others, own, width), bf16),
            pltpu.VMEM((others, own, width), bf16),
            pltpu.VMEM((own, width), f32),
            pltpu.VMEM((2, width, tile_of(units)), bf16),
            pltpu.SemaphoreType.DMA((6,)),
            pltpu.SemaphoreType.DMA((3 * others * pieces,)),
            pltpu.SemaphoreType.DMA((3 * others * pieces,)),
            pltpu.SemaphoreType.DMA((2,)),
            pltpu.SemaphoreType.DMA((1,)),
        ]
        + scratch
        + [
            pltpu.SemaphoreType.DMA((count, copies)),
            pltpu.SemaphoreType.DMA((count, copies)),
            pltpu.SemaphoreType.DMA((count, a * b)),
        ],
        compiler_params=pltpu.CompilerParams(
            collective_id=3, has_side_effects=True, vmem_limit_bytes=62 * 2**20
        ),
        name="mlp_back",
    )(*near, *streams, *grads)


def last_mlp_kernel(row_size, head_size, pieces, *refs):
    attended, residual, owner, table, incoming, mlp_grads = refs[:6]
    streams, refs = refs[6:9], refs[9:]
    block_out, branch, normed, mlp_out, grad_in, grad_mid, branch_out, grad_att = refs[:8]
    grads_out = refs[8]
    weights, refs = refs[9:12], refs[12:]
    proj, gu, down = weights
    inputs, gate_up, hidden, ggu, branch_all, parcel, landed = refs[:7]
    middle, inverse, own_part, own_mlp, buffer = refs[7:12]
    loads, sends, recvs, tile_sems, out_sem = refs[12:]
    place = Place(row_size, head_size)
    own, width = residual.shape
    units = hidden.shape[1]
    work = Mlp(place, pieces, own, width, units, sends, recvs)
    step_units = tile_of(units)
    copies = [
        pltpu.make_async_copy(source, target, loads.at[i])
        for i, (source, target) in enumerate(zip(streams, weights))
    ]
    for copy in copies:
        copy.start()
    place.greet(True)
    copies[0].wait()
    first, second = work.front(
        attended,
        proj,
        residual,
        table,
        owner,
        parcel.at[0],
        landed.at[0],
        own_part,
        branch,
        middle,
        normed,
        inverse,
        inputs,
    )
    copies[1].wait()
    copies[2].wait()
    work.gate_up(inputs, gu, gate_up, hidden, 0, 0, own)
    work.hidden_back(mlp_grads, down, gate_up, ggu, 0, 0, own)
    fourth = work.sum_stage(parcel.at[1], landed.at[1], 3)
    for by, p in work.others:
        second.arrived(by, p)
        begin = p * work.rows
        work.gate_up(inputs, gu, gate_up, hidden, by, begin, work.rows)
        work.hidden_back(mlp_grads, down, gate_up, ggu, by, begin, work.rows)
        work.partial(parcel.at[1, by - 1, work.at(p)], ggu, work.flat(by, p), gu)
        fourth.start(by, p)
    work.partial(own_part, ggu, pl.ds(0, own), gu)
    out = Streamed(buffer, grads_out, tile_sems, step_units)

    def body(step, at):
        out.put(
            step,
            dot_tn(inputs[...].reshape(head_size * own, width), ggu[:, pl.ds(at, step_units)]),
        )

    tiles(2 * units, step_units, body)
    fifth = work.spread_stage(branch_all, 4)
    for p in range(pieces):
        at = work.at(p)
        work.arrive_all(fourth, p)
        value = work.total(own_part, landed.at[1], p)
        grad_in[at] = value
        unit = normed[at]
        value = value * (1.0 + work.modulation(table, owner, 4, p))
        value = incoming[at].astype(jnp.float32) + inverse[at] * (
            value
            - jnp.mean(value, axis=-1, keepdims=True)
            - unit * jnp.mean(value * unit, axis=-1, keepdims=True)
        )
        grad_mid[at] = value
        branch_all[0, at] = (work.modulation(table, owner, 2, p) * value).astype(jnp.bfloat16)
        work.send_all(fifth, p)
    first.left()
    third = work.sum_stage(parcel.at[0], landed.at[0], 2)
    for by, p in work.others:
        work.partial(parcel.at[0, by - 1, work.at(p)], hidden, work.flat(by, p), down)
        third.start(by, p)
    work.partial(own_mlp, hidden, pl.ds(0, own), down)
    out.drain(2 * units // step_units)
    out = Streamed(buffer, grads_out, tile_sems, step_units, 2 * units)

    def body(step, at):
        out.put(
            step,
            dot_tn(mlp_grads[...].reshape(head_size * own, width), hidden[:, pl.ds(at, step_units)]),
        )

    tiles(units, step_units, body)
    grad_att[pl.ds(0, own), :] = dot_nn(branch_all[0], proj[...]).astype(jnp.bfloat16)
    for by, p in work.others:
        fifth.arrived(by, p)
        grad_att[work.flat(by, p), :] = dot_nn(branch_all[by, work.at(p)], proj[...]).astype(
            jnp.bfloat16
        )
    keep = pltpu.make_async_copy(branch_all, branch_out, out_sem.at[0])
    keep.start()
    for p in range(pieces):
        at = work.at(p)
        work.arrive_all(third, p)
        value = work.total(own_mlp, landed.at[0], p)
        mlp_out[at] = value
        block_out[at] = (middle[at] + work.modulation(table, owner, 5, p) * value).astype(
            jnp.bfloat16
        )
    out.drain(units // step_units)
    for stage in (second, third, fourth, fifth):
        stage.left()
    keep.wait()


def last_mlp_call(row_size, head_size, attended, residual, owner, table, incoming, mlp_grads, weights):
    own, width = residual.shape
    tokens = attended.shape[0]
    units = weights[2].shape[1]
    pieces = pieces_of(own)
    others = head_size - 1
    anywhere = pl.BlockSpec(memory_space=pl.ANY)
    vmem = pl.BlockSpec(memory_space=pltpu.VMEM)
    shape = jax.ShapeDtypeStruct
    f32, bf16 = jnp.float32, jnp.bfloat16
    return pl.pallas_call(
        functools.partial(last_mlp_kernel, row_size, head_size, pieces),
        out_shape=[
            shape((own, width), bf16),
            shape((own, width), f32),
            shape((own, width), f32),
            shape((own, width), f32),
            shape((own, width), f32),
            shape((own, width), f32),
            shape((head_size, own, width), bf16),
            shape(attended.shape, bf16),
            shape((width, 3 * units), bf16),
        ],
        in_specs=[vmem] * 6 + [anywhere] * 3,
        out_specs=[vmem] * 6 + [anywhere, vmem, anywhere],
        scratch_shapes=[pltpu.VMEM(item.shape, item.dtype) for item in weights]
        + [
            pltpu.VMEM((head_size, own, width), bf16),
            pltpu.VMEM((tokens, 2 * units), f32),
            pltpu.VMEM((tokens, units), bf16),
            pltpu.VMEM((tokens, 2 * units), bf16),
            pltpu.VMEM((head_size, own, width), bf16),
            pltpu.VMEM((2, others, own, width), bf16),
            pltpu.VMEM((2, others, own, width), bf16),
            pltpu.VMEM((own, width), f32),
            pltpu.VMEM((own, 1), f32),
            pltpu.VMEM((own, width), f32),
            pltpu.VMEM((own, width), f32),
            pltpu.VMEM((2, width, tile_of(units)), bf16),
            pltpu.SemaphoreType.DMA((3,)),
            pltpu.SemaphoreType.DMA((5 * others * pieces,)),
            pltpu.SemaphoreType.DMA((5 * others * pieces,)),
            pltpu.SemaphoreType.DMA((2,)),
            pltpu.SemaphoreType.DMA((1,)),
        ],
        compiler_params=pltpu.CompilerParams(
            collective_id=5, has_side_effects=True, vmem_limit_bytes=60 * 2**20
        ),
        name="last_mlp",
    )(attended, residual, owner, table, incoming, mlp_grads, *weights)


def rope_parts(coords):
    angle = angles(coords, HD // 4)
    return jnp.cos(angle), jnp.sin(angle)


def turn(vectors, geometry, sign):
    row_cos, row_sin, col_cos, col_sin = [item[:, :, None, :] for item in geometry]
    quarter = HD // 4
    a, b, c, d = [vectors[..., quarter * i : quarter * (i + 1)] for i in range(4)]
    return jnp.concatenate(
        [
            a * row_cos - b * (sign * row_sin),
            b * row_cos + a * (sign * row_sin),
            c * col_cos - d * (sign * col_sin),
            d * col_cos + c * (sign * col_sin),
        ],
        axis=-1,
    )


def masked_scores(queries, key_rows, image_ids):
    scores = jnp.einsum(
        "rqhe,rkhe->rhqk", queries, key_rows, preferred_element_type=jnp.float32
    ) * HD ** (-0.5)
    same_image = image_ids[:, :, None] == image_ids[:, None, :]
    return jnp.where(same_image[:, None], scores, -1e30)


def attend(queries, key_rows, value_rows, image_ids):
    scores = masked_scores(queries, key_rows, image_ids)
    maximum = jnp.max(scores, axis=-1, keepdims=True)
    scaled_exp = jnp.exp(scores - maximum)
    denominator = jnp.sum(scaled_exp, axis=-1, keepdims=True)
    weights = (scaled_exp / denominator).astype(jnp.bfloat16)
    attended = jnp.einsum("rhqk,rkhe->rqhe", weights, value_rows, preferred_element_type=jnp.float32)
    return (attended.astype(jnp.bfloat16), (maximum + jnp.log(denominator))[..., 0])


def attend_back(queries, key_rows, value_rows, image_ids, logsum, grad_attended):
    score_scale = HD ** (-0.5)
    probs = jnp.exp(masked_scores(queries, key_rows, image_ids) - logsum[..., None])
    weights = probs.astype(jnp.bfloat16)
    grad_value = jnp.einsum(
        "rhqk,rqhe->rkhe", weights, grad_attended, preferred_element_type=jnp.float32
    )
    grad_probs = jnp.einsum(
        "rqhe,rkhe->rhqk", grad_attended, value_rows, preferred_element_type=jnp.float32
    )
    inner_sum = jnp.sum(probs * grad_probs, axis=-1, keepdims=True)
    grad_scores = (probs * (grad_probs - inner_sum)).astype(jnp.bfloat16)
    grad_query = (
        jnp.einsum("rhqk,rkhe->rqhe", grad_scores, key_rows, preferred_element_type=jnp.float32)
        * score_scale
    )
    grad_key = (
        jnp.einsum("rhqk,rqhe->rkhe", grad_scores, queries, preferred_element_type=jnp.float32)
        * score_scale
    )
    return (grad_query, grad_key, grad_value)


def spread(values):
    arrived = [head_move(values, flip) for flip in range(1, lax.axis_size("heads"))]
    return jnp.concatenate([values] + arrived, axis=0)


def collect(operand, product, own_rows, beside):
    arrived = []
    for flip in range(1, lax.axis_size("heads")):
        partial = product(operand[flip * own_rows : (flip + 1) * own_rows])
        arrived.append(head_move(partial.astype(jnp.bfloat16), flip))
    total = product(operand[:own_rows])
    total, arrived, beside = lax.optimization_barrier((total, arrived, beside))
    for item in arrived:
        total = total + item.astype(jnp.float32)
    return total, beside


def plain_dot(operand, other):
    return jnp.dot(operand, other, preferred_element_type=jnp.float32)


def piece_of(mods, picks, index):
    width = mods.shape[1] // 6
    value = mods[:, index * width : (index + 1) * width]
    total = jnp.zeros((picks.shape[0], width), jnp.float32)
    for image in range(mods.shape[0]):
        total = jnp.where(picks[:, None] == image, value[image][None, :], total)
    return total


def attention(input_attn, qkv_full, qkv_b, image_ids, geometry):
    count_rows, row_len = image_ids.shape
    packed = plain_dot(input_attn, qkv_full) + qkv_b
    heads_here = packed.shape[1] // (3 * HD)
    packed = packed.reshape(count_rows, row_len, heads_here, 3, HD)
    queries = turn(packed[:, :, :, 0], geometry, 1.0).astype(jnp.bfloat16)
    key_rows = turn(packed[:, :, :, 1], geometry, 1.0).astype(jnp.bfloat16)
    value_rows = packed[:, :, :, 2].astype(jnp.bfloat16)
    attended, logsum = attend(queries, key_rows, value_rows, image_ids)
    attended = attended.reshape(count_rows * row_len, heads_here * HD)
    return attended, (queries, key_rows, value_rows, logsum)


def attention_back(grad_attended, stored, image_ids, geometry):
    queries, key_rows, value_rows, logsum = stored
    count_rows, row_len = image_ids.shape
    heads_here = queries.shape[2]
    grad_attended = grad_attended.reshape(count_rows, row_len, heads_here, HD)
    grad_query, grad_key, grad_value = attend_back(
        queries, key_rows, value_rows, image_ids, logsum, grad_attended
    )
    grad_query = turn(grad_query, geometry, -1.0)
    grad_key = turn(grad_key, geometry, -1.0)
    grad_packed = (
        jnp.stack([grad_query, grad_key, grad_value], axis=3)
        .reshape(count_rows * row_len, heads_here * 3 * HD)
        .astype(jnp.bfloat16)
    )
    return grad_packed, jnp.sum(grad_packed, axis=0, dtype=jnp.float32)


def image_sum(picker, values):
    return lax.dot_general(picker, values, (((0,), (0,)), ((), ())), precision=lax.Precision.HIGH)


def shards(
    tokens,
    cond,
    image_of,
    grid_row,
    grid_col,
    ada_weight,
    ada_bias,
    qkv_weight,
    qkv_bias,
    proj_weight,
    gu_weight,
    down_weight,
    cotangent,
):
    own_rows = tokens.shape[0]
    image_count = cond.shape[0]
    block_count = qkv_weight.shape[0]
    row_size = lax.axis_size("rows")
    head_size = lax.axis_size("heads")
    head_index = lax.axis_index("heads")

    def device_order(values):
        parts = values.reshape(head_size, own_rows)
        picked = [
            lax.dynamic_index_in_dim(parts, head_index ^ flip, 0, keepdims=False)
            for flip in range(head_size)
        ]
        return jnp.concatenate(picked).reshape(values.shape)

    image_ids = device_order(image_of - lax.axis_index("rows") * image_count)
    own_images = image_ids.reshape(-1)[:own_rows]
    picker = (own_images[:, None] == jnp.arange(image_count, dtype=jnp.int32)[None, :]).astype(
        jnp.float32
    )
    geometry = lax.optimization_barrier(
        rope_parts(device_order(grid_row)) + rope_parts(device_order(grid_col))
    )
    shard_rows = qkv_weight.shape[1]

    def gathered(shard):
        return lax.all_gather(shard, "rows", axis=0, tiled=True)

    cond_wide = cond.astype(jnp.float32)
    cond_act = jax.nn.silu(cond_wide).astype(jnp.bfloat16)
    pad = -image_count % 16
    bias_rows = jnp.repeat(ada_bias.astype(jnp.float32), image_count, axis=0)
    *early, mods, cond_mine = start_call(
        row_size,
        head_size,
        jnp.pad(cond_act, ((0, pad), (0, 0))),
        ada_weight,
        bias_rows,
        [qkv_weight[0], proj_weight[0].T, down_weight[0].T],
    )
    qkv_full, proj_t, down_t = [[item.reshape(-1, item.shape[-1])] for item in early]
    gu_full = [gathered(item.reshape(shard_rows, -1)) for item in gu_weight]
    for b in range(1, block_count):
        down_t.append(gathered(down_weight[b].T))
    mod_all = mods.reshape(head_size, block_count, image_count, -1)
    modulation = [
        jnp.concatenate([mod_all[index, b] for index in range(head_size)], axis=1)
        for b in range(block_count)
    ]
    last = block_count - 1
    all_images = image_ids.reshape(-1)
    owner = own_images[:, None]
    every_token = spread(tokens).astype(jnp.float32)
    normed, inverse = normalize(every_token)
    shift, scale = [piece_of(modulation[0], all_images, index) for index in range(2)]
    input_attn = (normed * (1.0 + scale) + shift).astype(jnp.bfloat16)
    normed_attn, inverse_attn = [normed[:own_rows]], [inverse[:own_rows]]
    inputs_attn = [input_attn]
    gate = piece_of(modulation[last], all_images, 5)
    mlp_grads = (gate * spread(cotangent).astype(jnp.float32)).astype(jnp.bfloat16)
    mlp_grads = mlp_grads.reshape(head_size, own_rows, -1)
    residual = tokens.astype(jnp.float32)
    attentions, attended = [], []
    for b in range(block_count):
        item, kept = attention(
            inputs_attn[b], qkv_full[b], qkv_bias[b].astype(jnp.float32), image_ids, geometry
        )
        attended.append(item)
        attentions.append(kept)
        weights = (proj_t[b], gu_full[b], down_t[b])
        if b < last:
            (
                branch,
                normed_mlp,
                input_mlp,
                gate_up,
                hidden,
                inverse_mlp,
                mlp_out,
                residual,
                next_normed,
                next_inverse,
                next_input,
                next_qkv,
                next_proj,
            ) = mlp_call(
                row_size,
                head_size,
                item,
                residual,
                owner,
                modulation[b],
                modulation[b + 1],
                weights,
                [qkv_weight[b + 1], proj_weight[b + 1].T],
            )
            normed_attn.append(next_normed)
            inverse_attn.append(next_inverse)
            inputs_attn.append(next_input.reshape(inputs_attn[0].shape))
            qkv_full.append(next_qkv.reshape(qkv_full[0].shape))
            proj_t.append(next_proj.reshape(proj_t[0].shape))
            stored = (branch, normed_mlp, input_mlp, gate_up, hidden, inverse_mlp, mlp_out)
    (
        block_out,
        last_branch,
        last_normed,
        last_out,
        grad_input_mlp,
        grad_middle,
        gathered_branch,
        grad_attended,
        mlp_grad,
    ) = last_mlp_call(
        row_size,
        head_size,
        attended[last],
        residual,
        owner,
        modulation[last],
        cotangent,
        mlp_grads,
        weights,
    )

    def scattered(grad):
        return lax.psum_scatter(grad, "rows", scatter_dimension=0, tiled=True).astype(jnp.float32)

    def late_sums(middle, branch, incoming, normed, grad, out):
        return [
            image_sum(picker, item)
            for item in (middle * branch, grad, grad * normed, incoming * out)
        ]

    gu_outs, bias_sums, image_sums = [None] * 2, [None] * 2, [None] * 2
    mlp_sum = scattered(mlp_grad)
    units = mlp_sum.shape[1] // 3
    gathered_branch = gathered_branch.reshape(-1, gathered_branch.shape[-1])
    grad_packed, bias_sums[1] = attention_back(grad_attended, attentions[1], image_ids, geometry)
    qkv_grad, proj_grad = weight_grads(
        (inputs_attn[1], grad_packed), (gathered_branch, attended[1])
    )
    late = late_sums(
        grad_middle,
        last_branch,
        cotangent.astype(jnp.float32),
        last_normed,
        grad_input_mlp,
        last_out,
    )
    grad_input_attn, (qkv_grad, proj_grad, late) = collect(
        grad_packed, lambda rows: tail_dot(rows, qkv_full[1]), own_rows, (qkv_grad, proj_grad, late)
    )
    scale = piece_of(modulation[1], own_images, 1)
    incoming = grad_middle + norm_back(
        grad_input_attn * (1.0 + scale), normed_attn[1], inverse_attn[1]
    )
    image_sums[1] = jnp.concatenate(
        [
            image_sum(picker, grad_input_attn),
            image_sum(picker, grad_input_attn * normed_attn[1]),
        ]
        + late,
        axis=1,
    )
    branch, normed_mlp, input_mlp, gate_up, hidden, inverse_mlp, mlp_out = stored
    block_sums = [None] * 2
    (
        grad_input_mlp,
        grad_middle,
        gathered_branch,
        grad_attended,
        gu_grad,
        down_grad,
        *block_sums[1],
    ) = mlp_back_call(
        row_size,
        head_size,
        (
            incoming,
            owner,
            modulation[0],
            normed_mlp,
            inverse_mlp,
        ),
        (
            down_t[0],
            gate_up,
            gu_full[0],
            input_mlp.reshape(-1, input_mlp.shape[-1]),
            hidden,
            proj_t[0],
        ),
        [item.reshape(row_size, shard_rows, -1) for item in (qkv_grad, proj_grad)],
    )
    gu_grad, mlp_sum = lax.optimization_barrier((gu_grad, mlp_sum))
    gu_outs[0] = scattered(gu_grad)
    gathered_branch = gathered_branch.reshape(-1, gathered_branch.shape[-1])
    grad_packed, bias_sums[0] = attention_back(grad_attended, attentions[0], image_ids, geometry)
    late = late_sums(grad_middle, branch, incoming, normed_mlp, grad_input_mlp, mlp_out)
    image_sums[0] = jnp.concatenate([jnp.zeros_like(late[0])] * 2 + late, axis=1)
    gu_outs[1] = mlp_sum[:, : 2 * units]
    block_sums[1] = [mlp_sum[:, 2 * units :]] + block_sums[1]
    sheets = jnp.stack(image_sums).reshape(block_count * image_count, head_size, -1)
    sheets = sheets.transpose(1, 0, 2)
    wide = sheets.shape[-1]
    bias_sums = jnp.stack(bias_sums)
    bias_high = bias_sums.astype(jnp.bfloat16).astype(jnp.float32)
    bias_rest = bias_sums - bias_high
    bias_middle = bias_rest.astype(jnp.bfloat16).astype(jnp.float32)
    bias_parts = jnp.stack([bias_high, bias_middle, bias_rest - bias_middle], axis=1)
    bias_parts = jnp.pad(bias_parts, ((0, 0), (0, 0), (0, wide - bias_sums.shape[1])))
    bias_parts = bias_parts.reshape(-1, wide)
    used = sheets.shape[1] + bias_parts.shape[0]
    small_rows = used + -used % 16
    bias_parts = jnp.pad(bias_parts, ((sheets.shape[1], small_rows - used), (0, 0)))
    cond_rows = cond_mine.reshape(row_size, -1, shard_rows)[:, :image_count]
    row = jnp.arange(small_rows)
    mine = []
    for b in range(block_count):
        first = b * image_count
        lead = jnp.pad(cond_rows, ((0, 0), (first, small_rows - first - image_count), (0, 0)))
        is_image = (row >= first) & (row < first + image_count)
        start = block_count * image_count + 3 * b
        is_bias = (row >= start) & (row < start + 3)
        ones = jnp.stack([is_image, is_bias], axis=1).astype(jnp.bfloat16)
        ones = jnp.broadcast_to(ones[None], (row_size,) + ones.shape)
        both = jnp.concatenate([lead, ones], axis=2)
        both = jnp.pad(both, ((0, 0), (0, 0), (0, -both.shape[2] % 128)))
        mine.append(both.reshape(-1, both.shape[2]))
    logistic = jax.nn.sigmoid(cond_wide)
    factor = logistic * (1.0 + cond_wide * (1.0 - logistic))
    factor = jnp.pad(factor, ((0, -image_count % 8), (0, 0)))
    tokens_grad, ada_grads, ada_bias_grads, qkv_bias_out, cond_grad, *block_sums[0] = finish_call(
        row_size,
        head_size,
        image_count,
        (
            grad_packed,
            qkv_full[0],
            inputs_attn[0],
            attended[0],
            gathered_branch,
            grad_middle,
            piece_of(modulation[0], own_images, 1),
            normed_attn[0],
            inverse_attn[0],
            owner,
        ),
        sheets,
        bias_parts,
        jnp.stack(mine),
        ada_weight,
        factor,
        down_grad.reshape(row_size, shard_rows, -1),
    )
    cond_grad = cond_grad[:image_count]
    return (
        block_out,
        tokens_grad,
        cond_grad,
        ada_grads,
        ada_bias_grads,
        jnp.stack([item[1] for item in block_sums]),
        qkv_bias_out,
        jnp.stack([item[2].T for item in block_sums]),
        jnp.stack([item.reshape(gu_weight.shape[1:]) for item in gu_outs]),
        jnp.stack([item[0].T for item in block_sums]),
    )


def solution(mesh):
    in_specs = (
        P(("rows", "heads"), None),
        P("rows", None),
        P("rows", None),
        P("rows", None),
        P("rows", None),
        P(None, "rows", "heads"),
        P(None, "heads"),
        P(None, "rows", "heads"),
        P(None, "heads"),
        P(None, "heads", "rows"),
        P(None, "rows", None, "heads"),
        P(None, "heads", "rows"),
        P(("rows", "heads"), None),
    )
    out_specs = (
        P(("rows", "heads"), None),
        P(("rows", "heads"), None),
        P("rows", None),
        P(None, "rows", "heads"),
        P(None, "heads"),
        P(None, "rows", "heads"),
        P(None, "heads"),
        P(None, "heads", "rows"),
        P(None, "rows", None, "heads"),
        P(None, "heads", "rows"),
    )
    return jax.shard_map(shards, mesh=mesh, in_specs=in_specs, out_specs=out_specs, check_vma=False)
```

```python
import functools

import jax
import jax.numpy as jnp
from jax import lax
from jax.experimental import pallas as pl
from jax.experimental.pallas import tpu as pltpu
from jax.sharding import PartitionSpec as P

HD = 72


epsilon = 1e-06
theta_base = 10000.0
highest = lax.Precision.HIGHEST


def normalize(values):
    center = values - jnp.mean(values, axis=-1, keepdims=True)
    inverse = lax.rsqrt(jnp.mean(center * center, axis=-1, keepdims=True) + epsilon)
    return (center * inverse, inverse)


def norm_back(incoming, normed, inverse):
    return inverse * (
        incoming
        - jnp.mean(incoming, axis=-1, keepdims=True)
        - normed * jnp.mean(incoming * normed, axis=-1, keepdims=True)
    )


def lead_dot(operand, other):
    return lax.dot_general(
        operand, other, (((0,), (0,)), ((), ())), preferred_element_type=jnp.float32
    )


def tail_dot(operand, other):
    return lax.dot_general(
        operand, other, (((1,), (1,)), ((), ())), preferred_element_type=jnp.float32
    )


def angles(coords, quarter):
    frequency = theta_base ** (-jnp.arange(quarter, dtype=jnp.float32) / quarter)
    return coords.astype(jnp.float32)[..., None] * frequency


def head_move(value, flip):
    size = lax.axis_size("heads")
    return lax.ppermute(value, "heads", [(index, index ^ flip) for index in range(size)])


MESH = pl.DeviceIdType.MESH


class Place:
    def __init__(self, row_size, head_size):
        self.sizes = (4, row_size // 8, 2)
        index = lax.axis_index("rows")
        a, b, c = self.sizes
        self.mine = (index // (b * c), (index // c) % b, index % c)
        self.heads = head_size
        self.head = lax.axis_index("heads")

    def step(self, dim, by):
        return (self.mine[dim] + by + self.sizes[dim]) % self.sizes[dim]

    def row(self, a, b, c):
        return (a * self.sizes[1] + b) * self.sizes[2] + c

    def near(self, dim, by):
        at = list(self.mine)
        at[dim] = self.step(dim, by)
        return {"rows": self.row(*at)}

    def flip(self, by):
        return {"heads": self.head ^ by}

    def partners(self, with_heads):
        found = [self.near(dim, by) for dim in range(3) for by in range(1, self.sizes[dim])]
        if with_heads:
            found += [self.flip(by) for by in range(1, self.heads)]
        return found

    def greet(self, with_heads):
        barrier = pltpu.get_barrier_semaphore()
        found = self.partners(with_heads)
        for partner in found:
            pl.semaphore_signal(barrier, inc=1, device_id=partner, device_id_type=MESH)
        pl.semaphore_wait(barrier, len(found))


def gather_count(row_size):
    a, b, c = 4, row_size // 8, 2
    return 2 * (a - 1) + (2 * a - 1) * (2 * b - 1)


class Gather:
    def __init__(self, place, shard, out, send, recv, local):
        self.place, self.shard, self.out = place, shard, out
        self.send, self.recv = send, recv
        self.used = 0
        self.keep = pltpu.make_async_copy(shard, out.at[place.row(*place.mine)], local)
        a, b, _ = place.sizes
        self.hops, self.along_b, self.along_c = {}, {}, {}
        names = [(0, 0)] + [(way, k) for k in range(1, a) for way in (1, -1)]
        for way, k in names:
            if k:
                self.hops[way, k] = self.copy(way, k - 1, 0, place.near(0, way))
        for way, k in names:
            for j in range(1, b):
                self.along_b[way, k, j] = self.copy(way, k, 0, place.near(1, j))
        for way, k in names:
            for j in range(b):
                self.along_c[way, k, j] = self.copy(way, k, j, place.near(2, 1))

    def copy(self, way, k, j, device):
        place, slot = self.place, self.used
        self.used += 1
        index = place.row(place.step(0, -way * k), place.step(1, -j), place.mine[2])
        return pltpu.make_async_remote_copy(
            src_ref=self.shard if k == 0 and j == 0 else self.out.at[index],
            dst_ref=self.out.at[index],
            send_sem=self.send.at[slot],
            recv_sem=self.recv.at[slot],
            device_id=device,
            device_id_type=MESH,
        )

    def holds(self, way, k):
        at = self.place.mine[0]
        return at >= k if way > 0 else at < self.place.sizes[0] - k

    def hop(self, way, k):
        at = self.place.mine[0]
        last = self.place.sizes[0] - 1
        return (at < last) & (at >= k - 1) if way > 0 else (at > 0) & (at <= last - (k - 1))

    def begin(self):
        self.keep.start()
        for way in (1, -1):
            pl.when(self.hop(way, 1))(self.hops[way, 1].start)
        self.pass_on(0, 0)

    def pass_on(self, way, k):
        for j in range(1, self.place.sizes[1]):
            self.along_b[way, k, j].start()
        self.along_c[way, k, 0].start()

    def first(self, k):
        for way in (1, -1):

            @pl.when(self.holds(way, k))
            def _():
                self.hops[way, k].wait_recv()
                if k + 1 < self.place.sizes[0]:
                    pl.when(self.hop(way, k + 1))(self.hops[way, k + 1].start)
                self.pass_on(way, k)

    def each(self, way, k, action):
        if k:
            pl.when(self.holds(way, k))(action)
        else:
            action()

    def second(self):
        for way, k, j in self.along_b:

            def action():
                self.along_b[way, k, j].wait_recv()
                self.along_c[way, k, j].start()

            self.each(way, k, action)

    def finish(self):
        for way, k, j in self.along_c:

            def action():
                self.along_c[way, k, j].wait_recv()
                self.along_c[way, k, j].wait_send()

            self.each(way, k, action)
        for way, k, j in self.along_b:
            self.each(way, k, self.along_b[way, k, j].wait_send)
        for way, k in self.hops:
            pl.when(self.hop(way, k))(self.hops[way, k].wait_send)
        self.keep.wait()


def gather_all(items):
    count = len(items)
    items[0].begin()
    for step in range(count + 1):
        if step < count:
            items[step].first(1)
            if step + 1 < count:
                items[step + 1].begin()
            for k in range(2, items[step].place.sizes[0]):
                items[step].first(k)
        if step >= 1:
            items[step - 1].second()
    for item in items:
        item.finish()


def scatter_count(row_size):
    a, b, c = 4, row_size // 8, 2
    return a * b + a * (b - 1) + (a - 1)


class Scatter:
    def __init__(self, place, source, out, held, met, side, far, send, recv, load):
        self.place, self.source, self.out = place, source, out
        self.held, self.met, self.side, self.far = held, met, side, far
        self.send, self.recv, self.load = send, recv, load

    def remote(self, source, target, slot, device):
        return pltpu.make_async_remote_copy(
            src_ref=source,
            dst_ref=target,
            send_sem=self.send.at[slot],
            recv_sem=self.recv.at[slot],
            device_id=device,
            device_id_type=MESH,
        )

    def across(self, k, j):
        place = self.place
        a, b = place.step(0, k), place.step(1, j)
        other = place.step(2, 1)
        return self.remote(
            self.source.at[place.row(a, b, other)],
            self.met.at[a, b],
            k * place.sizes[1] + j,
            place.near(2, 1),
        )

    def fetch(self, k, j):
        place = self.place
        a, b = place.step(0, k), place.step(1, j)
        return pltpu.make_async_copy(
            self.source.at[place.row(a, b, place.mine[2])],
            self.held.at[a, b],
            self.load.at[k * place.sizes[1] + j],
        )

    def along_b(self, k, j):
        place = self.place
        a, b = place.step(0, k), place.step(1, j)
        base = place.sizes[0] * place.sizes[1]
        return self.remote(
            self.held.at[a, b],
            self.side.at[j - 1, a],
            base + (j - 1) * place.sizes[0] + k,
            place.near(1, j),
        )

    def along_a(self, k):
        place = self.place
        base = place.sizes[0] * (2 * place.sizes[1] - 1)
        return self.remote(
            self.held.at[place.step(0, k), place.mine[1]],
            self.far.at[k - 1],
            base + k - 1,
            place.near(0, k),
        )

    def order(self):
        a, b, _ = self.place.sizes
        return [(k, j) for j in list(range(1, b)) + [0] for k in list(range(1, a)) + [0]]

    def begin(self):
        for k, j in self.order():
            self.fetch(k, j).start()
            self.across(k, j).start()

    def first(self):
        place = self.place
        a, b, _ = place.sizes
        for j in range(1, b):
            for k in list(range(1, a)) + [0]:
                self.fetch(k, j).wait()
                self.across(k, j).wait_recv()
                at = (place.step(0, k), place.step(1, j))
                self.held[at] = (
                    self.held[at].astype(jnp.float32) + self.met[at].astype(jnp.float32)
                ).astype(self.held.dtype)
                self.along_b(k, j).start()

    def total(self, k):
        place = self.place
        a, b = place.step(0, k), place.mine[1]
        value = self.held[a, b].astype(jnp.float32) + self.met[a, b].astype(jnp.float32)
        for j in range(1, place.sizes[1]):
            value = value + self.side[j - 1, a].astype(jnp.float32)
        return value

    def second(self):
        place = self.place
        a, b, _ = place.sizes
        for k in list(range(1, a)) + [0]:
            self.fetch(k, 0).wait()
            self.across(k, 0).wait_recv()
            for j in range(1, b):
                self.along_b(k, j).wait_recv()
            if k:
                self.held[place.step(0, k), place.mine[1]] = self.total(k).astype(self.held.dtype)
                self.along_a(k).start()
            else:
                self.out[...] = self.total(0)

    def finish(self):
        place = self.place
        a, b, _ = place.sizes
        for k in range(1, a):
            self.along_a(k).wait_recv()
            self.out[...] = self.out[...] + self.far[k - 1].astype(jnp.float32)
        for k, j in self.order():
            self.across(k, j).wait_send()
            if j:
                self.along_b(k, j).wait_send()
        for k in range(1, a):
            self.along_a(k).wait_send()


def scatter_all(items):
    count = len(items)
    for item in items:
        item.begin()
    for step in range(count + 2):
        if step < count:
            items[step].first()
        if 1 <= step <= count:
            items[step - 1].second()
        if step >= 2:
            items[step - 2].finish()


def start_kernel(row_size, head_size, images, blocks, weights, *refs):
    cond, ada, bias, tokens, cotangent, owner = refs[:6]
    shards = [ref.at[0] for ref in refs[6 : 6 + weights]]
    outs = refs[6 + weights : 6 + 2 * weights]
    refs = refs[6 + 2 * weights :]
    table, mine_out, inputs_out, normed_out, inverse_out, grads_out = refs[:6]
    every_token, every_cotangent, token_send, token_recv = refs[6:10]
    refs = refs[10:]
    (conds, part, held, met, side, far, total, every, sends, recvs, keeps) = refs[:11]
    (mod_send, mod_recv, mod_load, head_send, head_recv) = refs[11:]
    place = Place(row_size, head_size)
    place.greet(True)
    items = [
        Gather(place, shard, out, sends.at[i], recvs.at[i], keeps.at[i])
        for i, (shard, out) in enumerate(zip((cond,) + tuple(shards), (conds,) + outs))
    ]
    lead, bulk = items[0], items[1:]
    lead.begin()
    own = tokens.shape[0]
    every_token[0] = tokens[...]
    every_cotangent[0] = cotangent[...]
    raws = [
        Across(place, lambda by: ref.at[0], lambda by: ref.at[by], token_send, token_recv, stage)
        for stage, ref in enumerate((every_token, every_cotangent))
    ]
    for raw in raws:
        for by in range(1, head_size):
            raw.start(by)
    bulk[0].begin()
    hops = range(1, place.sizes[0])
    for k in hops:
        lead.first(k)
    lead.second()
    lead.finish()
    width = cond.shape[1]
    share = ada.shape[1]
    pad = cond.shape[0]
    lane = lax.broadcasted_iota(jnp.int32, (width, share), 0)
    slot = lax.broadcasted_iota(jnp.int32, (width, share), 1)
    pick = jnp.where(lane == lax.axis_index("rows") * share + slot, 1.0, 0.0).astype(jnp.bfloat16)
    mine = jnp.dot(
        conds[...].reshape(row_size * pad, width), pick, preferred_element_type=jnp.float32
    ).astype(jnp.bfloat16)
    mine_out[...] = mine
    for b in range(blocks):
        value = jnp.dot(mine, ada[b], preferred_element_type=jnp.float32)
        part[:, b * images : (b + 1) * images, :] = value.reshape(row_size, pad, -1)[:, :images]
    sums = Scatter(place, part, total, held, met, side, far, mod_send, mod_recv, mod_load)
    sums.begin()
    bulk[0].first(1)
    for item in bulk[1:]:
        item.begin()
    sums.first()
    for k in hops[1:]:
        bulk[0].first(k)
    sums.second()
    for item in bulk[1:]:
        for k in hops:
            item.first(k)
    sums.finish()
    every[place.head] = total[...] + bias[...]
    across = [
        pltpu.make_async_remote_copy(
            src_ref=every.at[place.head],
            dst_ref=every.at[place.head],
            send_sem=head_send.at[by - 1],
            recv_sem=head_recv.at[by - 1],
            device_id=place.flip(by),
            device_id_type=MESH,
        )
        for by in range(1, head_size)
    ]
    for copy in across:
        copy.start()
    for item in bulk:
        item.second()
    for copy in across:
        copy.wait()
    wide = every.shape[2]
    for head in range(head_size):
        table[:, head * wide : (head + 1) * wide] = every[head]
    for raw in raws:
        for by in range(1, head_size):
            raw.arrived(by)
    columns = tokens.shape[1]
    half = own // pieces_of(own)

    def modulation(here, first, index):
        value = jnp.zeros((half, columns), jnp.float32)
        for image in range(images):
            row = table[first + image : first + image + 1, index * columns : (index + 1) * columns]
            value = jnp.where(here == image, row, value)
        return value

    last = (blocks - 1) * images

    @pl.loop(0, head_size * (own // half))
    def _(step):
        slot = step // (own // half)
        rows = pl.ds(pl.multiple_of(step % (own // half) * half, 8), half)
        here = owner[pl.ds(pl.multiple_of(step * half, 8), half), :]
        unit, scale = normalize(every_token[slot, rows].astype(jnp.float32))
        inputs_out[slot, rows] = (
            unit * (1.0 + modulation(here, 0, 1)) + modulation(here, 0, 0)
        ).astype(jnp.bfloat16)
        grads_out[slot, rows] = (
            modulation(here, last, 5) * every_cotangent[slot, rows].astype(jnp.float32)
        ).astype(jnp.bfloat16)

        @pl.when(slot == 0)
        def _():
            normed_out[rows] = unit
            inverse_out[rows] = scale

    for raw in raws:
        raw.left()
    for item in bulk:
        item.finish()


def start_call(row_size, head_size, cond, ada, bias, tokens, cotangent, owner, shards):
    images = bias.shape[0] // ada.shape[0]
    blocks = ada.shape[0]
    count = len(shards)
    a, b = 4, row_size // 8
    chunk = bias.shape
    copies = gather_count(row_size)
    anywhere = pl.BlockSpec(memory_space=pl.ANY)
    vmem = pl.BlockSpec(memory_space=pltpu.VMEM)
    f32, bf16 = jnp.float32, jnp.bfloat16
    own, width = tokens.shape
    shape = jax.ShapeDtypeStruct
    return pl.pallas_call(
        functools.partial(start_kernel, row_size, head_size, images, blocks, count),
        out_shape=[jax.ShapeDtypeStruct((row_size,) + item.shape[1:], item.dtype) for item in shards]
        + [
            shape((chunk[0], head_size * chunk[1]), f32),
            shape((row_size * cond.shape[0], ada.shape[1]), cond.dtype),
            shape((head_size, own, width), bf16),
            shape((own, width), f32),
            shape((own, 1), f32),
            shape((head_size, own, width), bf16),
        ],
        in_specs=[vmem] * 6 + [anywhere] * count,
        out_specs=[anywhere] * count + [vmem] * 6,
        scratch_shapes=[
            pltpu.VMEM((head_size, own, width), bf16),
            pltpu.VMEM((head_size, own, width), bf16),
            pltpu.SemaphoreType.DMA((2 * (head_size - 1),)),
            pltpu.SemaphoreType.DMA((2 * (head_size - 1),)),
            pltpu.VMEM((row_size,) + cond.shape, cond.dtype),
            pltpu.VMEM((row_size,) + chunk, f32),
            pltpu.VMEM((a, b) + chunk, f32),
            pltpu.VMEM((a, b) + chunk, f32),
            pltpu.VMEM((b - 1, a) + chunk, f32),
            pltpu.VMEM((a - 1,) + chunk, f32),
            pltpu.VMEM(chunk, f32),
            pltpu.VMEM((head_size,) + chunk, f32),
            pltpu.SemaphoreType.DMA((count + 1, copies)),
            pltpu.SemaphoreType.DMA((count + 1, copies)),
            pltpu.SemaphoreType.DMA((count + 1,)),
            pltpu.SemaphoreType.DMA((scatter_count(row_size),)),
            pltpu.SemaphoreType.DMA((scatter_count(row_size),)),
            pltpu.SemaphoreType.DMA((a * b,)),
            pltpu.SemaphoreType.DMA((head_size - 1,)),
            pltpu.SemaphoreType.DMA((head_size - 1,)),
        ],
        compiler_params=pltpu.CompilerParams(
            collective_id=1, has_side_effects=True, vmem_limit_bytes=48 * 2**20
        ),
        name="start",
    )(cond, ada, bias, tokens, cotangent, owner, *shards)


def weight_grads_kernel(*refs):
    count = len(refs) // 3
    for i in range(count):
        left, right, out = refs[2 * i], refs[2 * i + 1], refs[2 * count + i]
        columns = out.shape[1]
        for at in range(0, columns, 256):
            size = min(256, columns - at)
            out[:, at : at + size] = dot_tn(left[...], right[:, at : at + size]).astype(out.dtype)


def weight_grads(*pairs):
    vmem = pl.BlockSpec(memory_space=pltpu.VMEM)
    flat = [item for pair in pairs for item in pair]
    flops = sum(2 * left.size * right.shape[1] for left, right in pairs)
    moved = sum(2 * (left.size + right.size + left.shape[1] * right.shape[1]) for left, right in pairs)
    return pl.pallas_call(
        weight_grads_kernel,
        out_shape=[
            jax.ShapeDtypeStruct((left.shape[1], right.shape[1]), jnp.bfloat16)
            for left, right in pairs
        ],
        in_specs=[vmem] * len(flat),
        out_specs=[vmem] * len(pairs),
        compiler_params=pltpu.CompilerParams(vmem_limit_bytes=48 * 2**20),
        cost_estimate=pl.CostEstimate(flops=flops, bytes_accessed=moved, transcendentals=0),
        name="weight_grads",
    )(*flat)


def tile_of(width):
    return next(size for size in (256, 128, width) if width % size == 0)


def dot_nn(left, right):
    return jnp.dot(left, right, preferred_element_type=jnp.float32)


def dot_nt(left, right):
    return lax.dot_general(left, right, (((1,), (1,)), ((), ())), preferred_element_type=jnp.float32)


def dot_tn(left, right):
    return lax.dot_general(left, right, (((0,), (0,)), ((), ())), preferred_element_type=jnp.float32)


def tiles(width, size, body):
    @pl.loop(0, width // size)
    def _(step):
        body(step, pl.multiple_of(step * size, size))


class Across:
    def __init__(self, place, sources, targets, send, recv, stage):
        count = place.heads - 1
        self.copies = [
            pltpu.make_async_remote_copy(
                src_ref=sources(by),
                dst_ref=targets(by),
                send_sem=send.at[stage * count + by - 1],
                recv_sem=recv.at[stage * count + by - 1],
                device_id=place.flip(by),
                device_id_type=MESH,
            )
            for by in range(1, place.heads)
        ]

    def start(self, by):
        self.copies[by - 1].start()

    def arrived(self, by):
        self.copies[by - 1].wait_recv()

    def left(self):
        for copy in self.copies:
            copy.wait_send()


class Streamed:
    def __init__(self, buffer, out, sems, size, begin=0):
        self.buffer, self.out, self.sems, self.size, self.begin = buffer, out, sems, size, begin

    def copy(self, step):
        at = pl.multiple_of(self.begin + step * self.size, 128)
        return pltpu.make_async_copy(
            self.buffer.at[step % 2], self.out.at[:, pl.ds(at, self.size)], self.sems.at[step % 2]
        )

    def put(self, step, value):
        @pl.when(step >= 2)
        def _():
            self.copy(step - 2).wait()

        self.buffer[step % 2] = value.astype(self.buffer.dtype)
        self.copy(step).start()

    def drain(self, steps):
        for step in range(max(steps - 2, 0), steps):
            self.copy(step).wait()


def finish_kernel(row_size, head_size, images, blocks, *refs):
    (packed, qkv, inputs, attended, branch, middle, scale, normed, inverse, owner) = refs[:10]
    known, bias, mine, ada, factor = refs[10:15]
    done, down = refs[15:18], refs[18]
    grad_tokens, ada_out, ada_bias_out, qkv_bias_out, cond_out = refs[19:24]
    stacks = refs[24:27]
    outs = [ref.at[0] for ref in stacks]
    refs = refs[3:]
    parcel, landed, sheet, share_in, small, qkv_grad, proj_grad = refs[24:31]
    head_send, head_recv = refs[31:33]
    refs = refs[33:]
    scratch = refs[:12]
    every, part, held, met, side, far, total, cond_in = refs[12:20]
    send, recv, load, small_send, small_recv, small_keep = refs[20:26]
    cond_send, cond_recv, cond_load = refs[26:]
    place = Place(row_size, head_size)
    own, width = middle.shape
    step_width = tile_of(width)
    place.greet(True)
    for stack, item in zip(stacks, done):
        stack[1] = item[...]
    items = [
        Scatter(
            place, source, outs[i], *scratch[4 * i : 4 * i + 4], send.at[i], recv.at[i], load.at[i]
        )
        for i, source in enumerate((down, qkv_grad, proj_grad))
    ]
    items[0].begin()
    first = Across(
        place, lambda by: parcel.at[by - 1], lambda by: landed.at[by - 1], head_send, head_recv, 0
    )
    for by in range(1, head_size):

        def body(step, at):
            parcel[by - 1, :, pl.ds(at, step_width)] = dot_nt(
                packed[pl.ds(by * own, own), :], qkv[pl.ds(at, step_width), :]
            ).astype(jnp.bfloat16)

        tiles(width, step_width, body)
        first.start(by)
    for left, right, out, item in (
        (inputs, packed, qkv_grad, items[1]),
        (branch, attended, proj_grad, items[2]),
    ):
        share = out.shape[1]
        for at in range(0, out.shape[2], 256):
            size = min(256, out.shape[2] - at)
            value = dot_tn(left[...], right[:, at : at + size])
            for row in range(row_size):
                out[row, :, at : at + size] = value[row * share : (row + 1) * share].astype(out.dtype)
        item.begin()
    items[0].first()
    value = dot_nt(packed[pl.ds(0, own), :], qkv[...])
    for by in range(1, head_size):
        first.arrived(by)
        value = value + landed[by - 1].astype(jnp.float32)
    scaled = value * (1.0 + scale[...])
    grad_tokens[...] = middle[...] + inverse[...] * (
        scaled
        - jnp.mean(scaled, axis=-1, keepdims=True)
        - normed[...] * jnp.mean(scaled * normed[...], axis=-1, keepdims=True)
    )
    sheet[...] = known[...]
    wide = sheet.shape[2]
    for image in range(images):
        here = owner[...] == image
        for piece, item in enumerate((value, value * normed[...])):
            row = jnp.sum(jnp.where(here, item, 0.0), axis=0, keepdims=True)
            begin = piece * width
            while begin < (piece + 1) * width:
                end = min((begin // wide + 1) * wide, (piece + 1) * width)
                sheet[begin // wide, image : image + 1, begin % wide : begin % wide + end - begin] = (
                    row[:, begin - piece * width : end - piece * width]
                )
                begin = end
    shares = Across(
        place,
        lambda by: sheet.at[place.head ^ by],
        lambda by: share_in.at[by - 1],
        head_send,
        head_recv,
        1,
    )
    for by in range(1, head_size):
        shares.start(by)
    mod_grads = sheet[place.head]
    for by in range(1, head_size):
        shares.arrived(by)
        mod_grads = mod_grads + share_in[by - 1]
    known_rows = mod_grads.shape[0]
    small[...] = jnp.concatenate([mod_grads, bias[known_rows:, :]], axis=0).astype(small.dtype)
    lead = Gather(place, small, every, small_send, small_recv, small_keep.at[0])
    lead.begin()
    for k in range(1, place.sizes[0]):
        lead.first(k)
    items[1].first()
    items[0].second()
    lead.second()
    lead.finish()
    rows = small.shape[0]
    share = ada.shape[1]
    grads = every[...].reshape(row_size * rows, -1)
    columns = qkv_bias_out.shape[1]
    for b in range(blocks):
        value = dot_tn(mine[b], grads)
        ada_out[b] = value[:share]
        ada_bias_out[b : b + 1, :] = value[share : share + 1]
        qkv_bias_out[b : b + 1, :] = value[share + 1 : share + 2, :columns]
    lane = lax.broadcasted_iota(jnp.int32, (share, width), 1)
    slot = lax.broadcasted_iota(jnp.int32, (share, width), 0)
    pick = jnp.where(lane == lax.axis_index("rows") * share + slot, 1.0, 0.0).astype(jnp.bfloat16)
    back = 0.0
    for b in range(blocks):
        value = dot_nt(grads, ada[b]).reshape(row_size, rows, share)
        back = back + value[:, b * images : (b + 1) * images]
    back = back.reshape(row_size * images, share).astype(jnp.bfloat16)
    part[...] = jnp.zeros_like(part)
    part[:, :images, :] = dot_nn(back, pick).reshape(row_size, images, width)
    sums = Scatter(place, part, total, held, met, side, far, cond_send, cond_recv, cond_load)
    sums.begin()
    sums.first()
    items[2].first()
    items[1].second()
    sums.second()
    items[2].second()
    sums.finish()
    last = Across(
        place, lambda by: total, lambda by: cond_in.at[by - 1], head_send, head_recv, 2
    )
    for by in range(1, head_size):
        last.start(by)
    for item in items:
        item.finish()
    value = total[...]
    for by in range(1, head_size):
        last.arrived(by)
        value = value + cond_in[by - 1]
    cond_out[...] = value * factor[...]
    for stage in (first, shares, last):
        stage.left()


def finish_call(row_size, head_size, images, near, known, bias, mine, ada, factor, done, down):
    packed, qkv, inputs, attended, branch, middle = near[:6]
    copies = scatter_count(row_size)
    small_copies = gather_count(row_size)
    blocks, share, wide = ada.shape
    own, width = middle.shape
    a, b = 4, row_size // 8
    f32, bf16 = jnp.float32, jnp.bfloat16
    shape = jax.ShapeDtypeStruct
    chunks = [(share, columns) for columns in (down.shape[2], qkv.shape[1], attended.shape[1])]
    scratch = []
    for chunk in chunks:
        for lead in ((a, b), (a, b), (b - 1, a), (a - 1,)):
            scratch.append(pltpu.VMEM(lead + chunk, bf16))
    chunk = factor.shape
    anywhere = pl.BlockSpec(memory_space=pl.ANY)
    vmem = pl.BlockSpec(memory_space=pltpu.VMEM)
    others = head_size - 1
    return pl.pallas_call(
        functools.partial(finish_kernel, row_size, head_size, images, blocks),
        out_shape=[
            shape((own, width), f32),
            shape(ada.shape, f32),
            shape((blocks, wide), f32),
            shape((blocks, qkv.shape[1]), f32),
            shape(factor.shape, f32),
        ]
        + [shape((2,) + item, f32) for item in chunks],
        in_specs=[vmem] * 18 + [anywhere],
        out_specs=[vmem] * 8,
        scratch_shapes=[
            pltpu.VMEM((others, own, width), bf16),
            pltpu.VMEM((others, own, width), bf16),
            pltpu.VMEM(known.shape, f32),
            pltpu.VMEM((others,) + known.shape[1:], f32),
            pltpu.VMEM(bias.shape, bf16),
            pltpu.VMEM((row_size,) + chunks[1], bf16),
            pltpu.VMEM((row_size,) + chunks[2], bf16),
            pltpu.SemaphoreType.DMA((3 * others,)),
            pltpu.SemaphoreType.DMA((3 * others,)),
        ]
        + scratch
        + [
            pltpu.VMEM((row_size,) + bias.shape, bf16),
            pltpu.VMEM((row_size,) + chunk, f32),
            pltpu.VMEM((a, b) + chunk, f32),
            pltpu.VMEM((a, b) + chunk, f32),
            pltpu.VMEM((b - 1, a) + chunk, f32),
            pltpu.VMEM((a - 1,) + chunk, f32),
            pltpu.VMEM(chunk, f32),
            pltpu.VMEM((others,) + chunk, f32),
            pltpu.SemaphoreType.DMA((3, copies)),
            pltpu.SemaphoreType.DMA((3, copies)),
            pltpu.SemaphoreType.DMA((3, a * b)),
            pltpu.SemaphoreType.DMA((small_copies,)),
            pltpu.SemaphoreType.DMA((small_copies,)),
            pltpu.SemaphoreType.DMA((1,)),
            pltpu.SemaphoreType.DMA((copies,)),
            pltpu.SemaphoreType.DMA((copies,)),
            pltpu.SemaphoreType.DMA((a * b,)),
        ],
        compiler_params=pltpu.CompilerParams(
            collective_id=2, has_side_effects=True, vmem_limit_bytes=60 * 2**20
        ),
        name="finish",
    )(*near, known, bias, mine, ada, factor, *done, down)


class Pieces:
    def __init__(self, place, pieces, source, target, send, recv, stage):
        self.copies = {}
        for by in range(1, place.heads):
            for piece in range(pieces):
                slot = (stage * (place.heads - 1) + by - 1) * pieces + piece
                self.copies[by, piece] = pltpu.make_async_remote_copy(
                    src_ref=source(by, piece),
                    dst_ref=target(by, piece),
                    send_sem=send.at[slot],
                    recv_sem=recv.at[slot],
                    device_id=place.flip(by),
                    device_id_type=MESH,
                )

    def start(self, by, piece):
        self.copies[by, piece].start()

    def arrived(self, by, piece):
        self.copies[by, piece].wait_recv()

    def left(self):
        for key in self.copies:
            self.copies[key].wait_send()


class Mlp:
    def __init__(self, place, pieces, own, width, units, sends, recvs):
        self.place, self.pieces, self.own, self.width, self.units = place, pieces, own, width, units
        self.sends, self.recvs = sends, recvs
        self.rows = own // pieces
        self.others = [(by, p) for p in range(pieces) for by in range(1, place.heads)]

    def at(self, piece):
        return pl.ds(piece * self.rows, self.rows)

    def flat(self, by, piece):
        return pl.ds(by * self.own + piece * self.rows, self.rows)

    def sum_stage(self, parcel, landed, stage):
        return Pieces(
            self.place,
            self.pieces,
            lambda by, p: parcel.at[by - 1, self.at(p)],
            lambda by, p: landed.at[by - 1, self.at(p)],
            self.sends,
            self.recvs,
            stage,
        )

    def spread_stage(self, every, stage):
        return Pieces(
            self.place,
            self.pieces,
            lambda by, p: every.at[0, self.at(p)],
            lambda by, p: every.at[by, self.at(p)],
            self.sends,
            self.recvs,
            stage,
        )

    def send_all(self, stage, piece):
        for by in range(1, self.place.heads):
            stage.start(by, piece)

    def arrive_all(self, stage, piece):
        for by in range(1, self.place.heads):
            stage.arrived(by, piece)

    def total(self, own_part, landed, piece):
        value = own_part[self.at(piece)]
        for by in range(1, self.place.heads):
            value = value + landed[by - 1, self.at(piece)].astype(jnp.float32)
        return value

    def modulation(self, table, owner, index, piece):
        here = owner[self.at(piece)]
        total = jnp.zeros((self.rows, self.width), jnp.float32)
        for image in range(table.shape[0]):
            row = table[image : image + 1, index * self.width : (index + 1) * self.width]
            total = jnp.where(here == image, row, total)
        return total

    def partial(self, out, left, rows, right):
        size = tile_of(self.width)

        def body(step, at):
            out[:, pl.ds(at, size)] = dot_nt(left[rows, :], right[pl.ds(at, size), :]).astype(out.dtype)

        tiles(self.width, size, body)

    def front(self, attended, proj, residual, table, owner, parcel, landed, own_part, branch, middle, normed, inverse, inputs, tick=None):
        first = self.sum_stage(parcel, landed, 0)
        for by, p in self.others:
            parcel[by - 1, self.at(p)] = dot_nt(attended[self.flat(by, p), :], proj[...]).astype(
                jnp.bfloat16
            )
            first.start(by, p)
        own_part[...] = dot_nt(attended[pl.ds(0, self.own), :], proj[...])
        if tick:
            tick()
        second = self.spread_stage(inputs, 1)
        for p in range(self.pieces):
            at = self.at(p)
            self.arrive_all(first, p)
            value = self.total(own_part, landed, p)
            branch[at] = value
            value = residual[at] + self.modulation(table, owner, 2, p) * value
            middle[at] = value
            unit, scale = normalize(value)
            normed[at] = unit
            inverse[at] = scale
            inputs[0, at] = (
                unit * (1.0 + self.modulation(table, owner, 4, p))
                + self.modulation(table, owner, 3, p)
            ).astype(jnp.bfloat16)
            self.send_all(second, p)
        return first, second

    def gate_up(self, inputs, gu, out, hidden, by, begin, rows):
        flat = pl.ds(by * self.own + begin, rows)
        size = tile_of(self.units)

        def body(step, at):
            far = pl.ds(pl.multiple_of(self.units + at, 128), size)
            value = inputs[by, pl.ds(begin, rows)]
            gate = dot_nn(value, gu[:, pl.ds(at, size)])
            up = dot_nn(value, gu[:, far])
            out[flat, pl.ds(at, size)] = gate
            out[flat, far] = up
            hidden[flat, pl.ds(at, size)] = (jax.nn.silu(gate) * up).astype(jnp.bfloat16)

        tiles(self.units, size, body)

    def hidden_back(self, grads, down, gate_up, ggu, by, begin, rows):
        flat = pl.ds(by * self.own + begin, rows)
        size = tile_of(self.units)

        def body(step, at):
            far = pl.ds(pl.multiple_of(self.units + at, 128), size)
            gate = gate_up[flat, pl.ds(at, size)]
            up = gate_up[flat, far]
            grad = dot_nn(grads[by, pl.ds(begin, rows)], down[:, pl.ds(at, size)])
            logistic = jax.nn.sigmoid(gate)
            ggu[flat, pl.ds(at, size)] = (
                grad * up * logistic * (1.0 + gate * (1.0 - logistic))
            ).astype(jnp.bfloat16)
            ggu[flat, far] = (grad * gate * logistic).astype(jnp.bfloat16)

        tiles(self.units, size, body)


def mlp_kernel(row_size, head_size, pieces, count, which, *refs):
    attended, residual, owner, table, following = refs[:5]
    streams, shards = refs[5:8], [ref.at[which] for ref in refs[8 : 8 + count]]
    refs = refs[8 + count :]
    kept_out, refs = refs[:5], refs[5:]
    inverse, mlp_out, result, next_normed, next_inverse, next_out = refs[:6]
    gathered, refs = refs[6 : 6 + count], refs[6 + count :]
    weights, kept = refs[:3], refs[3:8]
    proj, gu, down = weights
    branch, normed, inputs, gate_up, hidden = kept
    parcel, landed, middle, own_part, next_all = refs[8:13]
    loads, stores, sends, recvs, gather_send, gather_recv, gather_keep = refs[13:]
    place = Place(row_size, head_size)
    own, width = residual.shape
    units = hidden.shape[1]
    work = Mlp(place, pieces, own, width, units, sends, recvs)
    copies = [
        pltpu.make_async_copy(source, target, loads.at[i])
        for i, (source, target) in enumerate(zip(streams, weights))
    ]
    out_copies = [
        pltpu.make_async_copy(source, target, stores.at[i])
        for i, (source, target) in enumerate(zip(kept, kept_out))
    ]
    items = [
        Gather(place, shards[i], gathered[i], gather_send.at[i], gather_recv.at[i], gather_keep.at[i])
        for i in range(count)
    ]
    for copy in copies:
        copy.start()
    place.greet(True)
    for item in items:
        item.begin()

    def hop(k):
        for item in items:
            item.first(k)

    copies[0].wait()
    first, second = work.front(
        attended,
        proj,
        residual,
        table,
        owner,
        parcel.at[0],
        landed.at[0],
        own_part,
        branch,
        middle,
        normed,
        inverse,
        inputs,
        lambda: hop(1),
    )
    hop(2)
    out_copies[0].start()
    out_copies[1].start()
    copies[1].wait()
    work.gate_up(inputs, gu, gate_up, hidden, 0, 0, own)
    for k in range(3, place.sizes[0]):
        hop(k)
    copies[2].wait()
    third = work.sum_stage(parcel.at[1], landed.at[1], 2)
    for by, p in work.others:
        second.arrived(by, p)
        work.gate_up(inputs, gu, gate_up, hidden, by, p * work.rows, work.rows)
        work.partial(parcel.at[1, by - 1, work.at(p)], hidden, work.flat(by, p), down)
        third.start(by, p)
    for copy in out_copies[2:]:
        copy.start()
    work.partial(own_part, hidden, pl.ds(0, own), down)
    for item in items:
        item.second()
    fourth = work.spread_stage(next_all, 3)
    for p in range(pieces):
        at = work.at(p)
        work.arrive_all(third, p)
        value = work.total(own_part, landed.at[1], p)
        mlp_out[at] = value
        value = middle[at] + work.modulation(table, owner, 5, p) * value
        result[at] = value
        unit, scale = normalize(value)
        next_normed[at] = unit
        next_inverse[at] = scale
        next_all[0, at] = (
            unit * (1.0 + work.modulation(following, owner, 1, p))
            + work.modulation(following, owner, 0, p)
        ).astype(jnp.bfloat16)
        work.send_all(fourth, p)
    next_out[0] = next_all[0]
    for by, p in work.others:
        fourth.arrived(by, p)
        next_out[by, work.at(p)] = next_all[by, work.at(p)]
    for item in items:
        item.finish()
    for stage in (first, second, third, fourth):
        stage.left()
    for copy in out_copies:
        copy.wait()


def pieces_of(own):
    return 2 if own % 32 == 0 else 1


def mlp_call(row_size, head_size, attended, residual, owner, table, following, weights, which, shards):
    own, width = residual.shape
    tokens = attended.shape[0]
    units = weights[2].shape[1]
    count = len(shards)
    pieces = pieces_of(own)
    others = head_size - 1
    copies = gather_count(row_size)
    anywhere = pl.BlockSpec(memory_space=pl.ANY)
    vmem = pl.BlockSpec(memory_space=pltpu.VMEM)
    shape = jax.ShapeDtypeStruct
    f32, bf16 = jnp.float32, jnp.bfloat16
    kept = [
        shape((own, width), f32),
        shape((own, width), f32),
        shape((head_size, own, width), bf16),
        shape((tokens, 2 * units), f32),
        shape((tokens, units), bf16),
    ]
    return pl.pallas_call(
        functools.partial(mlp_kernel, row_size, head_size, pieces, count, which),
        out_shape=kept
        + [
            shape((own, 1), f32),
            shape((own, width), f32),
            shape((own, width), f32),
            shape((own, width), f32),
            shape((own, 1), f32),
            shape((head_size, own, width), bf16),
        ]
        + [shape((row_size,) + item.shape[1:], item.dtype) for item in shards],
        in_specs=[vmem] * 5 + [anywhere] * (3 + count),
        out_specs=[anywhere] * 5 + [vmem] * 6 + [anywhere] * count,
        scratch_shapes=[pltpu.VMEM(item.shape, item.dtype) for item in weights]
        + [pltpu.VMEM(item.shape, item.dtype) for item in kept]
        + [
            pltpu.VMEM((2, others, own, width), bf16),
            pltpu.VMEM((2, others, own, width), bf16),
            pltpu.VMEM((own, width), f32),
            pltpu.VMEM((own, width), f32),
            pltpu.VMEM((head_size, own, width), bf16),
            pltpu.SemaphoreType.DMA((3,)),
            pltpu.SemaphoreType.DMA((5,)),
            pltpu.SemaphoreType.DMA((4 * others * pieces,)),
            pltpu.SemaphoreType.DMA((4 * others * pieces,)),
            pltpu.SemaphoreType.DMA((count, copies)),
            pltpu.SemaphoreType.DMA((count, copies)),
            pltpu.SemaphoreType.DMA((count,)),
        ],
        compiler_params=pltpu.CompilerParams(
            collective_id=4, has_side_effects=True, vmem_limit_bytes=60 * 2**20
        ),
        name="mlp",
    )(attended, residual, owner, table, following, *weights, *shards)


def mlp_back_kernel(row_size, head_size, pieces, count, *refs):
    incoming, owner, table, normed, inverse = refs[:5]
    streams = refs[5:11]
    grads = refs[11 : 11 + count]
    outs = refs[11 + count : 17 + 2 * count]
    grad_in, grad_mid, branch_out, grad_att, gu_out, down_out = outs[:6]
    sums = outs[6:]
    refs = refs[17 + 2 * count :]
    down, gate_up, gu, inputs, hidden, proj = refs[:6]
    mlp_all, branch_all, ggu, parcel, landed, own_part, buffer = refs[6:13]
    loads, sends, recvs, tile_sems, out_sem = refs[13:18]
    scratch = refs[18 : 18 + 4 * count]
    sum_send, sum_recv, sum_load = refs[18 + 4 * count :]
    place = Place(row_size, head_size)
    own, width = incoming.shape
    units = hidden.shape[1]
    work = Mlp(place, pieces, own, width, units, sends, recvs)
    step_units = tile_of(units)
    copies = [
        pltpu.make_async_copy(source, target, loads.at[i])
        for i, (source, target) in enumerate(
            zip(streams, (down, gate_up, gu, inputs, hidden, proj))
        )
    ]
    for copy in copies:
        copy.start()
    place.greet(True)
    first = work.spread_stage(mlp_all, 0)
    for p in range(pieces):
        at = work.at(p)
        mlp_all[0, at] = (work.modulation(table, owner, 5, p) * incoming[at]).astype(jnp.bfloat16)
        work.send_all(first, p)
    items = [
        Scatter(
            place,
            grads[i],
            sums[i],
            *scratch[4 * i : 4 * i + 4],
            sum_send.at[i],
            sum_recv.at[i],
            sum_load.at[i],
        )
        for i in range(count)
    ]
    for item in items:
        item.begin()
    copies[0].wait()
    copies[1].wait()
    work.hidden_back(mlp_all, down, gate_up, ggu, 0, 0, own)
    for item in items:
        item.first()
    copies[2].wait()
    second = work.sum_stage(parcel, landed, 1)
    for by, p in work.others:
        first.arrived(by, p)
        work.hidden_back(mlp_all, down, gate_up, ggu, by, p * work.rows, work.rows)
        work.partial(parcel.at[by - 1, work.at(p)], ggu, work.flat(by, p), gu)
        second.start(by, p)
    work.partial(own_part, ggu, pl.ds(0, own), gu)
    copies[3].wait()
    out = Streamed(buffer, gu_out, tile_sems, step_units)

    def body(step, at):
        out.put(step, dot_tn(inputs[...], ggu[:, pl.ds(at, step_units)]))

    tiles(2 * units, step_units, body)
    for item in items[:1]:
        item.second()
    third = work.spread_stage(branch_all, 2)
    for p in range(pieces):
        at = work.at(p)
        work.arrive_all(second, p)
        value = work.total(own_part, landed, p)
        grad_in[at] = value
        unit = normed[at]
        value = value * (1.0 + work.modulation(table, owner, 4, p))
        value = incoming[at] + inverse[at] * (
            value
            - jnp.mean(value, axis=-1, keepdims=True)
            - unit * jnp.mean(value * unit, axis=-1, keepdims=True)
        )
        grad_mid[at] = value
        branch_all[0, at] = (work.modulation(table, owner, 2, p) * value).astype(jnp.bfloat16)
        work.send_all(third, p)
    out.drain(2 * units // step_units)
    copies[4].wait()
    copies[5].wait()
    out = Streamed(buffer, down_out, tile_sems, step_units)

    def body(step, at):
        out.put(
            step,
            dot_tn(mlp_all[...].reshape(head_size * own, width), hidden[:, pl.ds(at, step_units)]),
        )

    tiles(units, step_units, body)
    for item in items[1:]:
        item.second()
    grad_att[pl.ds(0, own), :] = dot_nn(branch_all[0], proj[...]).astype(jnp.bfloat16)
    for by, p in work.others:
        third.arrived(by, p)
        grad_att[work.flat(by, p), :] = dot_nn(branch_all[by, work.at(p)], proj[...]).astype(
            jnp.bfloat16
        )
    keep = pltpu.make_async_copy(branch_all, branch_out, out_sem.at[0])
    keep.start()
    out.drain(units // step_units)
    for item in items:
        item.finish()
    for stage in (first, second, third):
        stage.left()
    keep.wait()


def mlp_back_call(row_size, head_size, near, streams, grads):
    count = len(grads)
    own, width = near[0].shape
    pieces = pieces_of(own)
    others = head_size - 1
    down, gate_up, gu, inputs, hidden, proj = streams
    units = hidden.shape[1]
    tokens = hidden.shape[0]
    a, b = 4, row_size // 8
    copies = scatter_count(row_size)
    scratch = []
    for grad in grads:
        chunk = grad.shape[1:]
        for lead in ((a, b), (a, b), (b - 1, a), (a - 1,)):
            scratch.append(pltpu.VMEM(lead + chunk, grad.dtype))
    anywhere = pl.BlockSpec(memory_space=pl.ANY)
    vmem = pl.BlockSpec(memory_space=pltpu.VMEM)
    shape = jax.ShapeDtypeStruct
    f32, bf16 = jnp.float32, jnp.bfloat16
    return pl.pallas_call(
        functools.partial(mlp_back_kernel, row_size, head_size, pieces, count),
        out_shape=[
            shape((own, width), f32),
            shape((own, width), f32),
            shape((head_size, own, width), bf16),
            shape((tokens, proj.shape[1]), bf16),
            shape((width, 2 * units), bf16),
            shape((width, units), bf16),
        ]
        + [shape(grad.shape[1:], f32) for grad in grads],
        in_specs=[vmem] * 5 + [anywhere] * (6 + count),
        out_specs=[vmem, vmem, anywhere, vmem, anywhere, anywhere] + [vmem] * count,
        scratch_shapes=[pltpu.VMEM(item.shape, item.dtype) for item in streams]
        + [
            pltpu.VMEM((head_size, own, width), bf16),
            pltpu.VMEM((head_size, own, width), bf16),
            pltpu.VMEM((tokens, 2 * units), bf16),
            pltpu.VMEM((others, own, width), bf16),
            pltpu.VMEM((others, own, width), bf16),
            pltpu.VMEM((own, width), f32),
            pltpu.VMEM((2, width, tile_of(units)), bf16),
            pltpu.SemaphoreType.DMA((6,)),
            pltpu.SemaphoreType.DMA((3 * others * pieces,)),
            pltpu.SemaphoreType.DMA((3 * others * pieces,)),
            pltpu.SemaphoreType.DMA((2,)),
            pltpu.SemaphoreType.DMA((1,)),
        ]
        + scratch
        + [
            pltpu.SemaphoreType.DMA((count, copies)),
            pltpu.SemaphoreType.DMA((count, copies)),
            pltpu.SemaphoreType.DMA((count, a * b)),
        ],
        compiler_params=pltpu.CompilerParams(
            collective_id=3, has_side_effects=True, vmem_limit_bytes=62 * 2**20
        ),
        name="mlp_back",
    )(*near, *streams, *grads)


def last_mlp_kernel(row_size, head_size, pieces, *refs):
    attended, residual, owner, table, incoming, mlp_grads = refs[:6]
    streams, refs = refs[6:9], refs[9:]
    block_out, branch, normed, mlp_out, grad_in, grad_mid, branch_out, grad_att = refs[:8]
    grads_out = refs[8]
    weights, refs = refs[9:12], refs[12:]
    proj, gu, down = weights
    inputs, gate_up, hidden, ggu, branch_all, parcel, landed = refs[:7]
    middle, inverse, own_part, own_mlp, buffer = refs[7:12]
    loads, sends, recvs, tile_sems, out_sem = refs[12:]
    place = Place(row_size, head_size)
    own, width = residual.shape
    units = hidden.shape[1]
    work = Mlp(place, pieces, own, width, units, sends, recvs)
    step_units = tile_of(units)
    copies = [
        pltpu.make_async_copy(source, target, loads.at[i])
        for i, (source, target) in enumerate(zip(streams, weights))
    ]
    for copy in copies:
        copy.start()
    place.greet(True)
    copies[0].wait()
    first, second = work.front(
        attended,
        proj,
        residual,
        table,
        owner,
        parcel.at[0],
        landed.at[0],
        own_part,
        branch,
        middle,
        normed,
        inverse,
        inputs,
    )
    copies[1].wait()
    copies[2].wait()
    work.gate_up(inputs, gu, gate_up, hidden, 0, 0, own)
    work.hidden_back(mlp_grads, down, gate_up, ggu, 0, 0, own)
    fourth = work.sum_stage(parcel.at[1], landed.at[1], 3)
    for by, p in work.others:
        second.arrived(by, p)
        begin = p * work.rows
        work.gate_up(inputs, gu, gate_up, hidden, by, begin, work.rows)
        work.hidden_back(mlp_grads, down, gate_up, ggu, by, begin, work.rows)
        work.partial(parcel.at[1, by - 1, work.at(p)], ggu, work.flat(by, p), gu)
        fourth.start(by, p)
    work.partial(own_part, ggu, pl.ds(0, own), gu)
    out = Streamed(buffer, grads_out, tile_sems, step_units)

    def body(step, at):
        out.put(
            step,
            dot_tn(inputs[...].reshape(head_size * own, width), ggu[:, pl.ds(at, step_units)]),
        )

    tiles(2 * units, step_units, body)
    fifth = work.spread_stage(branch_all, 4)
    for p in range(pieces):
        at = work.at(p)
        work.arrive_all(fourth, p)
        value = work.total(own_part, landed.at[1], p)
        grad_in[at] = value
        unit = normed[at]
        value = value * (1.0 + work.modulation(table, owner, 4, p))
        value = incoming[at].astype(jnp.float32) + inverse[at] * (
            value
            - jnp.mean(value, axis=-1, keepdims=True)
            - unit * jnp.mean(value * unit, axis=-1, keepdims=True)
        )
        grad_mid[at] = value
        branch_all[0, at] = (work.modulation(table, owner, 2, p) * value).astype(jnp.bfloat16)
        work.send_all(fifth, p)
    first.left()
    third = work.sum_stage(parcel.at[0], landed.at[0], 2)
    for by, p in work.others:
        work.partial(parcel.at[0, by - 1, work.at(p)], hidden, work.flat(by, p), down)
        third.start(by, p)
    work.partial(own_mlp, hidden, pl.ds(0, own), down)
    out.drain(2 * units // step_units)
    out = Streamed(buffer, grads_out, tile_sems, step_units, 2 * units)

    def body(step, at):
        out.put(
            step,
            dot_tn(mlp_grads[...].reshape(head_size * own, width), hidden[:, pl.ds(at, step_units)]),
        )

    tiles(units, step_units, body)
    grad_att[pl.ds(0, own), :] = dot_nn(branch_all[0], proj[...]).astype(jnp.bfloat16)
    for by, p in work.others:
        fifth.arrived(by, p)
        grad_att[work.flat(by, p), :] = dot_nn(branch_all[by, work.at(p)], proj[...]).astype(
            jnp.bfloat16
        )
    keep = pltpu.make_async_copy(branch_all, branch_out, out_sem.at[0])
    keep.start()
    for p in range(pieces):
        at = work.at(p)
        work.arrive_all(third, p)
        value = work.total(own_mlp, landed.at[0], p)
        mlp_out[at] = value
        block_out[at] = (middle[at] + work.modulation(table, owner, 5, p) * value).astype(
            jnp.bfloat16
        )
    out.drain(units // step_units)
    for stage in (second, third, fourth, fifth):
        stage.left()
    keep.wait()


def last_mlp_call(row_size, head_size, attended, residual, owner, table, incoming, mlp_grads, weights):
    own, width = residual.shape
    tokens = attended.shape[0]
    units = weights[2].shape[1]
    pieces = pieces_of(own)
    others = head_size - 1
    anywhere = pl.BlockSpec(memory_space=pl.ANY)
    vmem = pl.BlockSpec(memory_space=pltpu.VMEM)
    shape = jax.ShapeDtypeStruct
    f32, bf16 = jnp.float32, jnp.bfloat16
    return pl.pallas_call(
        functools.partial(last_mlp_kernel, row_size, head_size, pieces),
        out_shape=[
            shape((own, width), bf16),
            shape((own, width), f32),
            shape((own, width), f32),
            shape((own, width), f32),
            shape((own, width), f32),
            shape((own, width), f32),
            shape((head_size, own, width), bf16),
            shape(attended.shape, bf16),
            shape((width, 3 * units), bf16),
        ],
        in_specs=[vmem] * 6 + [anywhere] * 3,
        out_specs=[vmem] * 6 + [anywhere, vmem, anywhere],
        scratch_shapes=[pltpu.VMEM(item.shape, item.dtype) for item in weights]
        + [
            pltpu.VMEM((head_size, own, width), bf16),
            pltpu.VMEM((tokens, 2 * units), f32),
            pltpu.VMEM((tokens, units), bf16),
            pltpu.VMEM((tokens, 2 * units), bf16),
            pltpu.VMEM((head_size, own, width), bf16),
            pltpu.VMEM((2, others, own, width), bf16),
            pltpu.VMEM((2, others, own, width), bf16),
            pltpu.VMEM((own, width), f32),
            pltpu.VMEM((own, 1), f32),
            pltpu.VMEM((own, width), f32),
            pltpu.VMEM((own, width), f32),
            pltpu.VMEM((2, width, tile_of(units)), bf16),
            pltpu.SemaphoreType.DMA((3,)),
            pltpu.SemaphoreType.DMA((5 * others * pieces,)),
            pltpu.SemaphoreType.DMA((5 * others * pieces,)),
            pltpu.SemaphoreType.DMA((2,)),
            pltpu.SemaphoreType.DMA((1,)),
        ],
        compiler_params=pltpu.CompilerParams(
            collective_id=5, has_side_effects=True, vmem_limit_bytes=60 * 2**20
        ),
        name="last_mlp",
    )(attended, residual, owner, table, incoming, mlp_grads, *weights)


def rope_parts(coords):
    angle = angles(coords, HD // 4)
    return jnp.cos(angle), jnp.sin(angle)


def turn(vectors, geometry, sign):
    row_cos, row_sin, col_cos, col_sin = [item[:, :, None, :] for item in geometry]
    quarter = HD // 4
    a, b, c, d = [vectors[..., quarter * i : quarter * (i + 1)] for i in range(4)]
    return jnp.concatenate(
        [
            a * row_cos - b * (sign * row_sin),
            b * row_cos + a * (sign * row_sin),
            c * col_cos - d * (sign * col_sin),
            d * col_cos + c * (sign * col_sin),
        ],
        axis=-1,
    )


def masked_scores(queries, key_rows, image_ids):
    scores = jnp.einsum(
        "rqhe,rkhe->rhqk", queries, key_rows, preferred_element_type=jnp.float32
    ) * HD ** (-0.5)
    same_image = image_ids[:, :, None] == image_ids[:, None, :]
    return jnp.where(same_image[:, None], scores, -1e30)


def attend(queries, key_rows, value_rows, image_ids):
    scores = masked_scores(queries, key_rows, image_ids)
    maximum = jnp.max(scores, axis=-1, keepdims=True)
    scaled_exp = jnp.exp(scores - maximum)
    denominator = jnp.sum(scaled_exp, axis=-1, keepdims=True)
    weights = (scaled_exp / denominator).astype(jnp.bfloat16)
    attended = jnp.einsum("rhqk,rkhe->rqhe", weights, value_rows, preferred_element_type=jnp.float32)
    return (attended.astype(jnp.bfloat16), (maximum + jnp.log(denominator))[..., 0])


def attend_back(queries, key_rows, value_rows, image_ids, logsum, grad_attended):
    score_scale = HD ** (-0.5)
    probs = jnp.exp(masked_scores(queries, key_rows, image_ids) - logsum[..., None])
    weights = probs.astype(jnp.bfloat16)
    grad_value = jnp.einsum(
        "rhqk,rqhe->rkhe", weights, grad_attended, preferred_element_type=jnp.float32
    )
    grad_probs = jnp.einsum(
        "rqhe,rkhe->rhqk", grad_attended, value_rows, preferred_element_type=jnp.float32
    )
    inner_sum = jnp.sum(probs * grad_probs, axis=-1, keepdims=True)
    grad_scores = (probs * (grad_probs - inner_sum)).astype(jnp.bfloat16)
    grad_query = (
        jnp.einsum("rhqk,rkhe->rqhe", grad_scores, key_rows, preferred_element_type=jnp.float32)
        * score_scale
    )
    grad_key = (
        jnp.einsum("rhqk,rqhe->rkhe", grad_scores, queries, preferred_element_type=jnp.float32)
        * score_scale
    )
    return (grad_query, grad_key, grad_value)


def spread(values):
    arrived = [head_move(values, flip) for flip in range(1, lax.axis_size("heads"))]
    return jnp.concatenate([values] + arrived, axis=0)


def collect(operand, product, own_rows, beside):
    arrived = []
    for flip in range(1, lax.axis_size("heads")):
        partial = product(operand[flip * own_rows : (flip + 1) * own_rows])
        arrived.append(head_move(partial.astype(jnp.bfloat16), flip))
    total = product(operand[:own_rows])
    total, arrived, beside = lax.optimization_barrier((total, arrived, beside))
    for item in arrived:
        total = total + item.astype(jnp.float32)
    return total, beside


def plain_dot(operand, other):
    return jnp.dot(operand, other, preferred_element_type=jnp.float32)


def piece_of(mods, picks, index):
    width = mods.shape[1] // 6
    value = mods[:, index * width : (index + 1) * width]
    total = jnp.zeros((picks.shape[0], width), jnp.float32)
    for image in range(mods.shape[0]):
        total = jnp.where(picks[:, None] == image, value[image][None, :], total)
    return total


def attention(input_attn, qkv_full, qkv_b, image_ids, geometry):
    count_rows, row_len = image_ids.shape
    packed = plain_dot(input_attn, qkv_full) + qkv_b
    heads_here = packed.shape[1] // (3 * HD)
    packed = packed.reshape(count_rows, row_len, heads_here, 3, HD)
    queries = turn(packed[:, :, :, 0], geometry, 1.0).astype(jnp.bfloat16)
    key_rows = turn(packed[:, :, :, 1], geometry, 1.0).astype(jnp.bfloat16)
    value_rows = packed[:, :, :, 2].astype(jnp.bfloat16)
    attended, logsum = attend(queries, key_rows, value_rows, image_ids)
    attended = attended.reshape(count_rows * row_len, heads_here * HD)
    return attended, (queries, key_rows, value_rows, logsum)


def attention_back(grad_attended, stored, image_ids, geometry):
    queries, key_rows, value_rows, logsum = stored
    count_rows, row_len = image_ids.shape
    heads_here = queries.shape[2]
    grad_attended = grad_attended.reshape(count_rows, row_len, heads_here, HD)
    grad_query, grad_key, grad_value = attend_back(
        queries, key_rows, value_rows, image_ids, logsum, grad_attended
    )
    grad_query = turn(grad_query, geometry, -1.0)
    grad_key = turn(grad_key, geometry, -1.0)
    grad_packed = (
        jnp.stack([grad_query, grad_key, grad_value], axis=3)
        .reshape(count_rows * row_len, heads_here * 3 * HD)
        .astype(jnp.bfloat16)
    )
    return grad_packed, jnp.sum(grad_packed, axis=0, dtype=jnp.float32)


def image_sum(picker, values):
    return lax.dot_general(picker, values, (((0,), (0,)), ((), ())), precision=lax.Precision.HIGH)


def shards(
    tokens,
    cond,
    image_of,
    grid_row,
    grid_col,
    ada_weight,
    ada_bias,
    qkv_weight,
    qkv_bias,
    proj_weight,
    gu_weight,
    down_weight,
    cotangent,
):
    own_rows = tokens.shape[0]
    image_count = cond.shape[0]
    block_count = qkv_weight.shape[0]
    row_size = lax.axis_size("rows")
    head_size = lax.axis_size("heads")
    head_index = lax.axis_index("heads")

    def device_order(values):
        parts = values.reshape(head_size, own_rows)
        picked = [
            lax.dynamic_index_in_dim(parts, head_index ^ flip, 0, keepdims=False)
            for flip in range(head_size)
        ]
        return jnp.concatenate(picked).reshape(values.shape)

    image_ids = device_order(image_of - lax.axis_index("rows") * image_count)
    own_images = image_ids.reshape(-1)[:own_rows]
    picker = (own_images[:, None] == jnp.arange(image_count, dtype=jnp.int32)[None, :]).astype(
        jnp.float32
    )
    geometry = lax.optimization_barrier(
        rope_parts(device_order(grid_row)) + rope_parts(device_order(grid_col))
    )
    shard_rows = qkv_weight.shape[1]

    def gathered(shard):
        return lax.all_gather(shard, "rows", axis=0, tiled=True)

    cond_wide = cond.astype(jnp.float32)
    cond_act = jax.nn.silu(cond_wide).astype(jnp.bfloat16)
    pad = -image_count % 16
    bias_rows = jnp.repeat(ada_bias.astype(jnp.float32), image_count, axis=0)
    proj_flat, down_flat = proj_weight.transpose(0, 2, 1), down_weight.transpose(0, 2, 1)
    *early, table, cond_mine, input_attn, normed, inverse, mlp_grads = start_call(
        row_size,
        head_size,
        jnp.pad(cond_act, ((0, pad), (0, 0))),
        ada_weight,
        bias_rows,
        tokens,
        cotangent,
        image_ids.reshape(-1, 1),
        [qkv_weight, proj_flat, down_flat],
    )
    qkv_full, proj_t, down_t = [[item.reshape(-1, item.shape[-1])] for item in early]
    gu_full = [gathered(item.reshape(shard_rows, -1)) for item in gu_weight]
    for b in range(1, block_count):
        down_t.append(gathered(down_flat[b]))
    modulation = [table[b * image_count : (b + 1) * image_count] for b in range(block_count)]
    last = block_count - 1
    owner = own_images[:, None]
    input_attn = input_attn.reshape(-1, input_attn.shape[-1])
    normed_attn, inverse_attn = [normed], [inverse]
    inputs_attn = [input_attn]
    residual = tokens.astype(jnp.float32)
    attentions, attended = [], []
    for b in range(block_count):
        item, kept = attention(
            inputs_attn[b], qkv_full[b], qkv_bias[b].astype(jnp.float32), image_ids, geometry
        )
        attended.append(item)
        attentions.append(kept)
        weights = (proj_t[b], gu_full[b], down_t[b])
        if b < last:
            (
                branch,
                normed_mlp,
                input_mlp,
                gate_up,
                hidden,
                inverse_mlp,
                mlp_out,
                residual,
                next_normed,
                next_inverse,
                next_input,
                next_qkv,
                next_proj,
            ) = mlp_call(
                row_size,
                head_size,
                item,
                residual,
                owner,
                modulation[b],
                modulation[b + 1],
                weights,
                b + 1,
                [qkv_weight, proj_flat],
            )
            normed_attn.append(next_normed)
            inverse_attn.append(next_inverse)
            inputs_attn.append(next_input.reshape(inputs_attn[0].shape))
            qkv_full.append(next_qkv.reshape(qkv_full[0].shape))
            proj_t.append(next_proj.reshape(proj_t[0].shape))
            stored = (branch, normed_mlp, input_mlp, gate_up, hidden, inverse_mlp, mlp_out)
    (
        block_out,
        last_branch,
        last_normed,
        last_out,
        grad_input_mlp,
        grad_middle,
        gathered_branch,
        grad_attended,
        mlp_grad,
    ) = last_mlp_call(
        row_size,
        head_size,
        attended[last],
        residual,
        owner,
        modulation[last],
        cotangent,
        mlp_grads,
        weights,
    )

    def scattered(grad):
        return lax.psum_scatter(grad, "rows", scatter_dimension=0, tiled=True).astype(jnp.float32)

    def late_sums(middle, branch, incoming, normed, grad, out):
        return [
            image_sum(picker, item)
            for item in (middle * branch, grad, grad * normed, incoming * out)
        ]

    gu_outs, bias_sums, image_sums = [None] * 2, [None] * 2, [None] * 2
    mlp_sum = scattered(mlp_grad)
    units = mlp_sum.shape[1] // 3
    gathered_branch = gathered_branch.reshape(-1, gathered_branch.shape[-1])
    grad_packed, bias_sums[1] = attention_back(grad_attended, attentions[1], image_ids, geometry)
    qkv_grad, proj_grad = weight_grads(
        (inputs_attn[1], grad_packed), (gathered_branch, attended[1])
    )
    late = late_sums(
        grad_middle,
        last_branch,
        cotangent.astype(jnp.float32),
        last_normed,
        grad_input_mlp,
        last_out,
    )
    grad_input_attn, (qkv_grad, proj_grad, late) = collect(
        grad_packed, lambda rows: tail_dot(rows, qkv_full[1]), own_rows, (qkv_grad, proj_grad, late)
    )
    scale = piece_of(modulation[1], own_images, 1)
    incoming = grad_middle + norm_back(
        grad_input_attn * (1.0 + scale), normed_attn[1], inverse_attn[1]
    )
    image_sums[1] = jnp.concatenate(
        [
            image_sum(picker, grad_input_attn),
            image_sum(picker, grad_input_attn * normed_attn[1]),
        ]
        + late,
        axis=1,
    )
    branch, normed_mlp, input_mlp, gate_up, hidden, inverse_mlp, mlp_out = stored
    block_sums = [None] * 2
    (
        grad_input_mlp,
        grad_middle,
        gathered_branch,
        grad_attended,
        gu_grad,
        down_grad,
        *block_sums[1],
    ) = mlp_back_call(
        row_size,
        head_size,
        (
            incoming,
            owner,
            modulation[0],
            normed_mlp,
            inverse_mlp,
        ),
        (
            down_t[0],
            gate_up,
            gu_full[0],
            input_mlp.reshape(-1, input_mlp.shape[-1]),
            hidden,
            proj_t[0],
        ),
        [item.reshape(row_size, shard_rows, -1) for item in (qkv_grad, proj_grad)],
    )
    gathered_branch = gathered_branch.reshape(-1, gathered_branch.shape[-1])
    grad_packed, bias_sums[0] = attention_back(grad_attended, attentions[0], image_ids, geometry)
    grad_packed, mlp_sum, gu_grad = lax.optimization_barrier((grad_packed, mlp_sum, gu_grad))
    gu_outs[0] = scattered(gu_grad)
    late = late_sums(grad_middle, branch, incoming, normed_mlp, grad_input_mlp, mlp_out)
    image_sums[0] = jnp.concatenate([jnp.zeros_like(late[0])] * 2 + late, axis=1)
    gu_outs[1] = mlp_sum[:, : 2 * units]
    sheets = jnp.stack(image_sums).reshape(block_count * image_count, head_size, -1)
    sheets = sheets.transpose(1, 0, 2)
    wide = sheets.shape[-1]
    bias_sums = jnp.stack(bias_sums)
    bias_high = bias_sums.astype(jnp.bfloat16).astype(jnp.float32)
    bias_rest = bias_sums - bias_high
    bias_middle = bias_rest.astype(jnp.bfloat16).astype(jnp.float32)
    bias_parts = jnp.stack([bias_high, bias_middle, bias_rest - bias_middle], axis=1)
    bias_parts = jnp.pad(bias_parts, ((0, 0), (0, 0), (0, wide - bias_sums.shape[1])))
    bias_parts = bias_parts.reshape(-1, wide)
    used = sheets.shape[1] + bias_parts.shape[0]
    small_rows = used + -used % 16
    bias_parts = jnp.pad(bias_parts, ((sheets.shape[1], small_rows - used), (0, 0)))
    cond_rows = cond_mine.reshape(row_size, -1, shard_rows)[:, :image_count]
    row = jnp.arange(small_rows)
    mine = []
    for b in range(block_count):
        first = b * image_count
        lead = jnp.pad(cond_rows, ((0, 0), (first, small_rows - first - image_count), (0, 0)))
        is_image = (row >= first) & (row < first + image_count)
        start = block_count * image_count + 3 * b
        is_bias = (row >= start) & (row < start + 3)
        ones = jnp.stack([is_image, is_bias], axis=1).astype(jnp.bfloat16)
        ones = jnp.broadcast_to(ones[None], (row_size,) + ones.shape)
        both = jnp.concatenate([lead, ones], axis=2)
        both = jnp.pad(both, ((0, 0), (0, 0), (0, -both.shape[2] % 128)))
        mine.append(both.reshape(-1, both.shape[2]))
    logistic = jax.nn.sigmoid(cond_wide)
    factor = logistic * (1.0 + cond_wide * (1.0 - logistic))
    factor = jnp.pad(factor, ((0, -image_count % 8), (0, 0)))
    tokens_grad, ada_grads, ada_bias_grads, qkv_bias_out, cond_grad, *stacked = finish_call(
        row_size,
        head_size,
        image_count,
        (
            grad_packed,
            qkv_full[0],
            inputs_attn[0],
            attended[0],
            gathered_branch,
            grad_middle,
            piece_of(modulation[0], own_images, 1),
            normed_attn[0],
            inverse_attn[0],
            owner,
        ),
        sheets,
        bias_parts,
        jnp.stack(mine),
        ada_weight,
        factor,
        [mlp_sum[:, 2 * units :]] + block_sums[1],
        down_grad.reshape(row_size, shard_rows, -1),
    )
    cond_grad = cond_grad[:image_count]
    return (
        block_out,
        tokens_grad,
        cond_grad,
        ada_grads,
        ada_bias_grads,
        stacked[1],
        qkv_bias_out,
        stacked[2].transpose(0, 2, 1),
        jnp.stack([item.reshape(gu_weight.shape[1:]) for item in gu_outs]),
        stacked[0].transpose(0, 2, 1),
    )


def solution(mesh):
    in_specs = (
        P(("rows", "heads"), None),
        P("rows", None),
        P("rows", None),
        P("rows", None),
        P("rows", None),
        P(None, "rows", "heads"),
        P(None, "heads"),
        P(None, "rows", "heads"),
        P(None, "heads"),
        P(None, "heads", "rows"),
        P(None, "rows", None, "heads"),
        P(None, "heads", "rows"),
        P(("rows", "heads"), None),
    )
    out_specs = (
        P(("rows", "heads"), None),
        P(("rows", "heads"), None),
        P("rows", None),
        P(None, "rows", "heads"),
        P(None, "heads"),
        P(None, "rows", "heads"),
        P(None, "heads"),
        P(None, "heads", "rows"),
        P(None, "rows", None, "heads"),
        P(None, "heads", "rows"),
    )
    return jax.shard_map(shards, mesh=mesh, in_specs=in_specs, out_specs=out_specs, check_vma=False)
```

```python
import functools

import jax
import jax.numpy as jnp
from jax import lax
from jax.experimental import pallas as pl
from jax.experimental.pallas import tpu as pltpu
from jax.sharding import PartitionSpec as P

HD = 72


epsilon = 1e-06
theta_base = 10000.0
highest = lax.Precision.HIGHEST


def normalize(values):
    center = values - jnp.mean(values, axis=-1, keepdims=True)
    inverse = lax.rsqrt(jnp.mean(center * center, axis=-1, keepdims=True) + epsilon)
    return (center * inverse, inverse)


def norm_back(incoming, normed, inverse):
    return inverse * (
        incoming
        - jnp.mean(incoming, axis=-1, keepdims=True)
        - normed * jnp.mean(incoming * normed, axis=-1, keepdims=True)
    )


def lead_dot(operand, other):
    return lax.dot_general(
        operand, other, (((0,), (0,)), ((), ())), preferred_element_type=jnp.float32
    )


def tail_dot(operand, other):
    return lax.dot_general(
        operand, other, (((1,), (1,)), ((), ())), preferred_element_type=jnp.float32
    )


def angles(coords, quarter):
    frequency = theta_base ** (-jnp.arange(quarter, dtype=jnp.float32) / quarter)
    return coords.astype(jnp.float32)[..., None] * frequency


def head_move(value, flip):
    size = lax.axis_size("heads")
    return lax.ppermute(value, "heads", [(index, index ^ flip) for index in range(size)])


MESH = pl.DeviceIdType.MESH


class Place:
    def __init__(self, row_size, head_size):
        self.sizes = (4, row_size // 8, 2)
        index = lax.axis_index("rows")
        a, b, c = self.sizes
        self.mine = (index // (b * c), (index // c) % b, index % c)
        self.heads = head_size
        self.head = lax.axis_index("heads")

    def step(self, dim, by):
        return (self.mine[dim] + by + self.sizes[dim]) % self.sizes[dim]

    def row(self, a, b, c):
        return (a * self.sizes[1] + b) * self.sizes[2] + c

    def near(self, dim, by):
        at = list(self.mine)
        at[dim] = self.step(dim, by)
        return {"rows": self.row(*at)}

    def flip(self, by):
        return {"heads": self.head ^ by}

    def partners(self, with_heads):
        found = [self.near(dim, by) for dim in range(3) for by in range(1, self.sizes[dim])]
        if with_heads:
            found += [self.flip(by) for by in range(1, self.heads)]
        return found

    def greet(self, with_heads):
        barrier = pltpu.get_barrier_semaphore()
        found = self.partners(with_heads)
        for partner in found:
            pl.semaphore_signal(barrier, inc=1, device_id=partner, device_id_type=MESH)
        pl.semaphore_wait(barrier, len(found))


def gather_count(row_size):
    a, b, c = 4, row_size // 8, 2
    return 2 * (a - 1) + (2 * a - 1) * (2 * b - 1)


class Gather:
    def __init__(self, place, shard, out, send, recv, local):
        self.place, self.shard, self.out = place, shard, out
        self.send, self.recv = send, recv
        self.used = 0
        self.keep = pltpu.make_async_copy(shard, out.at[place.row(*place.mine)], local)
        a, b, _ = place.sizes
        self.hops, self.along_b, self.along_c = {}, {}, {}
        names = [(0, 0)] + [(way, k) for k in range(1, a) for way in (1, -1)]
        for way, k in names:
            if k:
                self.hops[way, k] = self.copy(way, k - 1, 0, place.near(0, way))
        for way, k in names:
            for j in range(1, b):
                self.along_b[way, k, j] = self.copy(way, k, 0, place.near(1, j))
        for way, k in names:
            for j in range(b):
                self.along_c[way, k, j] = self.copy(way, k, j, place.near(2, 1))

    def copy(self, way, k, j, device):
        place, slot = self.place, self.used
        self.used += 1
        index = place.row(place.step(0, -way * k), place.step(1, -j), place.mine[2])
        return pltpu.make_async_remote_copy(
            src_ref=self.shard if k == 0 and j == 0 else self.out.at[index],
            dst_ref=self.out.at[index],
            send_sem=self.send.at[slot],
            recv_sem=self.recv.at[slot],
            device_id=device,
            device_id_type=MESH,
        )

    def holds(self, way, k):
        at = self.place.mine[0]
        return at >= k if way > 0 else at < self.place.sizes[0] - k

    def hop(self, way, k):
        at = self.place.mine[0]
        last = self.place.sizes[0] - 1
        return (at < last) & (at >= k - 1) if way > 0 else (at > 0) & (at <= last - (k - 1))

    def begin(self):
        self.keep.start()
        for way in (1, -1):
            pl.when(self.hop(way, 1))(self.hops[way, 1].start)
        self.pass_on(0, 0)

    def pass_on(self, way, k):
        for j in range(1, self.place.sizes[1]):
            self.along_b[way, k, j].start()
        self.along_c[way, k, 0].start()

    def first(self, k):
        for way in (1, -1):

            @pl.when(self.holds(way, k))
            def _():
                self.hops[way, k].wait_recv()
                if k + 1 < self.place.sizes[0]:
                    pl.when(self.hop(way, k + 1))(self.hops[way, k + 1].start)
                self.pass_on(way, k)

    def each(self, way, k, action):
        if k:
            pl.when(self.holds(way, k))(action)
        else:
            action()

    def second(self):
        for way, k, j in self.along_b:

            def action():
                self.along_b[way, k, j].wait_recv()
                self.along_c[way, k, j].start()

            self.each(way, k, action)

    def finish(self):
        for way, k, j in self.along_c:

            def action():
                self.along_c[way, k, j].wait_recv()
                self.along_c[way, k, j].wait_send()

            self.each(way, k, action)
        for way, k, j in self.along_b:
            self.each(way, k, self.along_b[way, k, j].wait_send)
        for way, k in self.hops:
            pl.when(self.hop(way, k))(self.hops[way, k].wait_send)
        self.keep.wait()


def gather_all(items):
    count = len(items)
    items[0].begin()
    for step in range(count + 1):
        if step < count:
            items[step].first(1)
            if step + 1 < count:
                items[step + 1].begin()
            for k in range(2, items[step].place.sizes[0]):
                items[step].first(k)
        if step >= 1:
            items[step - 1].second()
    for item in items:
        item.finish()


def scatter_count(row_size):
    a, b, c = 4, row_size // 8, 2
    return a * b + a * (b - 1) + (a - 1)


class Scatter:
    def __init__(self, place, source, out, held, met, side, far, send, recv, load):
        self.place, self.source, self.out = place, source, out
        self.held, self.met, self.side, self.far = held, met, side, far
        self.send, self.recv, self.load = send, recv, load

    def remote(self, source, target, slot, device):
        return pltpu.make_async_remote_copy(
            src_ref=source,
            dst_ref=target,
            send_sem=self.send.at[slot],
            recv_sem=self.recv.at[slot],
            device_id=device,
            device_id_type=MESH,
        )

    def across(self, k, j):
        place = self.place
        a, b = place.step(0, k), place.step(1, j)
        other = place.step(2, 1)
        return self.remote(
            self.source.at[place.row(a, b, other)],
            self.met.at[a, b],
            k * place.sizes[1] + j,
            place.near(2, 1),
        )

    def fetch(self, k, j):
        place = self.place
        a, b = place.step(0, k), place.step(1, j)
        return pltpu.make_async_copy(
            self.source.at[place.row(a, b, place.mine[2])],
            self.held.at[a, b],
            self.load.at[k * place.sizes[1] + j],
        )

    def along_b(self, k, j):
        place = self.place
        a, b = place.step(0, k), place.step(1, j)
        base = place.sizes[0] * place.sizes[1]
        return self.remote(
            self.held.at[a, b],
            self.side.at[j - 1, a],
            base + (j - 1) * place.sizes[0] + k,
            place.near(1, j),
        )

    def along_a(self, k):
        place = self.place
        base = place.sizes[0] * (2 * place.sizes[1] - 1)
        return self.remote(
            self.held.at[place.step(0, k), place.mine[1]],
            self.far.at[k - 1],
            base + k - 1,
            place.near(0, k),
        )

    def order(self):
        a, b, _ = self.place.sizes
        return [(k, j) for j in list(range(1, b)) + [0] for k in list(range(1, a)) + [0]]

    def begin(self):
        for k, j in self.order():
            self.fetch(k, j).start()
            self.across(k, j).start()

    def first(self):
        place = self.place
        a, b, _ = place.sizes
        for j in range(1, b):
            for k in list(range(1, a)) + [0]:
                self.fetch(k, j).wait()
                self.across(k, j).wait_recv()
                at = (place.step(0, k), place.step(1, j))
                self.held[at] = (
                    self.held[at].astype(jnp.float32) + self.met[at].astype(jnp.float32)
                ).astype(self.held.dtype)
                self.along_b(k, j).start()

    def total(self, k):
        place = self.place
        a, b = place.step(0, k), place.mine[1]
        value = self.held[a, b].astype(jnp.float32) + self.met[a, b].astype(jnp.float32)
        for j in range(1, place.sizes[1]):
            value = value + self.side[j - 1, a].astype(jnp.float32)
        return value

    def second(self):
        place = self.place
        a, b, _ = place.sizes
        for k in list(range(1, a)) + [0]:
            self.fetch(k, 0).wait()
            self.across(k, 0).wait_recv()
            for j in range(1, b):
                self.along_b(k, j).wait_recv()
            if k:
                self.held[place.step(0, k), place.mine[1]] = self.total(k).astype(self.held.dtype)
                self.along_a(k).start()
            else:
                self.out[...] = self.total(0)

    def finish(self):
        place = self.place
        a, b, _ = place.sizes
        for k in range(1, a):
            self.along_a(k).wait_recv()
            self.out[...] = self.out[...] + self.far[k - 1].astype(jnp.float32)
        for k, j in self.order():
            self.across(k, j).wait_send()
            if j:
                self.along_b(k, j).wait_send()
        for k in range(1, a):
            self.along_a(k).wait_send()


def scatter_all(items):
    count = len(items)
    for item in items:
        item.begin()
    for step in range(count + 2):
        if step < count:
            items[step].first()
        if 1 <= step <= count:
            items[step - 1].second()
        if step >= 2:
            items[step - 2].finish()


def start_kernel(row_size, head_size, images, blocks, weights, *refs):
    cond, ada, bias, tokens, cotangent, owner = refs[:6]
    shards = [ref.at[0] for ref in refs[6 : 6 + weights]]
    outs = refs[6 + weights : 6 + 2 * weights]
    refs = refs[6 + 2 * weights :]
    table, mine_out, inputs_out, normed_out, inverse_out, grads_out = refs[:6]
    every_token, every_cotangent, token_send, token_recv = refs[6:10]
    refs = refs[10:]
    (conds, part, held, met, side, far, total, every, sends, recvs, keeps) = refs[:11]
    (mod_send, mod_recv, mod_load, head_send, head_recv) = refs[11:]
    place = Place(row_size, head_size)
    place.greet(True)
    items = [
        Gather(place, shard, out, sends.at[i], recvs.at[i], keeps.at[i])
        for i, (shard, out) in enumerate(zip((cond,) + tuple(shards), (conds,) + outs))
    ]
    lead, bulk = items[0], items[1:]
    lead.begin()
    own = tokens.shape[0]
    every_token[0] = tokens[...]
    every_cotangent[0] = cotangent[...]
    raws = [
        Across(place, lambda by: ref.at[0], lambda by: ref.at[by], token_send, token_recv, stage)
        for stage, ref in enumerate((every_token, every_cotangent))
    ]
    for raw in raws:
        for by in range(1, head_size):
            raw.start(by)
    hops = range(1, place.sizes[0])
    for k in hops:
        lead.first(k)
    lead.second()
    lead.finish()
    width = cond.shape[1]
    share = ada.shape[1]
    pad = cond.shape[0]
    lane = lax.broadcasted_iota(jnp.int32, (width, share), 0)
    slot = lax.broadcasted_iota(jnp.int32, (width, share), 1)
    pick = jnp.where(lane == lax.axis_index("rows") * share + slot, 1.0, 0.0).astype(jnp.bfloat16)
    mine = jnp.dot(
        conds[...].reshape(row_size * pad, width), pick, preferred_element_type=jnp.float32
    ).astype(jnp.bfloat16)
    mine_out[...] = mine
    for b in range(blocks):
        value = jnp.dot(mine, ada[b], preferred_element_type=jnp.float32)
        part[:, b * images : (b + 1) * images, :] = value.reshape(row_size, pad, -1)[:, :images]
    sums = Scatter(place, part, total, held, met, side, far, mod_send, mod_recv, mod_load)
    sums.begin()
    sums.first()
    bulk[0].begin()
    sums.second()
    bulk[0].first(1)
    for item in bulk[1:]:
        item.begin()
    for k in hops[1:]:
        bulk[0].first(k)
    for item in bulk[1:]:
        for k in hops:
            item.first(k)
    sums.finish()
    every[place.head] = total[...] + bias[...]
    across = [
        pltpu.make_async_remote_copy(
            src_ref=every.at[place.head],
            dst_ref=every.at[place.head],
            send_sem=head_send.at[by - 1],
            recv_sem=head_recv.at[by - 1],
            device_id=place.flip(by),
            device_id_type=MESH,
        )
        for by in range(1, head_size)
    ]
    for copy in across:
        copy.start()
    for item in bulk:
        item.second()
    for copy in across:
        copy.wait()
    wide = every.shape[2]
    for head in range(head_size):
        table[:, head * wide : (head + 1) * wide] = every[head]
    for raw in raws:
        for by in range(1, head_size):
            raw.arrived(by)
    columns = tokens.shape[1]
    half = own // pieces_of(own)

    def modulation(here, first, index):
        value = jnp.zeros((half, columns), jnp.float32)
        for image in range(images):
            row = table[first + image : first + image + 1, index * columns : (index + 1) * columns]
            value = jnp.where(here == image, row, value)
        return value

    last = (blocks - 1) * images

    @pl.loop(0, head_size * (own // half))
    def _(step):
        slot = step // (own // half)
        rows = pl.ds(pl.multiple_of(step % (own // half) * half, 8), half)
        here = owner[pl.ds(pl.multiple_of(step * half, 8), half), :]
        unit, scale = normalize(every_token[slot, rows].astype(jnp.float32))
        inputs_out[slot, rows] = (
            unit * (1.0 + modulation(here, 0, 1)) + modulation(here, 0, 0)
        ).astype(jnp.bfloat16)
        grads_out[slot, rows] = (
            modulation(here, last, 5) * every_cotangent[slot, rows].astype(jnp.float32)
        ).astype(jnp.bfloat16)

        @pl.when(slot == 0)
        def _():
            normed_out[rows] = unit
            inverse_out[rows] = scale

    for raw in raws:
        raw.left()
    for item in bulk:
        item.finish()


def start_call(row_size, head_size, cond, ada, bias, tokens, cotangent, owner, shards):
    images = bias.shape[0] // ada.shape[0]
    blocks = ada.shape[0]
    count = len(shards)
    a, b = 4, row_size // 8
    chunk = bias.shape
    copies = gather_count(row_size)
    anywhere = pl.BlockSpec(memory_space=pl.ANY)
    vmem = pl.BlockSpec(memory_space=pltpu.VMEM)
    f32, bf16 = jnp.float32, jnp.bfloat16
    own, width = tokens.shape
    shape = jax.ShapeDtypeStruct
    return pl.pallas_call(
        functools.partial(start_kernel, row_size, head_size, images, blocks, count),
        out_shape=[jax.ShapeDtypeStruct((row_size,) + item.shape[1:], item.dtype) for item in shards]
        + [
            shape((chunk[0], head_size * chunk[1]), f32),
            shape((row_size * cond.shape[0], ada.shape[1]), cond.dtype),
            shape((head_size, own, width), bf16),
            shape((own, width), f32),
            shape((own, 1), f32),
            shape((head_size, own, width), bf16),
        ],
        in_specs=[vmem] * 6 + [anywhere] * count,
        out_specs=[anywhere] * count + [vmem] * 6,
        scratch_shapes=[
            pltpu.VMEM((head_size, own, width), bf16),
            pltpu.VMEM((head_size, own, width), bf16),
            pltpu.SemaphoreType.DMA((2 * (head_size - 1),)),
            pltpu.SemaphoreType.DMA((2 * (head_size - 1),)),
            pltpu.VMEM((row_size,) + cond.shape, cond.dtype),
            pltpu.VMEM((row_size,) + chunk, f32),
            pltpu.VMEM((a, b) + chunk, f32),
            pltpu.VMEM((a, b) + chunk, f32),
            pltpu.VMEM((b - 1, a) + chunk, f32),
            pltpu.VMEM((a - 1,) + chunk, f32),
            pltpu.VMEM(chunk, f32),
            pltpu.VMEM((head_size,) + chunk, f32),
            pltpu.SemaphoreType.DMA((count + 1, copies)),
            pltpu.SemaphoreType.DMA((count + 1, copies)),
            pltpu.SemaphoreType.DMA((count + 1,)),
            pltpu.SemaphoreType.DMA((scatter_count(row_size),)),
            pltpu.SemaphoreType.DMA((scatter_count(row_size),)),
            pltpu.SemaphoreType.DMA((a * b,)),
            pltpu.SemaphoreType.DMA((head_size - 1,)),
            pltpu.SemaphoreType.DMA((head_size - 1,)),
        ],
        compiler_params=pltpu.CompilerParams(
            collective_id=1, has_side_effects=True, vmem_limit_bytes=48 * 2**20
        ),
        name="start",
    )(cond, ada, bias, tokens, cotangent, owner, *shards)


def weight_grads_kernel(*refs):
    count = len(refs) // 3
    for i in range(count):
        left, right, out = refs[2 * i], refs[2 * i + 1], refs[2 * count + i]
        columns = out.shape[1]
        for at in range(0, columns, 256):
            size = min(256, columns - at)
            out[:, at : at + size] = dot_tn(left[...], right[:, at : at + size]).astype(out.dtype)


def weight_grads(*pairs):
    vmem = pl.BlockSpec(memory_space=pltpu.VMEM)
    flat = [item for pair in pairs for item in pair]
    flops = sum(2 * left.size * right.shape[1] for left, right in pairs)
    moved = sum(2 * (left.size + right.size + left.shape[1] * right.shape[1]) for left, right in pairs)
    return pl.pallas_call(
        weight_grads_kernel,
        out_shape=[
            jax.ShapeDtypeStruct((left.shape[1], right.shape[1]), jnp.bfloat16)
            for left, right in pairs
        ],
        in_specs=[vmem] * len(flat),
        out_specs=[vmem] * len(pairs),
        compiler_params=pltpu.CompilerParams(vmem_limit_bytes=48 * 2**20),
        cost_estimate=pl.CostEstimate(flops=flops, bytes_accessed=moved, transcendentals=0),
        name="weight_grads",
    )(*flat)


def tile_of(width):
    return next(size for size in (256, 128, width) if width % size == 0)


def dot_nn(left, right):
    return jnp.dot(left, right, preferred_element_type=jnp.float32)


def dot_nt(left, right):
    return lax.dot_general(left, right, (((1,), (1,)), ((), ())), preferred_element_type=jnp.float32)


def dot_tn(left, right):
    return lax.dot_general(left, right, (((0,), (0,)), ((), ())), preferred_element_type=jnp.float32)


def tiles(width, size, body):
    @pl.loop(0, width // size)
    def _(step):
        body(step, pl.multiple_of(step * size, size))


class Across:
    def __init__(self, place, sources, targets, send, recv, stage):
        count = place.heads - 1
        self.copies = [
            pltpu.make_async_remote_copy(
                src_ref=sources(by),
                dst_ref=targets(by),
                send_sem=send.at[stage * count + by - 1],
                recv_sem=recv.at[stage * count + by - 1],
                device_id=place.flip(by),
                device_id_type=MESH,
            )
            for by in range(1, place.heads)
        ]

    def start(self, by):
        self.copies[by - 1].start()

    def arrived(self, by):
        self.copies[by - 1].wait_recv()

    def left(self):
        for copy in self.copies:
            copy.wait_send()


class Streamed:
    def __init__(self, buffer, out, sems, size, begin=0):
        self.buffer, self.out, self.sems, self.size, self.begin = buffer, out, sems, size, begin

    def copy(self, step):
        at = pl.multiple_of(self.begin + step * self.size, 128)
        return pltpu.make_async_copy(
            self.buffer.at[step % 2], self.out.at[:, pl.ds(at, self.size)], self.sems.at[step % 2]
        )

    def put(self, step, value):
        @pl.when(step >= 2)
        def _():
            self.copy(step - 2).wait()

        self.buffer[step % 2] = value.astype(self.buffer.dtype)
        self.copy(step).start()

    def drain(self, steps):
        for step in range(max(steps - 2, 0), steps):
            self.copy(step).wait()


def finish_kernel(row_size, head_size, images, blocks, *refs):
    (packed, qkv, inputs, attended, branch, middle, scale, normed, inverse, owner) = refs[:10]
    known, bias, mine, ada, factor = refs[10:15]
    done, down = refs[15:18], refs[18]
    grad_tokens, ada_out, ada_bias_out, qkv_bias_out, cond_out = refs[19:24]
    stacks = refs[24:27]
    outs = [ref.at[0] for ref in stacks]
    refs = refs[3:]
    parcel, landed, sheet, share_in, small, qkv_grad, proj_grad = refs[24:31]
    head_send, head_recv = refs[31:33]
    refs = refs[33:]
    scratch = refs[:12]
    every, part, held, met, side, far, total, cond_in = refs[12:20]
    send, recv, load, small_send, small_recv, small_keep = refs[20:26]
    cond_send, cond_recv, cond_load = refs[26:]
    place = Place(row_size, head_size)
    own, width = middle.shape
    step_width = tile_of(width)
    place.greet(True)
    for stack, item in zip(stacks, done):
        stack[1] = item[...]
    items = [
        Scatter(
            place, source, outs[i], *scratch[4 * i : 4 * i + 4], send.at[i], recv.at[i], load.at[i]
        )
        for i, source in enumerate((down, qkv_grad, proj_grad))
    ]
    items[0].begin()
    first = Across(
        place, lambda by: parcel.at[by - 1], lambda by: landed.at[by - 1], head_send, head_recv, 0
    )
    for by in range(1, head_size):

        def body(step, at):
            parcel[by - 1, :, pl.ds(at, step_width)] = dot_nt(
                packed[pl.ds(by * own, own), :], qkv[pl.ds(at, step_width), :]
            ).astype(jnp.bfloat16)

        tiles(width, step_width, body)
        first.start(by)
    for left, right, out, item in (
        (inputs, packed, qkv_grad, items[1]),
        (branch, attended, proj_grad, items[2]),
    ):
        share = out.shape[1]
        for at in range(0, out.shape[2], 256):
            size = min(256, out.shape[2] - at)
            value = dot_tn(left[...], right[:, at : at + size])
            for row in range(row_size):
                out[row, :, at : at + size] = value[row * share : (row + 1) * share].astype(out.dtype)
        item.begin()
    items[0].first()
    value = dot_nt(packed[pl.ds(0, own), :], qkv[...])
    for by in range(1, head_size):
        first.arrived(by)
        value = value + landed[by - 1].astype(jnp.float32)
    scaled = value * (1.0 + scale[...])
    grad_tokens[...] = middle[...] + inverse[...] * (
        scaled
        - jnp.mean(scaled, axis=-1, keepdims=True)
        - normed[...] * jnp.mean(scaled * normed[...], axis=-1, keepdims=True)
    )
    sheet[...] = known[...]
    wide = sheet.shape[2]
    for image in range(images):
        here = owner[...] == image
        for piece, item in enumerate((value, value * normed[...])):
            row = jnp.sum(jnp.where(here, item, 0.0), axis=0, keepdims=True)
            begin = piece * width
            while begin < (piece + 1) * width:
                end = min((begin // wide + 1) * wide, (piece + 1) * width)
                sheet[begin // wide, image : image + 1, begin % wide : begin % wide + end - begin] = (
                    row[:, begin - piece * width : end - piece * width]
                )
                begin = end
    shares = Across(
        place,
        lambda by: sheet.at[place.head ^ by],
        lambda by: share_in.at[by - 1],
        head_send,
        head_recv,
        1,
    )
    for by in range(1, head_size):
        shares.start(by)
    mod_grads = sheet[place.head]
    for by in range(1, head_size):
        shares.arrived(by)
        mod_grads = mod_grads + share_in[by - 1]
    known_rows = mod_grads.shape[0]
    small[...] = jnp.concatenate([mod_grads, bias[known_rows:, :]], axis=0).astype(small.dtype)
    lead = Gather(place, small, every, small_send, small_recv, small_keep.at[0])
    lead.begin()
    for k in range(1, place.sizes[0]):
        lead.first(k)
    items[0].second()
    lead.second()
    lead.finish()
    rows = small.shape[0]
    share = ada.shape[1]
    grads = every[...].reshape(row_size * rows, -1)
    columns = qkv_bias_out.shape[1]
    for b in range(blocks):
        value = dot_tn(mine[b], grads)
        ada_out[b] = value[:share]
        ada_bias_out[b : b + 1, :] = value[share : share + 1]
        qkv_bias_out[b : b + 1, :] = value[share + 1 : share + 2, :columns]
    lane = lax.broadcasted_iota(jnp.int32, (share, width), 1)
    slot = lax.broadcasted_iota(jnp.int32, (share, width), 0)
    pick = jnp.where(lane == lax.axis_index("rows") * share + slot, 1.0, 0.0).astype(jnp.bfloat16)
    back = 0.0
    for b in range(blocks):
        value = dot_nt(grads, ada[b]).reshape(row_size, rows, share)
        back = back + value[:, b * images : (b + 1) * images]
    back = back.reshape(row_size * images, share).astype(jnp.bfloat16)
    part[...] = jnp.zeros_like(part)
    part[:, :images, :] = dot_nn(back, pick).reshape(row_size, images, width)
    sums = Scatter(place, part, total, held, met, side, far, cond_send, cond_recv, cond_load)
    sums.begin()
    sums.first()
    items[1].first()
    items[2].first()
    sums.second()
    items[1].second()
    sums.finish()
    last = Across(
        place, lambda by: total, lambda by: cond_in.at[by - 1], head_send, head_recv, 2
    )
    for by in range(1, head_size):
        last.start(by)
    items[2].second()
    for item in items:
        item.finish()
    value = total[...]
    for by in range(1, head_size):
        last.arrived(by)
        value = value + cond_in[by - 1]
    cond_out[...] = value * factor[...]
    for stage in (first, shares, last):
        stage.left()


def finish_call(row_size, head_size, images, near, known, bias, mine, ada, factor, done, down):
    packed, qkv, inputs, attended, branch, middle = near[:6]
    copies = scatter_count(row_size)
    small_copies = gather_count(row_size)
    blocks, share, wide = ada.shape
    own, width = middle.shape
    a, b = 4, row_size // 8
    f32, bf16 = jnp.float32, jnp.bfloat16
    shape = jax.ShapeDtypeStruct
    chunks = [(share, columns) for columns in (down.shape[2], qkv.shape[1], attended.shape[1])]
    scratch = []
    for chunk in chunks:
        for lead in ((a, b), (a, b), (b - 1, a), (a - 1,)):
            scratch.append(pltpu.VMEM(lead + chunk, bf16))
    chunk = factor.shape
    anywhere = pl.BlockSpec(memory_space=pl.ANY)
    vmem = pl.BlockSpec(memory_space=pltpu.VMEM)
    others = head_size - 1
    return pl.pallas_call(
        functools.partial(finish_kernel, row_size, head_size, images, blocks),
        out_shape=[
            shape((own, width), f32),
            shape(ada.shape, f32),
            shape((blocks, wide), f32),
            shape((blocks, qkv.shape[1]), f32),
            shape(factor.shape, f32),
        ]
        + [shape((2,) + item, f32) for item in chunks],
        in_specs=[vmem] * 18 + [anywhere],
        out_specs=[vmem] * 8,
        scratch_shapes=[
            pltpu.VMEM((others, own, width), bf16),
            pltpu.VMEM((others, own, width), bf16),
            pltpu.VMEM(known.shape, f32),
            pltpu.VMEM((others,) + known.shape[1:], f32),
            pltpu.VMEM(bias.shape, bf16),
            pltpu.VMEM((row_size,) + chunks[1], bf16),
            pltpu.VMEM((row_size,) + chunks[2], bf16),
            pltpu.SemaphoreType.DMA((3 * others,)),
            pltpu.SemaphoreType.DMA((3 * others,)),
        ]
        + scratch
        + [
            pltpu.VMEM((row_size,) + bias.shape, bf16),
            pltpu.VMEM((row_size,) + chunk, f32),
            pltpu.VMEM((a, b) + chunk, f32),
            pltpu.VMEM((a, b) + chunk, f32),
            pltpu.VMEM((b - 1, a) + chunk, f32),
            pltpu.VMEM((a - 1,) + chunk, f32),
            pltpu.VMEM(chunk, f32),
            pltpu.VMEM((others,) + chunk, f32),
            pltpu.SemaphoreType.DMA((3, copies)),
            pltpu.SemaphoreType.DMA((3, copies)),
            pltpu.SemaphoreType.DMA((3, a * b)),
            pltpu.SemaphoreType.DMA((small_copies,)),
            pltpu.SemaphoreType.DMA((small_copies,)),
            pltpu.SemaphoreType.DMA((1,)),
            pltpu.SemaphoreType.DMA((copies,)),
            pltpu.SemaphoreType.DMA((copies,)),
            pltpu.SemaphoreType.DMA((a * b,)),
        ],
        compiler_params=pltpu.CompilerParams(
            collective_id=2, has_side_effects=True, vmem_limit_bytes=60 * 2**20
        ),
        name="finish",
    )(*near, known, bias, mine, ada, factor, *done, down)


class Pieces:
    def __init__(self, place, pieces, source, target, send, recv, stage):
        self.copies = {}
        for by in range(1, place.heads):
            for piece in range(pieces):
                slot = (stage * (place.heads - 1) + by - 1) * pieces + piece
                self.copies[by, piece] = pltpu.make_async_remote_copy(
                    src_ref=source(by, piece),
                    dst_ref=target(by, piece),
                    send_sem=send.at[slot],
                    recv_sem=recv.at[slot],
                    device_id=place.flip(by),
                    device_id_type=MESH,
                )

    def start(self, by, piece):
        self.copies[by, piece].start()

    def arrived(self, by, piece):
        self.copies[by, piece].wait_recv()

    def left(self):
        for key in self.copies:
            self.copies[key].wait_send()


class Mlp:
    def __init__(self, place, pieces, own, width, units, sends, recvs):
        self.place, self.pieces, self.own, self.width, self.units = place, pieces, own, width, units
        self.sends, self.recvs = sends, recvs
        self.rows = own // pieces
        self.others = [(by, p) for p in range(pieces) for by in range(1, place.heads)]

    def at(self, piece):
        return pl.ds(piece * self.rows, self.rows)

    def flat(self, by, piece):
        return pl.ds(by * self.own + piece * self.rows, self.rows)

    def sum_stage(self, parcel, landed, stage):
        return Pieces(
            self.place,
            self.pieces,
            lambda by, p: parcel.at[by - 1, self.at(p)],
            lambda by, p: landed.at[by - 1, self.at(p)],
            self.sends,
            self.recvs,
            stage,
        )

    def spread_stage(self, every, stage):
        return Pieces(
            self.place,
            self.pieces,
            lambda by, p: every.at[0, self.at(p)],
            lambda by, p: every.at[by, self.at(p)],
            self.sends,
            self.recvs,
            stage,
        )

    def send_all(self, stage, piece):
        for by in range(1, self.place.heads):
            stage.start(by, piece)

    def arrive_all(self, stage, piece):
        for by in range(1, self.place.heads):
            stage.arrived(by, piece)

    def total(self, own_part, landed, piece):
        value = own_part[self.at(piece)]
        for by in range(1, self.place.heads):
            value = value + landed[by - 1, self.at(piece)].astype(jnp.float32)
        return value

    def modulation(self, table, owner, index, piece):
        here = owner[self.at(piece)]
        total = jnp.zeros((self.rows, self.width), jnp.float32)
        for image in range(table.shape[0]):
            row = table[image : image + 1, index * self.width : (index + 1) * self.width]
            total = jnp.where(here == image, row, total)
        return total

    def partial(self, out, left, rows, right):
        size = tile_of(self.width)

        def body(step, at):
            out[:, pl.ds(at, size)] = dot_nt(left[rows, :], right[pl.ds(at, size), :]).astype(out.dtype)

        tiles(self.width, size, body)

    def front(self, attended, proj, residual, table, owner, parcel, landed, own_part, branch, middle, normed, inverse, inputs, tick=None):
        first = self.sum_stage(parcel, landed, 0)
        for by, p in self.others:
            parcel[by - 1, self.at(p)] = dot_nt(attended[self.flat(by, p), :], proj[...]).astype(
                jnp.bfloat16
            )
            first.start(by, p)
        own_part[...] = dot_nt(attended[pl.ds(0, self.own), :], proj[...])
        if tick:
            tick()
        second = self.spread_stage(inputs, 1)
        for p in range(self.pieces):
            at = self.at(p)
            self.arrive_all(first, p)
            value = self.total(own_part, landed, p)
            branch[at] = value
            value = residual[at] + self.modulation(table, owner, 2, p) * value
            middle[at] = value
            unit, scale = normalize(value)
            normed[at] = unit
            inverse[at] = scale
            inputs[0, at] = (
                unit * (1.0 + self.modulation(table, owner, 4, p))
                + self.modulation(table, owner, 3, p)
            ).astype(jnp.bfloat16)
            self.send_all(second, p)
        return first, second

    def gate_up(self, inputs, gu, out, hidden, by, begin, rows):
        flat = pl.ds(by * self.own + begin, rows)
        size = tile_of(self.units)

        def body(step, at):
            far = pl.ds(pl.multiple_of(self.units + at, 128), size)
            value = inputs[by, pl.ds(begin, rows)]
            gate = dot_nn(value, gu[:, pl.ds(at, size)])
            up = dot_nn(value, gu[:, far])
            out[flat, pl.ds(at, size)] = gate
            out[flat, far] = up
            hidden[flat, pl.ds(at, size)] = (jax.nn.silu(gate) * up).astype(jnp.bfloat16)

        tiles(self.units, size, body)

    def hidden_back(self, grads, down, gate_up, ggu, by, begin, rows):
        flat = pl.ds(by * self.own + begin, rows)
        size = tile_of(self.units)

        def body(step, at):
            far = pl.ds(pl.multiple_of(self.units + at, 128), size)
            gate = gate_up[flat, pl.ds(at, size)]
            up = gate_up[flat, far]
            grad = dot_nn(grads[by, pl.ds(begin, rows)], down[:, pl.ds(at, size)])
            logistic = jax.nn.sigmoid(gate)
            ggu[flat, pl.ds(at, size)] = (
                grad * up * logistic * (1.0 + gate * (1.0 - logistic))
            ).astype(jnp.bfloat16)
            ggu[flat, far] = (grad * gate * logistic).astype(jnp.bfloat16)

        tiles(self.units, size, body)


def mlp_kernel(row_size, head_size, pieces, count, which, *refs):
    attended, residual, owner, table, following = refs[:5]
    streams, shards = refs[5:8], [ref.at[which] for ref in refs[8 : 8 + count]]
    refs = refs[8 + count :]
    kept_out, refs = refs[:5], refs[5:]
    inverse, mlp_out, result, next_normed, next_inverse, next_out = refs[:6]
    gathered, refs = refs[6 : 6 + count], refs[6 + count :]
    weights, kept = refs[:3], refs[3:8]
    proj, gu, down = weights
    branch, normed, inputs, gate_up, hidden = kept
    parcel, landed, middle, own_part, next_all = refs[8:13]
    loads, stores, sends, recvs, gather_send, gather_recv, gather_keep = refs[13:]
    place = Place(row_size, head_size)
    own, width = residual.shape
    units = hidden.shape[1]
    work = Mlp(place, pieces, own, width, units, sends, recvs)
    copies = [
        pltpu.make_async_copy(source, target, loads.at[i])
        for i, (source, target) in enumerate(zip(streams, weights))
    ]
    out_copies = [
        pltpu.make_async_copy(source, target, stores.at[i])
        for i, (source, target) in enumerate(zip(kept, kept_out))
    ]
    items = [
        Gather(place, shards[i], gathered[i], gather_send.at[i], gather_recv.at[i], gather_keep.at[i])
        for i in range(count)
    ]
    for copy in copies:
        copy.start()
    place.greet(True)
    for item in items:
        item.begin()

    def hop(k):
        for item in items:
            item.first(k)

    copies[0].wait()
    first, second = work.front(
        attended,
        proj,
        residual,
        table,
        owner,
        parcel.at[0],
        landed.at[0],
        own_part,
        branch,
        middle,
        normed,
        inverse,
        inputs,
        lambda: hop(1),
    )
    hop(2)
    out_copies[0].start()
    out_copies[1].start()
    copies[1].wait()
    work.gate_up(inputs, gu, gate_up, hidden, 0, 0, own)
    for k in range(3, place.sizes[0]):
        hop(k)
    copies[2].wait()
    third = work.sum_stage(parcel.at[1], landed.at[1], 2)
    for by, p in work.others:
        second.arrived(by, p)
        work.gate_up(inputs, gu, gate_up, hidden, by, p * work.rows, work.rows)
        work.partial(parcel.at[1, by - 1, work.at(p)], hidden, work.flat(by, p), down)
        third.start(by, p)
    for copy in out_copies[2:]:
        copy.start()
    work.partial(own_part, hidden, pl.ds(0, own), down)
    for item in items:
        item.second()
    fourth = work.spread_stage(next_all, 3)
    for p in range(pieces):
        at = work.at(p)
        work.arrive_all(third, p)
        value = work.total(own_part, landed.at[1], p)
        mlp_out[at] = value
        value = middle[at] + work.modulation(table, owner, 5, p) * value
        result[at] = value
        unit, scale = normalize(value)
        next_normed[at] = unit
        next_inverse[at] = scale
        next_all[0, at] = (
            unit * (1.0 + work.modulation(following, owner, 1, p))
            + work.modulation(following, owner, 0, p)
        ).astype(jnp.bfloat16)
        work.send_all(fourth, p)
    next_out[0] = next_all[0]
    for by, p in work.others:
        fourth.arrived(by, p)
        next_out[by, work.at(p)] = next_all[by, work.at(p)]
    for item in items:
        item.finish()
    for stage in (first, second, third, fourth):
        stage.left()
    for copy in out_copies:
        copy.wait()


def pieces_of(own):
    return 2 if own % 32 == 0 else 1


def mlp_call(row_size, head_size, attended, residual, owner, table, following, weights, which, shards):
    own, width = residual.shape
    tokens = attended.shape[0]
    units = weights[2].shape[1]
    count = len(shards)
    pieces = pieces_of(own)
    others = head_size - 1
    copies = gather_count(row_size)
    anywhere = pl.BlockSpec(memory_space=pl.ANY)
    vmem = pl.BlockSpec(memory_space=pltpu.VMEM)
    shape = jax.ShapeDtypeStruct
    f32, bf16 = jnp.float32, jnp.bfloat16
    kept = [
        shape((own, width), f32),
        shape((own, width), f32),
        shape((head_size, own, width), bf16),
        shape((tokens, 2 * units), f32),
        shape((tokens, units), bf16),
    ]
    return pl.pallas_call(
        functools.partial(mlp_kernel, row_size, head_size, pieces, count, which),
        out_shape=kept
        + [
            shape((own, 1), f32),
            shape((own, width), f32),
            shape((own, width), f32),
            shape((own, width), f32),
            shape((own, 1), f32),
            shape((head_size, own, width), bf16),
        ]
        + [shape((row_size,) + item.shape[1:], item.dtype) for item in shards],
        in_specs=[vmem] * 5 + [anywhere] * (3 + count),
        out_specs=[anywhere] * 5 + [vmem] * 6 + [anywhere] * count,
        scratch_shapes=[pltpu.VMEM(item.shape, item.dtype) for item in weights]
        + [pltpu.VMEM(item.shape, item.dtype) for item in kept]
        + [
            pltpu.VMEM((2, others, own, width), bf16),
            pltpu.VMEM((2, others, own, width), bf16),
            pltpu.VMEM((own, width), f32),
            pltpu.VMEM((own, width), f32),
            pltpu.VMEM((head_size, own, width), bf16),
            pltpu.SemaphoreType.DMA((3,)),
            pltpu.SemaphoreType.DMA((5,)),
            pltpu.SemaphoreType.DMA((4 * others * pieces,)),
            pltpu.SemaphoreType.DMA((4 * others * pieces,)),
            pltpu.SemaphoreType.DMA((count, copies)),
            pltpu.SemaphoreType.DMA((count, copies)),
            pltpu.SemaphoreType.DMA((count,)),
        ],
        compiler_params=pltpu.CompilerParams(
            collective_id=4, has_side_effects=True, vmem_limit_bytes=60 * 2**20
        ),
        name="mlp",
    )(attended, residual, owner, table, following, *weights, *shards)


def mlp_back_kernel(row_size, head_size, pieces, count, *refs):
    incoming, owner, table, normed, inverse = refs[:5]
    streams = refs[5:11]
    grads = refs[11 : 11 + count]
    outs = refs[11 + count : 17 + 2 * count]
    grad_in, grad_mid, branch_out, grad_att, gu_out, down_out = outs[:6]
    sums = outs[6:]
    refs = refs[17 + 2 * count :]
    down, gate_up, gu, inputs, hidden, proj = refs[:6]
    mlp_all, branch_all, ggu, parcel, landed, own_part, buffer = refs[6:13]
    loads, sends, recvs, tile_sems, out_sem = refs[13:18]
    scratch = refs[18 : 18 + 4 * count]
    sum_send, sum_recv, sum_load = refs[18 + 4 * count :]
    place = Place(row_size, head_size)
    own, width = incoming.shape
    units = hidden.shape[1]
    work = Mlp(place, pieces, own, width, units, sends, recvs)
    step_units = tile_of(units)
    copies = [
        pltpu.make_async_copy(source, target, loads.at[i])
        for i, (source, target) in enumerate(
            zip(streams, (down, gate_up, gu, inputs, hidden, proj))
        )
    ]
    for copy in copies:
        copy.start()
    place.greet(True)
    first = work.spread_stage(mlp_all, 0)
    for p in range(pieces):
        at = work.at(p)
        mlp_all[0, at] = (work.modulation(table, owner, 5, p) * incoming[at]).astype(jnp.bfloat16)
        work.send_all(first, p)
    items = [
        Scatter(
            place,
            grads[i],
            sums[i],
            *scratch[4 * i : 4 * i + 4],
            sum_send.at[i],
            sum_recv.at[i],
            sum_load.at[i],
        )
        for i in range(count)
    ]
    for item in items:
        item.begin()
    copies[0].wait()
    copies[1].wait()
    work.hidden_back(mlp_all, down, gate_up, ggu, 0, 0, own)
    for item in items:
        item.first()
    copies[2].wait()
    second = work.sum_stage(parcel, landed, 1)
    for by, p in work.others:
        first.arrived(by, p)
        work.hidden_back(mlp_all, down, gate_up, ggu, by, p * work.rows, work.rows)
        work.partial(parcel.at[by - 1, work.at(p)], ggu, work.flat(by, p), gu)
        second.start(by, p)
    work.partial(own_part, ggu, pl.ds(0, own), gu)
    copies[3].wait()
    out = Streamed(buffer, gu_out, tile_sems, step_units)

    def body(step, at):
        out.put(step, dot_tn(inputs[...], ggu[:, pl.ds(at, step_units)]))

    tiles(2 * units, step_units, body)
    for item in items[:1]:
        item.second()
    third = work.spread_stage(branch_all, 2)
    for p in range(pieces):
        at = work.at(p)
        work.arrive_all(second, p)
        value = work.total(own_part, landed, p)
        grad_in[at] = value
        unit = normed[at]
        value = value * (1.0 + work.modulation(table, owner, 4, p))
        value = incoming[at] + inverse[at] * (
            value
            - jnp.mean(value, axis=-1, keepdims=True)
            - unit * jnp.mean(value * unit, axis=-1, keepdims=True)
        )
        grad_mid[at] = value
        branch_all[0, at] = (work.modulation(table, owner, 2, p) * value).astype(jnp.bfloat16)
        work.send_all(third, p)
    out.drain(2 * units // step_units)
    copies[4].wait()
    copies[5].wait()
    out = Streamed(buffer, down_out, tile_sems, step_units)

    def body(step, at):
        out.put(
            step,
            dot_tn(mlp_all[...].reshape(head_size * own, width), hidden[:, pl.ds(at, step_units)]),
        )

    tiles(units, step_units, body)
    for item in items[1:]:
        item.second()
    grad_att[pl.ds(0, own), :] = dot_nn(branch_all[0], proj[...]).astype(jnp.bfloat16)
    for by, p in work.others:
        third.arrived(by, p)
        grad_att[work.flat(by, p), :] = dot_nn(branch_all[by, work.at(p)], proj[...]).astype(
            jnp.bfloat16
        )
    keep = pltpu.make_async_copy(branch_all, branch_out, out_sem.at[0])
    keep.start()
    out.drain(units // step_units)
    for item in items:
        item.finish()
    for stage in (first, second, third):
        stage.left()
    keep.wait()


def mlp_back_call(row_size, head_size, near, streams, grads):
    count = len(grads)
    own, width = near[0].shape
    pieces = pieces_of(own)
    others = head_size - 1
    down, gate_up, gu, inputs, hidden, proj = streams
    units = hidden.shape[1]
    tokens = hidden.shape[0]
    a, b = 4, row_size // 8
    copies = scatter_count(row_size)
    scratch = []
    for grad in grads:
        chunk = grad.shape[1:]
        for lead in ((a, b), (a, b), (b - 1, a), (a - 1,)):
            scratch.append(pltpu.VMEM(lead + chunk, grad.dtype))
    anywhere = pl.BlockSpec(memory_space=pl.ANY)
    vmem = pl.BlockSpec(memory_space=pltpu.VMEM)
    shape = jax.ShapeDtypeStruct
    f32, bf16 = jnp.float32, jnp.bfloat16
    return pl.pallas_call(
        functools.partial(mlp_back_kernel, row_size, head_size, pieces, count),
        out_shape=[
            shape((own, width), f32),
            shape((own, width), f32),
            shape((head_size, own, width), bf16),
            shape((tokens, proj.shape[1]), bf16),
            shape((width, 2 * units), bf16),
            shape((width, units), bf16),
        ]
        + [shape(grad.shape[1:], f32) for grad in grads],
        in_specs=[vmem] * 5 + [anywhere] * (6 + count),
        out_specs=[vmem, vmem, anywhere, vmem, anywhere, anywhere] + [vmem] * count,
        scratch_shapes=[pltpu.VMEM(item.shape, item.dtype) for item in streams]
        + [
            pltpu.VMEM((head_size, own, width), bf16),
            pltpu.VMEM((head_size, own, width), bf16),
            pltpu.VMEM((tokens, 2 * units), bf16),
            pltpu.VMEM((others, own, width), bf16),
            pltpu.VMEM((others, own, width), bf16),
            pltpu.VMEM((own, width), f32),
            pltpu.VMEM((2, width, tile_of(units)), bf16),
            pltpu.SemaphoreType.DMA((6,)),
            pltpu.SemaphoreType.DMA((3 * others * pieces,)),
            pltpu.SemaphoreType.DMA((3 * others * pieces,)),
            pltpu.SemaphoreType.DMA((2,)),
            pltpu.SemaphoreType.DMA((1,)),
        ]
        + scratch
        + [
            pltpu.SemaphoreType.DMA((count, copies)),
            pltpu.SemaphoreType.DMA((count, copies)),
            pltpu.SemaphoreType.DMA((count, a * b)),
        ],
        compiler_params=pltpu.CompilerParams(
            collective_id=3, has_side_effects=True, vmem_limit_bytes=62 * 2**20
        ),
        name="mlp_back",
    )(*near, *streams, *grads)


def last_mlp_kernel(row_size, head_size, pieces, *refs):
    attended, residual, owner, table, incoming, mlp_grads = refs[:6]
    streams, refs = refs[6:9], refs[9:]
    block_out, branch, normed, mlp_out, grad_in, grad_mid, branch_out, grad_att = refs[:8]
    grads_out = refs[8]
    weights, refs = refs[9:12], refs[12:]
    proj, gu, down = weights
    inputs, gate_up, hidden, ggu, branch_all, parcel, landed = refs[:7]
    middle, inverse, own_part, own_mlp, buffer = refs[7:12]
    loads, sends, recvs, tile_sems, out_sem = refs[12:]
    place = Place(row_size, head_size)
    own, width = residual.shape
    units = hidden.shape[1]
    work = Mlp(place, pieces, own, width, units, sends, recvs)
    step_units = tile_of(units)
    copies = [
        pltpu.make_async_copy(source, target, loads.at[i])
        for i, (source, target) in enumerate(zip(streams, weights))
    ]
    for copy in copies:
        copy.start()
    place.greet(True)
    copies[0].wait()
    first, second = work.front(
        attended,
        proj,
        residual,
        table,
        owner,
        parcel.at[0],
        landed.at[0],
        own_part,
        branch,
        middle,
        normed,
        inverse,
        inputs,
    )
    copies[1].wait()
    copies[2].wait()
    work.gate_up(inputs, gu, gate_up, hidden, 0, 0, own)
    work.hidden_back(mlp_grads, down, gate_up, ggu, 0, 0, own)
    fourth = work.sum_stage(parcel.at[1], landed.at[1], 3)
    for by, p in work.others:
        second.arrived(by, p)
        begin = p * work.rows
        work.gate_up(inputs, gu, gate_up, hidden, by, begin, work.rows)
        work.hidden_back(mlp_grads, down, gate_up, ggu, by, begin, work.rows)
        work.partial(parcel.at[1, by - 1, work.at(p)], ggu, work.flat(by, p), gu)
        fourth.start(by, p)
    work.partial(own_part, ggu, pl.ds(0, own), gu)
    out = Streamed(buffer, grads_out, tile_sems, step_units)

    def body(step, at):
        out.put(
            step,
            dot_tn(inputs[...].reshape(head_size * own, width), ggu[:, pl.ds(at, step_units)]),
        )

    tiles(2 * units, step_units, body)
    fifth = work.spread_stage(branch_all, 4)
    for p in range(pieces):
        at = work.at(p)
        work.arrive_all(fourth, p)
        value = work.total(own_part, landed.at[1], p)
        grad_in[at] = value
        unit = normed[at]
        value = value * (1.0 + work.modulation(table, owner, 4, p))
        value = incoming[at].astype(jnp.float32) + inverse[at] * (
            value
            - jnp.mean(value, axis=-1, keepdims=True)
            - unit * jnp.mean(value * unit, axis=-1, keepdims=True)
        )
        grad_mid[at] = value
        branch_all[0, at] = (work.modulation(table, owner, 2, p) * value).astype(jnp.bfloat16)
        work.send_all(fifth, p)
    first.left()
    third = work.sum_stage(parcel.at[0], landed.at[0], 2)
    for by, p in work.others:
        work.partial(parcel.at[0, by - 1, work.at(p)], hidden, work.flat(by, p), down)
        third.start(by, p)
    work.partial(own_mlp, hidden, pl.ds(0, own), down)
    out.drain(2 * units // step_units)
    out = Streamed(buffer, grads_out, tile_sems, step_units, 2 * units)

    def body(step, at):
        out.put(
            step,
            dot_tn(mlp_grads[...].reshape(head_size * own, width), hidden[:, pl.ds(at, step_units)]),
        )

    tiles(units, step_units, body)
    grad_att[pl.ds(0, own), :] = dot_nn(branch_all[0], proj[...]).astype(jnp.bfloat16)
    for by, p in work.others:
        fifth.arrived(by, p)
        grad_att[work.flat(by, p), :] = dot_nn(branch_all[by, work.at(p)], proj[...]).astype(
            jnp.bfloat16
        )
    keep = pltpu.make_async_copy(branch_all, branch_out, out_sem.at[0])
    keep.start()
    for p in range(pieces):
        at = work.at(p)
        work.arrive_all(third, p)
        value = work.total(own_mlp, landed.at[0], p)
        mlp_out[at] = value
        block_out[at] = (middle[at] + work.modulation(table, owner, 5, p) * value).astype(
            jnp.bfloat16
        )
    out.drain(units // step_units)
    for stage in (second, third, fourth, fifth):
        stage.left()
    keep.wait()


def last_mlp_call(row_size, head_size, attended, residual, owner, table, incoming, mlp_grads, weights):
    own, width = residual.shape
    tokens = attended.shape[0]
    units = weights[2].shape[1]
    pieces = pieces_of(own)
    others = head_size - 1
    anywhere = pl.BlockSpec(memory_space=pl.ANY)
    vmem = pl.BlockSpec(memory_space=pltpu.VMEM)
    shape = jax.ShapeDtypeStruct
    f32, bf16 = jnp.float32, jnp.bfloat16
    return pl.pallas_call(
        functools.partial(last_mlp_kernel, row_size, head_size, pieces),
        out_shape=[
            shape((own, width), bf16),
            shape((own, width), f32),
            shape((own, width), f32),
            shape((own, width), f32),
            shape((own, width), f32),
            shape((own, width), f32),
            shape((head_size, own, width), bf16),
            shape(attended.shape, bf16),
            shape((width, 3 * units), bf16),
        ],
        in_specs=[vmem] * 6 + [anywhere] * 3,
        out_specs=[vmem] * 6 + [anywhere, vmem, anywhere],
        scratch_shapes=[pltpu.VMEM(item.shape, item.dtype) for item in weights]
        + [
            pltpu.VMEM((head_size, own, width), bf16),
            pltpu.VMEM((tokens, 2 * units), f32),
            pltpu.VMEM((tokens, units), bf16),
            pltpu.VMEM((tokens, 2 * units), bf16),
            pltpu.VMEM((head_size, own, width), bf16),
            pltpu.VMEM((2, others, own, width), bf16),
            pltpu.VMEM((2, others, own, width), bf16),
            pltpu.VMEM((own, width), f32),
            pltpu.VMEM((own, 1), f32),
            pltpu.VMEM((own, width), f32),
            pltpu.VMEM((own, width), f32),
            pltpu.VMEM((2, width, tile_of(units)), bf16),
            pltpu.SemaphoreType.DMA((3,)),
            pltpu.SemaphoreType.DMA((5 * others * pieces,)),
            pltpu.SemaphoreType.DMA((5 * others * pieces,)),
            pltpu.SemaphoreType.DMA((2,)),
            pltpu.SemaphoreType.DMA((1,)),
        ],
        compiler_params=pltpu.CompilerParams(
            collective_id=5, has_side_effects=True, vmem_limit_bytes=60 * 2**20
        ),
        name="last_mlp",
    )(attended, residual, owner, table, incoming, mlp_grads, *weights)


def rope_parts(coords):
    angle = angles(coords, HD // 4)
    return jnp.cos(angle), jnp.sin(angle)


def turn(vectors, geometry, sign):
    row_cos, row_sin, col_cos, col_sin = [item[:, :, None, :] for item in geometry]
    quarter = HD // 4
    a, b, c, d = [vectors[..., quarter * i : quarter * (i + 1)] for i in range(4)]
    return jnp.concatenate(
        [
            a * row_cos - b * (sign * row_sin),
            b * row_cos + a * (sign * row_sin),
            c * col_cos - d * (sign * col_sin),
            d * col_cos + c * (sign * col_sin),
        ],
        axis=-1,
    )


def masked_scores(queries, key_rows, image_ids):
    scores = jnp.einsum(
        "rqhe,rkhe->rhqk", queries, key_rows, preferred_element_type=jnp.float32
    ) * HD ** (-0.5)
    same_image = image_ids[:, :, None] == image_ids[:, None, :]
    return jnp.where(same_image[:, None], scores, -1e30)


def attend(queries, key_rows, value_rows, image_ids):
    scores = masked_scores(queries, key_rows, image_ids)
    maximum = jnp.max(scores, axis=-1, keepdims=True)
    scaled_exp = jnp.exp(scores - maximum)
    denominator = jnp.sum(scaled_exp, axis=-1, keepdims=True)
    weights = (scaled_exp / denominator).astype(jnp.bfloat16)
    attended = jnp.einsum("rhqk,rkhe->rqhe", weights, value_rows, preferred_element_type=jnp.float32)
    return (attended.astype(jnp.bfloat16), (maximum + jnp.log(denominator))[..., 0])


def attend_back(queries, key_rows, value_rows, image_ids, logsum, grad_attended):
    score_scale = HD ** (-0.5)
    probs = jnp.exp(masked_scores(queries, key_rows, image_ids) - logsum[..., None])
    weights = probs.astype(jnp.bfloat16)
    grad_value = jnp.einsum(
        "rhqk,rqhe->rkhe", weights, grad_attended, preferred_element_type=jnp.float32
    )
    grad_probs = jnp.einsum(
        "rqhe,rkhe->rhqk", grad_attended, value_rows, preferred_element_type=jnp.float32
    )
    inner_sum = jnp.sum(probs * grad_probs, axis=-1, keepdims=True)
    grad_scores = (probs * (grad_probs - inner_sum)).astype(jnp.bfloat16)
    grad_query = (
        jnp.einsum("rhqk,rkhe->rqhe", grad_scores, key_rows, preferred_element_type=jnp.float32)
        * score_scale
    )
    grad_key = (
        jnp.einsum("rhqk,rqhe->rkhe", grad_scores, queries, preferred_element_type=jnp.float32)
        * score_scale
    )
    return (grad_query, grad_key, grad_value)


def spread(values):
    arrived = [head_move(values, flip) for flip in range(1, lax.axis_size("heads"))]
    return jnp.concatenate([values] + arrived, axis=0)


def collect(operand, product, own_rows, beside):
    arrived = []
    for flip in range(1, lax.axis_size("heads")):
        partial = product(operand[flip * own_rows : (flip + 1) * own_rows])
        arrived.append(head_move(partial.astype(jnp.bfloat16), flip))
    total = product(operand[:own_rows])
    total, arrived, beside = lax.optimization_barrier((total, arrived, beside))
    for item in arrived:
        total = total + item.astype(jnp.float32)
    return total, beside


def plain_dot(operand, other):
    return jnp.dot(operand, other, preferred_element_type=jnp.float32)


def piece_of(mods, picks, index):
    width = mods.shape[1] // 6
    value = mods[:, index * width : (index + 1) * width]
    total = jnp.zeros((picks.shape[0], width), jnp.float32)
    for image in range(mods.shape[0]):
        total = jnp.where(picks[:, None] == image, value[image][None, :], total)
    return total


def attention(input_attn, qkv_full, qkv_b, image_ids, geometry):
    count_rows, row_len = image_ids.shape
    packed = plain_dot(input_attn, qkv_full) + qkv_b
    heads_here = packed.shape[1] // (3 * HD)
    packed = packed.reshape(count_rows, row_len, heads_here, 3, HD)
    queries = turn(packed[:, :, :, 0], geometry, 1.0).astype(jnp.bfloat16)
    key_rows = turn(packed[:, :, :, 1], geometry, 1.0).astype(jnp.bfloat16)
    value_rows = packed[:, :, :, 2].astype(jnp.bfloat16)
    attended, logsum = attend(queries, key_rows, value_rows, image_ids)
    attended = attended.reshape(count_rows * row_len, heads_here * HD)
    return attended, (queries, key_rows, value_rows, logsum)


def attention_back(grad_attended, stored, image_ids, geometry):
    queries, key_rows, value_rows, logsum = stored
    count_rows, row_len = image_ids.shape
    heads_here = queries.shape[2]
    grad_attended = grad_attended.reshape(count_rows, row_len, heads_here, HD)
    grad_query, grad_key, grad_value = attend_back(
        queries, key_rows, value_rows, image_ids, logsum, grad_attended
    )
    grad_query = turn(grad_query, geometry, -1.0)
    grad_key = turn(grad_key, geometry, -1.0)
    grad_packed = (
        jnp.stack([grad_query, grad_key, grad_value], axis=3)
        .reshape(count_rows * row_len, heads_here * 3 * HD)
        .astype(jnp.bfloat16)
    )
    return grad_packed, jnp.sum(grad_packed, axis=0, dtype=jnp.float32)


def image_sum(picker, values):
    return lax.dot_general(picker, values, (((0,), (0,)), ((), ())), precision=lax.Precision.HIGH)


def shards(
    tokens,
    cond,
    image_of,
    grid_row,
    grid_col,
    ada_weight,
    ada_bias,
    qkv_weight,
    qkv_bias,
    proj_weight,
    gu_weight,
    down_weight,
    cotangent,
):
    own_rows = tokens.shape[0]
    image_count = cond.shape[0]
    block_count = qkv_weight.shape[0]
    row_size = lax.axis_size("rows")
    head_size = lax.axis_size("heads")
    head_index = lax.axis_index("heads")

    def device_order(values):
        parts = values.reshape(head_size, own_rows)
        picked = [
            lax.dynamic_index_in_dim(parts, head_index ^ flip, 0, keepdims=False)
            for flip in range(head_size)
        ]
        return jnp.concatenate(picked).reshape(values.shape)

    image_ids = device_order(image_of - lax.axis_index("rows") * image_count)
    own_images = image_ids.reshape(-1)[:own_rows]
    picker = (own_images[:, None] == jnp.arange(image_count, dtype=jnp.int32)[None, :]).astype(
        jnp.float32
    )
    geometry = lax.optimization_barrier(
        rope_parts(device_order(grid_row)) + rope_parts(device_order(grid_col))
    )
    shard_rows = qkv_weight.shape[1]

    def gathered(shard):
        return lax.all_gather(shard, "rows", axis=0, tiled=True)

    cond_wide = cond.astype(jnp.float32)
    cond_act = jax.nn.silu(cond_wide).astype(jnp.bfloat16)
    pad = -image_count % 16
    bias_rows = jnp.repeat(ada_bias.astype(jnp.float32), image_count, axis=0)
    proj_flat, down_flat = proj_weight.transpose(0, 2, 1), down_weight.transpose(0, 2, 1)
    *early, table, cond_mine, input_attn, normed, inverse, mlp_grads = start_call(
        row_size,
        head_size,
        jnp.pad(cond_act, ((0, pad), (0, 0))),
        ada_weight,
        bias_rows,
        tokens,
        cotangent,
        image_ids.reshape(-1, 1),
        [qkv_weight, proj_flat, down_flat],
    )
    qkv_full, proj_t, down_t = [[item.reshape(-1, item.shape[-1])] for item in early]
    gu_full = [gathered(item.reshape(shard_rows, -1)) for item in gu_weight]
    for b in range(1, block_count):
        down_t.append(gathered(down_flat[b]))
    modulation = [table[b * image_count : (b + 1) * image_count] for b in range(block_count)]
    last = block_count - 1
    owner = own_images[:, None]
    input_attn = input_attn.reshape(-1, input_attn.shape[-1])
    normed_attn, inverse_attn = [normed], [inverse]
    inputs_attn = [input_attn]
    residual = tokens.astype(jnp.float32)
    attentions, attended = [], []
    for b in range(block_count):
        item, kept = attention(
            inputs_attn[b], qkv_full[b], qkv_bias[b].astype(jnp.float32), image_ids, geometry
        )
        attended.append(item)
        attentions.append(kept)
        weights = (proj_t[b], gu_full[b], down_t[b])
        if b < last:
            (
                branch,
                normed_mlp,
                input_mlp,
                gate_up,
                hidden,
                inverse_mlp,
                mlp_out,
                residual,
                next_normed,
                next_inverse,
                next_input,
                next_qkv,
                next_proj,
            ) = mlp_call(
                row_size,
                head_size,
                item,
                residual,
                owner,
                modulation[b],
                modulation[b + 1],
                weights,
                b + 1,
                [qkv_weight, proj_flat],
            )
            normed_attn.append(next_normed)
            inverse_attn.append(next_inverse)
            inputs_attn.append(next_input.reshape(inputs_attn[0].shape))
            qkv_full.append(next_qkv.reshape(qkv_full[0].shape))
            proj_t.append(next_proj.reshape(proj_t[0].shape))
            stored = (branch, normed_mlp, input_mlp, gate_up, hidden, inverse_mlp, mlp_out)
    (
        block_out,
        last_branch,
        last_normed,
        last_out,
        grad_input_mlp,
        grad_middle,
        gathered_branch,
        grad_attended,
        mlp_grad,
    ) = last_mlp_call(
        row_size,
        head_size,
        attended[last],
        residual,
        owner,
        modulation[last],
        cotangent,
        mlp_grads,
        weights,
    )

    def scattered(grad):
        return lax.psum_scatter(grad, "rows", scatter_dimension=0, tiled=True).astype(jnp.float32)

    def late_sums(middle, branch, incoming, normed, grad, out):
        return [
            image_sum(picker, item)
            for item in (middle * branch, grad, grad * normed, incoming * out)
        ]

    gu_outs, bias_sums, image_sums = [None] * 2, [None] * 2, [None] * 2
    mlp_sum = scattered(mlp_grad)
    units = mlp_sum.shape[1] // 3
    gathered_branch = gathered_branch.reshape(-1, gathered_branch.shape[-1])
    grad_packed, bias_sums[1] = attention_back(grad_attended, attentions[1], image_ids, geometry)
    qkv_grad, proj_grad = weight_grads(
        (inputs_attn[1], grad_packed), (gathered_branch, attended[1])
    )
    late = late_sums(
        grad_middle,
        last_branch,
        cotangent.astype(jnp.float32),
        last_normed,
        grad_input_mlp,
        last_out,
    )
    grad_input_attn, (qkv_grad, proj_grad, late) = collect(
        grad_packed, lambda rows: tail_dot(rows, qkv_full[1]), own_rows, (qkv_grad, proj_grad, late)
    )
    scale = piece_of(modulation[1], own_images, 1)
    incoming = grad_middle + norm_back(
        grad_input_attn * (1.0 + scale), normed_attn[1], inverse_attn[1]
    )
    image_sums[1] = jnp.concatenate(
        [
            image_sum(picker, grad_input_attn),
            image_sum(picker, grad_input_attn * normed_attn[1]),
        ]
        + late,
        axis=1,
    )
    branch, normed_mlp, input_mlp, gate_up, hidden, inverse_mlp, mlp_out = stored
    block_sums = [None] * 2
    (
        grad_input_mlp,
        grad_middle,
        gathered_branch,
        grad_attended,
        gu_grad,
        down_grad,
        *block_sums[1],
    ) = mlp_back_call(
        row_size,
        head_size,
        (
            incoming,
            owner,
            modulation[0],
            normed_mlp,
            inverse_mlp,
        ),
        (
            down_t[0],
            gate_up,
            gu_full[0],
            input_mlp.reshape(-1, input_mlp.shape[-1]),
            hidden,
            proj_t[0],
        ),
        [item.reshape(row_size, shard_rows, -1) for item in (qkv_grad, proj_grad)],
    )
    gathered_branch = gathered_branch.reshape(-1, gathered_branch.shape[-1])
    grad_packed, bias_sums[0] = attention_back(grad_attended, attentions[0], image_ids, geometry)
    grad_packed, mlp_sum, gu_grad = lax.optimization_barrier((grad_packed, mlp_sum, gu_grad))
    gu_outs[0] = scattered(gu_grad)
    late = late_sums(grad_middle, branch, incoming, normed_mlp, grad_input_mlp, mlp_out)
    image_sums[0] = jnp.concatenate([jnp.zeros_like(late[0])] * 2 + late, axis=1)
    gu_outs[1] = mlp_sum[:, : 2 * units]
    sheets = jnp.stack(image_sums).reshape(block_count * image_count, head_size, -1)
    sheets = sheets.transpose(1, 0, 2)
    wide = sheets.shape[-1]
    bias_sums = jnp.stack(bias_sums)
    bias_high = bias_sums.astype(jnp.bfloat16).astype(jnp.float32)
    bias_rest = bias_sums - bias_high
    bias_middle = bias_rest.astype(jnp.bfloat16).astype(jnp.float32)
    bias_parts = jnp.stack([bias_high, bias_middle, bias_rest - bias_middle], axis=1)
    bias_parts = jnp.pad(bias_parts, ((0, 0), (0, 0), (0, wide - bias_sums.shape[1])))
    bias_parts = bias_parts.reshape(-1, wide)
    used = sheets.shape[1] + bias_parts.shape[0]
    small_rows = used + -used % 16
    bias_parts = jnp.pad(bias_parts, ((sheets.shape[1], small_rows - used), (0, 0)))
    cond_rows = cond_mine.reshape(row_size, -1, shard_rows)[:, :image_count]
    row = jnp.arange(small_rows)
    mine = []
    for b in range(block_count):
        first = b * image_count
        lead = jnp.pad(cond_rows, ((0, 0), (first, small_rows - first - image_count), (0, 0)))
        is_image = (row >= first) & (row < first + image_count)
        start = block_count * image_count + 3 * b
        is_bias = (row >= start) & (row < start + 3)
        ones = jnp.stack([is_image, is_bias], axis=1).astype(jnp.bfloat16)
        ones = jnp.broadcast_to(ones[None], (row_size,) + ones.shape)
        both = jnp.concatenate([lead, ones], axis=2)
        both = jnp.pad(both, ((0, 0), (0, 0), (0, -both.shape[2] % 128)))
        mine.append(both.reshape(-1, both.shape[2]))
    logistic = jax.nn.sigmoid(cond_wide)
    factor = logistic * (1.0 + cond_wide * (1.0 - logistic))
    factor = jnp.pad(factor, ((0, -image_count % 8), (0, 0)))
    tokens_grad, ada_grads, ada_bias_grads, qkv_bias_out, cond_grad, *stacked = finish_call(
        row_size,
        head_size,
        image_count,
        (
            grad_packed,
            qkv_full[0],
            inputs_attn[0],
            attended[0],
            gathered_branch,
            grad_middle,
            piece_of(modulation[0], own_images, 1),
            normed_attn[0],
            inverse_attn[0],
            owner,
        ),
        sheets,
        bias_parts,
        jnp.stack(mine),
        ada_weight,
        factor,
        [mlp_sum[:, 2 * units :]] + block_sums[1],
        down_grad.reshape(row_size, shard_rows, -1),
    )
    cond_grad = cond_grad[:image_count]
    return (
        block_out,
        tokens_grad,
        cond_grad,
        ada_grads,
        ada_bias_grads,
        stacked[1],
        qkv_bias_out,
        stacked[2].transpose(0, 2, 1),
        jnp.stack([item.reshape(gu_weight.shape[1:]) for item in gu_outs]),
        stacked[0].transpose(0, 2, 1),
    )


def solution(mesh):
    in_specs = (
        P(("rows", "heads"), None),
        P("rows", None),
        P("rows", None),
        P("rows", None),
        P("rows", None),
        P(None, "rows", "heads"),
        P(None, "heads"),
        P(None, "rows", "heads"),
        P(None, "heads"),
        P(None, "heads", "rows"),
        P(None, "rows", None, "heads"),
        P(None, "heads", "rows"),
        P(("rows", "heads"), None),
    )
    out_specs = (
        P(("rows", "heads"), None),
        P(("rows", "heads"), None),
        P("rows", None),
        P(None, "rows", "heads"),
        P(None, "heads"),
        P(None, "rows", "heads"),
        P(None, "heads"),
        P(None, "heads", "rows"),
        P(None, "rows", None, "heads"),
        P(None, "heads", "rows"),
    )
    return jax.shard_map(shards, mesh=mesh, in_specs=in_specs, out_specs=out_specs, check_vma=False)
```

```python
import functools

import jax
import jax.numpy as jnp
from jax import lax
from jax.experimental import pallas as pl
from jax.experimental.pallas import tpu as pltpu
from jax.sharding import PartitionSpec as P

HD = 72


epsilon = 1e-06
theta_base = 10000.0
highest = lax.Precision.HIGHEST


def normalize(values):
    center = values - jnp.mean(values, axis=-1, keepdims=True)
    inverse = lax.rsqrt(jnp.mean(center * center, axis=-1, keepdims=True) + epsilon)
    return (center * inverse, inverse)


def norm_back(incoming, normed, inverse):
    return inverse * (
        incoming
        - jnp.mean(incoming, axis=-1, keepdims=True)
        - normed * jnp.mean(incoming * normed, axis=-1, keepdims=True)
    )


def lead_dot(operand, other):
    return lax.dot_general(
        operand, other, (((0,), (0,)), ((), ())), preferred_element_type=jnp.float32
    )


def tail_dot(operand, other):
    return lax.dot_general(
        operand, other, (((1,), (1,)), ((), ())), preferred_element_type=jnp.float32
    )


def angles(coords, quarter):
    frequency = theta_base ** (-jnp.arange(quarter, dtype=jnp.float32) / quarter)
    return coords.astype(jnp.float32)[..., None] * frequency


def head_move(value, flip):
    size = lax.axis_size("heads")
    return lax.ppermute(value, "heads", [(index, index ^ flip) for index in range(size)])


MESH = pl.DeviceIdType.MESH


class Place:
    def __init__(self, row_size, head_size):
        self.sizes = (4, row_size // 8, 2)
        index = lax.axis_index("rows")
        a, b, c = self.sizes
        self.mine = (index // (b * c), (index // c) % b, index % c)
        self.heads = head_size
        self.head = lax.axis_index("heads")

    def step(self, dim, by):
        return (self.mine[dim] + by + self.sizes[dim]) % self.sizes[dim]

    def row(self, a, b, c):
        return (a * self.sizes[1] + b) * self.sizes[2] + c

    def near(self, dim, by):
        at = list(self.mine)
        at[dim] = self.step(dim, by)
        return {"rows": self.row(*at)}

    def flip(self, by):
        return {"heads": self.head ^ by}

    def partners(self, with_heads):
        found = [self.near(dim, by) for dim in range(3) for by in range(1, self.sizes[dim])]
        if with_heads:
            found += [self.flip(by) for by in range(1, self.heads)]
        return found

    def greet(self, with_heads):
        barrier = pltpu.get_barrier_semaphore()
        found = self.partners(with_heads)
        for partner in found:
            pl.semaphore_signal(barrier, inc=1, device_id=partner, device_id_type=MESH)
        pl.semaphore_wait(barrier, len(found))


def gather_count(row_size):
    a, b, c = 4, row_size // 8, 2
    return 2 * (a - 1) + (2 * a - 1) * (2 * b - 1)


class Gather:
    def __init__(self, place, shard, out, send, recv, local):
        self.place, self.shard, self.out = place, shard, out
        self.send, self.recv = send, recv
        self.used = 0
        self.keep = pltpu.make_async_copy(shard, out.at[place.row(*place.mine)], local)
        a, b, _ = place.sizes
        self.hops, self.along_b, self.along_c = {}, {}, {}
        names = [(0, 0)] + [(way, k) for k in range(1, a) for way in (1, -1)]
        for way, k in names:
            if k:
                self.hops[way, k] = self.copy(way, k - 1, 0, place.near(0, way))
        for way, k in names:
            for j in range(1, b):
                self.along_b[way, k, j] = self.copy(way, k, 0, place.near(1, j))
        for way, k in names:
            for j in range(b):
                self.along_c[way, k, j] = self.copy(way, k, j, place.near(2, 1))

    def copy(self, way, k, j, device):
        place, slot = self.place, self.used
        self.used += 1
        index = place.row(place.step(0, -way * k), place.step(1, -j), place.mine[2])
        return pltpu.make_async_remote_copy(
            src_ref=self.shard if k == 0 and j == 0 else self.out.at[index],
            dst_ref=self.out.at[index],
            send_sem=self.send.at[slot],
            recv_sem=self.recv.at[slot],
            device_id=device,
            device_id_type=MESH,
        )

    def holds(self, way, k):
        at = self.place.mine[0]
        return at >= k if way > 0 else at < self.place.sizes[0] - k

    def hop(self, way, k):
        at = self.place.mine[0]
        last = self.place.sizes[0] - 1
        return (at < last) & (at >= k - 1) if way > 0 else (at > 0) & (at <= last - (k - 1))

    def begin(self):
        self.keep.start()
        for way in (1, -1):
            pl.when(self.hop(way, 1))(self.hops[way, 1].start)
        self.pass_on(0, 0)

    def pass_on(self, way, k):
        for j in range(1, self.place.sizes[1]):
            self.along_b[way, k, j].start()
        self.along_c[way, k, 0].start()

    def first(self, k):
        for way in (1, -1):

            @pl.when(self.holds(way, k))
            def _():
                self.hops[way, k].wait_recv()
                if k + 1 < self.place.sizes[0]:
                    pl.when(self.hop(way, k + 1))(self.hops[way, k + 1].start)
                self.pass_on(way, k)

    def each(self, way, k, action):
        if k:
            pl.when(self.holds(way, k))(action)
        else:
            action()

    def second(self):
        for way, k, j in self.along_b:

            def action():
                self.along_b[way, k, j].wait_recv()
                self.along_c[way, k, j].start()

            self.each(way, k, action)

    def finish(self):
        for way, k, j in self.along_c:

            def action():
                self.along_c[way, k, j].wait_recv()
                self.along_c[way, k, j].wait_send()

            self.each(way, k, action)
        for way, k, j in self.along_b:
            self.each(way, k, self.along_b[way, k, j].wait_send)
        for way, k in self.hops:
            pl.when(self.hop(way, k))(self.hops[way, k].wait_send)
        self.keep.wait()


def gather_all(items):
    count = len(items)
    items[0].begin()
    for step in range(count + 1):
        if step < count:
            items[step].first(1)
            if step + 1 < count:
                items[step + 1].begin()
            for k in range(2, items[step].place.sizes[0]):
                items[step].first(k)
        if step >= 1:
            items[step - 1].second()
    for item in items:
        item.finish()


def scatter_count(row_size):
    a, b, c = 4, row_size // 8, 2
    return a * b + a * (b - 1) + (a - 1)


class Scatter:
    def __init__(self, place, source, out, held, met, side, far, send, recv, load):
        self.place, self.source, self.out = place, source, out
        self.held, self.met, self.side, self.far = held, met, side, far
        self.send, self.recv, self.load = send, recv, load

    def remote(self, source, target, slot, device):
        return pltpu.make_async_remote_copy(
            src_ref=source,
            dst_ref=target,
            send_sem=self.send.at[slot],
            recv_sem=self.recv.at[slot],
            device_id=device,
            device_id_type=MESH,
        )

    def across(self, k, j):
        place = self.place
        a, b = place.step(0, k), place.step(1, j)
        other = place.step(2, 1)
        return self.remote(
            self.source.at[place.row(a, b, other)],
            self.met.at[a, b],
            k * place.sizes[1] + j,
            place.near(2, 1),
        )

    def fetch(self, k, j):
        place = self.place
        a, b = place.step(0, k), place.step(1, j)
        return pltpu.make_async_copy(
            self.source.at[place.row(a, b, place.mine[2])],
            self.held.at[a, b],
            self.load.at[k * place.sizes[1] + j],
        )

    def along_b(self, k, j):
        place = self.place
        a, b = place.step(0, k), place.step(1, j)
        base = place.sizes[0] * place.sizes[1]
        return self.remote(
            self.held.at[a, b],
            self.side.at[j - 1, a],
            base + (j - 1) * place.sizes[0] + k,
            place.near(1, j),
        )

    def along_a(self, k):
        place = self.place
        base = place.sizes[0] * (2 * place.sizes[1] - 1)
        return self.remote(
            self.held.at[place.step(0, k), place.mine[1]],
            self.far.at[k - 1],
            base + k - 1,
            place.near(0, k),
        )

    def order(self):
        a, b, _ = self.place.sizes
        return [(k, j) for j in list(range(1, b)) + [0] for k in list(range(1, a)) + [0]]

    def begin(self):
        for k, j in self.order():
            self.fetch(k, j).start()
            self.across(k, j).start()

    def first(self):
        place = self.place
        a, b, _ = place.sizes
        for j in range(1, b):
            for k in list(range(1, a)) + [0]:
                self.fetch(k, j).wait()
                self.across(k, j).wait_recv()
                at = (place.step(0, k), place.step(1, j))
                self.held[at] = (
                    self.held[at].astype(jnp.float32) + self.met[at].astype(jnp.float32)
                ).astype(self.held.dtype)
                self.along_b(k, j).start()

    def total(self, k):
        place = self.place
        a, b = place.step(0, k), place.mine[1]
        value = self.held[a, b].astype(jnp.float32) + self.met[a, b].astype(jnp.float32)
        for j in range(1, place.sizes[1]):
            value = value + self.side[j - 1, a].astype(jnp.float32)
        return value

    def second(self):
        place = self.place
        a, b, _ = place.sizes
        for k in list(range(1, a)) + [0]:
            self.fetch(k, 0).wait()
            self.across(k, 0).wait_recv()
            for j in range(1, b):
                self.along_b(k, j).wait_recv()
            if k:
                self.held[place.step(0, k), place.mine[1]] = self.total(k).astype(self.held.dtype)
                self.along_a(k).start()
            else:
                self.out[...] = self.total(0)

    def finish(self):
        place = self.place
        a, b, _ = place.sizes
        for k in range(1, a):
            self.along_a(k).wait_recv()
            self.out[...] = self.out[...] + self.far[k - 1].astype(jnp.float32)
        for k, j in self.order():
            self.across(k, j).wait_send()
            if j:
                self.along_b(k, j).wait_send()
        for k in range(1, a):
            self.along_a(k).wait_send()


def scatter_all(items):
    count = len(items)
    for item in items:
        item.begin()
    for step in range(count + 2):
        if step < count:
            items[step].first()
        if 1 <= step <= count:
            items[step - 1].second()
        if step >= 2:
            items[step - 2].finish()


def start_kernel(row_size, head_size, images, blocks, weights, *refs):
    cond, ada, bias, tokens, cotangent, owner = refs[:6]
    shards = [ref.at[0] for ref in refs[6 : 6 + weights]]
    outs = refs[6 + weights : 6 + 2 * weights]
    refs = refs[6 + 2 * weights :]
    table, mine_out, inputs_out, normed_out, inverse_out, grads_out = refs[:6]
    every_token, every_cotangent, token_send, token_recv = refs[6:10]
    refs = refs[10:]
    (conds, part, held, met, side, far, total, every, sends, recvs, keeps) = refs[:11]
    (mod_send, mod_recv, mod_load, head_send, head_recv) = refs[11:]
    place = Place(row_size, head_size)
    place.greet(True)
    items = [
        Gather(place, shard, out, sends.at[i], recvs.at[i], keeps.at[i])
        for i, (shard, out) in enumerate(zip((cond,) + tuple(shards), (conds,) + outs))
    ]
    lead, bulk = items[0], items[1:]
    lead.begin()
    own = tokens.shape[0]
    every_token[0] = tokens[...]
    every_cotangent[0] = cotangent[...]
    raws = [
        Across(place, lambda by: ref.at[0], lambda by: ref.at[by], token_send, token_recv, stage)
        for stage, ref in enumerate((every_token, every_cotangent))
    ]
    for raw in raws:
        for by in range(1, head_size):
            raw.start(by)
    hops = range(1, place.sizes[0])
    for k in hops:
        lead.first(k)
    lead.second()
    lead.finish()
    width = cond.shape[1]
    share = ada.shape[1]
    pad = cond.shape[0]
    lane = lax.broadcasted_iota(jnp.int32, (width, share), 0)
    slot = lax.broadcasted_iota(jnp.int32, (width, share), 1)
    pick = jnp.where(lane == lax.axis_index("rows") * share + slot, 1.0, 0.0).astype(jnp.bfloat16)
    mine = jnp.dot(
        conds[...].reshape(row_size * pad, width), pick, preferred_element_type=jnp.float32
    ).astype(jnp.bfloat16)
    mine_out[...] = mine
    for b in range(blocks):
        value = jnp.dot(mine, ada[b], preferred_element_type=jnp.float32)
        part[:, b * images : (b + 1) * images, :] = value.reshape(row_size, pad, -1)[:, :images]
    sums = Scatter(place, part, total, held, met, side, far, mod_send, mod_recv, mod_load)
    sums.begin()
    sums.first()
    bulk[0].begin()
    sums.second()
    bulk[0].first(1)
    for item in bulk[1:]:
        item.begin()
    for k in hops[1:]:
        bulk[0].first(k)
    for item in bulk[1:]:
        for k in hops:
            item.first(k)
    sums.finish()
    every[place.head] = total[...] + bias[...]
    across = [
        pltpu.make_async_remote_copy(
            src_ref=every.at[place.head],
            dst_ref=every.at[place.head],
            send_sem=head_send.at[by - 1],
            recv_sem=head_recv.at[by - 1],
            device_id=place.flip(by),
            device_id_type=MESH,
        )
        for by in range(1, head_size)
    ]
    for copy in across:
        copy.start()
    for item in bulk:
        item.second()
    for copy in across:
        copy.wait()
    wide = every.shape[2]
    for head in range(head_size):
        table[:, head * wide : (head + 1) * wide] = every[head]
    for raw in raws:
        for by in range(1, head_size):
            raw.arrived(by)
    columns = tokens.shape[1]
    half = own // pieces_of(own)

    def modulation(here, first, index):
        value = jnp.zeros((half, columns), jnp.float32)
        for image in range(images):
            row = table[first + image : first + image + 1, index * columns : (index + 1) * columns]
            value = jnp.where(here == image, row, value)
        return value

    last = (blocks - 1) * images

    @pl.loop(0, head_size * (own // half))
    def _(step):
        slot = step // (own // half)
        rows = pl.ds(pl.multiple_of(step % (own // half) * half, 8), half)
        here = owner[pl.ds(pl.multiple_of(step * half, 8), half), :]
        unit, scale = normalize(every_token[slot, rows].astype(jnp.float32))
        inputs_out[slot, rows] = (
            unit * (1.0 + modulation(here, 0, 1)) + modulation(here, 0, 0)
        ).astype(jnp.bfloat16)
        grads_out[slot, rows] = (
            modulation(here, last, 5) * every_cotangent[slot, rows].astype(jnp.float32)
        ).astype(jnp.bfloat16)

        @pl.when(slot == 0)
        def _():
            normed_out[rows] = unit
            inverse_out[rows] = scale

    for raw in raws:
        raw.left()
    for item in bulk:
        item.finish()


def start_call(row_size, head_size, cond, ada, bias, tokens, cotangent, owner, shards):
    images = bias.shape[0] // ada.shape[0]
    blocks = ada.shape[0]
    count = len(shards)
    a, b = 4, row_size // 8
    chunk = bias.shape
    copies = gather_count(row_size)
    anywhere = pl.BlockSpec(memory_space=pl.ANY)
    vmem = pl.BlockSpec(memory_space=pltpu.VMEM)
    f32, bf16 = jnp.float32, jnp.bfloat16
    own, width = tokens.shape
    shape = jax.ShapeDtypeStruct
    return pl.pallas_call(
        functools.partial(start_kernel, row_size, head_size, images, blocks, count),
        out_shape=[jax.ShapeDtypeStruct((row_size,) + item.shape[1:], item.dtype) for item in shards]
        + [
            shape((chunk[0], head_size * chunk[1]), f32),
            shape((row_size * cond.shape[0], ada.shape[1]), cond.dtype),
            shape((head_size, own, width), bf16),
            shape((own, width), f32),
            shape((own, 1), f32),
            shape((head_size, own, width), bf16),
        ],
        in_specs=[vmem] * 6 + [anywhere] * count,
        out_specs=[anywhere] * count + [vmem] * 6,
        scratch_shapes=[
            pltpu.VMEM((head_size, own, width), bf16),
            pltpu.VMEM((head_size, own, width), bf16),
            pltpu.SemaphoreType.DMA((2 * (head_size - 1),)),
            pltpu.SemaphoreType.DMA((2 * (head_size - 1),)),
            pltpu.VMEM((row_size,) + cond.shape, cond.dtype),
            pltpu.VMEM((row_size,) + chunk, f32),
            pltpu.VMEM((a, b) + chunk, f32),
            pltpu.VMEM((a, b) + chunk, f32),
            pltpu.VMEM((b - 1, a) + chunk, f32),
            pltpu.VMEM((a - 1,) + chunk, f32),
            pltpu.VMEM(chunk, f32),
            pltpu.VMEM((head_size,) + chunk, f32),
            pltpu.SemaphoreType.DMA((count + 1, copies)),
            pltpu.SemaphoreType.DMA((count + 1, copies)),
            pltpu.SemaphoreType.DMA((count + 1,)),
            pltpu.SemaphoreType.DMA((scatter_count(row_size),)),
            pltpu.SemaphoreType.DMA((scatter_count(row_size),)),
            pltpu.SemaphoreType.DMA((a * b,)),
            pltpu.SemaphoreType.DMA((head_size - 1,)),
            pltpu.SemaphoreType.DMA((head_size - 1,)),
        ],
        compiler_params=pltpu.CompilerParams(
            collective_id=1, has_side_effects=True, vmem_limit_bytes=48 * 2**20
        ),
        name="start",
    )(cond, ada, bias, tokens, cotangent, owner, *shards)


def head_part_kernel(begin, packed, weight, out):
    rows, width = out.shape
    size = tile_of(width)

    def body(step, at):
        out[:, pl.ds(at, size)] = dot_nt(
            packed[pl.ds(begin, rows), :], weight[pl.ds(at, size), :]
        ).astype(out.dtype)

    tiles(width, size, body)


def head_part(packed, weight, rows, slot, dtype):
    vmem = pl.BlockSpec(memory_space=pltpu.VMEM)
    width, depth = weight.shape
    return pl.pallas_call(
        functools.partial(head_part_kernel, slot * rows),
        out_shape=jax.ShapeDtypeStruct((rows, width), dtype),
        in_specs=[vmem] * 2,
        out_specs=vmem,
        compiler_params=pltpu.CompilerParams(vmem_limit_bytes=32 * 2**20),
        cost_estimate=pl.CostEstimate(
            flops=2 * rows * width * depth,
            bytes_accessed=2 * (packed.size + weight.size) + 4 * rows * width,
            transcendentals=0,
        ),
        name="head_part",
    )(packed, weight)


def weight_grads_kernel(*refs):
    count = len(refs) // 3
    for i in range(count):
        left, right, out = refs[2 * i], refs[2 * i + 1], refs[2 * count + i]
        columns = out.shape[1]
        for at in range(0, columns, 256):
            size = min(256, columns - at)
            out[:, at : at + size] = dot_tn(left[...], right[:, at : at + size]).astype(out.dtype)


def weight_grads(*pairs):
    vmem = pl.BlockSpec(memory_space=pltpu.VMEM)
    flat = [item for pair in pairs for item in pair]
    flops = sum(2 * left.size * right.shape[1] for left, right in pairs)
    moved = sum(2 * (left.size + right.size + left.shape[1] * right.shape[1]) for left, right in pairs)
    return pl.pallas_call(
        weight_grads_kernel,
        out_shape=[
            jax.ShapeDtypeStruct((left.shape[1], right.shape[1]), jnp.bfloat16)
            for left, right in pairs
        ],
        in_specs=[vmem] * len(flat),
        out_specs=[vmem] * len(pairs),
        compiler_params=pltpu.CompilerParams(vmem_limit_bytes=48 * 2**20),
        cost_estimate=pl.CostEstimate(flops=flops, bytes_accessed=moved, transcendentals=0),
        name="weight_grads",
    )(*flat)


def tile_of(width):
    return next(size for size in (256, 128, width) if width % size == 0)


def dot_nn(left, right):
    return jnp.dot(left, right, preferred_element_type=jnp.float32)


def dot_nt(left, right):
    return lax.dot_general(left, right, (((1,), (1,)), ((), ())), preferred_element_type=jnp.float32)


def dot_tn(left, right):
    return lax.dot_general(left, right, (((0,), (0,)), ((), ())), preferred_element_type=jnp.float32)


def tiles(width, size, body):
    @pl.loop(0, width // size)
    def _(step):
        body(step, pl.multiple_of(step * size, size))


class Across:
    def __init__(self, place, sources, targets, send, recv, stage):
        count = place.heads - 1
        self.copies = [
            pltpu.make_async_remote_copy(
                src_ref=sources(by),
                dst_ref=targets(by),
                send_sem=send.at[stage * count + by - 1],
                recv_sem=recv.at[stage * count + by - 1],
                device_id=place.flip(by),
                device_id_type=MESH,
            )
            for by in range(1, place.heads)
        ]

    def start(self, by):
        self.copies[by - 1].start()

    def arrived(self, by):
        self.copies[by - 1].wait_recv()

    def left(self):
        for copy in self.copies:
            copy.wait_send()


class Streamed:
    def __init__(self, buffer, out, sems, size, begin=0):
        self.buffer, self.out, self.sems, self.size, self.begin = buffer, out, sems, size, begin

    def copy(self, step):
        at = pl.multiple_of(self.begin + step * self.size, 128)
        return pltpu.make_async_copy(
            self.buffer.at[step % 2], self.out.at[:, pl.ds(at, self.size)], self.sems.at[step % 2]
        )

    def put(self, step, value):
        @pl.when(step >= 2)
        def _():
            self.copy(step - 2).wait()

        self.buffer[step % 2] = value.astype(self.buffer.dtype)
        self.copy(step).start()

    def drain(self, steps):
        for step in range(max(steps - 2, 0), steps):
            self.copy(step).wait()


def finish_kernel(row_size, head_size, images, blocks, *refs):
    (packed, qkv, inputs, attended, branch, middle, scale, normed, inverse, owner) = refs[:10]
    known, bias, mine, ada, factor = refs[10:15]
    done, down = refs[15:18], refs[18]
    grad_tokens, ada_out, ada_bias_out, qkv_bias_out, cond_out = refs[19:24]
    stacks = refs[24:27]
    outs = [ref.at[0] for ref in stacks]
    refs = refs[3:]
    parcel, landed, sheet, share_in, small, qkv_grad, proj_grad = refs[24:31]
    head_send, head_recv = refs[31:33]
    refs = refs[33:]
    scratch = refs[:12]
    every, part, held, met, side, far, total, cond_in = refs[12:20]
    send, recv, load, small_send, small_recv, small_keep = refs[20:26]
    cond_send, cond_recv, cond_load = refs[26:]
    place = Place(row_size, head_size)
    own, width = middle.shape
    step_width = tile_of(width)
    place.greet(True)
    for stack, item in zip(stacks, done):
        stack[1] = item[...].astype(jnp.float32)
    items = [
        Scatter(
            place, source, outs[i], *scratch[4 * i : 4 * i + 4], send.at[i], recv.at[i], load.at[i]
        )
        for i, source in enumerate((down, qkv_grad, proj_grad))
    ]
    items[0].begin()
    first = Across(
        place, lambda by: parcel.at[by - 1], lambda by: landed.at[by - 1], head_send, head_recv, 0
    )
    for by in range(1, head_size):

        def body(step, at):
            parcel[by - 1, :, pl.ds(at, step_width)] = dot_nt(
                packed[pl.ds(by * own, own), :], qkv[pl.ds(at, step_width), :]
            ).astype(jnp.bfloat16)

        tiles(width, step_width, body)
        first.start(by)
    for left, right, out, item in (
        (inputs, packed, qkv_grad, items[1]),
        (branch, attended, proj_grad, items[2]),
    ):
        share = out.shape[1]
        for at in range(0, out.shape[2], 256):
            size = min(256, out.shape[2] - at)
            value = dot_tn(left[...], right[:, at : at + size])
            for row in range(row_size):
                out[row, :, at : at + size] = value[row * share : (row + 1) * share].astype(out.dtype)
        item.begin()
    items[0].first()
    value = dot_nt(packed[pl.ds(0, own), :], qkv[...])
    for by in range(1, head_size):
        first.arrived(by)
        value = value + landed[by - 1].astype(jnp.float32)
    scaled = value * (1.0 + scale[...])
    grad_tokens[...] = middle[...] + inverse[...] * (
        scaled
        - jnp.mean(scaled, axis=-1, keepdims=True)
        - normed[...] * jnp.mean(scaled * normed[...], axis=-1, keepdims=True)
    )
    sheet[...] = known[...]
    wide = sheet.shape[2]
    for image in range(images):
        here = owner[...] == image
        for piece, item in enumerate((value, value * normed[...])):
            row = jnp.sum(jnp.where(here, item, 0.0), axis=0, keepdims=True)
            begin = piece * width
            while begin < (piece + 1) * width:
                end = min((begin // wide + 1) * wide, (piece + 1) * width)
                sheet[begin // wide, image : image + 1, begin % wide : begin % wide + end - begin] = (
                    row[:, begin - piece * width : end - piece * width]
                )
                begin = end
    shares = Across(
        place,
        lambda by: sheet.at[place.head ^ by],
        lambda by: share_in.at[by - 1],
        head_send,
        head_recv,
        1,
    )
    for by in range(1, head_size):
        shares.start(by)
    mod_grads = sheet[place.head]
    for by in range(1, head_size):
        shares.arrived(by)
        mod_grads = mod_grads + share_in[by - 1]
    known_rows = mod_grads.shape[0]
    small[...] = jnp.concatenate([mod_grads, bias[known_rows:, :]], axis=0).astype(small.dtype)
    lead = Gather(place, small, every, small_send, small_recv, small_keep.at[0])
    lead.begin()
    for k in range(1, place.sizes[0]):
        lead.first(k)
    items[0].second()
    lead.second()
    lead.finish()
    rows = small.shape[0]
    share = ada.shape[1]
    grads = every[...].reshape(row_size * rows, -1)
    columns = qkv_bias_out.shape[1]
    for b in range(blocks):
        value = dot_tn(mine[b], grads)
        ada_out[b] = value[:share]
        ada_bias_out[b : b + 1, :] = value[share : share + 1]
        qkv_bias_out[b : b + 1, :] = value[share + 1 : share + 2, :columns]
    lane = lax.broadcasted_iota(jnp.int32, (share, width), 1)
    slot = lax.broadcasted_iota(jnp.int32, (share, width), 0)
    pick = jnp.where(lane == lax.axis_index("rows") * share + slot, 1.0, 0.0).astype(jnp.bfloat16)
    back = 0.0
    for b in range(blocks):
        value = dot_nt(grads, ada[b]).reshape(row_size, rows, share)
        back = back + value[:, b * images : (b + 1) * images]
    back = back.reshape(row_size * images, share).astype(jnp.bfloat16)
    part[...] = jnp.zeros_like(part)
    part[:, :images, :] = dot_nn(back, pick).reshape(row_size, images, width)
    sums = Scatter(place, part, total, held, met, side, far, cond_send, cond_recv, cond_load)
    sums.begin()
    sums.first()
    items[1].first()
    items[2].first()
    sums.second()
    items[1].second()
    sums.finish()
    last = Across(
        place, lambda by: total, lambda by: cond_in.at[by - 1], head_send, head_recv, 2
    )
    for by in range(1, head_size):
        last.start(by)
    items[2].second()
    for item in items:
        item.finish()
    value = total[...]
    for by in range(1, head_size):
        last.arrived(by)
        value = value + cond_in[by - 1]
    cond_out[...] = value * factor[...]
    for stage in (first, shares, last):
        stage.left()


def finish_call(row_size, head_size, images, near, known, bias, mine, ada, factor, done, down):
    packed, qkv, inputs, attended, branch, middle = near[:6]
    copies = scatter_count(row_size)
    small_copies = gather_count(row_size)
    blocks, share, wide = ada.shape
    own, width = middle.shape
    a, b = 4, row_size // 8
    f32, bf16 = jnp.float32, jnp.bfloat16
    shape = jax.ShapeDtypeStruct
    chunks = [(share, columns) for columns in (down.shape[2], qkv.shape[1], attended.shape[1])]
    scratch = []
    for chunk in chunks:
        for lead in ((a, b), (a, b), (b - 1, a), (a - 1,)):
            scratch.append(pltpu.VMEM(lead + chunk, bf16))
    chunk = factor.shape
    anywhere = pl.BlockSpec(memory_space=pl.ANY)
    vmem = pl.BlockSpec(memory_space=pltpu.VMEM)
    others = head_size - 1
    return pl.pallas_call(
        functools.partial(finish_kernel, row_size, head_size, images, blocks),
        out_shape=[
            shape((own, width), f32),
            shape(ada.shape, f32),
            shape((blocks, wide), f32),
            shape((blocks, qkv.shape[1]), f32),
            shape(factor.shape, f32),
        ]
        + [shape((2,) + item, f32) for item in chunks],
        in_specs=[vmem] * 18 + [anywhere],
        out_specs=[vmem] * 8,
        scratch_shapes=[
            pltpu.VMEM((others, own, width), bf16),
            pltpu.VMEM((others, own, width), bf16),
            pltpu.VMEM(known.shape, f32),
            pltpu.VMEM((others,) + known.shape[1:], f32),
            pltpu.VMEM(bias.shape, bf16),
            pltpu.VMEM((row_size,) + chunks[1], bf16),
            pltpu.VMEM((row_size,) + chunks[2], bf16),
            pltpu.SemaphoreType.DMA((3 * others,)),
            pltpu.SemaphoreType.DMA((3 * others,)),
        ]
        + scratch
        + [
            pltpu.VMEM((row_size,) + bias.shape, bf16),
            pltpu.VMEM((row_size,) + chunk, f32),
            pltpu.VMEM((a, b) + chunk, f32),
            pltpu.VMEM((a, b) + chunk, f32),
            pltpu.VMEM((b - 1, a) + chunk, f32),
            pltpu.VMEM((a - 1,) + chunk, f32),
            pltpu.VMEM(chunk, f32),
            pltpu.VMEM((others,) + chunk, f32),
            pltpu.SemaphoreType.DMA((3, copies)),
            pltpu.SemaphoreType.DMA((3, copies)),
            pltpu.SemaphoreType.DMA((3, a * b)),
            pltpu.SemaphoreType.DMA((small_copies,)),
            pltpu.SemaphoreType.DMA((small_copies,)),
            pltpu.SemaphoreType.DMA((1,)),
            pltpu.SemaphoreType.DMA((copies,)),
            pltpu.SemaphoreType.DMA((copies,)),
            pltpu.SemaphoreType.DMA((a * b,)),
        ],
        compiler_params=pltpu.CompilerParams(
            collective_id=2, has_side_effects=True, vmem_limit_bytes=60 * 2**20
        ),
        name="finish",
    )(*near, known, bias, mine, ada, factor, *done, down)


class Pieces:
    def __init__(self, place, pieces, source, target, send, recv, stage):
        self.copies = {}
        for by in range(1, place.heads):
            for piece in range(pieces):
                slot = (stage * (place.heads - 1) + by - 1) * pieces + piece
                self.copies[by, piece] = pltpu.make_async_remote_copy(
                    src_ref=source(by, piece),
                    dst_ref=target(by, piece),
                    send_sem=send.at[slot],
                    recv_sem=recv.at[slot],
                    device_id=place.flip(by),
                    device_id_type=MESH,
                )

    def start(self, by, piece):
        self.copies[by, piece].start()

    def arrived(self, by, piece):
        self.copies[by, piece].wait_recv()

    def left(self):
        for key in self.copies:
            self.copies[key].wait_send()


class Mlp:
    def __init__(self, place, pieces, own, width, units, sends, recvs):
        self.place, self.pieces, self.own, self.width, self.units = place, pieces, own, width, units
        self.sends, self.recvs = sends, recvs
        self.rows = own // pieces
        self.others = [(by, p) for p in range(pieces) for by in range(1, place.heads)]

    def at(self, piece):
        return pl.ds(piece * self.rows, self.rows)

    def flat(self, by, piece):
        return pl.ds(by * self.own + piece * self.rows, self.rows)

    def sum_stage(self, parcel, landed, stage):
        return Pieces(
            self.place,
            self.pieces,
            lambda by, p: parcel.at[by - 1, self.at(p)],
            lambda by, p: landed.at[by - 1, self.at(p)],
            self.sends,
            self.recvs,
            stage,
        )

    def spread_stage(self, every, stage):
        return Pieces(
            self.place,
            self.pieces,
            lambda by, p: every.at[0, self.at(p)],
            lambda by, p: every.at[by, self.at(p)],
            self.sends,
            self.recvs,
            stage,
        )

    def send_all(self, stage, piece):
        for by in range(1, self.place.heads):
            stage.start(by, piece)

    def arrive_all(self, stage, piece):
        for by in range(1, self.place.heads):
            stage.arrived(by, piece)

    def total(self, own_part, landed, piece):
        value = own_part[self.at(piece)]
        for by in range(1, self.place.heads):
            value = value + landed[by - 1, self.at(piece)].astype(jnp.float32)
        return value

    def modulation(self, table, owner, index, piece):
        here = owner[self.at(piece)]
        total = jnp.zeros((self.rows, self.width), jnp.float32)
        for image in range(table.shape[0]):
            row = table[image : image + 1, index * self.width : (index + 1) * self.width]
            total = jnp.where(here == image, row, total)
        return total

    def partial(self, out, left, rows, right):
        size = tile_of(self.width)

        def body(step, at):
            out[:, pl.ds(at, size)] = dot_nt(left[rows, :], right[pl.ds(at, size), :]).astype(out.dtype)

        tiles(self.width, size, body)

    def front(self, attended, proj, residual, table, owner, parcel, landed, own_part, branch, middle, normed, inverse, inputs, tick=None):
        first = self.sum_stage(parcel, landed, 0)
        for by, p in self.others:
            parcel[by - 1, self.at(p)] = dot_nt(attended[self.flat(by, p), :], proj[...]).astype(
                jnp.bfloat16
            )
            first.start(by, p)
        own_part[...] = dot_nt(attended[pl.ds(0, self.own), :], proj[...])
        if tick:
            tick()
        second = self.spread_stage(inputs, 1)
        for p in range(self.pieces):
            at = self.at(p)
            self.arrive_all(first, p)
            value = self.total(own_part, landed, p)
            branch[at] = value
            value = residual[at].astype(jnp.float32) + self.modulation(table, owner, 2, p) * value
            middle[at] = value
            unit, scale = normalize(value)
            normed[at] = unit
            inverse[at] = scale
            inputs[0, at] = (
                unit * (1.0 + self.modulation(table, owner, 4, p))
                + self.modulation(table, owner, 3, p)
            ).astype(jnp.bfloat16)
            self.send_all(second, p)
        return first, second

    def gate_up(self, inputs, gu, out, hidden, by, begin, rows):
        flat = pl.ds(by * self.own + begin, rows)
        size = tile_of(self.units)

        def body(step, at):
            far = pl.ds(pl.multiple_of(self.units + at, 128), size)
            value = inputs[by, pl.ds(begin, rows)]
            gate = dot_nn(value, gu[:, pl.ds(at, size)])
            up = dot_nn(value, gu[:, far])
            out[flat, pl.ds(at, size)] = gate
            out[flat, far] = up
            hidden[flat, pl.ds(at, size)] = (jax.nn.silu(gate) * up).astype(jnp.bfloat16)

        tiles(self.units, size, body)

    def hidden_back(self, grads, down, gate_up, ggu, by, begin, rows):
        flat = pl.ds(by * self.own + begin, rows)
        size = tile_of(self.units)

        def body(step, at):
            far = pl.ds(pl.multiple_of(self.units + at, 128), size)
            gate = gate_up[flat, pl.ds(at, size)]
            up = gate_up[flat, far]
            grad = dot_nn(grads[by, pl.ds(begin, rows)], down[:, pl.ds(at, size)])
            logistic = jax.nn.sigmoid(gate)
            ggu[flat, pl.ds(at, size)] = (
                grad * up * logistic * (1.0 + gate * (1.0 - logistic))
            ).astype(jnp.bfloat16)
            ggu[flat, far] = (grad * gate * logistic).astype(jnp.bfloat16)

        tiles(self.units, size, body)


def mlp_kernel(row_size, head_size, pieces, count, which, *refs):
    attended, residual, owner, table, following = refs[:5]
    streams, shards = refs[5:8], [ref.at[which] for ref in refs[8 : 8 + count]]
    refs = refs[8 + count :]
    kept_out, refs = refs[:5], refs[5:]
    inverse, mlp_out, result, next_normed, next_inverse, next_out = refs[:6]
    gathered, refs = refs[6 : 6 + count], refs[6 + count :]
    weights, kept = refs[:3], refs[3:8]
    proj, gu, down = weights
    branch, normed, inputs, gate_up, hidden = kept
    parcel, landed, middle, own_part, next_all = refs[8:13]
    loads, stores, sends, recvs, gather_send, gather_recv, gather_keep = refs[13:]
    place = Place(row_size, head_size)
    own, width = residual.shape
    units = hidden.shape[1]
    work = Mlp(place, pieces, own, width, units, sends, recvs)
    copies = [
        pltpu.make_async_copy(source, target, loads.at[i])
        for i, (source, target) in enumerate(zip(streams, weights))
    ]
    out_copies = [
        pltpu.make_async_copy(source, target, stores.at[i])
        for i, (source, target) in enumerate(zip(kept, kept_out))
    ]
    items = [
        Gather(place, shards[i], gathered[i], gather_send.at[i], gather_recv.at[i], gather_keep.at[i])
        for i in range(count)
    ]
    for copy in copies:
        copy.start()
    place.greet(True)
    for item in items:
        item.begin()

    def hop(k):
        for item in items:
            item.first(k)

    copies[0].wait()
    first, second = work.front(
        attended,
        proj,
        residual,
        table,
        owner,
        parcel.at[0],
        landed.at[0],
        own_part,
        branch,
        middle,
        normed,
        inverse,
        inputs,
        lambda: hop(1),
    )
    hop(2)
    out_copies[0].start()
    out_copies[1].start()
    copies[1].wait()
    work.gate_up(inputs, gu, gate_up, hidden, 0, 0, own)
    for k in range(3, place.sizes[0]):
        hop(k)
    copies[2].wait()
    third = work.sum_stage(parcel.at[1], landed.at[1], 2)
    for by, p in work.others:
        second.arrived(by, p)
        work.gate_up(inputs, gu, gate_up, hidden, by, p * work.rows, work.rows)
        work.partial(parcel.at[1, by - 1, work.at(p)], hidden, work.flat(by, p), down)
        third.start(by, p)
    for copy in out_copies[2:]:
        copy.start()
    work.partial(own_part, hidden, pl.ds(0, own), down)
    for item in items:
        item.second()
    fourth = work.spread_stage(next_all, 3)
    for p in range(pieces):
        at = work.at(p)
        work.arrive_all(third, p)
        value = work.total(own_part, landed.at[1], p)
        mlp_out[at] = value
        value = middle[at] + work.modulation(table, owner, 5, p) * value
        result[at] = value
        unit, scale = normalize(value)
        next_normed[at] = unit
        next_inverse[at] = scale
        next_all[0, at] = (
            unit * (1.0 + work.modulation(following, owner, 1, p))
            + work.modulation(following, owner, 0, p)
        ).astype(jnp.bfloat16)
        work.send_all(fourth, p)
    next_out[0] = next_all[0]
    for by, p in work.others:
        fourth.arrived(by, p)
        next_out[by, work.at(p)] = next_all[by, work.at(p)]
    for item in items:
        item.finish()
    for stage in (first, second, third, fourth):
        stage.left()
    for copy in out_copies:
        copy.wait()


def pieces_of(own):
    return 2 if own % 32 == 0 else 1


def mlp_call(row_size, head_size, attended, residual, owner, table, following, weights, which, shards):
    own, width = residual.shape
    tokens = attended.shape[0]
    units = weights[2].shape[1]
    count = len(shards)
    pieces = pieces_of(own)
    others = head_size - 1
    copies = gather_count(row_size)
    anywhere = pl.BlockSpec(memory_space=pl.ANY)
    vmem = pl.BlockSpec(memory_space=pltpu.VMEM)
    shape = jax.ShapeDtypeStruct
    f32, bf16 = jnp.float32, jnp.bfloat16
    kept = [
        shape((own, width), f32),
        shape((own, width), f32),
        shape((head_size, own, width), bf16),
        shape((tokens, 2 * units), f32),
        shape((tokens, units), bf16),
    ]
    return pl.pallas_call(
        functools.partial(mlp_kernel, row_size, head_size, pieces, count, which),
        out_shape=kept
        + [
            shape((own, 1), f32),
            shape((own, width), f32),
            shape((own, width), f32),
            shape((own, width), f32),
            shape((own, 1), f32),
            shape((head_size, own, width), bf16),
        ]
        + [shape((row_size,) + item.shape[1:], item.dtype) for item in shards],
        in_specs=[vmem] * 5 + [anywhere] * (3 + count),
        out_specs=[anywhere] * 5 + [vmem] * 6 + [anywhere] * count,
        scratch_shapes=[pltpu.VMEM(item.shape, item.dtype) for item in weights]
        + [pltpu.VMEM(item.shape, item.dtype) for item in kept]
        + [
            pltpu.VMEM((2, others, own, width), bf16),
            pltpu.VMEM((2, others, own, width), bf16),
            pltpu.VMEM((own, width), f32),
            pltpu.VMEM((own, width), f32),
            pltpu.VMEM((head_size, own, width), bf16),
            pltpu.SemaphoreType.DMA((3,)),
            pltpu.SemaphoreType.DMA((5,)),
            pltpu.SemaphoreType.DMA((4 * others * pieces,)),
            pltpu.SemaphoreType.DMA((4 * others * pieces,)),
            pltpu.SemaphoreType.DMA((count, copies)),
            pltpu.SemaphoreType.DMA((count, copies)),
            pltpu.SemaphoreType.DMA((count,)),
        ],
        compiler_params=pltpu.CompilerParams(
            collective_id=4, has_side_effects=True, vmem_limit_bytes=60 * 2**20
        ),
        name="mlp",
    )(attended, residual, owner, table, following, *weights, *shards)


def mlp_back_kernel(row_size, head_size, pieces, count, *refs):
    incoming, owner, table, normed, inverse = refs[:5]
    streams = refs[5:11]
    grads = refs[11 : 11 + count]
    outs = refs[11 + count : 17 + 2 * count]
    grad_in, grad_mid, branch_out, grad_att, gu_out, down_out = outs[:6]
    sums = outs[6:]
    refs = refs[17 + 2 * count :]
    down, gate_up, gu, inputs, hidden, proj = refs[:6]
    mlp_all, branch_all, ggu, parcel, landed, own_part, buffer = refs[6:13]
    loads, sends, recvs, tile_sems, out_sem = refs[13:18]
    scratch = refs[18 : 18 + 4 * count]
    sum_send, sum_recv, sum_load = refs[18 + 4 * count :]
    place = Place(row_size, head_size)
    own, width = incoming.shape
    units = hidden.shape[1]
    work = Mlp(place, pieces, own, width, units, sends, recvs)
    step_units = tile_of(units)
    copies = [
        pltpu.make_async_copy(source, target, loads.at[i])
        for i, (source, target) in enumerate(
            zip(streams, (down, gate_up, gu, inputs, hidden, proj))
        )
    ]
    for copy in copies:
        copy.start()
    place.greet(True)
    first = work.spread_stage(mlp_all, 0)
    for p in range(pieces):
        at = work.at(p)
        mlp_all[0, at] = (work.modulation(table, owner, 5, p) * incoming[at]).astype(jnp.bfloat16)
        work.send_all(first, p)
    items = [
        Scatter(
            place,
            grads[i],
            sums[i],
            *scratch[4 * i : 4 * i + 4],
            sum_send.at[i],
            sum_recv.at[i],
            sum_load.at[i],
        )
        for i in range(count)
    ]
    for item in items:
        item.begin()
    copies[0].wait()
    copies[1].wait()
    work.hidden_back(mlp_all, down, gate_up, ggu, 0, 0, own)
    for item in items:
        item.first()
    copies[2].wait()
    second = work.sum_stage(parcel, landed, 1)
    for by, p in work.others:
        first.arrived(by, p)
        work.hidden_back(mlp_all, down, gate_up, ggu, by, p * work.rows, work.rows)
        work.partial(parcel.at[by - 1, work.at(p)], ggu, work.flat(by, p), gu)
        second.start(by, p)
    work.partial(own_part, ggu, pl.ds(0, own), gu)
    copies[3].wait()
    out = Streamed(buffer, gu_out, tile_sems, step_units)

    def body(step, at):
        out.put(step, dot_tn(inputs[...], ggu[:, pl.ds(at, step_units)]))

    tiles(2 * units, step_units, body)
    for item in items[:1]:
        item.second()
    third = work.spread_stage(branch_all, 2)
    for p in range(pieces):
        at = work.at(p)
        work.arrive_all(second, p)
        value = work.total(own_part, landed, p)
        grad_in[at] = value
        unit = normed[at]
        value = value * (1.0 + work.modulation(table, owner, 4, p))
        value = incoming[at] + inverse[at] * (
            value
            - jnp.mean(value, axis=-1, keepdims=True)
            - unit * jnp.mean(value * unit, axis=-1, keepdims=True)
        )
        grad_mid[at] = value
        branch_all[0, at] = (work.modulation(table, owner, 2, p) * value).astype(jnp.bfloat16)
        work.send_all(third, p)
    out.drain(2 * units // step_units)
    copies[4].wait()
    copies[5].wait()
    out = Streamed(buffer, down_out, tile_sems, step_units)

    def body(step, at):
        out.put(
            step,
            dot_tn(mlp_all[...].reshape(head_size * own, width), hidden[:, pl.ds(at, step_units)]),
        )

    tiles(units, step_units, body)
    for item in items[1:]:
        item.second()
    grad_att[pl.ds(0, own), :] = dot_nn(branch_all[0], proj[...]).astype(jnp.bfloat16)
    for by, p in work.others:
        third.arrived(by, p)
        grad_att[work.flat(by, p), :] = dot_nn(branch_all[by, work.at(p)], proj[...]).astype(
            jnp.bfloat16
        )
    keep = pltpu.make_async_copy(branch_all, branch_out, out_sem.at[0])
    keep.start()
    out.drain(units // step_units)
    for item in items:
        item.finish()
    for stage in (first, second, third):
        stage.left()
    keep.wait()


def mlp_back_call(row_size, head_size, near, streams, grads):
    count = len(grads)
    own, width = near[0].shape
    pieces = pieces_of(own)
    others = head_size - 1
    down, gate_up, gu, inputs, hidden, proj = streams
    units = hidden.shape[1]
    tokens = hidden.shape[0]
    a, b = 4, row_size // 8
    copies = scatter_count(row_size)
    scratch = []
    for grad in grads:
        chunk = grad.shape[1:]
        for lead in ((a, b), (a, b), (b - 1, a), (a - 1,)):
            scratch.append(pltpu.VMEM(lead + chunk, grad.dtype))
    anywhere = pl.BlockSpec(memory_space=pl.ANY)
    vmem = pl.BlockSpec(memory_space=pltpu.VMEM)
    shape = jax.ShapeDtypeStruct
    f32, bf16 = jnp.float32, jnp.bfloat16
    return pl.pallas_call(
        functools.partial(mlp_back_kernel, row_size, head_size, pieces, count),
        out_shape=[
            shape((own, width), f32),
            shape((own, width), f32),
            shape((head_size, own, width), bf16),
            shape((tokens, proj.shape[1]), bf16),
            shape((width, 2 * units), bf16),
            shape((width, units), bf16),
        ]
        + [shape(grad.shape[1:], f32) for grad in grads],
        in_specs=[vmem] * 5 + [anywhere] * (6 + count),
        out_specs=[vmem, vmem, anywhere, vmem, anywhere, anywhere] + [vmem] * count,
        scratch_shapes=[pltpu.VMEM(item.shape, item.dtype) for item in streams]
        + [
            pltpu.VMEM((head_size, own, width), bf16),
            pltpu.VMEM((head_size, own, width), bf16),
            pltpu.VMEM((tokens, 2 * units), bf16),
            pltpu.VMEM((others, own, width), bf16),
            pltpu.VMEM((others, own, width), bf16),
            pltpu.VMEM((own, width), f32),
            pltpu.VMEM((2, width, tile_of(units)), bf16),
            pltpu.SemaphoreType.DMA((6,)),
            pltpu.SemaphoreType.DMA((3 * others * pieces,)),
            pltpu.SemaphoreType.DMA((3 * others * pieces,)),
            pltpu.SemaphoreType.DMA((2,)),
            pltpu.SemaphoreType.DMA((1,)),
        ]
        + scratch
        + [
            pltpu.SemaphoreType.DMA((count, copies)),
            pltpu.SemaphoreType.DMA((count, copies)),
            pltpu.SemaphoreType.DMA((count, a * b)),
        ],
        compiler_params=pltpu.CompilerParams(
            collective_id=3, has_side_effects=True, vmem_limit_bytes=62 * 2**20
        ),
        name="mlp_back",
    )(*near, *streams, *grads)


def last_mlp_kernel(row_size, head_size, pieces, *refs):
    attended, residual, owner, table, incoming, mlp_grads = refs[:6]
    streams, refs = refs[6:9], refs[9:]
    block_out, branch, normed, mlp_out, grad_in, grad_mid, branch_out, grad_att = refs[:8]
    grads_out = refs[8]
    weights, refs = refs[9:12], refs[12:]
    proj, gu, down = weights
    inputs, gate_up, hidden, ggu, branch_all, parcel, landed = refs[:7]
    middle, inverse, own_part, own_mlp, buffer = refs[7:12]
    loads, sends, recvs, tile_sems, out_sem = refs[12:]
    place = Place(row_size, head_size)
    own, width = residual.shape
    units = hidden.shape[1]
    work = Mlp(place, pieces, own, width, units, sends, recvs)
    step_units = tile_of(units)
    copies = [
        pltpu.make_async_copy(source, target, loads.at[i])
        for i, (source, target) in enumerate(zip(streams, weights))
    ]
    for copy in copies:
        copy.start()
    place.greet(True)
    copies[0].wait()
    first, second = work.front(
        attended,
        proj,
        residual,
        table,
        owner,
        parcel.at[0],
        landed.at[0],
        own_part,
        branch,
        middle,
        normed,
        inverse,
        inputs,
    )
    copies[1].wait()
    copies[2].wait()
    work.gate_up(inputs, gu, gate_up, hidden, 0, 0, own)
    work.hidden_back(mlp_grads, down, gate_up, ggu, 0, 0, own)
    fourth = work.sum_stage(parcel.at[1], landed.at[1], 3)
    for by, p in work.others:
        second.arrived(by, p)
        begin = p * work.rows
        work.gate_up(inputs, gu, gate_up, hidden, by, begin, work.rows)
        work.hidden_back(mlp_grads, down, gate_up, ggu, by, begin, work.rows)
        work.partial(parcel.at[1, by - 1, work.at(p)], ggu, work.flat(by, p), gu)
        fourth.start(by, p)
    work.partial(own_part, ggu, pl.ds(0, own), gu)
    out = Streamed(buffer, grads_out, tile_sems, step_units)

    def body(step, at):
        out.put(
            step,
            dot_tn(inputs[...].reshape(head_size * own, width), ggu[:, pl.ds(at, step_units)]),
        )

    tiles(2 * units, step_units, body)
    fifth = work.spread_stage(branch_all, 4)
    for p in range(pieces):
        at = work.at(p)
        work.arrive_all(fourth, p)
        value = work.total(own_part, landed.at[1], p)
        grad_in[at] = value
        unit = normed[at]
        value = value * (1.0 + work.modulation(table, owner, 4, p))
        value = incoming[at].astype(jnp.float32) + inverse[at] * (
            value
            - jnp.mean(value, axis=-1, keepdims=True)
            - unit * jnp.mean(value * unit, axis=-1, keepdims=True)
        )
        grad_mid[at] = value
        branch_all[0, at] = (work.modulation(table, owner, 2, p) * value).astype(jnp.bfloat16)
        work.send_all(fifth, p)
    first.left()
    third = work.sum_stage(parcel.at[0], landed.at[0], 2)
    for by, p in work.others:
        work.partial(parcel.at[0, by - 1, work.at(p)], hidden, work.flat(by, p), down)
        third.start(by, p)
    work.partial(own_mlp, hidden, pl.ds(0, own), down)
    out.drain(2 * units // step_units)
    out = Streamed(buffer, grads_out, tile_sems, step_units, 2 * units)

    def body(step, at):
        out.put(
            step,
            dot_tn(mlp_grads[...].reshape(head_size * own, width), hidden[:, pl.ds(at, step_units)]),
        )

    tiles(units, step_units, body)
    grad_att[pl.ds(0, own), :] = dot_nn(branch_all[0], proj[...]).astype(jnp.bfloat16)
    for by, p in work.others:
        fifth.arrived(by, p)
        grad_att[work.flat(by, p), :] = dot_nn(branch_all[by, work.at(p)], proj[...]).astype(
            jnp.bfloat16
        )
    keep = pltpu.make_async_copy(branch_all, branch_out, out_sem.at[0])
    keep.start()
    for p in range(pieces):
        at = work.at(p)
        work.arrive_all(third, p)
        value = work.total(own_mlp, landed.at[0], p)
        mlp_out[at] = value
        block_out[at] = (middle[at] + work.modulation(table, owner, 5, p) * value).astype(
            jnp.bfloat16
        )
    out.drain(units // step_units)
    for stage in (second, third, fourth, fifth):
        stage.left()
    keep.wait()


def last_mlp_call(row_size, head_size, attended, residual, owner, table, incoming, mlp_grads, weights):
    own, width = residual.shape
    tokens = attended.shape[0]
    units = weights[2].shape[1]
    pieces = pieces_of(own)
    others = head_size - 1
    anywhere = pl.BlockSpec(memory_space=pl.ANY)
    vmem = pl.BlockSpec(memory_space=pltpu.VMEM)
    shape = jax.ShapeDtypeStruct
    f32, bf16 = jnp.float32, jnp.bfloat16
    return pl.pallas_call(
        functools.partial(last_mlp_kernel, row_size, head_size, pieces),
        out_shape=[
            shape((own, width), bf16),
            shape((own, width), f32),
            shape((own, width), f32),
            shape((own, width), f32),
            shape((own, width), f32),
            shape((own, width), f32),
            shape((head_size, own, width), bf16),
            shape(attended.shape, bf16),
            shape((width, 3 * units), bf16),
        ],
        in_specs=[vmem] * 6 + [anywhere] * 3,
        out_specs=[vmem] * 6 + [anywhere, vmem, anywhere],
        scratch_shapes=[pltpu.VMEM(item.shape, item.dtype) for item in weights]
        + [
            pltpu.VMEM((head_size, own, width), bf16),
            pltpu.VMEM((tokens, 2 * units), f32),
            pltpu.VMEM((tokens, units), bf16),
            pltpu.VMEM((tokens, 2 * units), bf16),
            pltpu.VMEM((head_size, own, width), bf16),
            pltpu.VMEM((2, others, own, width), bf16),
            pltpu.VMEM((2, others, own, width), bf16),
            pltpu.VMEM((own, width), f32),
            pltpu.VMEM((own, 1), f32),
            pltpu.VMEM((own, width), f32),
            pltpu.VMEM((own, width), f32),
            pltpu.VMEM((2, width, tile_of(units)), bf16),
            pltpu.SemaphoreType.DMA((3,)),
            pltpu.SemaphoreType.DMA((5 * others * pieces,)),
            pltpu.SemaphoreType.DMA((5 * others * pieces,)),
            pltpu.SemaphoreType.DMA((2,)),
            pltpu.SemaphoreType.DMA((1,)),
        ],
        compiler_params=pltpu.CompilerParams(
            collective_id=5, has_side_effects=True, vmem_limit_bytes=60 * 2**20
        ),
        name="last_mlp",
    )(attended, residual, owner, table, incoming, mlp_grads, *weights)


def rope_parts(coords):
    angle = angles(coords, HD // 4)
    return jnp.cos(angle), jnp.sin(angle)


def turn(vectors, geometry, sign):
    row_cos, row_sin, col_cos, col_sin = [item[:, :, None, :] for item in geometry]
    quarter = HD // 4
    a, b, c, d = [vectors[..., quarter * i : quarter * (i + 1)] for i in range(4)]
    return jnp.concatenate(
        [
            a * row_cos - b * (sign * row_sin),
            b * row_cos + a * (sign * row_sin),
            c * col_cos - d * (sign * col_sin),
            d * col_cos + c * (sign * col_sin),
        ],
        axis=-1,
    )


def masked_scores(queries, key_rows, image_ids):
    scores = jnp.einsum(
        "rqhe,rkhe->rhqk", queries, key_rows, preferred_element_type=jnp.float32
    ) * HD ** (-0.5)
    same_image = image_ids[:, :, None] == image_ids[:, None, :]
    return jnp.where(same_image[:, None], scores, -1e30)


def attend(queries, key_rows, value_rows, image_ids):
    scores = masked_scores(queries, key_rows, image_ids)
    maximum = jnp.max(scores, axis=-1, keepdims=True)
    scaled_exp = jnp.exp(scores - maximum)
    denominator = jnp.sum(scaled_exp, axis=-1, keepdims=True)
    weights = (scaled_exp / denominator).astype(jnp.bfloat16)
    attended = jnp.einsum("rhqk,rkhe->rqhe", weights, value_rows, preferred_element_type=jnp.float32)
    return (attended.astype(jnp.bfloat16), (maximum + jnp.log(denominator))[..., 0])


def attend_back(queries, key_rows, value_rows, image_ids, logsum, grad_attended):
    score_scale = HD ** (-0.5)
    probs = jnp.exp(masked_scores(queries, key_rows, image_ids) - logsum[..., None])
    weights = probs.astype(jnp.bfloat16)
    grad_value = jnp.einsum(
        "rhqk,rqhe->rkhe", weights, grad_attended, preferred_element_type=jnp.float32
    )
    grad_probs = jnp.einsum(
        "rqhe,rkhe->rhqk", grad_attended, value_rows, preferred_element_type=jnp.float32
    )
    inner_sum = jnp.sum(probs * grad_probs, axis=-1, keepdims=True)
    grad_scores = (probs * (grad_probs - inner_sum)).astype(jnp.bfloat16)
    grad_query = (
        jnp.einsum("rhqk,rkhe->rqhe", grad_scores, key_rows, preferred_element_type=jnp.float32)
        * score_scale
    )
    grad_key = (
        jnp.einsum("rhqk,rqhe->rkhe", grad_scores, queries, preferred_element_type=jnp.float32)
        * score_scale
    )
    return (grad_query, grad_key, grad_value)


def spread(values):
    arrived = [head_move(values, flip) for flip in range(1, lax.axis_size("heads"))]
    return jnp.concatenate([values] + arrived, axis=0)


def collect(part, beside):
    arrived = [
        head_move(part(flip, jnp.bfloat16), flip) for flip in range(1, lax.axis_size("heads"))
    ]
    total = part(0, jnp.float32)
    total, arrived, beside = lax.optimization_barrier((total, arrived, beside))
    for item in arrived:
        total = total + item.astype(jnp.float32)
    return total, beside


def plain_dot(operand, other):
    return jnp.dot(operand, other, preferred_element_type=jnp.float32)


def piece_of(mods, picks, index):
    width = mods.shape[1] // 6
    value = mods[:, index * width : (index + 1) * width]
    total = jnp.zeros((picks.shape[0], width), jnp.float32)
    for image in range(mods.shape[0]):
        total = jnp.where(picks[:, None] == image, value[image][None, :], total)
    return total


def attention(input_attn, qkv_full, qkv_b, image_ids, geometry):
    count_rows, row_len = image_ids.shape
    packed = plain_dot(input_attn, qkv_full) + qkv_b
    heads_here = packed.shape[1] // (3 * HD)
    packed = packed.reshape(count_rows, row_len, heads_here, 3, HD)
    queries = turn(packed[:, :, :, 0], geometry, 1.0).astype(jnp.bfloat16)
    key_rows = turn(packed[:, :, :, 1], geometry, 1.0).astype(jnp.bfloat16)
    value_rows = packed[:, :, :, 2].astype(jnp.bfloat16)
    attended, logsum = attend(queries, key_rows, value_rows, image_ids)
    attended = attended.reshape(count_rows * row_len, heads_here * HD)
    return attended, (queries, key_rows, value_rows, logsum)


def attention_back(grad_attended, stored, image_ids, geometry):
    queries, key_rows, value_rows, logsum = stored
    count_rows, row_len = image_ids.shape
    heads_here = queries.shape[2]
    grad_attended = grad_attended.reshape(count_rows, row_len, heads_here, HD)
    grad_query, grad_key, grad_value = attend_back(
        queries, key_rows, value_rows, image_ids, logsum, grad_attended
    )
    grad_query = turn(grad_query, geometry, -1.0)
    grad_key = turn(grad_key, geometry, -1.0)
    grad_packed = (
        jnp.stack([grad_query, grad_key, grad_value], axis=3)
        .reshape(count_rows * row_len, heads_here * 3 * HD)
        .astype(jnp.bfloat16)
    )
    return grad_packed, jnp.sum(grad_packed, axis=0, dtype=jnp.float32)


def image_sum(picker, values):
    return lax.dot_general(picker, values, (((0,), (0,)), ((), ())), precision=lax.Precision.HIGH)


def shards(
    tokens,
    cond,
    image_of,
    grid_row,
    grid_col,
    ada_weight,
    ada_bias,
    qkv_weight,
    qkv_bias,
    proj_weight,
    gu_weight,
    down_weight,
    cotangent,
):
    own_rows = tokens.shape[0]
    image_count = cond.shape[0]
    block_count = qkv_weight.shape[0]
    row_size = lax.axis_size("rows")
    head_size = lax.axis_size("heads")
    head_index = lax.axis_index("heads")

    def device_order(values):
        parts = values.reshape(head_size, own_rows)
        picked = [
            lax.dynamic_index_in_dim(parts, head_index ^ flip, 0, keepdims=False)
            for flip in range(head_size)
        ]
        return jnp.concatenate(picked).reshape(values.shape)

    image_ids = device_order(image_of - lax.axis_index("rows") * image_count)
    own_images = image_ids.reshape(-1)[:own_rows]
    picker = (own_images[:, None] == jnp.arange(image_count, dtype=jnp.int32)[None, :]).astype(
        jnp.float32
    )
    geometry = lax.optimization_barrier(
        rope_parts(device_order(grid_row)) + rope_parts(device_order(grid_col))
    )
    shard_rows = qkv_weight.shape[1]

    def gathered(shard):
        return lax.all_gather(shard, "rows", axis=0, tiled=True)

    cond_wide = cond.astype(jnp.float32)
    cond_act = jax.nn.silu(cond_wide).astype(jnp.bfloat16)
    pad = -image_count % 16
    bias_rows = jnp.repeat(ada_bias.astype(jnp.float32), image_count, axis=0)
    proj_flat, down_flat = proj_weight.transpose(0, 2, 1), down_weight.transpose(0, 2, 1)
    *early, table, cond_mine, input_attn, normed, inverse, mlp_grads = start_call(
        row_size,
        head_size,
        jnp.pad(cond_act, ((0, pad), (0, 0))),
        ada_weight,
        bias_rows,
        tokens,
        cotangent,
        image_ids.reshape(-1, 1),
        [qkv_weight, proj_flat, down_flat],
    )
    qkv_full, proj_t, down_t = [[item.reshape(-1, item.shape[-1])] for item in early]
    gu_full = [gathered(item.reshape(shard_rows, -1)) for item in gu_weight]
    for b in range(1, block_count):
        down_t.append(gathered(down_flat[b]))
    modulation = [table[b * image_count : (b + 1) * image_count] for b in range(block_count)]
    last = block_count - 1
    owner = own_images[:, None]
    input_attn = input_attn.reshape(-1, input_attn.shape[-1])
    normed_attn, inverse_attn = [normed], [inverse]
    inputs_attn = [input_attn]
    residual = tokens
    attentions, attended = [], []
    for b in range(block_count):
        item, kept = attention(
            inputs_attn[b], qkv_full[b], qkv_bias[b].astype(jnp.float32), image_ids, geometry
        )
        attended.append(item)
        attentions.append(kept)
        weights = (proj_t[b], gu_full[b], down_t[b])
        if b < last:
            (
                branch,
                normed_mlp,
                input_mlp,
                gate_up,
                hidden,
                inverse_mlp,
                mlp_out,
                residual,
                next_normed,
                next_inverse,
                next_input,
                next_qkv,
                next_proj,
            ) = mlp_call(
                row_size,
                head_size,
                item,
                residual,
                owner,
                modulation[b],
                modulation[b + 1],
                weights,
                b + 1,
                [qkv_weight, proj_flat],
            )
            normed_attn.append(next_normed)
            inverse_attn.append(next_inverse)
            inputs_attn.append(next_input.reshape(inputs_attn[0].shape))
            qkv_full.append(next_qkv.reshape(qkv_full[0].shape))
            proj_t.append(next_proj.reshape(proj_t[0].shape))
            stored = (branch, normed_mlp, input_mlp, gate_up, hidden, inverse_mlp, mlp_out)
    (
        block_out,
        last_branch,
        last_normed,
        last_out,
        grad_input_mlp,
        grad_middle,
        gathered_branch,
        grad_attended,
        mlp_grad,
    ) = last_mlp_call(
        row_size,
        head_size,
        attended[last],
        residual,
        owner,
        modulation[last],
        cotangent,
        mlp_grads,
        weights,
    )

    def scattered(grad):
        return lax.psum_scatter(grad, "rows", scatter_dimension=0, tiled=True)

    def late_sums(middle, branch, incoming, normed, grad, out):
        return [
            image_sum(picker, item)
            for item in (middle * branch, grad, grad * normed, incoming * out)
        ]

    gu_outs, bias_sums, image_sums = [None] * 2, [None] * 2, [None] * 2
    mlp_sum = scattered(mlp_grad)
    units = mlp_sum.shape[1] // 3
    gathered_branch = gathered_branch.reshape(-1, gathered_branch.shape[-1])
    grad_packed, bias_sums[1] = attention_back(grad_attended, attentions[1], image_ids, geometry)
    qkv_grad, proj_grad = weight_grads(
        (inputs_attn[1], grad_packed), (gathered_branch, attended[1])
    )
    late = late_sums(
        grad_middle,
        last_branch,
        cotangent.astype(jnp.float32),
        last_normed,
        grad_input_mlp,
        last_out,
    )
    grad_input_attn, (qkv_grad, proj_grad, late) = collect(
        lambda slot, dtype: head_part(grad_packed, qkv_full[1], own_rows, slot, dtype),
        (qkv_grad, proj_grad, late),
    )
    scale = piece_of(modulation[1], own_images, 1)
    incoming = grad_middle + norm_back(
        grad_input_attn * (1.0 + scale), normed_attn[1], inverse_attn[1]
    )
    image_sums[1] = jnp.concatenate(
        [
            image_sum(picker, grad_input_attn),
            image_sum(picker, grad_input_attn * normed_attn[1]),
        ]
        + late,
        axis=1,
    )
    branch, normed_mlp, input_mlp, gate_up, hidden, inverse_mlp, mlp_out = stored
    block_sums = [None] * 2
    (
        grad_input_mlp,
        grad_middle,
        gathered_branch,
        grad_attended,
        gu_grad,
        down_grad,
        *block_sums[1],
    ) = mlp_back_call(
        row_size,
        head_size,
        (
            incoming,
            owner,
            modulation[0],
            normed_mlp,
            inverse_mlp,
        ),
        (
            down_t[0],
            gate_up,
            gu_full[0],
            input_mlp.reshape(-1, input_mlp.shape[-1]),
            hidden,
            proj_t[0],
        ),
        [item.reshape(row_size, shard_rows, -1) for item in (qkv_grad, proj_grad)],
    )
    gathered_branch = gathered_branch.reshape(-1, gathered_branch.shape[-1])
    grad_packed, bias_sums[0] = attention_back(grad_attended, attentions[0], image_ids, geometry)
    grad_packed, mlp_sum, gu_grad = lax.optimization_barrier((grad_packed, mlp_sum, gu_grad))
    gu_outs[0] = scattered(gu_grad)
    late = late_sums(grad_middle, branch, incoming, normed_mlp, grad_input_mlp, mlp_out)
    image_sums[0] = jnp.concatenate([jnp.zeros_like(late[0])] * 2 + late, axis=1)
    gu_outs[1] = mlp_sum[:, : 2 * units]
    sheets = jnp.stack(image_sums).reshape(block_count * image_count, head_size, -1)
    sheets = sheets.transpose(1, 0, 2)
    wide = sheets.shape[-1]
    bias_sums = jnp.stack(bias_sums)
    bias_high = bias_sums.astype(jnp.bfloat16).astype(jnp.float32)
    bias_rest = bias_sums - bias_high
    bias_middle = bias_rest.astype(jnp.bfloat16).astype(jnp.float32)
    bias_parts = jnp.stack([bias_high, bias_middle, bias_rest - bias_middle], axis=1)
    bias_parts = jnp.pad(bias_parts, ((0, 0), (0, 0), (0, wide - bias_sums.shape[1])))
    bias_parts = bias_parts.reshape(-1, wide)
    used = sheets.shape[1] + bias_parts.shape[0]
    small_rows = used + -used % 16
    bias_parts = jnp.pad(bias_parts, ((sheets.shape[1], small_rows - used), (0, 0)))
    cond_rows = cond_mine.reshape(row_size, -1, shard_rows)[:, :image_count]
    row = jnp.arange(small_rows)
    mine = []
    for b in range(block_count):
        first = b * image_count
        lead = jnp.pad(cond_rows, ((0, 0), (first, small_rows - first - image_count), (0, 0)))
        is_image = (row >= first) & (row < first + image_count)
        start = block_count * image_count + 3 * b
        is_bias = (row >= start) & (row < start + 3)
        ones = jnp.stack([is_image, is_bias], axis=1).astype(jnp.bfloat16)
        ones = jnp.broadcast_to(ones[None], (row_size,) + ones.shape)
        both = jnp.concatenate([lead, ones], axis=2)
        both = jnp.pad(both, ((0, 0), (0, 0), (0, -both.shape[2] % 128)))
        mine.append(both.reshape(-1, both.shape[2]))
    logistic = jax.nn.sigmoid(cond_wide)
    factor = logistic * (1.0 + cond_wide * (1.0 - logistic))
    factor = jnp.pad(factor, ((0, -image_count % 8), (0, 0)))
    tokens_grad, ada_grads, ada_bias_grads, qkv_bias_out, cond_grad, *stacked = finish_call(
        row_size,
        head_size,
        image_count,
        (
            grad_packed,
            qkv_full[0],
            inputs_attn[0],
            attended[0],
            gathered_branch,
            grad_middle,
            piece_of(modulation[0], own_images, 1),
            normed_attn[0],
            inverse_attn[0],
            owner,
        ),
        sheets,
        bias_parts,
        jnp.stack(mine),
        ada_weight,
        factor,
        [mlp_sum[:, 2 * units :]] + block_sums[1],
        down_grad.reshape(row_size, shard_rows, -1),
    )
    cond_grad = cond_grad[:image_count]
    return (
        block_out,
        tokens_grad,
        cond_grad,
        ada_grads,
        ada_bias_grads,
        stacked[1],
        qkv_bias_out,
        stacked[2].transpose(0, 2, 1),
        jnp.stack([item.reshape(gu_weight.shape[1:]).astype(jnp.float32) for item in gu_outs]),
        stacked[0].transpose(0, 2, 1),
    )


def solution(mesh):
    in_specs = (
        P(("rows", "heads"), None),
        P("rows", None),
        P("rows", None),
        P("rows", None),
        P("rows", None),
        P(None, "rows", "heads"),
        P(None, "heads"),
        P(None, "rows", "heads"),
        P(None, "heads"),
        P(None, "heads", "rows"),
        P(None, "rows", None, "heads"),
        P(None, "heads", "rows"),
        P(("rows", "heads"), None),
    )
    out_specs = (
        P(("rows", "heads"), None),
        P(("rows", "heads"), None),
        P("rows", None),
        P(None, "rows", "heads"),
        P(None, "heads"),
        P(None, "rows", "heads"),
        P(None, "heads"),
        P(None, "heads", "rows"),
        P(None, "rows", None, "heads"),
        P(None, "heads", "rows"),
    )
    return jax.shard_map(shards, mesh=mesh, in_specs=in_specs, out_specs=out_specs, check_vma=False)
```
